256 devices in a mesh: space: 64 (over y, z, core), occ: 2 (over x_lo), resp: 2 (over x_hi).
Axes of the slice: x: 4 (x_hi: 2, x_lo: 2; x = x_hi * 2 + x_lo), y: 4, z: 8, core: 2. Of those that a mesh axis runs over, the one named last changes fastest.
Arguments:
- psi_occ: float32 [32, 2, 64, 240, 128], P('occ', None, 'space'), may hold values from -12 to 12
- psi_resp: float32 [8, 2, 64, 240, 128], P('resp', None, 'space'), may hold values from -16 to 16
- initial_guess: float32 [8, 2, 64, 240, 128], P('resp', None, 'space'), may hold values from -22 to 22
- local_potential: float32 [64, 240, 128], P('space'), may hold values from 0.8 to 2.5
- potential_change: float32 [2, 64, 240, 128], P(None, 'space'), may hold values from 0.2 to 1.2
- band_energy: float32 [8], P('resp'), may hold values from -0.5 to 0.5
- q_index: int32 [3], replicated, may hold values from 1 to 7
- atom_cells: int32 [1536, 3], P('space'), may hold values from 0 to 239, as said below
- offsets: int32 [128, 3], replicated, may hold values from -4 to 4, as said below
- projector: float32 [1536, 128], P('space'), may hold values from -1.2 to 1.2
- strength: float32 [1536], P('space'), may hold values from 0.5 to 2
Outputs:
- response: float32 [8, 2, 64, 240, 128], P('resp', None, 'space')
- residual: float32 [8, 2, 64, 240, 128], P('resp', None, 'space')
The draws below stay inside these ranges and needn't reach their ends.
Inputs may be any that keep to these rules, and one draw needn't show every extreme that they name: `atom_cells`: atom i has its z cell among the 1 planes numbered from (i // 24); its x cell is below 240 and its y cell below 128. The z offset is -1, 0 or 1 and takes -1 and 1; x and y offsets lie within -4 to 4 and reach both ends.
All inputs are finite; a program needn't handle non-finite values.
Results may differ from the reference program's by a relative error of at most 0.0003.
Values sent between devices are 32-bit elements; how exact they have to be, the bound alone decides.
No kernel may reach another device: no remote copies, remote signals or barrier semaphores. Data moves between devices by JAX's collectives and lax.ppermute only.
A program may use at most 128 MiB of HBM per device.

```python
import math
import jax
import jax.numpy as jnp
from jax import lax

OCC = 32
RESP = 8
CZ = 1
NX = 240
NY = 128
ATOMS_DEV = 24
PTS = 128
RAD = 4
QDIV = 8
ITERS = 2
NZ = 64
ATOMS = 1536


def band_field(key, band_number):
    noise = jax.random.normal(jax.random.fold_in(key, 1000 + band_number), (2, NZ, NX, NY), jnp.float32)
    return 0.7 * jnp.clip(noise, -5.0, 5.0)


def shared_bands(key, first_band, band_count):
    return jax.vmap(lambda band_number: band_field(key, band_number))(jnp.arange(band_count) + first_band)


def draw_psi_occ(key, part):
    bands = shared_bands(key, 0, OCC)
    return bands


def draw_psi_resp(key, part):
    bands = shared_bands(key, 0, RESP)
    key = jax.random.fold_in(key, 2)
    noise = jnp.clip(jax.random.normal(key, (RESP, 2, NZ, NX, NY), jnp.float32), -5.0, 5.0)
    return 0.8 * bands + 0.42 * noise


def draw_initial_guess(key, part):
    near_bands = shared_bands(key, RESP, RESP)
    far_bands = shared_bands(key, 2 * RESP, RESP)
    key = jax.random.fold_in(key, 3)
    noise = jnp.clip(jax.random.normal(key, (RESP, 2, NZ, NX, NY), jnp.float32), -5.0, 5.0)
    return 0.6 * (near_bands + far_bands) + 0.5 * noise


def draw_atom_cells(key, part):
    key = jax.random.fold_in(key, 4)
    key_list = jax.random.split(key, 3)
    owner = jnp.arange(ATOMS, dtype=jnp.int32) // ATOMS_DEV
    z_cell = owner * CZ + jax.random.randint(key_list[0], (ATOMS,), 0, CZ, jnp.int32)
    x_cell = jax.random.randint(key_list[1], (ATOMS,), 0, NX, jnp.int32)
    y_cell = jax.random.randint(key_list[2], (ATOMS,), 0, NY, jnp.int32)
    z_cell = z_cell.at[0].set(0).at[ATOMS - 1].set(NZ - 1)
    x_cell = x_cell.at[0].set(NX - 1)
    y_cell = y_cell.at[1].set(NY - 1)
    return jnp.stack([z_cell, x_cell, y_cell], axis=1)


def draw_offsets(key, part):
    key = jax.random.fold_in(key, 5)
    key_list = jax.random.split(key, 3)
    z_step = jax.random.randint(key_list[0], (PTS,), -1, 2, jnp.int32)
    x_step = jax.random.randint(key_list[1], (PTS,), -RAD, RAD + 1, jnp.int32)
    y_step = jax.random.randint(key_list[2], (PTS,), -RAD, RAD + 1, jnp.int32)
    z_step = z_step.at[0].set(-1).at[1].set(1)
    x_step = x_step.at[0].set(-RAD).at[1].set(RAD)
    y_step = y_step.at[0].set(RAD).at[1].set(-RAD)
    return jnp.stack([z_step, x_step, y_step], axis=1)


def steps_of(own_key, shape, cuts, low, high):
    gain = 1.0
    for position, blocks in cuts:
        heights = jax.random.uniform(jax.random.fold_in(jax.random.fold_in(own_key, 6), position), (blocks,), jnp.float32, low / len(cuts), high / len(cuts))
        gain = gain * jnp.repeat(jnp.exp(heights), shape[position] // blocks).reshape((-1,) + (1,) * (len(shape) - 1 - position))
    return gain


def normal_values(rng, shape, scale, limit, pieces=(), kind=jnp.bfloat16):
    gain = steps_of(rng, shape, pieces, -0.22, 0.18) if pieces else 1.0
    values = jax.random.normal(rng, shape, jnp.float32) * scale * gain
    return jnp.minimum(jnp.maximum(values, -limit), limit).astype(kind)


def setup_inputs(seed: int = 0) -> dict:
    arg_keys = jax.random.split(jax.random.key(seed), 12)
    return {
        "psi_occ": draw_psi_occ(jax.random.fold_in(arg_keys[11], 71), 0),
        "psi_resp": draw_psi_resp(jax.random.fold_in(arg_keys[11], 71), 0),
        "initial_guess": draw_initial_guess(jax.random.fold_in(arg_keys[11], 71), 0),
        "local_potential": jnp.clip(0.8 + 1.7 * jax.random.uniform(arg_keys[3], (NZ, NX, NY), jnp.float32) ** steps_of(arg_keys[3], (NZ, NX, NY), ((0, 64),), -0.2, 0.2), 0.8, 2.5),
        "potential_change": jnp.clip(0.2 + 1 * jax.random.uniform(arg_keys[4], (2, NZ, NX, NY), jnp.float32) ** steps_of(arg_keys[4], (2, NZ, NX, NY), ((1, 64),), -0.2, 0.2), 0.2, 1.2),
        "band_energy": jnp.clip(jax.random.uniform(arg_keys[5], (RESP,), jnp.float32, -0.5, 0.5) * steps_of(arg_keys[5], (RESP,), ((0, 2),), -0.4, 0.0), -0.5, 0.5),
        "q_index": jax.random.randint(arg_keys[6], (3,), 1, QDIV).astype(jnp.int32),
        "atom_cells": draw_atom_cells(jax.random.fold_in(arg_keys[11], 71), 0),
        "offsets": draw_offsets(jax.random.fold_in(arg_keys[11], 71), 0),
        "projector": normal_values(arg_keys[9], (ATOMS, PTS), 0.2, 1.2, ((0, 64),), jnp.float32),
        "strength": jnp.clip(jnp.exp(math.log(2.0) - 1.3862944 * jax.random.uniform(arg_keys[10], (ATOMS,), jnp.float32) ** steps_of(arg_keys[10], (ATOMS,), ((0, 64),), -0.2, 0.2)), 0.5, 2.0),
    }


SHIFT_WEIGHT = 3.0
PRECISE = lax.Precision.HIGHEST


def rotate(grid_field, cosine, sine_part):
    real_part = grid_field[:, 0]
    imag_part = grid_field[:, 1]
    return jnp.stack([real_part * cosine - imag_part * sine_part, real_part * sine_part + imag_part * cosine], axis=1)


def twisted(grid_field, along_axis, shift_by, cosine, sine_part):
    extent = grid_field.shape[along_axis]
    moved_field = jnp.roll(grid_field, -shift_by, axis=along_axis)
    turned = rotate(moved_field, cosine, shift_by * sine_part)
    mask_shape = [1] * grid_field.ndim
    mask_shape[along_axis] = extent
    edge_row = extent - 1 if shift_by > 0 else 0
    at_edge = (jnp.arange(extent) == edge_row).reshape(mask_shape)
    return jnp.where(at_edge, turned, moved_field)


def project_bands(occ_bands, grid_field):
    band_count = occ_bands.shape[0]
    resp_count = grid_field.shape[0]
    gram_matrix = lax.dot_general(occ_bands.reshape(band_count * 2, -1), grid_field.reshape(resp_count * 2, -1), (((1,), (1,)), ((), ())), precision=PRECISE, preferred_element_type=jnp.float32).reshape(band_count, 2, resp_count, 2)
    return gram_matrix[:, 0, :, 0] + gram_matrix[:, 1, :, 1], gram_matrix[:, 0, :, 1] - gram_matrix[:, 1, :, 0]


def combine(occ_bands, real_part, imag_part, shape):
    band_count = occ_bands.shape[0]
    resp_count = real_part.shape[1]
    coeffs = jnp.stack([jnp.stack([real_part, imag_part], axis=2), jnp.stack([-imag_part, real_part], axis=2)], axis=1)
    result = lax.dot_general(coeffs.reshape(band_count * 2, resp_count * 2), occ_bands.reshape(band_count * 2, -1), (((0,), (0,)), ((), ())), precision=PRECISE, preferred_element_type=jnp.float32)
    return result.reshape(shape)


def nonlocal_apply(grid_field, atom_cells, offsets, projector, strength, thetas):
    extents = jnp.array([NZ, NX, NY], dtype=jnp.int32)
    points = atom_cells[:, None, :] + offsets[None, :, :]
    wrap_count = jnp.floor_divide(points, extents)
    cell_index = points - wrap_count * extents
    angles = jnp.sum(thetas * wrap_count.astype(thetas.dtype), axis=-1)
    flat_index = (cell_index[..., 0] * NX + cell_index[..., 1]) * NY + cell_index[..., 2]
    resp_count = grid_field.shape[0]
    flat_field = grid_field.reshape(resp_count, 2, -1)
    picked = flat_field[:, :, flat_index]
    phase_cos = jnp.cos(angles)
    phase_sin = jnp.sin(angles)
    turned_re = picked[:, 0] * phase_cos - picked[:, 1] * phase_sin
    turned_im = picked[:, 0] * phase_sin + picked[:, 1] * phase_cos
    proj_re = jnp.sum(turned_re * projector, axis=-1) * strength
    proj_im = jnp.sum(turned_im * projector, axis=-1) * strength
    back_re = proj_re[..., None] * projector
    back_im = proj_im[..., None] * projector
    put_re = back_re * phase_cos + back_im * phase_sin
    put_im = back_im * phase_cos - back_re * phase_sin
    spread = jnp.zeros_like(flat_field).at[:, :, flat_index].add(jnp.stack([put_re, put_im], axis=1))
    return spread.reshape(grid_field.shape)


def band_sum(left_field, right_field):
    return jnp.sum(left_field * right_field, axis=(1, 2, 3, 4))


def reference(psi_occ, psi_resp, initial_guess, local_potential, potential_change, band_energy, q_index, atom_cells, offsets, projector, strength):
    thetas = q_index.astype(jnp.float32) * (2.0 * math.pi / QDIV)
    cosines = jnp.cos(thetas)
    sines = jnp.sin(thetas)
    weight = 1.0 / (NZ * NX * NY)

    def apply_operator(grid_field):
        beside = jnp.zeros_like(grid_field)
        for along_axis in (2, 3, 4):
            cosine = cosines[along_axis - 2]
            sine_part = sines[along_axis - 2]
            beside = beside + twisted(grid_field, along_axis, 1, cosine, sine_part) + twisted(grid_field, along_axis, -1, cosine, sine_part)
        kinetic = 3.0 * grid_field - 0.5 * beside
        local_term = (local_potential[None, None] - band_energy[:, None, None, None, None]) * grid_field
        nonlocal_term = nonlocal_apply(grid_field, atom_cells, offsets, projector, strength, thetas)
        real_part, imag_part = project_bands(psi_occ, grid_field)
        occupied = combine(psi_occ, real_part, imag_part, grid_field.shape)
        return kinetic + local_term + nonlocal_term + SHIFT_WEIGHT * weight * occupied

    psi_re = psi_resp[:, 0]
    psi_im = psi_resp[:, 1]
    product = jnp.stack([potential_change[0] * psi_re - potential_change[1] * psi_im, potential_change[0] * psi_im + potential_change[1] * psi_re], axis=1)
    real_part, imag_part = project_bands(psi_occ, product)
    source_term = -(product - weight * combine(psi_occ, real_part, imag_part, product.shape))
    solution = initial_guess
    residual = source_term - apply_operator(initial_guess)
    direction = residual
    norm_now = band_sum(residual, residual)
    for sweep_index in range(ITERS):
        image_field = apply_operator(direction)
        curvature = band_sum(direction, image_field)
        step_size = (norm_now / curvature)[:, None, None, None, None]
        solution = solution + step_size * direction
        residual = residual - step_size * image_field
        if sweep_index + 1 < ITERS:
            norm_next = band_sum(residual, residual)
            growth_ratio = norm_next / norm_now
            direction = residual + growth_ratio[:, None, None, None, None] * direction
            norm_now = norm_next
    return solution, residual
```

```python
import functools
import math

import jax
import jax.numpy as jnp
from jax import lax
from jax.experimental import pallas as pl
from jax.experimental.pallas import tpu as pltpu
from jax.sharding import PartitionSpec as P

RAD = 4
QDIV = 8
EDGE = 8
WIN = 16
SHIFT_WEIGHT = 3.0
PRECISE = lax.Precision.HIGHEST
SWAP = [(0, 1), (1, 0)]

VMEM = pl.BlockSpec(memory_space=pltpu.VMEM)
SMEM = pl.BlockSpec(memory_space=pltpu.SMEM)


def params(mib):
    return pltpu.CompilerParams(vmem_limit_bytes=mib * 1024 * 1024)


def sum_rows(values):
    total = jnp.sum(values, axis=2, keepdims=True)
    row = lax.broadcasted_iota(jnp.int32, values.shape, 0)
    lane = lax.broadcasted_iota(jnp.int32, values.shape, 2)
    picked = jnp.sum(jnp.where(row == lane, total, 0.0), axis=0)
    return jnp.sum(picked, axis=0, keepdims=True)


def rows8(index):
    return pl.ds(pl.multiple_of(index * 8, 8), 8)


def first_corr_kernel(occ_ref, resp_ref, pot_ref, guess_ref, out_ref, prod, red):
    bands, _, rows, _ = resp_ref.shape
    for n in range(bands):
        re = resp_ref[n, 0]
        im = resp_ref[n, 1]
        prod[2 * n] = pot_ref[0] * re - pot_ref[1] * im
        prod[2 * n + 1] = pot_ref[0] * im + pot_ref[1] * re
    count = occ_ref.shape[0]

    def pair(g, _):
        def row(i, accs):
            at = rows8(i)
            occ = [(occ_ref[2 * g + k, 0, at], occ_ref[2 * g + k, 1, at]) for k in range(2)]
            accs = list(accs)
            for n in range(2 * bands):
                if n < bands:
                    re, im = prod[2 * n, at], prod[2 * n + 1, at]
                else:
                    re, im = guess_ref[n - bands, 0, at], guess_ref[n - bands, 1, at]
                for k in range(2):
                    pr, pi = occ[k]
                    j = (k * 2 * bands + n) * 2
                    accs[j] = accs[j] + (pr * re + pi * im)
                    accs[j + 1] = accs[j + 1] + (pr * im - pi * re)
            return tuple(accs)

        zero = jnp.zeros((8, 128), jnp.float32)
        accs = lax.fori_loop(0, rows // 8, row, (zero,) * (8 * bands))
        for k in range(2):
            for n in range(2 * bands):
                for c in range(2):
                    which = n // bands
                    spot = ((2 * g + k) * bands + n % bands) * 2 + c
                    red[which, spot] = accs[(k * 2 * bands + n) * 2 + c]
        return 0

    lax.fori_loop(0, count // 2, pair, 0)
    out_ref[...] = jnp.zeros(out_ref.shape, jnp.float32)
    out_ref[0:1] = sum_rows(red[0])
    out_ref[1:2] = sum_rows(red[1])


def first_corr(psi_occ, psi_resp, pot, guess):
    return pl.pallas_call(
        first_corr_kernel,
        out_shape=jax.ShapeDtypeStruct((8, 128), jnp.float32),
        in_specs=[VMEM] * 4,
        out_specs=VMEM,
        scratch_shapes=[
            pltpu.VMEM((psi_resp.shape[0] * 2,) + psi_resp.shape[2:], jnp.float32),
            pltpu.VMEM((2, 128, 8, 128), jnp.float32),
        ],
        compiler_params=params(28),
        name="first_corr",
    )(psi_occ, psi_resp, pot, guess)


def gather_kernel(start_ref, rot_ref, str_ref, mid_ref, low_ref, high_ref, img_ref, zsum_ref, out_ref, low, high, red):
    fields = mid_ref.shape[0]
    half = zsum_ref.shape[1]
    for n in range(fields // 2):
        for src, dst, j in ((low_ref, low, 0), (high_ref, high, 2)):
            c, s = rot_ref[j], rot_ref[j + 1]
            re, im = src[2 * n], src[2 * n + 1]
            dst[2 * n] = re * c - im * s
            dst[2 * n + 1] = re * s + im * c
        for k in range(2):
            f = 2 * n + k
            zsum_ref[f] = low[f, EDGE : EDGE + half] + high[f, EDGE : EDGE + half]
    atoms = img_ref.shape[0]

    def atom(a, _):
        begin = pl.multiple_of(start_ref[a], 8)
        accs = [jnp.zeros((8, 128), jnp.float32)] * fields
        for z, src in enumerate((low, mid_ref, high)):
            for k in range(2):
                at = pl.ds(pl.multiple_of(begin + 8 * k, 8), 8)
                ire = img_ref[a, z, 0, 8 * k : 8 * k + 8]
                iim = img_ref[a, z, 1, 8 * k : 8 * k + 8]
                for n in range(fields // 2):
                    re, im = src[2 * n, at], src[2 * n + 1, at]
                    accs[2 * n] = accs[2 * n] + (re * ire - im * iim)
                    accs[2 * n + 1] = accs[2 * n + 1] + (re * iim + im * ire)
        for f in range(fields):
            red[a * fields + f] = accs[f] * str_ref[a]
        return 0

    lax.fori_loop(0, atoms, atom, 0)
    total = atoms * fields
    for b in range(out_ref.shape[0]):
        stop = min(total, 128 * b + 128)
        out_ref[b : b + 1] = sum_rows(red[128 * b : stop])


def gather(starts, rot, strength, mid, low, high, img):
    fields, rows, cols = mid.shape
    atoms = img.shape[0]
    blocks = -(-atoms * fields // 128)
    return pl.pallas_call(
        gather_kernel,
        out_shape=(
            jax.ShapeDtypeStruct((fields, rows - 2 * EDGE, cols), jnp.float32),
            jax.ShapeDtypeStruct((blocks, 128), jnp.float32),
        ),
        in_specs=[SMEM] * 3 + [VMEM] * 4,
        out_specs=(VMEM, VMEM),
        scratch_shapes=[
            pltpu.VMEM(mid.shape, jnp.float32),
            pltpu.VMEM(mid.shape, jnp.float32),
            pltpu.VMEM((atoms * fields, 8, 128), jnp.float32),
        ],
        compiler_params=params(28),
        name="gather",
    )(starts, rot, strength, mid, low, high, img)


def stencil_kernel(which_ref, energy_ref, twist_ref, mid_ref, zsum_ref, pot_ref, out_ref):
    fields, half, cols = out_ref.shape
    lane = lax.broadcasted_iota(jnp.int32, (half, cols), 1)
    first, last = lane == 0, lane == cols - 1
    c, s = twist_ref[0], twist_ref[1]
    pot = pot_ref[0] + 3.0
    for n in range(fields // 2):
        re = mid_ref[2 * n, EDGE : EDGE + half]
        im = mid_ref[2 * n + 1, EDGE : EDGE + half]
        re_next, im_next = pltpu.roll(re, cols - 1, 1), pltpu.roll(im, cols - 1, 1)
        re_prev, im_prev = pltpu.roll(re, 1, 1), pltpu.roll(im, 1, 1)
        y_re = jnp.where(last, re_next * c - im_next * s, re_next) + jnp.where(
            first, re_prev * c + im_prev * s, re_prev
        )
        y_im = jnp.where(last, re_next * s + im_next * c, im_next) + jnp.where(
            first, im_prev * c - re_prev * s, im_prev
        )
        scale = pot - energy_ref[n]
        for f, value, beside in ((2 * n, re, y_re), (2 * n + 1, im, y_im)):
            beside = beside + zsum_ref[f]
            beside = beside + mid_ref[f, EDGE - 1 : EDGE - 1 + half]
            beside = beside + mid_ref[f, EDGE + 1 : EDGE + 1 + half]
            out_ref[f] = scale * value - 0.5 * beside


def stencil(which, energy, twist, mid, zsum, pot):
    fields, half, cols = zsum.shape
    return pl.pallas_call(
        stencil_kernel,
        out_shape=jax.ShapeDtypeStruct(zsum.shape, jnp.float32),
        grid_spec=pltpu.PrefetchScalarGridSpec(
            num_scalar_prefetch=1,
            grid=(1,),
            in_specs=[
                SMEM,
                SMEM,
                pl.BlockSpec(mid.shape, lambda i, w: (0, 0, 0)),
                pl.BlockSpec(zsum.shape, lambda i, w: (0, 0, 0)),
                pl.BlockSpec((1, half, cols), lambda i, w: (0, w[0], 0)),
            ],
            out_specs=pl.BlockSpec(zsum.shape, lambda i, w: (0, 0, 0)),
        ),
        compiler_params=params(28),
        name="stencil",
    )(which, energy, twist, mid, zsum, pot)


def spread_into(acc, starts_ref, coef_ref, images):
    fields = acc.shape[0]
    atoms = images[0].shape[0]

    def atom(a, _):
        for j, img in enumerate(images):
            begin = pl.multiple_of(starts_ref[j, a], 8)
            for k in range(2):
                at = pl.ds(pl.multiple_of(begin + 8 * k, 8), 8)
                ire = img[a, 0, 8 * k : 8 * k + 8]
                iim = img[a, 1, 8 * k : 8 * k + 8]
                for n in range(fields // 2):
                    pr = coef_ref[j, a * fields + 2 * n]
                    pi = coef_ref[j, a * fields + 2 * n + 1]
                    acc[2 * n, at] = acc[2 * n, at] + (pr * ire + pi * iim)
                    acc[2 * n + 1, at] = acc[2 * n + 1, at] + (pi * ire - pr * iim)
        return 0

    lax.fori_loop(0, atoms, atom, 0)


def occupied_into(dst, sums_ref, own_ref, other_ref, base, block):
    fields, half, cols = dst.shape
    count = own_ref.shape[0]

    def rows_of(b, _):
        at = pl.ds(pl.multiple_of(b * block, 8), block)

        def band(m, accs):
            accs = list(accs)
            for which, occ in enumerate((own_ref, other_ref)):
                pr, pi = occ[m, 0, at], occ[m, 1, at]
                for n in range(fields // 2):
                    sr = sums_ref[which, m * fields + 2 * n]
                    si = sums_ref[which, m * fields + 2 * n + 1]
                    accs[2 * n] = accs[2 * n] + (pr * sr - pi * si)
                    accs[2 * n + 1] = accs[2 * n + 1] + (pr * si + pi * sr)
            return tuple(accs)

        accs = lax.fori_loop(0, count, band, tuple(base(f, at) for f in range(fields)))
        for f in range(fields):
            dst[f, at] = accs[f]
        return 0

    lax.fori_loop(0, half // block, rows_of, 0)


def correlate_into(red, src, own_ref, other_ref):
    fields, half, cols = src.shape
    count = own_ref.shape[0]
    bands = fields // 2

    def pair(g, _):
        def row(i, accs):
            at = rows8(i)
            accs = list(accs)
            occ = []
            for ref in (own_ref, other_ref):
                for k in range(2):
                    occ.append((ref[2 * g + k, 0, at], ref[2 * g + k, 1, at]))
            for n in range(bands):
                re, im = src[2 * n, at], src[2 * n + 1, at]
                for q, (pr, pi) in enumerate(occ):
                    j = (q * bands + n) * 2
                    accs[j] = accs[j] + (pr * re + pi * im)
                    accs[j + 1] = accs[j + 1] + (pr * im - pi * re)
            return tuple(accs)

        zero = jnp.zeros((8, 128), jnp.float32)
        accs = lax.fori_loop(0, half // 8, row, (zero,) * (8 * bands))
        for q in range(4):
            for j in range(fields):
                red[q // 2, (2 * g + q % 2) * fields + j] = accs[q * fields + j]
        return 0

    lax.fori_loop(0, count // 2, pair, 0)


def dots_into(red_dot, pairs):
    fields, half = pairs[0][3], pairs[0][4]
    bands = fields // 2

    def row(i, accs):
        at = rows8(i)
        accs = list(accs)
        for p, (_, left, right, _, _) in enumerate(pairs):
            for n in range(bands):
                value = left(2 * n, at) * right(2 * n, at) + left(2 * n + 1, at) * right(2 * n + 1, at)
                accs[p * bands + n] = accs[p * bands + n] + value
        return tuple(accs)

    zero = jnp.zeros((8, 128), jnp.float32)
    accs = lax.fori_loop(0, half // 8, row, (zero,) * (bands * len(pairs)))
    for p, (slot, _, _, _, _) in enumerate(pairs):
        for n in range(bands):
            red_dot[slot * bands + n] = accs[p * bands + n]


def pick_block(half):
    return next(b for b in (24, 16, 8) if half % b == 0)


def residual_kernel(which_ref, starts_ref, coef_ref, sums_ref, lap_ref, img_ref, low_ref, high_ref,
                    own_ref, other_ref, resp_ref, pot_ref, out_ref, sum_ref, acc, red, red_dot):
    fields, half, cols = out_ref.shape
    acc[...] = jnp.zeros(acc.shape, jnp.float32)
    acc[:, EDGE : EDGE + half] = lap_ref[...]
    spread_into(acc, starts_ref, coef_ref, (img_ref.at[:, 1], low_ref, high_ref))

    def base(f, at):
        re, im = resp_ref[f // 2, 0, at], resp_ref[f // 2, 1, at]
        if f % 2 == 0:
            prod = pot_ref[0, at] * re - pot_ref[1, at] * im
        else:
            prod = pot_ref[0, at] * im + pot_ref[1, at] * re
        moved = pl.ds(pl.multiple_of(at.start + EDGE, 8), at.size)
        return -prod - acc[f, moved]

    occupied_into(out_ref, sums_ref, own_ref, other_ref, base, pick_block(half))
    correlate_into(red, out_ref, own_ref, other_ref)
    load = lambda f, at: out_ref[f, at]
    dots_into(red_dot, [(0, load, load, fields, half)])
    sum_ref[...] = jnp.zeros(sum_ref.shape, jnp.float32)
    sum_ref[0:1] = sum_rows(red[0])
    sum_ref[1:2] = sum_rows(red[1])
    sum_ref[2:3] = sum_rows(red_dot[0 : fields // 2])


def half_specs(own, half, cols):
    count = own.shape[0]
    return pl.BlockSpec((count, 2, half, cols), lambda i, w: (0, 0, w[0], 0))


def whole(shape):
    return pl.BlockSpec(shape, lambda i, w: (0,) * len(shape))


def residual_call(which, starts, coef, sums, lap, img, low_img, high_img, psi_occ, other, resp, pot):
    fields, half, cols = lap.shape
    return pl.pallas_call(
        residual_kernel,
        out_shape=(
            jax.ShapeDtypeStruct(lap.shape, jnp.float32),
            jax.ShapeDtypeStruct((8, 128), jnp.float32),
        ),
        grid_spec=pltpu.PrefetchScalarGridSpec(
            num_scalar_prefetch=1,
            grid=(1,),
            in_specs=[
                SMEM,
                SMEM,
                SMEM,
                whole(lap.shape),
                whole(img.shape),
                whole(low_img.shape),
                whole(high_img.shape),
                half_specs(psi_occ, half, cols),
                whole(other.shape),
                half_specs(resp, half, cols),
                pl.BlockSpec((2, half, cols), lambda i, w: (0, w[0], 0)),
            ],
            out_specs=(whole(lap.shape), whole((8, 128))),
            scratch_shapes=[
                pltpu.VMEM((fields, half + 2 * EDGE + WIN, cols), jnp.float32),
                pltpu.VMEM((2, 128, 8, 128), jnp.float32),
                pltpu.VMEM((16, 8, 128), jnp.float32),
            ],
        ),
        compiler_params=params(40),
        name="residual",
    )(which, starts, coef, sums, lap, img, low_img, high_img, psi_occ, other, resp, pot)


def image_kernel(which_ref, starts_ref, coef_ref, sums_ref, lap_ref, img_ref, low_ref, high_ref,
                 own_ref, other_ref, res_ref, out_ref, sum_ref, acc, red, red_dot):
    fields, half, cols = out_ref.shape
    acc[...] = jnp.zeros(acc.shape, jnp.float32)
    acc[:, EDGE : EDGE + half] = lap_ref[...]
    spread_into(acc, starts_ref, coef_ref, (img_ref.at[:, 1], low_ref, high_ref))

    def base(f, at):
        moved = pl.ds(pl.multiple_of(at.start + EDGE, 8), at.size)
        return acc[f, moved]

    occupied_into(out_ref, sums_ref, own_ref, other_ref, base, pick_block(half))
    correlate_into(red, out_ref, own_ref, other_ref)
    load = lambda f, at: out_ref[f, at]
    other_side = lambda f, at: res_ref[f, at]
    dots_into(red_dot, [(0, other_side, load, fields, half), (1, load, load, fields, half)])
    sum_ref[...] = jnp.zeros(sum_ref.shape, jnp.float32)
    sum_ref[0:1] = sum_rows(red[0])
    sum_ref[1:2] = sum_rows(red[1])
    sum_ref[2:3] = sum_rows(red_dot[0:fields])


def image_call(which, starts, coef, sums, lap, img, low_img, high_img, psi_occ, other, res):
    fields, half, cols = lap.shape
    return pl.pallas_call(
        image_kernel,
        out_shape=(
            jax.ShapeDtypeStruct(lap.shape, jnp.float32),
            jax.ShapeDtypeStruct((8, 128), jnp.float32),
        ),
        grid_spec=pltpu.PrefetchScalarGridSpec(
            num_scalar_prefetch=1,
            grid=(1,),
            in_specs=[
                SMEM,
                SMEM,
                SMEM,
                whole(lap.shape),
                whole(img.shape),
                whole(low_img.shape),
                whole(high_img.shape),
                half_specs(psi_occ, half, cols),
                whole(other.shape),
                whole(res.shape),
            ],
            out_specs=(whole(lap.shape), whole((8, 128))),
            scratch_shapes=[
                pltpu.VMEM((fields, half + 2 * EDGE + WIN, cols), jnp.float32),
                pltpu.VMEM((2, 128, 8, 128), jnp.float32),
                pltpu.VMEM((16, 8, 128), jnp.float32),
            ],
        ),
        compiler_params=params(40),
        name="image",
    )(which, starts, coef, sums, lap, img, low_img, high_img, psi_occ, other, res)


def local_kernel(starts_ref, coef_ref, lap_ref, img_ref, low_ref, high_ref, field_ref, part_ref,
                 out_ref, sum_ref, acc, red_dot):
    fields, half, cols = out_ref.shape
    acc[...] = jnp.zeros(acc.shape, jnp.float32)
    acc[:, EDGE : EDGE + half] = lap_ref[...]
    spread_into(acc, starts_ref, coef_ref, (img_ref.at[:, 1], low_ref, high_ref))
    out_ref[...] = acc[:, EDGE : EDGE + half]
    load = lambda f, at: out_ref[f, at]
    other_side = lambda f, at: field_ref[f, at]
    dots_into(red_dot, [(0, other_side, load, fields, half)])
    sum_ref[...] = part_ref[...]
    sum_ref[3:4] = sum_rows(red_dot[0 : fields // 2])


def local_call(starts, coef, lap, img, low_img, high_img, field, part):
    fields, half, cols = lap.shape
    return pl.pallas_call(
        local_kernel,
        out_shape=(
            jax.ShapeDtypeStruct(lap.shape, jnp.float32),
            jax.ShapeDtypeStruct((8, 128), jnp.float32),
        ),
        in_specs=[SMEM, SMEM] + [VMEM] * 6,
        out_specs=(VMEM, VMEM),
        scratch_shapes=[
            pltpu.VMEM((fields, half + 2 * EDGE + WIN, cols), jnp.float32),
            pltpu.VMEM((16, 8, 128), jnp.float32),
        ],
        compiler_params=params(28),
        name="local",
    )(starts, coef, lap, img, low_img, high_img, field, part)


def last_kernel(which_ref, sums_ref, mix_ref, own_ref, other_ref, res_ref, first_ref, second_ref, out_ref):
    fields, half, cols = out_ref.shape

    def base(f, at):
        n = f // 2
        return res_ref[f, at] + mix_ref[0, n] * first_ref[f, at] + mix_ref[1, n] * second_ref[f, at]

    occupied_into(out_ref, sums_ref, own_ref, other_ref, base, pick_block(half))


def last_call(which, sums, mix, psi_occ, other, res, first, second):
    fields, half, cols = res.shape
    return pl.pallas_call(
        last_kernel,
        out_shape=jax.ShapeDtypeStruct(res.shape, jnp.float32),
        grid_spec=pltpu.PrefetchScalarGridSpec(
            num_scalar_prefetch=1,
            grid=(1,),
            in_specs=[
                SMEM,
                SMEM,
                half_specs(psi_occ, half, cols),
                whole(other.shape),
                whole(res.shape),
                whole(first.shape),
                whole(second.shape),
            ],
            out_specs=whole(res.shape),
        ),
        compiler_params=params(40),
        name="last",
    )(which, sums, mix, psi_occ, other, res, first, second)


def factors_of(count):
    out = []
    while count > 1:
        step = 4 if count % 4 == 0 else 2
        out.append(step)
        count //= step
    return out


def space_sum(block):
    count = lax.axis_size("space")
    stride = 1
    for factor in factors_of(count):
        total = block
        for d in range(1, factor):
            route = []
            for i in range(count):
                q = (i // stride) % factor
                route.append((i, i + ((q + d) % factor - q) * stride))
            total = total + lax.ppermute(block, "space", route)
        block = total
        stride *= factor
    return block


def exchange(block):
    return lax.ppermute(block, "occ", SWAP)


def from_behind(block, distance):
    count = lax.axis_size("space")
    return lax.ppermute(block, "space", [((i - distance) % count, i) for i in range(count)])


def turn(fields, cosine, sine_part):
    pairs = fields.reshape((-1, 2) + fields.shape[1:])
    re, im = pairs[:, 0], pairs[:, 1]
    out = jnp.stack([re * cosine - im * sine_part, re * sine_part + im * cosine], axis=1)
    return out.reshape(fields.shape)


def window_images(x_cell, y_cell, offsets, values, theta_y, rows_y, planes):
    y_raw = y_cell[:, None] + offsets[None, :, 2]
    y_wrap = jnp.floor_divide(y_raw, rows_y)
    y_at = y_raw - y_wrap * rows_y
    angles = theta_y * y_wrap.astype(jnp.float32)
    row = x_cell[:, None] + offsets[None, :, 1] + RAD
    slot = []
    for plane in planes:
        wanted = (row[:, None, :] == jnp.arange(WIN, dtype=jnp.int32)[None, :, None]) & (
            offsets[:, 0] == plane
        )[None, None, :]
        slot.append(wanted)
    slots = jnp.stack(slot, axis=1)
    weights = jnp.stack([values * jnp.cos(angles), values * jnp.sin(angles)], axis=1)
    left = jnp.where(slots[:, :, None], weights[:, None, :, None, :], 0.0)
    atoms = left.shape[0]
    left = left.reshape(atoms, len(planes) * 2 * WIN, -1)
    right = (y_at[:, :, None] == jnp.arange(rows_y, dtype=jnp.int32)[None, None, :]).astype(jnp.float32)
    image = jnp.einsum("apk,aky->apy", left, right, precision=PRECISE)
    return image.reshape(atoms, len(planes), 2, WIN, rows_y)


def shards(
    psi_occ,
    psi_resp,
    initial_guess,
    local_potential,
    potential_change,
    band_energy,
    q_index,
    atom_cells,
    offsets,
    projector,
    strength,
):
    slab_count = lax.axis_size("space")
    slab_index = lax.axis_index("space")
    side = lax.axis_index("occ")
    layers, rows_x, rows_y = local_potential.shape
    half = rows_x // 2
    atoms = atom_cells.shape[0]
    bands = psi_resp.shape[0]
    fields = 2 * bands
    weight = 1.0 / (layers * slab_count * rows_x * rows_y)
    thetas = q_index.astype(jnp.float32) * (2.0 * math.pi / QDIV)
    cosines = jnp.cos(thetas)
    sines = jnp.sin(thetas)
    at_first = slab_index == 0
    at_last = slab_index == slab_count - 1
    z_rot = jnp.stack(
        [
            jnp.where(at_first, cosines[0], 1.0),
            jnp.where(at_first, -sines[0], 0.0),
            jnp.where(at_last, cosines[0], 1.0),
            jnp.where(at_last, sines[0], 0.0),
        ]
    )
    x_low = (jnp.where(side == 0, cosines[1], 1.0), jnp.where(side == 0, -sines[1], 0.0))
    x_high = (jnp.where(side == 1, cosines[1], 1.0), jnp.where(side == 1, sines[1], 0.0))
    y_twist = jnp.stack([cosines[2], sines[2]])
    which = side.astype(jnp.int32).reshape(1)

    occ = psi_occ.reshape(psi_occ.shape[0], 2, rows_x, rows_y)
    resp = psi_resp.reshape(bands, 2, rows_x, rows_y)
    guess = initial_guess.reshape(bands, 2, rows_x, rows_y)
    change = potential_change.reshape(2, rows_x, rows_y)

    occ_other = exchange(lax.dynamic_slice_in_dim(occ, (1 - side) * half, half, axis=2))

    flat = guess.reshape(fields, rows_x, rows_y)
    ring = jnp.concatenate(
        [
            turn(flat[:, rows_x - EDGE :], cosines[1], -sines[1]),
            flat,
            turn(flat[:, :EDGE], cosines[1], sines[1]),
        ],
        axis=1,
    )
    guess_mid = lax.dynamic_slice_in_dim(ring, side * half, half + 2 * EDGE, axis=1)

    packed = jnp.stack(
        [
            projector,
            jnp.pad(atom_cells.astype(jnp.float32), ((0, 0), (0, projector.shape[1] - 3))),
        ],
        axis=1,
    )
    below = from_behind(packed, 1)
    above = from_behind(packed, -1)
    cells = [atom_cells]
    for side_pack in (below, above):
        cells.append(side_pack[:, 1, :3].astype(jnp.int32))
    all_x = jnp.stack([c[:, 1] for c in cells])
    all_y = jnp.stack([c[:, 2] for c in cells])
    at_row = jnp.mod(all_x - RAD - side * half + EDGE, rows_x)
    inner = at_row % 8
    touching = at_row < half + EDGE
    put_starts = jnp.where(touching, at_row - inner, half + 2 * EDGE).astype(jnp.int32)
    get_starts = jnp.where(touching[0], at_row[0] - inner[0], 0).astype(jnp.int32)
    img = window_images(inner[0], all_y[0], offsets, projector, thetas[2], rows_y, (-1, 0, 1))
    low_img = window_images(inner[1], all_y[1], offsets, below[:, 0], thetas[2], rows_y, (1,))[:, 0]
    high_img = window_images(inner[2], all_y[2], offsets, above[:, 0], thetas[2], rows_y, (-1,))[:, 0]

    def extend(half_field):
        edges = jnp.concatenate([half_field[:, :EDGE], half_field[:, half - EDGE :]], axis=1)
        got = exchange(edges)
        return jnp.concatenate(
            [turn(got[:, EDGE:], *x_low), half_field, turn(got[:, :EDGE], *x_high)], axis=1
        )

    def local_part(mid):
        low = from_behind(mid, 1)
        high = from_behind(mid, -1)
        zsum, proj = gather(get_starts, z_rot, strength, mid, low, high, img)
        proj_low = from_behind(proj, 1)
        proj_high = from_behind(proj, -1)
        lap = stencil(which, band_energy, y_twist, mid, zsum, local_potential)

        def rotated(block, cosine, sine_part):
            pairs = block.reshape(-1, 2)
            re, im = pairs[:, 0], pairs[:, 1]
            out = jnp.stack([re * cosine - im * sine_part, re * sine_part + im * cosine], axis=1)
            return out.reshape(-1)

        coef = jnp.stack(
            [
                proj.reshape(-1),
                rotated(proj_low, z_rot[0], z_rot[1]),
                rotated(proj_high, z_rot[2], z_rot[3]),
            ]
        )
        return lap, coef

    def total(part):
        summed = space_sum(part)
        got = exchange(summed)
        return jnp.concatenate([summed[0:2] + got[1::-1], summed[2:] + got[2:]], axis=0)

    first = space_sum(first_corr(occ, resp, change, guess))
    coef_occ = weight * first[0] - SHIFT_WEIGHT * weight * first[1]
    first_sums = jnp.stack([coef_occ, exchange(coef_occ.reshape(1, 128))[0]])
    lap, coef = local_part(guess_mid)
    residual, part = residual_call(
        which, put_starts, coef, first_sums, lap, img, low_img, high_img, occ, occ_other, resp, change
    )
    tot = total(part)
    norm0 = tot[2, :bands]
    lap, coef = local_part(extend(residual))
    image, part = image_call(
        which, put_starts, coef, SHIFT_WEIGHT * weight * tot[0:2], lap, img, low_img, high_img, occ, occ_other, residual
    )
    residual_other = exchange(residual)
    lap, coef = local_part(extend(image))
    image_other = exchange(image)
    image2, part = local_call(put_starts, coef, lap, img, low_img, high_img, image, part)
    tot = total(part)
    sums = tot[0:2]
    cross = tot[2, :bands]
    square = tot[2, bands : 2 * bands]
    occ_square = jnp.sum((sums * sums).reshape(-1, bands, 2), axis=(0, 2))
    triple = tot[3, :bands] + SHIFT_WEIGHT * weight * occ_square
    step0 = norm0 / cross
    norm1 = norm0 - 2.0 * step0 * cross + step0 * step0 * square
    growth = norm1 / norm0
    lead = 1.0 + growth
    curvature = lead * lead * cross - 2.0 * lead * step0 * square + step0 * step0 * triple
    step1 = norm1 / curvature
    mix0 = -step0 - step1 * lead
    mix1 = step1 * step0
    per_band = jnp.repeat(mix1, 2)
    last_sums = SHIFT_WEIGHT * weight * (sums.reshape(2, -1, fields) * per_band[None, None, :]).reshape(2, -1)
    mine = last_call(
        which, last_sums, jnp.stack([mix0, mix1]), occ, occ_other, residual, image, image2
    )
    theirs = exchange(mine)

    def join(own_half, other_half):
        lower = jnp.where(side == 0, own_half, other_half)
        upper = jnp.where(side == 0, other_half, own_half)
        return jnp.concatenate([lower, upper], axis=1).reshape(bands, 2, 1, rows_x, rows_y)

    wide = lambda v: v[:, None, None, None, None]
    response = (
        initial_guess
        + wide(step0 + step1 * lead) * join(residual, residual_other)
        - wide(step0 * step1) * join(image, image_other)
    )
    return response, join(mine, theirs)


def solution(mesh):
    return jax.shard_map(
        shards,
        mesh=mesh,
        in_specs=(
            P("occ", None, "space", None, None),
            P("resp", None, "space", None, None),
            P("resp", None, "space", None, None),
            P("space", None, None),
            P(None, "space", None, None),
            P("resp"),
            P(),
            P("space", None),
            P(),
            P("space", None),
            P("space"),
        ),
        out_specs=(P("resp", None, "space", None, None), P("resp", None, "space", None, None)),
        check_vma=False,
    )
```

```python
import functools
import math

import jax
import jax.numpy as jnp
from jax import lax
from jax.experimental import pallas as pl
from jax.experimental.pallas import tpu as pltpu
from jax.sharding import PartitionSpec as P

RAD = 4
QDIV = 8
EDGE = 8
WIN = 16
SHIFT_WEIGHT = 3.0
PRECISE = lax.Precision.HIGHEST
SWAP = [(0, 1), (1, 0)]

VMEM = pl.BlockSpec(memory_space=pltpu.VMEM)
SMEM = pl.BlockSpec(memory_space=pltpu.SMEM)
HBM = pl.BlockSpec(memory_space=pl.ANY)


def params(mib):
    return pltpu.CompilerParams(vmem_limit_bytes=mib * 1024 * 1024)


def sum_rows(values):
    total = jnp.sum(values, axis=2, keepdims=True)
    row = lax.broadcasted_iota(jnp.int32, values.shape, 0)
    lane = lax.broadcasted_iota(jnp.int32, values.shape, 2)
    picked = jnp.sum(jnp.where(row == lane, total, 0.0), axis=0)
    return jnp.sum(picked, axis=0, keepdims=True)


def rows8(index):
    return pl.ds(pl.multiple_of(index * 8, 8), 8)


def prep_kernel(which_ref, rot_ref, guess_ref, out_ref):
    fields, wide, _ = out_ref.shape
    half = wide - 2 * EDGE
    rows = guess_ref.shape[2]
    side = which_ref[0]
    begin = pl.multiple_of(side * half, 8)
    low = pl.multiple_of((1 - side) * half + half - EDGE, 8)
    high = pl.multiple_of((1 - side) * half, 8)
    for n in range(fields // 2):
        for k in range(2):
            out_ref[2 * n + k, EDGE : EDGE + half] = guess_ref[n, k, pl.ds(begin, half)]
        for start, spot, j in ((low, 0, 0), (high, EDGE + half, 2)):
            c, s = rot_ref[j], rot_ref[j + 1]
            re, im = guess_ref[n, 0, pl.ds(start, EDGE)], guess_ref[n, 1, pl.ds(start, EDGE)]
            out_ref[2 * n, spot : spot + EDGE] = re * c - im * s
            out_ref[2 * n + 1, spot : spot + EDGE] = re * s + im * c


def prep_call(which, x_rot, guess):
    bands, _, rows, cols = guess.shape
    return pl.pallas_call(
        prep_kernel,
        out_shape=jax.ShapeDtypeStruct((2 * bands, rows // 2 + 2 * EDGE, cols), jnp.float32),
        in_specs=[SMEM, SMEM, VMEM],
        out_specs=VMEM,
        compiler_params=params(6),
        name="prep",
    )(which, x_rot, guess)


def fill_kernel(rot_ref, got_ref, ext_ref, out_ref, low, high, sems):
    fields, wide, _ = out_ref.shape
    for n in range(fields // 2):
        for dst, at, j in ((low, EDGE, 0), (high, 0, 2)):
            c, s = rot_ref[j], rot_ref[j + 1]
            re, im = got_ref[2 * n, at : at + EDGE], got_ref[2 * n + 1, at : at + EDGE]
            dst[2 * n] = re * c - im * s
            dst[2 * n + 1] = re * s + im * c
    one = pltpu.make_async_copy(low, out_ref.at[:, 0:EDGE], sems.at[0])
    two = pltpu.make_async_copy(high, out_ref.at[:, wide - EDGE : wide], sems.at[1])
    one.start()
    two.start()
    one.wait()
    two.wait()


def fill_call(x_rot, got, ext):
    shape = (ext.shape[0], EDGE, ext.shape[2])
    return pl.pallas_call(
        fill_kernel,
        out_shape=jax.ShapeDtypeStruct(ext.shape, jnp.float32),
        in_specs=[SMEM, VMEM, HBM],
        out_specs=HBM,
        scratch_shapes=[
            pltpu.VMEM(shape, jnp.float32),
            pltpu.VMEM(shape, jnp.float32),
            pltpu.SemaphoreType.DMA((2,)),
        ],
        input_output_aliases={2: 0},
        compiler_params=params(4),
        name="fill",
    )(x_rot, got, ext)


def first_corr_kernel(which_ref, occ_ref, resp_ref, pot_ref, guess_ref, out_ref, mixed, red):
    bands, _, rows, _ = resp_ref.shape
    group = occ_ref.shape[0]
    step = pl.program_id(0)

    @pl.when(step == 0)
    def _():
        for n in range(bands):
            re = resp_ref[n, 0]
            im = resp_ref[n, 1]
            mixed[2 * n] = pot_ref[0] * re - pot_ref[1] * im - SHIFT_WEIGHT * guess_ref[n, 0]
            mixed[2 * n + 1] = pot_ref[0] * im + pot_ref[1] * re - SHIFT_WEIGHT * guess_ref[n, 1]

    def row(i, accs):
        at = rows8(i)
        occ = [(occ_ref[k, 0, at], occ_ref[k, 1, at]) for k in range(group)]
        accs = list(accs)
        for n in range(bands):
            re, im = mixed[2 * n, at], mixed[2 * n + 1, at]
            for k, (pr, pi) in enumerate(occ):
                j = (k * bands + n) * 2
                accs[j] = accs[j] + (pr * re + pi * im)
                accs[j + 1] = accs[j + 1] + (pr * im - pi * re)
        return tuple(accs)

    zero = jnp.zeros((8, 128), jnp.float32)
    count = 2 * bands * group
    accs = lax.fori_loop(0, rows // 8, row, (zero,) * count)
    for j in range(count):
        red[step * count + j] = accs[j]

    @pl.when(step == pl.num_programs(0) - 1)
    def _():
        out_ref[...] = jnp.zeros(out_ref.shape, jnp.float32)
        total = sum_rows(red[...])
        side = which_ref[0]
        out_ref[0:1] = jnp.where(side == 0, total, 0.0)
        out_ref[1:2] = jnp.where(side == 0, 0.0, total)


def first_corr(which, psi_occ, psi_resp, pot, guess):
    group = 4
    count, _, rows, cols = psi_occ.shape
    fixed = lambda shape: pl.BlockSpec(shape, lambda i: (0,) * len(shape))
    return pl.pallas_call(
        first_corr_kernel,
        out_shape=jax.ShapeDtypeStruct((8, 128), jnp.float32),
        grid=(count // group,),
        in_specs=[
            SMEM,
            pl.BlockSpec((group, 2, rows, cols), lambda i: (i, 0, 0, 0)),
            fixed(psi_resp.shape),
            fixed(pot.shape),
            fixed(guess.shape),
        ],
        out_specs=fixed((8, 128)),
        scratch_shapes=[
            pltpu.VMEM((psi_resp.shape[0] * 2, rows, cols), jnp.float32),
            pltpu.VMEM((128, 8, 128), jnp.float32),
        ],
        compiler_params=params(14),
        name="first_corr",
    )(which, psi_occ, psi_resp, pot, guess)


def gather_kernel(start_ref, rot_ref, str_ref, mid_ref, low_ref, high_ref, img_ref,
                  zsum_ref, out_ref, up_ref, down_ref, low, high, red):
    fields = mid_ref.shape[0]
    half = zsum_ref.shape[1]
    for n in range(fields // 2):
        for src, dst, j in ((low_ref, low, 0), (high_ref, high, 2)):
            c, s = rot_ref[j], rot_ref[j + 1]
            re, im = src[2 * n], src[2 * n + 1]
            dst[2 * n] = re * c - im * s
            dst[2 * n + 1] = re * s + im * c
        for k in range(2):
            f = 2 * n + k
            zsum_ref[f] = low[f, EDGE : EDGE + half] + high[f, EDGE : EDGE + half]
    atoms = img_ref.shape[0]

    def atom(a, _):
        begin = pl.multiple_of(start_ref[a], 8)
        accs = [jnp.zeros((8, 128), jnp.float32)] * fields
        for z, src in enumerate((low, mid_ref, high)):
            for k in range(2):
                at = pl.ds(pl.multiple_of(begin + 8 * k, 8), 8)
                ire = img_ref[a, z, 0, 8 * k : 8 * k + 8]
                iim = img_ref[a, z, 1, 8 * k : 8 * k + 8]
                for n in range(fields // 2):
                    re, im = src[2 * n, at], src[2 * n + 1, at]
                    accs[2 * n] = accs[2 * n] + (re * ire - im * iim)
                    accs[2 * n + 1] = accs[2 * n + 1] + (re * iim + im * ire)
        for f in range(fields):
            red[a * fields + f] = accs[f] * str_ref[a]
        return 0

    lax.fori_loop(0, atoms, atom, 0)
    total = atoms * fields
    even = lax.broadcasted_iota(jnp.int32, (1, 128), 1) % 2 == 0
    for b in range(out_ref.shape[0]):
        stop = min(total, 128 * b + 128)
        value = sum_rows(red[128 * b : stop])
        times_i = jnp.where(even, -pltpu.roll(value, 127, 1), pltpu.roll(value, 1, 1))
        out_ref[b : b + 1] = value
        up_ref[b : b + 1] = value * rot_ref[4] + times_i * rot_ref[5]
        down_ref[b : b + 1] = value * rot_ref[6] + times_i * rot_ref[7]


def gather(starts, rot, strength, mid, low, high, img):
    fields, rows, cols = mid.shape
    atoms = img.shape[0]
    blocks = -(-atoms * fields // 128)
    coef = jax.ShapeDtypeStruct((blocks, 128), jnp.float32)
    return pl.pallas_call(
        gather_kernel,
        out_shape=(
            jax.ShapeDtypeStruct((fields, rows - 2 * EDGE, cols), jnp.float32),
            coef,
            coef,
            coef,
        ),
        in_specs=[SMEM] * 3 + [VMEM] * 4,
        out_specs=(VMEM,) * 4,
        scratch_shapes=[
            pltpu.VMEM(mid.shape, jnp.float32),
            pltpu.VMEM(mid.shape, jnp.float32),
            pltpu.VMEM((atoms * fields, 8, 128), jnp.float32),
        ],
        compiler_params=params(10),
        name="gather",
    )(starts, rot, strength, mid, low, high, img)


def spread_into(acc, start_of, coef_ref, image_of, atoms):
    fields = acc.shape[0]

    def atom(a, _):
        begin = pl.multiple_of(start_of(a), 8)
        line = lax.div(a * fields, 128)
        lane = lax.rem(a * fields, 128)
        for k in range(2):
            at = pl.ds(pl.multiple_of(begin + 8 * k, 8), 8)
            ire = image_of(a, 0, k)
            iim = image_of(a, 1, k)
            for n in range(fields // 2):
                pr = coef_ref[line, lane + 2 * n]
                pi = coef_ref[line, lane + 2 * n + 1]
                acc[2 * n, at] = acc[2 * n, at] + (pr * ire + pi * iim)
                acc[2 * n + 1, at] = acc[2 * n + 1, at] + (pi * ire - pr * iim)
        return 0

    lax.fori_loop(0, atoms, atom, 0)


def stencil_kernel(which_ref, energy_ref, twist_ref, starts_ref, coef_ref, mid_ref, zsum_ref, pot_ref, img_ref, out_ref):
    fields, half, cols = zsum_ref.shape
    lane = lax.broadcasted_iota(jnp.int32, (half, cols), 1)
    first, last = lane == 0, lane == cols - 1
    c, s = twist_ref[0], twist_ref[1]
    pot = pot_ref[0, pl.ds(pl.multiple_of(which_ref[0] * half, 8), half)] + 3.0
    for n in range(fields // 2):
        re = mid_ref[2 * n, EDGE : EDGE + half]
        im = mid_ref[2 * n + 1, EDGE : EDGE + half]
        re_next, im_next = pltpu.roll(re, cols - 1, 1), pltpu.roll(im, cols - 1, 1)
        re_prev, im_prev = pltpu.roll(re, 1, 1), pltpu.roll(im, 1, 1)
        y_re = jnp.where(last, re_next * c - im_next * s, re_next) + jnp.where(
            first, re_prev * c + im_prev * s, re_prev
        )
        y_im = jnp.where(last, re_next * s + im_next * c, im_next) + jnp.where(
            first, im_prev * c - re_prev * s, im_prev
        )
        scale = pot - energy_ref[n]
        for f, value, beside in ((2 * n, re, y_re), (2 * n + 1, im, y_im)):
            beside = beside + zsum_ref[f]
            beside = beside + mid_ref[f, EDGE - 1 : EDGE - 1 + half]
            beside = beside + mid_ref[f, EDGE + 1 : EDGE + 1 + half]
            out_ref[f, EDGE : EDGE + half] = scale * value - 0.5 * beside
            out_ref[f, 0:EDGE] = jnp.zeros((EDGE, cols), jnp.float32)
            out_ref[f, EDGE + half :] = jnp.zeros((EDGE + WIN, cols), jnp.float32)
    atoms = img_ref.shape[0]
    image = lambda a, part, k: img_ref[a, 1, part, 8 * k : 8 * k + 8]
    spread_into(out_ref, lambda a: starts_ref[0, a], coef_ref, image, atoms)


def stencil(which, energy, twist, starts, coef, mid, zsum, pot, img):
    fields, half, cols = zsum.shape
    return pl.pallas_call(
        stencil_kernel,
        out_shape=jax.ShapeDtypeStruct((fields, half + 2 * EDGE + WIN, cols), jnp.float32),
        in_specs=[SMEM] * 5 + [VMEM] * 4,
        out_specs=VMEM,
        compiler_params=params(10),
        name="stencil",
    )(which, energy, twist, starts, coef, mid, zsum, pot, img)


def spread_sides(acc, starts_ref, low_coef, high_coef, low_img, high_img):
    atoms = low_img.shape[0]
    for j, coef, img in ((1, low_coef, low_img), (2, high_coef, high_img)):
        image = lambda a, part, k, img=img: img[a, part, 8 * k : 8 * k + 8]
        spread_into(acc, lambda a, j=j: starts_ref[j, a], coef, image, atoms)


def occupied_into(store, half, fields, sums_ref, side, own_ref, other_ref, base, scale, block):
    count = own_ref.shape[0]

    def rows_of(b, _):
        at = pl.ds(pl.multiple_of(b * block, 8), block)

        def band(m, accs):
            accs = list(accs)
            for row, occ in ((side, own_ref), (1 - side, other_ref)):
                pr, pi = occ[m, 0, at], occ[m, 1, at]
                for n in range(fields // 2):
                    sr = sums_ref[row, m * fields + 2 * n]
                    si = sums_ref[row, m * fields + 2 * n + 1]
                    accs[2 * n] = accs[2 * n] + (pr * sr - pi * si)
                    accs[2 * n + 1] = accs[2 * n + 1] + (pr * si + pi * sr)
            return tuple(accs)

        zero = jnp.zeros((block, 128), jnp.float32)
        accs = lax.fori_loop(0, count, band, (zero,) * fields)
        for f in range(fields):
            store(f, b * block, base(f, b * block, block) + scale * accs[f])
        return 0

    lax.fori_loop(0, half // block, rows_of, 0)


def correlate_into(red, src, offset, half, own_ref, other_ref):
    fields = src.shape[0]
    count = own_ref.shape[0]
    bands = fields // 2

    def pair(g, _):
        def row(i, accs):
            at = rows8(i)
            moved = pl.ds(pl.multiple_of(i * 8 + offset, 8), 8)
            accs = list(accs)
            occ = []
            for ref in (own_ref, other_ref):
                for k in range(2):
                    occ.append((ref[2 * g + k, 0, at], ref[2 * g + k, 1, at]))
            for n in range(bands):
                re, im = src[2 * n, moved], src[2 * n + 1, moved]
                for q, (pr, pi) in enumerate(occ):
                    j = (q * bands + n) * 2
                    accs[j] = accs[j] + (pr * re + pi * im)
                    accs[j + 1] = accs[j + 1] + (pr * im - pi * re)
            return tuple(accs)

        zero = jnp.zeros((8, 128), jnp.float32)
        accs = lax.fori_loop(0, half // 8, row, (zero,) * (8 * bands))
        for q in range(4):
            for j in range(fields):
                red[q // 2, (2 * g + q % 2) * fields + j] = accs[q * fields + j]
        return 0

    lax.fori_loop(0, count // 2, pair, 0)


def dots_into(red_dot, half, fields, pairs):
    bands = fields // 2

    def row(i, accs):
        at = pl.ds(pl.multiple_of(i * 8 + EDGE, 8), 8)
        accs = list(accs)
        for p, (left, right) in enumerate(pairs):
            for n in range(bands):
                value = left[2 * n, at] * right[2 * n, at] + left[2 * n + 1, at] * right[2 * n + 1, at]
                accs[p * bands + n] = accs[p * bands + n] + value
        return tuple(accs)

    zero = jnp.zeros((8, 128), jnp.float32)
    accs = lax.fori_loop(0, half // 8, row, (zero,) * (bands * len(pairs)))
    for j in range(bands * len(pairs)):
        red_dot[j] = accs[j]


def pick_block(half):
    return next(b for b in (24, 16, 8) if half % b == 0)


def shift_rows(start, size):
    return pl.ds(pl.multiple_of(start + EDGE, 8), size)


def start_halves(which_ref, half, pairs, sems):
    begin = pl.multiple_of(which_ref[0] * half, 8)
    copies = []
    for j, (src, dst, cut) in enumerate(pairs):
        if cut:
            src = src.at[:, :, pl.ds(begin, half)] if len(src.shape) == 4 else src.at[:, pl.ds(begin, half)]
        copies.append(pltpu.make_async_copy(src, dst, sems.at[j]))
    for copy in copies:
        copy.start()
    return copies


def write_sums(sum_ref, side, red):
    mine, theirs = sum_rows(red[0]), sum_rows(red[1])
    sum_ref[...] = jnp.zeros(sum_ref.shape, jnp.float32)
    sum_ref[0:1] = jnp.where(side == 0, mine, theirs)
    sum_ref[1:2] = jnp.where(side == 0, theirs, mine)


def write_edges(edge_ref, out_ref, half):
    for f in range(out_ref.shape[0]):
        edge_ref[f, 0:EDGE] = out_ref[f, EDGE : 2 * EDGE]
        edge_ref[f, EDGE : 2 * EDGE] = out_ref[f, half : half + EDGE]


def residual_kernel(scale, which_ref, starts_ref, low_coef, high_coef, sums_ref, lap_ref, low_ref, high_ref,
                    occ_ref, occ_other_ref, resp_hbm, pot_hbm, out_ref, edge_ref, sum_ref,
                    acc, own, other, resp, pot, red, red_dot, sems):
    fields, wide, cols = out_ref.shape
    half = wide - 2 * EDGE
    side = which_ref[0]
    copies = start_halves(
        which_ref,
        half,
        [(occ_ref, own, True), (occ_other_ref, other, False), (resp_hbm, resp, True), (pot_hbm, pot, True)],
        sems,
    )
    acc[...] = lap_ref[...]
    spread_sides(acc, starts_ref, low_coef, high_coef, low_ref, high_ref)
    for copy in copies:
        copy.wait()

    def base(f, start, size):
        at = pl.ds(pl.multiple_of(start, 8), size)
        re, im = resp[f // 2, 0, at], resp[f // 2, 1, at]
        if f % 2 == 0:
            prod = pot[0, at] * re - pot[1, at] * im
        else:
            prod = pot[0, at] * im + pot[1, at] * re
        return -prod - acc[f, shift_rows(start, size)]

    block = pick_block(half)

    def store(f, start, value):
        out_ref[f, shift_rows(start, block)] = value

    occupied_into(store, half, fields, sums_ref, side, own, other, base, scale, block)
    write_edges(edge_ref, out_ref, half)
    correlate_into(red, out_ref, EDGE, half, own, other)
    dots_into(red_dot, half, fields, [(out_ref, out_ref)])
    write_sums(sum_ref, side, red)
    sum_ref[2:3] = sum_rows(red_dot[0 : fields // 2])


def field_outputs(fields, half, cols):
    return (
        jax.ShapeDtypeStruct((fields, half + 2 * EDGE, cols), jnp.float32),
        jax.ShapeDtypeStruct((fields, 2 * EDGE, cols), jnp.float32),
        jax.ShapeDtypeStruct((8, 128), jnp.float32),
    )


def residual_call(scale, which, starts, low_coef, high_coef, sums, lap, low_img, high_img, psi_occ, other, resp, pot):
    fields, long, cols = lap.shape
    half = long - 2 * EDGE - WIN
    return pl.pallas_call(
        functools.partial(residual_kernel, scale),
        out_shape=field_outputs(fields, half, cols),
        in_specs=[SMEM] * 5 + [VMEM] * 3 + [HBM] * 4,
        out_specs=(VMEM,) * 3,
        scratch_shapes=[
            pltpu.VMEM(lap.shape, jnp.float32),
            pltpu.VMEM(other.shape, jnp.float32),
            pltpu.VMEM(other.shape, jnp.float32),
            pltpu.VMEM(resp.shape[:2] + (half, cols), jnp.float32),
            pltpu.VMEM((2, half, cols), jnp.float32),
            pltpu.VMEM((2, 128, 8, 128), jnp.float32),
            pltpu.VMEM((16, 8, 128), jnp.float32),
            pltpu.SemaphoreType.DMA((4,)),
        ],
        compiler_params=params(16),
        name="residual",
    )(which, starts, low_coef, high_coef, sums, lap, low_img, high_img, psi_occ, other, resp, pot)


def image_kernel(scale, which_ref, starts_ref, low_coef, high_coef, sums_ref, lap_ref, low_ref, high_ref,
                 res_ref, occ_ref, occ_other_ref, out_ref, edge_ref, sum_ref,
                 acc, own, other, red, red_dot, sems):
    fields, wide, cols = out_ref.shape
    half = wide - 2 * EDGE
    side = which_ref[0]
    copies = start_halves(which_ref, half, [(occ_ref, own, True), (occ_other_ref, other, False)], sems)
    acc[...] = lap_ref[...]
    spread_sides(acc, starts_ref, low_coef, high_coef, low_ref, high_ref)
    for copy in copies:
        copy.wait()

    block = pick_block(half)

    def base(f, start, size):
        return acc[f, shift_rows(start, size)]

    def store(f, start, value):
        out_ref[f, shift_rows(start, block)] = value

    occupied_into(store, half, fields, sums_ref, side, own, other, base, scale, block)
    write_edges(edge_ref, out_ref, half)
    correlate_into(red, out_ref, EDGE, half, own, other)
    dots_into(red_dot, half, fields, [(res_ref, out_ref), (out_ref, out_ref)])
    write_sums(sum_ref, side, red)
    sum_ref[2:3] = sum_rows(red_dot[0:fields])


def image_call(scale, which, starts, low_coef, high_coef, sums, lap, low_img, high_img, res, psi_occ, other):
    fields, long, cols = lap.shape
    half = long - 2 * EDGE - WIN
    return pl.pallas_call(
        functools.partial(image_kernel, scale),
        out_shape=field_outputs(fields, half, cols),
        in_specs=[SMEM] * 5 + [VMEM] * 4 + [HBM] * 2,
        out_specs=(VMEM,) * 3,
        scratch_shapes=[
            pltpu.VMEM(lap.shape, jnp.float32),
            pltpu.VMEM(other.shape, jnp.float32),
            pltpu.VMEM(other.shape, jnp.float32),
            pltpu.VMEM((2, 128, 8, 128), jnp.float32),
            pltpu.VMEM((16, 8, 128), jnp.float32),
            pltpu.SemaphoreType.DMA((2,)),
        ],
        compiler_params=params(16),
        name="image",
    )(which, starts, low_coef, high_coef, sums, lap, low_img, high_img, res, psi_occ, other)


def local_kernel(starts_ref, low_coef, high_coef, lap_ref, low_ref, high_ref, field_ref, part_ref,
                 out_ref, sum_ref, red_dot):
    fields = out_ref.shape[0]
    half = field_ref.shape[1] - 2 * EDGE
    out_ref[...] = lap_ref[...]
    spread_sides(out_ref, starts_ref, low_coef, high_coef, low_ref, high_ref)
    dots_into(red_dot, half, fields, [(field_ref, out_ref)])
    sum_ref[...] = part_ref[...]
    sum_ref[3:4] = sum_rows(red_dot[0 : fields // 2])


def local_call(starts, low_coef, high_coef, lap, low_img, high_img, field, part):
    return pl.pallas_call(
        local_kernel,
        out_shape=(
            jax.ShapeDtypeStruct(lap.shape, jnp.float32),
            jax.ShapeDtypeStruct((8, 128), jnp.float32),
        ),
        in_specs=[SMEM] * 3 + [VMEM] * 5,
        out_specs=(VMEM, VMEM),
        scratch_shapes=[pltpu.VMEM((16, 8, 128), jnp.float32)],
        compiler_params=params(8),
        name="local",
    )(starts, low_coef, high_coef, lap, low_img, high_img, field, part)


def last_kernel(which_ref, sums_ref, mix_ref, res_ref, first_ref, second_ref, occ_ref, occ_other_ref,
                out_ref, own, other, sems):
    fields, half, cols = out_ref.shape
    side = which_ref[0]
    copies = start_halves(which_ref, half, [(occ_ref, own, True), (occ_other_ref, other, False)], sems)
    for copy in copies:
        copy.wait()
    block = pick_block(half)

    def base(f, start, size):
        n = f // 2
        at = shift_rows(start, size)
        return res_ref[f, at] + mix_ref[0, n] * first_ref[f, at] + mix_ref[1, n] * second_ref[f, at]

    def store(f, start, value):
        out_ref[f, pl.ds(pl.multiple_of(start, 8), block)] = value

    occupied_into(store, half, fields, sums_ref, side, own, other, base, 1.0, block)


def last_call(which, sums, mix, res, first, second, psi_occ, other):
    fields, wide, cols = res.shape
    half = wide - 2 * EDGE
    return pl.pallas_call(
        last_kernel,
        out_shape=jax.ShapeDtypeStruct((fields, half, cols), jnp.float32),
        in_specs=[SMEM] * 3 + [VMEM] * 3 + [HBM] * 2,
        out_specs=VMEM,
        scratch_shapes=[
            pltpu.VMEM(other.shape, jnp.float32),
            pltpu.VMEM(other.shape, jnp.float32),
            pltpu.SemaphoreType.DMA((2,)),
        ],
        compiler_params=params(12),
        name="last",
    )(which, sums, mix, res, first, second, psi_occ, other)


def xor_sum(block, bits):
    count = lax.axis_size("space") * lax.axis_size("occ")
    masks = [0]
    for bit in bits:
        masks = masks + [mask | bit for mask in masks]
    parts = [block]
    for mask in masks[1:]:
        parts.append(lax.ppermute(block, ("space", "occ"), [(i, i ^ mask) for i in range(count)]))
    while len(parts) > 1:
        parts = [parts[j] + parts[j + 1] for j in range(0, len(parts), 2)]
    return parts[0]


def total(block):
    count = lax.axis_size("space")
    bit = 2
    while count > 1:
        if count % 4 == 0:
            block = xor_sum(block, (bit, 2 * bit))
            bit, count = 4 * bit, count // 4
        else:
            block = xor_sum(block, (bit,))
            bit, count = 2 * bit, count // 2
    return xor_sum(block, (1,))


def exchange(block):
    return lax.ppermute(block, "occ", SWAP)


def from_behind(block, distance):
    count = lax.axis_size("space")
    return lax.ppermute(block, "space", [((i - distance) % count, i) for i in range(count)])


def window_images(x_cell, y_cell, offsets, values, theta_y, rows_y, planes):
    y_raw = y_cell[:, None] + offsets[None, :, 2]
    y_wrap = jnp.floor_divide(y_raw, rows_y)
    y_at = y_raw - y_wrap * rows_y
    angles = theta_y * y_wrap.astype(jnp.float32)
    row = x_cell[:, None] + offsets[None, :, 1] + RAD
    slot = []
    for plane in planes:
        wanted = (row[:, None, :] == jnp.arange(WIN, dtype=jnp.int32)[None, :, None]) & (
            offsets[:, 0] == plane
        )[None, None, :]
        slot.append(wanted)
    slots = jnp.stack(slot, axis=1)
    weights = jnp.stack([values * jnp.cos(angles), values * jnp.sin(angles)], axis=1)
    left = jnp.where(slots[:, :, None], weights[:, None, :, None, :], 0.0)
    atoms = left.shape[0]
    left = left.reshape(atoms, len(planes) * 2 * WIN, -1)
    right = (y_at[:, :, None] == jnp.arange(rows_y, dtype=jnp.int32)[None, None, :]).astype(jnp.float32)
    image = jnp.einsum("apk,aky->apy", left, right, precision=PRECISE)
    return image.reshape(atoms, len(planes), 2, WIN, rows_y)


def shards(
    psi_occ,
    psi_resp,
    initial_guess,
    local_potential,
    potential_change,
    band_energy,
    q_index,
    atom_cells,
    offsets,
    projector,
    strength,
):
    slab_count = lax.axis_size("space")
    slab_index = lax.axis_index("space")
    side = lax.axis_index("occ")
    layers, rows_x, rows_y = local_potential.shape
    half = rows_x // 2
    atoms = atom_cells.shape[0]
    bands = psi_resp.shape[0]
    fields = 2 * bands
    weight = 1.0 / (layers * slab_count * rows_x * rows_y)
    thetas = q_index.astype(jnp.float32) * (2.0 * math.pi / QDIV)
    cosines = jnp.cos(thetas)
    sines = jnp.sin(thetas)
    at_first = slab_index == 0
    at_last = slab_index == slab_count - 1
    z_rot = jnp.stack(
        [
            jnp.where(at_first, cosines[0], 1.0),
            jnp.where(at_first, -sines[0], 0.0),
            jnp.where(at_last, cosines[0], 1.0),
            jnp.where(at_last, sines[0], 0.0),
            jnp.where(at_last, cosines[0], 1.0),
            jnp.where(at_last, -sines[0], 0.0),
            jnp.where(at_first, cosines[0], 1.0),
            jnp.where(at_first, sines[0], 0.0),
        ]
    )
    x_rot = jnp.stack(
        [
            jnp.where(side == 0, cosines[1], 1.0),
            jnp.where(side == 0, -sines[1], 0.0),
            jnp.where(side == 1, cosines[1], 1.0),
            jnp.where(side == 1, sines[1], 0.0),
        ]
    )
    y_twist = jnp.stack([cosines[2], sines[2]])
    which = side.astype(jnp.int32).reshape(1)

    occ = psi_occ.reshape(psi_occ.shape[0], 2, rows_x, rows_y)
    resp = psi_resp.reshape(bands, 2, rows_x, rows_y)
    guess = initial_guess.reshape(bands, 2, rows_x, rows_y)
    change = potential_change.reshape(2, rows_x, rows_y)

    occ_other = exchange(lax.dynamic_slice_in_dim(occ, (1 - side) * half, half, axis=2))
    guess_mid = prep_call(which, x_rot, guess)

    packed = jnp.stack(
        [
            projector,
            jnp.pad(atom_cells.astype(jnp.float32), ((0, 0), (0, projector.shape[1] - 3))),
        ],
        axis=1,
    )
    below = from_behind(packed, 1)
    above = from_behind(packed, -1)
    cells = [atom_cells]
    for side_pack in (below, above):
        cells.append(side_pack[:, 1, :3].astype(jnp.int32))
    all_x = jnp.stack([c[:, 1] for c in cells])
    all_y = jnp.stack([c[:, 2] for c in cells])
    at_row = jnp.mod(all_x - RAD - side * half + EDGE, rows_x)
    inner = at_row % 8
    touching = at_row < half + EDGE
    put_starts = jnp.where(touching, at_row - inner, half + 2 * EDGE).astype(jnp.int32)
    get_starts = jnp.where(touching[0], at_row[0] - inner[0], 0).astype(jnp.int32)
    img = window_images(inner[0], all_y[0], offsets, projector, thetas[2], rows_y, (-1, 0, 1))
    low_img = window_images(inner[1], all_y[1], offsets, below[:, 0], thetas[2], rows_y, (1,))[:, 0]
    high_img = window_images(inner[2], all_y[2], offsets, above[:, 0], thetas[2], rows_y, (-1,))[:, 0]

    def local_part(mid):
        low = from_behind(mid, 1)
        high = from_behind(mid, -1)
        zsum, proj, up, down = gather(get_starts, z_rot, strength, mid, low, high, img)
        low_coef = from_behind(up, 1)
        high_coef = from_behind(down, -1)
        lap = stencil(which, band_energy, y_twist, put_starts, proj, mid, zsum, local_potential, img)
        return put_starts, low_coef, high_coef, lap

    first_sums = total(first_corr(which, occ, resp, change, guess))
    starts, low_coef, high_coef, lap = local_part(guess_mid)
    residual, edges, part = residual_call(
        weight, which, starts, low_coef, high_coef, first_sums, lap, low_img, high_img, occ, occ_other, resp, change
    )
    tot = total(part)
    norm0 = tot[2, :bands]
    residual = fill_call(x_rot, exchange(edges), residual)
    residual_other = exchange(residual)
    starts, low_coef, high_coef, lap = local_part(residual)
    image, edges, part = image_call(
        SHIFT_WEIGHT * weight, which, starts, low_coef, high_coef, tot, lap, low_img, high_img, residual, occ, occ_other
    )
    image = fill_call(x_rot, exchange(edges), image)
    image_other = exchange(image)
    starts, low_coef, high_coef, lap = local_part(image)
    image2, part = local_call(starts, low_coef, high_coef, lap, low_img, high_img, image, part)
    tot = total(part)
    sums = tot[0:2]
    cross = tot[2, :bands]
    square = tot[2, bands : 2 * bands]
    occ_square = jnp.sum((sums * sums).reshape(-1, bands, 2), axis=(0, 2))
    triple = tot[3, :bands] + SHIFT_WEIGHT * weight * occ_square
    step0 = norm0 / cross
    norm1 = norm0 - 2.0 * step0 * cross + step0 * step0 * square
    growth = norm1 / norm0
    lead = 1.0 + growth
    curvature = lead * lead * cross - 2.0 * lead * step0 * square + step0 * step0 * triple
    step1 = norm1 / curvature
    mix0 = -step0 - step1 * lead
    mix1 = step1 * step0
    per_lane = jnp.tile(jnp.repeat(mix1, 2), sums.shape[1] // fields)
    last_sums = SHIFT_WEIGHT * weight * sums * per_lane[None, :]
    mine = last_call(which, last_sums, jnp.stack([mix0, mix1]), residual, image, image2, occ, occ_other)
    theirs = exchange(mine)

    def join(own_half, other_half):
        lower = jnp.where(side == 0, own_half, other_half)
        upper = jnp.where(side == 0, other_half, own_half)
        return jnp.concatenate([lower, upper], axis=1).reshape(bands, 2, 1, rows_x, rows_y)

    inside = lambda v: v[:, EDGE : EDGE + half]
    wide = lambda v: v[:, None, None, None, None]
    response = (
        initial_guess
        + wide(step0 + step1 * lead) * join(inside(residual), inside(residual_other))
        - wide(step0 * step1) * join(inside(image), inside(image_other))
    )
    return response, join(mine, theirs)


def solution(mesh):
    return jax.shard_map(
        shards,
        mesh=mesh,
        in_specs=(
            P("occ", None, "space", None, None),
            P("resp", None, "space", None, None),
            P("resp", None, "space", None, None),
            P("space", None, None),
            P(None, "space", None, None),
            P("resp"),
            P(),
            P("space", None),
            P(),
            P("space", None),
            P("space"),
        ),
        out_specs=(P("resp", None, "space", None, None), P("resp", None, "space", None, None)),
        check_vma=False,
    )
```

```python
import functools
import math

import jax
import jax.numpy as jnp
from jax import lax
from jax.experimental import pallas as pl
from jax.experimental.pallas import tpu as pltpu
from jax.sharding import PartitionSpec as P

RAD = 4
QDIV = 8
EDGE = 8
WIN = 16
SHIFT_WEIGHT = 3.0
PRECISE = lax.Precision.HIGHEST
SWAP = [(0, 1), (1, 0)]

VMEM = pl.BlockSpec(memory_space=pltpu.VMEM)
SMEM = pl.BlockSpec(memory_space=pltpu.SMEM)
ANY = pl.BlockSpec(memory_space=pl.ANY)
HBM = pl.BlockSpec(memory_space=pltpu.HBM)


def params(mib):
    return pltpu.CompilerParams(vmem_limit_bytes=mib * 1024 * 1024)


def sum_rows(values):
    total = jnp.sum(values, axis=2, keepdims=True)
    row = lax.broadcasted_iota(jnp.int32, values.shape, 0)
    lane = lax.broadcasted_iota(jnp.int32, values.shape, 2)
    picked = jnp.sum(jnp.where(row == lane, total, 0.0), axis=0)
    return jnp.sum(picked, axis=0, keepdims=True)


def rows8(index):
    return pl.ds(pl.multiple_of(index * 8, 8), 8)


def prep_kernel(which_ref, rot_ref, guess_ref, occ_ref, out_ref, send_ref, middle, low, high, sems):
    fields, wide, _ = out_ref.shape
    half = wide - 2 * EDGE
    count = occ_ref.shape[0]
    side = which_ref[0]
    begin = pl.multiple_of(side * half, 8)
    away = pl.multiple_of((1 - side) * half, 8)
    under = pl.multiple_of((1 - side) * half + half - EDGE, 8)
    copies = []
    for j, (start, size, dst) in enumerate(((begin, half, middle), (under, EDGE, low), (away, EDGE, high))):
        copies.append(pltpu.make_async_copy(guess_ref.at[:, :, pl.ds(start, size)], dst, sems.at[j]))
    parts = sems.shape[0] - 3
    each = count // parts
    sends = []
    for j in range(parts):
        chosen = slice(j * each, (j + 1) * each)
        sends.append(
            pltpu.make_async_copy(occ_ref.at[chosen, :, pl.ds(away, half)], send_ref.at[chosen], sems.at[3 + j])
        )
    for copy in copies + sends:
        copy.start()
    for copy in copies:
        copy.wait()
    for n in range(fields // 2):
        for k in range(2):
            out_ref[2 * n + k, EDGE : EDGE + half] = middle[n, k]
        for src, spot, j in ((low, 0, 0), (high, EDGE + half, 2)):
            c, s = rot_ref[j], rot_ref[j + 1]
            re, im = src[n, 0], src[n, 1]
            out_ref[2 * n, spot : spot + EDGE] = re * c - im * s
            out_ref[2 * n + 1, spot : spot + EDGE] = re * s + im * c
    for copy in sends:
        copy.wait()


def prep_call(which, x_rot, guess, occ):
    bands, _, rows, cols = guess.shape
    half = rows // 2
    return pl.pallas_call(
        prep_kernel,
        out_shape=(
            jax.ShapeDtypeStruct((2 * bands, half + 2 * EDGE, cols), jnp.float32),
            jax.ShapeDtypeStruct((occ.shape[0], 2, half, cols), jnp.float32),
        ),
        in_specs=[SMEM, SMEM, HBM, HBM],
        out_specs=(VMEM, HBM),
        scratch_shapes=[
            pltpu.VMEM((bands, 2, half, cols), jnp.float32),
            pltpu.VMEM((bands, 2, EDGE, cols), jnp.float32),
            pltpu.VMEM((bands, 2, EDGE, cols), jnp.float32),
            pltpu.SemaphoreType.DMA((7,)),
        ],
        compiler_params=params(60),
        name="prep",
    )(which, x_rot, guess, occ)


def fill_kernel(rot_ref, got_ref, ext_ref, out_ref, low, high, sems):
    fields, wide, _ = out_ref.shape
    for n in range(fields // 2):
        for dst, at, j in ((low, EDGE, 0), (high, 0, 2)):
            c, s = rot_ref[j], rot_ref[j + 1]
            re, im = got_ref[2 * n, at : at + EDGE], got_ref[2 * n + 1, at : at + EDGE]
            dst[2 * n] = re * c - im * s
            dst[2 * n + 1] = re * s + im * c
    one = pltpu.make_async_copy(low, out_ref.at[:, 0:EDGE], sems.at[0])
    two = pltpu.make_async_copy(high, out_ref.at[:, wide - EDGE : wide], sems.at[1])
    one.start()
    two.start()
    one.wait()
    two.wait()


def fill_call(x_rot, got, ext):
    shape = (ext.shape[0], EDGE, ext.shape[2])
    return pl.pallas_call(
        fill_kernel,
        out_shape=jax.ShapeDtypeStruct(ext.shape, jnp.float32),
        in_specs=[SMEM, VMEM, ANY],
        out_specs=ANY,
        scratch_shapes=[
            pltpu.VMEM(shape, jnp.float32),
            pltpu.VMEM(shape, jnp.float32),
            pltpu.SemaphoreType.DMA((2,)),
        ],
        input_output_aliases={2: 0},
        compiler_params=params(4),
        name="fill",
    )(x_rot, got, ext)


def first_corr_kernel(which_ref, occ_ref, resp_ref, pot_ref, guess_ref, out_ref, mixed, red):
    bands, _, rows, _ = resp_ref.shape
    group = occ_ref.shape[0]
    step = pl.program_id(0)

    @pl.when(step == 0)
    def _():
        for n in range(bands):
            re = resp_ref[n, 0]
            im = resp_ref[n, 1]
            mixed[2 * n] = pot_ref[0] * re - pot_ref[1] * im - SHIFT_WEIGHT * guess_ref[n, 0]
            mixed[2 * n + 1] = pot_ref[0] * im + pot_ref[1] * re - SHIFT_WEIGHT * guess_ref[n, 1]

    def row(i, accs):
        at = rows8(i)
        occ = [(occ_ref[k, 0, at], occ_ref[k, 1, at]) for k in range(group)]
        accs = list(accs)
        for n in range(bands):
            re, im = mixed[2 * n, at], mixed[2 * n + 1, at]
            for k, (pr, pi) in enumerate(occ):
                j = (k * bands + n) * 2
                accs[j] = accs[j] + (pr * re + pi * im)
                accs[j + 1] = accs[j + 1] + (pr * im - pi * re)
        return tuple(accs)

    zero = jnp.zeros((8, 128), jnp.float32)
    count = 2 * bands * group
    accs = lax.fori_loop(0, rows // 8, row, (zero,) * count, unroll=3)
    for j in range(count):
        red[step * count + j] = accs[j]

    @pl.when(step == pl.num_programs(0) - 1)
    def _():
        out_ref[...] = jnp.zeros(out_ref.shape, jnp.float32)
        total = sum_rows(red[...])
        side = which_ref[0]
        out_ref[0:1] = jnp.where(side == 0, total, 0.0)
        out_ref[1:2] = jnp.where(side == 0, 0.0, total)


def first_corr(which, psi_occ, psi_resp, pot, guess):
    group = 4
    count, _, rows, cols = psi_occ.shape
    fixed = lambda shape: pl.BlockSpec(shape, lambda i: (0,) * len(shape))
    return pl.pallas_call(
        first_corr_kernel,
        out_shape=jax.ShapeDtypeStruct((8, 128), jnp.float32),
        grid=(count // group,),
        in_specs=[
            SMEM,
            pl.BlockSpec((group, 2, rows, cols), lambda i: (i, 0, 0, 0)),
            fixed(psi_resp.shape),
            fixed(pot.shape),
            fixed(guess.shape),
        ],
        out_specs=fixed((8, 128)),
        scratch_shapes=[
            pltpu.VMEM((psi_resp.shape[0] * 2, rows, cols), jnp.float32),
            pltpu.VMEM((128, 8, 128), jnp.float32),
        ],
        compiler_params=params(60),
        name="first_corr",
    )(which, psi_occ, psi_resp, pot, guess)


def gather_kernel(start_ref, rot_ref, str_ref, mid_ref, low_ref, high_ref, img_ref,
                  zsum_ref, out_ref, up_ref, down_ref, low, high, red):
    fields = mid_ref.shape[0]
    half = zsum_ref.shape[1]
    for n in range(fields // 2):
        for src, dst, j in ((low_ref, low, 0), (high_ref, high, 2)):
            c, s = rot_ref[j], rot_ref[j + 1]
            re, im = src[2 * n], src[2 * n + 1]
            dst[2 * n] = re * c - im * s
            dst[2 * n + 1] = re * s + im * c
        for k in range(2):
            f = 2 * n + k
            zsum_ref[f] = low[f, EDGE : EDGE + half] + high[f, EDGE : EDGE + half]
    atoms = img_ref.shape[0]

    def atom(a, _):
        begin = pl.multiple_of(start_ref[a], 8)
        accs = [jnp.zeros((8, 128), jnp.float32)] * fields
        for z, src in enumerate((low, mid_ref, high)):
            for k in range(2):
                at = pl.ds(pl.multiple_of(begin + 8 * k, 8), 8)
                ire = img_ref[a, z, 0, 8 * k : 8 * k + 8]
                iim = img_ref[a, z, 1, 8 * k : 8 * k + 8]
                for n in range(fields // 2):
                    re, im = src[2 * n, at], src[2 * n + 1, at]
                    accs[2 * n] = accs[2 * n] + (re * ire - im * iim)
                    accs[2 * n + 1] = accs[2 * n + 1] + (re * iim + im * ire)
        for f in range(fields):
            red[a * fields + f] = accs[f] * str_ref[a]
        return 0

    lax.fori_loop(0, atoms, atom, 0)
    total = atoms * fields
    even = lax.broadcasted_iota(jnp.int32, (1, 128), 1) % 2 == 0
    for b in range(out_ref.shape[0]):
        stop = min(total, 128 * b + 128)
        value = sum_rows(red[128 * b : stop])
        times_i = jnp.where(even, -pltpu.roll(value, 127, 1), pltpu.roll(value, 1, 1))
        out_ref[b : b + 1] = value
        up_ref[b : b + 1] = value * rot_ref[4] + times_i * rot_ref[5]
        down_ref[b : b + 1] = value * rot_ref[6] + times_i * rot_ref[7]


def gather(starts, rot, strength, mid, low, high, img):
    fields, rows, cols = mid.shape
    atoms = img.shape[0]
    blocks = -(-atoms * fields // 128)
    coef = jax.ShapeDtypeStruct((blocks, 128), jnp.float32)
    return pl.pallas_call(
        gather_kernel,
        out_shape=(
            jax.ShapeDtypeStruct((fields, rows - 2 * EDGE, cols), jnp.float32),
            coef,
            coef,
            coef,
        ),
        in_specs=[SMEM] * 3 + [VMEM] * 4,
        out_specs=(VMEM,) * 4,
        scratch_shapes=[
            pltpu.VMEM(mid.shape, jnp.float32),
            pltpu.VMEM(mid.shape, jnp.float32),
            pltpu.VMEM((atoms * fields, 8, 128), jnp.float32),
        ],
        compiler_params=params(10),
        name="gather",
    )(starts, rot, strength, mid, low, high, img)


def spread_into(acc, start_of, coef_ref, image_of, atoms):
    fields = acc.shape[0]

    def atom(a, _):
        begin = pl.multiple_of(start_of(a), 8)
        line = lax.div(a * fields, 128)
        lane = lax.rem(a * fields, 128)
        for k in range(2):
            at = pl.ds(pl.multiple_of(begin + 8 * k, 8), 8)
            ire = image_of(a, 0, k)
            iim = image_of(a, 1, k)
            for n in range(fields // 2):
                pr = coef_ref[line, lane + 2 * n]
                pi = coef_ref[line, lane + 2 * n + 1]
                acc[2 * n, at] = acc[2 * n, at] + (pr * ire + pi * iim)
                acc[2 * n + 1, at] = acc[2 * n + 1, at] + (pi * ire - pr * iim)
        return 0

    lax.fori_loop(0, atoms, atom, 0)


def stencil_kernel(which_ref, energy_ref, twist_ref, starts_ref, coef_ref, mid_ref, zsum_ref, pot_ref, img_ref, out_ref):
    fields, half, cols = zsum_ref.shape
    lane = lax.broadcasted_iota(jnp.int32, (half, cols), 1)
    first, last = lane == 0, lane == cols - 1
    c, s = twist_ref[0], twist_ref[1]
    pot = pot_ref[0, pl.ds(pl.multiple_of(which_ref[0] * half, 8), half)] + 3.0
    for n in range(fields // 2):
        re = mid_ref[2 * n, EDGE : EDGE + half]
        im = mid_ref[2 * n + 1, EDGE : EDGE + half]
        re_next, im_next = pltpu.roll(re, cols - 1, 1), pltpu.roll(im, cols - 1, 1)
        re_prev, im_prev = pltpu.roll(re, 1, 1), pltpu.roll(im, 1, 1)
        y_re = jnp.where(last, re_next * c - im_next * s, re_next) + jnp.where(
            first, re_prev * c + im_prev * s, re_prev
        )
        y_im = jnp.where(last, re_next * s + im_next * c, im_next) + jnp.where(
            first, im_prev * c - re_prev * s, im_prev
        )
        scale = pot - energy_ref[n]
        for f, value, beside in ((2 * n, re, y_re), (2 * n + 1, im, y_im)):
            beside = beside + zsum_ref[f]
            beside = beside + mid_ref[f, EDGE - 1 : EDGE - 1 + half]
            beside = beside + mid_ref[f, EDGE + 1 : EDGE + 1 + half]
            out_ref[f, EDGE : EDGE + half] = scale * value - 0.5 * beside
            out_ref[f, 0:EDGE] = jnp.zeros((EDGE, cols), jnp.float32)
            out_ref[f, EDGE + half :] = jnp.zeros((EDGE + WIN, cols), jnp.float32)
    atoms = img_ref.shape[0]
    image = lambda a, part, k: img_ref[a, 1, part, 8 * k : 8 * k + 8]
    spread_into(out_ref, lambda a: starts_ref[0, a], coef_ref, image, atoms)


def stencil(which, energy, twist, starts, coef, mid, zsum, pot, img):
    fields, half, cols = zsum.shape
    return pl.pallas_call(
        stencil_kernel,
        out_shape=jax.ShapeDtypeStruct((fields, half + 2 * EDGE + WIN, cols), jnp.float32),
        in_specs=[SMEM] * 5 + [VMEM] * 4,
        out_specs=VMEM,
        compiler_params=params(10),
        name="stencil",
    )(which, energy, twist, starts, coef, mid, zsum, pot, img)


def spread_sides(acc, starts_ref, low_coef, high_coef, low_img, high_img):
    atoms = low_img.shape[0]
    for j, coef, img in ((1, low_coef, low_img), (2, high_coef, high_img)):
        image = lambda a, part, k, img=img: img[a, part, 8 * k : 8 * k + 8]
        spread_into(acc, lambda a, j=j: starts_ref[j, a], coef, image, atoms)


def occupied_into(store, half, fields, sums_ref, side, own_ref, other_ref, base, scale, block, copies_of):
    count = own_ref.shape[0]

    def rows_of(b, _):
        at = pl.ds(pl.multiple_of(b * block, 8), block)
        for copy in copies_of(b):
            copy.wait()

        def band(m, accs):
            accs = list(accs)
            for row, occ in ((side, own_ref), (1 - side, other_ref)):
                pr, pi = occ[m, 0, at], occ[m, 1, at]
                for n in range(fields // 2):
                    sr = sums_ref[row, m * fields + 2 * n]
                    si = sums_ref[row, m * fields + 2 * n + 1]
                    accs[2 * n] = accs[2 * n] + (pr * sr - pi * si)
                    accs[2 * n + 1] = accs[2 * n + 1] + (pr * si + pi * sr)
            return tuple(accs)

        zero = jnp.zeros((block, 128), jnp.float32)
        accs = lax.fori_loop(0, count, band, (zero,) * fields, unroll=2)
        for f in range(fields):
            store(f, b * block, base(f, b * block, block) + scale * accs[f])
        return 0

    lax.fori_loop(0, half // block, rows_of, 0)


def correlate_into(red, src, offset, half, own_ref, other_ref):
    fields = src.shape[0]
    count = own_ref.shape[0]
    bands = fields // 2

    def pair(g, _):
        def row(i, accs):
            at = rows8(i)
            moved = pl.ds(pl.multiple_of(i * 8 + offset, 8), 8)
            accs = list(accs)
            occ = []
            for ref in (own_ref, other_ref):
                for k in range(2):
                    occ.append((ref[2 * g + k, 0, at], ref[2 * g + k, 1, at]))
            for n in range(bands):
                re, im = src[2 * n, moved], src[2 * n + 1, moved]
                for q, (pr, pi) in enumerate(occ):
                    j = (q * bands + n) * 2
                    accs[j] = accs[j] + (pr * re + pi * im)
                    accs[j + 1] = accs[j + 1] + (pr * im - pi * re)
            return tuple(accs)

        zero = jnp.zeros((8, 128), jnp.float32)
        accs = lax.fori_loop(0, half // 8, row, (zero,) * (8 * bands), unroll=3)
        for q in range(4):
            for j in range(fields):
                red[q // 2, (2 * g + q % 2) * fields + j] = accs[q * fields + j]
        return 0

    lax.fori_loop(0, count // 2, pair, 0)


def dots_into(red_dot, half, fields, pairs):
    bands = fields // 2

    def row(i, accs):
        at = pl.ds(pl.multiple_of(i * 8 + EDGE, 8), 8)
        accs = list(accs)
        for p, (left, right) in enumerate(pairs):
            for n in range(bands):
                value = left[2 * n, at] * right[2 * n, at] + left[2 * n + 1, at] * right[2 * n + 1, at]
                accs[p * bands + n] = accs[p * bands + n] + value
        return tuple(accs)

    zero = jnp.zeros((8, 128), jnp.float32)
    accs = lax.fori_loop(0, half // 8, row, (zero,) * (bands * len(pairs)), unroll=3)
    for j in range(bands * len(pairs)):
        red_dot[j] = accs[j]


def pick_block(half):
    return next(b for b in (24, 16, 8) if half % b == 0)


def shift_rows(start, size):
    return pl.ds(pl.multiple_of(start + EDGE, 8), size)


def band_copies(which_ref, half, block, b, occ_ref, occ_other_ref, own, other, sems):
    begin = pl.multiple_of(which_ref[0] * half + b * block, 8)
    at = pl.ds(pl.multiple_of(b * block, 8), block)
    return (
        pltpu.make_async_copy(occ_ref.at[:, :, pl.ds(begin, block)], own.at[:, :, at], sems.at[0, b]),
        pltpu.make_async_copy(occ_other_ref.at[:, :, at], other.at[:, :, at], sems.at[1, b]),
    )


def start_bands(half, block, copies_of):
    for b in range(half // block):
        for copy in copies_of(b):
            copy.start()


def write_sums(sum_ref, side, red):
    mine, theirs = sum_rows(red[0]), sum_rows(red[1])
    sum_ref[...] = jnp.zeros(sum_ref.shape, jnp.float32)
    sum_ref[0:1] = jnp.where(side == 0, mine, theirs)
    sum_ref[1:2] = jnp.where(side == 0, theirs, mine)


def write_edges(edge_ref, out_ref, half):
    for f in range(out_ref.shape[0]):
        edge_ref[f, 0:EDGE] = out_ref[f, EDGE : 2 * EDGE]
        edge_ref[f, EDGE : 2 * EDGE] = out_ref[f, half : half + EDGE]


def residual_kernel(scale, which_ref, starts_ref, low_coef, high_coef, sums_ref, lap_ref, low_ref, high_ref,
                    occ_ref, occ_other_ref, resp_hbm, pot_hbm, out_ref, edge_ref, sum_ref,
                    acc, own, other, resp, pot, red, red_dot, sems, more_sems):
    fields, wide, cols = out_ref.shape
    half = wide - 2 * EDGE
    side = which_ref[0]
    block = pick_block(half)
    begin = pl.multiple_of(side * half, 8)
    copies = (
        pltpu.make_async_copy(resp_hbm.at[:, :, pl.ds(begin, half)], resp, more_sems.at[0]),
        pltpu.make_async_copy(pot_hbm.at[:, pl.ds(begin, half)], pot, more_sems.at[1]),
    )
    for copy in copies:
        copy.start()
    copies_of = lambda b: band_copies(which_ref, half, block, b, occ_ref, occ_other_ref, own, other, sems)
    start_bands(half, block, copies_of)
    acc[...] = lap_ref[...]
    spread_sides(acc, starts_ref, low_coef, high_coef, low_ref, high_ref)
    for copy in copies:
        copy.wait()

    def base(f, start, size):
        at = pl.ds(pl.multiple_of(start, 8), size)
        re, im = resp[f // 2, 0, at], resp[f // 2, 1, at]
        if f % 2 == 0:
            prod = pot[0, at] * re - pot[1, at] * im
        else:
            prod = pot[0, at] * im + pot[1, at] * re
        return -prod - acc[f, shift_rows(start, size)]

    def store(f, start, value):
        out_ref[f, shift_rows(start, block)] = value

    occupied_into(store, half, fields, sums_ref, side, own, other, base, scale, block, copies_of)
    write_edges(edge_ref, out_ref, half)
    correlate_into(red, out_ref, EDGE, half, own, other)
    dots_into(red_dot, half, fields, [(out_ref, out_ref)])
    write_sums(sum_ref, side, red)
    sum_ref[2:3] = sum_rows(red_dot[0 : fields // 2])


def field_outputs(fields, half, cols):
    return (
        jax.ShapeDtypeStruct((fields, half + 2 * EDGE, cols), jnp.float32),
        jax.ShapeDtypeStruct((fields, 2 * EDGE, cols), jnp.float32),
        jax.ShapeDtypeStruct((8, 128), jnp.float32),
    )


def residual_call(scale, which, starts, low_coef, high_coef, sums, lap, low_img, high_img, psi_occ, other, resp, pot):
    fields, long, cols = lap.shape
    half = long - 2 * EDGE - WIN
    return pl.pallas_call(
        functools.partial(residual_kernel, scale),
        out_shape=field_outputs(fields, half, cols),
        in_specs=[SMEM] * 5 + [VMEM] * 3 + [HBM] * 4,
        out_specs=(VMEM,) * 3,
        scratch_shapes=[
            pltpu.VMEM(lap.shape, jnp.float32),
            pltpu.VMEM(other.shape, jnp.float32),
            pltpu.VMEM(other.shape, jnp.float32),
            pltpu.VMEM(resp.shape[:2] + (half, cols), jnp.float32),
            pltpu.VMEM((2, half, cols), jnp.float32),
            pltpu.VMEM((2, 128, 8, 128), jnp.float32),
            pltpu.VMEM((16, 8, 128), jnp.float32),
            pltpu.SemaphoreType.DMA((2, half // pick_block(half))),
            pltpu.SemaphoreType.DMA((2,)),
        ],
        compiler_params=params(16),
        name="residual",
    )(which, starts, low_coef, high_coef, sums, lap, low_img, high_img, psi_occ, other, resp, pot)


def image_kernel(scale, which_ref, starts_ref, low_coef, high_coef, sums_ref, lap_ref, low_ref, high_ref,
                 res_ref, occ_ref, occ_other_ref, out_ref, edge_ref, sum_ref,
                 acc, own, other, red, red_dot, sems):
    fields, wide, cols = out_ref.shape
    half = wide - 2 * EDGE
    side = which_ref[0]
    block = pick_block(half)
    copies_of = lambda b: band_copies(which_ref, half, block, b, occ_ref, occ_other_ref, own, other, sems)
    start_bands(half, block, copies_of)
    acc[...] = lap_ref[...]
    spread_sides(acc, starts_ref, low_coef, high_coef, low_ref, high_ref)

    def base(f, start, size):
        return acc[f, shift_rows(start, size)]

    def store(f, start, value):
        out_ref[f, shift_rows(start, block)] = value

    occupied_into(store, half, fields, sums_ref, side, own, other, base, scale, block, copies_of)
    write_edges(edge_ref, out_ref, half)
    correlate_into(red, out_ref, EDGE, half, own, other)
    dots_into(red_dot, half, fields, [(res_ref, out_ref), (out_ref, out_ref)])
    write_sums(sum_ref, side, red)
    sum_ref[2:3] = sum_rows(red_dot[0:fields])


def image_call(scale, which, starts, low_coef, high_coef, sums, lap, low_img, high_img, res, psi_occ, other):
    fields, long, cols = lap.shape
    half = long - 2 * EDGE - WIN
    return pl.pallas_call(
        functools.partial(image_kernel, scale),
        out_shape=field_outputs(fields, half, cols),
        in_specs=[SMEM] * 5 + [VMEM] * 4 + [HBM] * 2,
        out_specs=(VMEM,) * 3,
        scratch_shapes=[
            pltpu.VMEM(lap.shape, jnp.float32),
            pltpu.VMEM(other.shape, jnp.float32),
            pltpu.VMEM(other.shape, jnp.float32),
            pltpu.VMEM((2, 128, 8, 128), jnp.float32),
            pltpu.VMEM((16, 8, 128), jnp.float32),
            pltpu.SemaphoreType.DMA((2, half // pick_block(half))),
        ],
        compiler_params=params(16),
        name="image",
    )(which, starts, low_coef, high_coef, sums, lap, low_img, high_img, res, psi_occ, other)


def local_kernel(starts_ref, low_coef, high_coef, lap_ref, low_ref, high_ref, field_ref, part_ref,
                 out_ref, sum_ref, red_dot):
    fields = out_ref.shape[0]
    half = field_ref.shape[1] - 2 * EDGE
    out_ref[...] = lap_ref[...]
    spread_sides(out_ref, starts_ref, low_coef, high_coef, low_ref, high_ref)
    dots_into(red_dot, half, fields, [(field_ref, out_ref)])
    sum_ref[...] = part_ref[...]
    sum_ref[3:4] = sum_rows(red_dot[0 : fields // 2])


def local_call(starts, low_coef, high_coef, lap, low_img, high_img, field, part):
    return pl.pallas_call(
        local_kernel,
        out_shape=(
            jax.ShapeDtypeStruct(lap.shape, jnp.float32),
            jax.ShapeDtypeStruct((8, 128), jnp.float32),
        ),
        in_specs=[SMEM] * 3 + [VMEM] * 5,
        out_specs=(VMEM, VMEM),
        scratch_shapes=[pltpu.VMEM((16, 8, 128), jnp.float32)],
        compiler_params=params(8),
        name="local",
    )(starts, low_coef, high_coef, lap, low_img, high_img, field, part)


def last_kernel(which_ref, sums_ref, mix_ref, res_hbm, first_hbm, second_hbm, occ_ref, occ_other_ref,
                out_ref, res, first, second, own, other, sems, more_sems):
    fields, half, cols = out_ref.shape
    side = which_ref[0]
    block = pick_block(half)

    def copies_of(b):
        at = pl.ds(pl.multiple_of(b * block, 8), block)
        moved = shift_rows(b * block, block)
        own_copies = tuple(
            pltpu.make_async_copy(src.at[:, moved], dst.at[:, at], more_sems.at[j, b])
            for j, (src, dst) in enumerate(((res_hbm, res), (first_hbm, first), (second_hbm, second)))
        )
        return own_copies + band_copies(which_ref, half, block, b, occ_ref, occ_other_ref, own, other, sems)

    start_bands(half, block, copies_of)

    def base(f, start, size):
        n = f // 2
        at = pl.ds(pl.multiple_of(start, 8), size)
        return res[f, at] + mix_ref[0, n] * first[f, at] + mix_ref[1, n] * second[f, at]

    def store(f, start, value):
        out_ref[f, pl.ds(pl.multiple_of(start, 8), block)] = value

    occupied_into(store, half, fields, sums_ref, side, own, other, base, 1.0, block, copies_of)


def last_call(which, sums, mix, res, first, second, psi_occ, other):
    fields, wide, cols = res.shape
    half = wide - 2 * EDGE
    blocks = half // pick_block(half)
    field = pltpu.VMEM((fields, half, cols), jnp.float32)
    return pl.pallas_call(
        last_kernel,
        out_shape=jax.ShapeDtypeStruct((fields, half, cols), jnp.float32),
        in_specs=[SMEM] * 3 + [HBM] * 5,
        out_specs=VMEM,
        scratch_shapes=[
            field,
            field,
            field,
            pltpu.VMEM(other.shape, jnp.float32),
            pltpu.VMEM(other.shape, jnp.float32),
            pltpu.SemaphoreType.DMA((2, blocks)),
            pltpu.SemaphoreType.DMA((3, blocks)),
        ],
        compiler_params=params(60),
        name="last",
    )(which, sums, mix, res, first, second, psi_occ, other)


def xor_sum(block, bits):
    count = lax.axis_size("space") * lax.axis_size("occ")
    masks = [0]
    for bit in bits:
        masks = masks + [mask | bit for mask in masks]
    parts = [block]
    for mask in masks[1:]:
        parts.append(lax.ppermute(block, ("space", "occ"), [(i, i ^ mask) for i in range(count)]))
    while len(parts) > 1:
        parts = [parts[j] + parts[j + 1] for j in range(0, len(parts), 2)]
    return parts[0]


def total(block):
    count = lax.axis_size("space")
    bit = 2
    while count > 1:
        if count % 4 == 0:
            block = xor_sum(block, (bit, 2 * bit))
            bit, count = 4 * bit, count // 4
        else:
            block = xor_sum(block, (bit,))
            bit, count = 2 * bit, count // 2
    return xor_sum(block, (1,))


def exchange(block):
    return lax.ppermute(block, "occ", SWAP)


def from_behind(block, distance):
    count = lax.axis_size("space")
    return lax.ppermute(block, "space", [((i - distance) % count, i) for i in range(count)])


def window_images(x_cell, y_cell, offsets, values, theta_y, rows_y, planes):
    y_raw = y_cell[:, None] + offsets[None, :, 2]
    y_wrap = jnp.floor_divide(y_raw, rows_y)
    y_at = y_raw - y_wrap * rows_y
    angles = theta_y * y_wrap.astype(jnp.float32)
    row = x_cell[:, None] + offsets[None, :, 1] + RAD
    slot = []
    for plane in planes:
        wanted = (row[:, None, :] == jnp.arange(WIN, dtype=jnp.int32)[None, :, None]) & (
            offsets[:, 0] == plane
        )[None, None, :]
        slot.append(wanted)
    slots = jnp.stack(slot, axis=1)
    weights = jnp.stack([values * jnp.cos(angles), values * jnp.sin(angles)], axis=1)
    left = jnp.where(slots[:, :, None], weights[:, None, :, None, :], 0.0)
    atoms = left.shape[0]
    left = left.reshape(atoms, len(planes) * 2 * WIN, -1)
    right = (y_at[:, :, None] == jnp.arange(rows_y, dtype=jnp.int32)[None, None, :]).astype(jnp.float32)
    image = jnp.einsum("apk,aky->apy", left, right, precision=PRECISE)
    return image.reshape(atoms, len(planes), 2, WIN, rows_y)


def shards(
    psi_occ,
    psi_resp,
    initial_guess,
    local_potential,
    potential_change,
    band_energy,
    q_index,
    atom_cells,
    offsets,
    projector,
    strength,
):
    slab_count = lax.axis_size("space")
    slab_index = lax.axis_index("space")
    side = lax.axis_index("occ")
    layers, rows_x, rows_y = local_potential.shape
    half = rows_x // 2
    atoms = atom_cells.shape[0]
    bands = psi_resp.shape[0]
    fields = 2 * bands
    weight = 1.0 / (layers * slab_count * rows_x * rows_y)
    thetas = q_index.astype(jnp.float32) * (2.0 * math.pi / QDIV)
    cosines = jnp.cos(thetas)
    sines = jnp.sin(thetas)
    at_first = slab_index == 0
    at_last = slab_index == slab_count - 1
    z_rot = jnp.stack(
        [
            jnp.where(at_first, cosines[0], 1.0),
            jnp.where(at_first, -sines[0], 0.0),
            jnp.where(at_last, cosines[0], 1.0),
            jnp.where(at_last, sines[0], 0.0),
            jnp.where(at_last, cosines[0], 1.0),
            jnp.where(at_last, -sines[0], 0.0),
            jnp.where(at_first, cosines[0], 1.0),
            jnp.where(at_first, sines[0], 0.0),
        ]
    )
    x_rot = jnp.stack(
        [
            jnp.where(side == 0, cosines[1], 1.0),
            jnp.where(side == 0, -sines[1], 0.0),
            jnp.where(side == 1, cosines[1], 1.0),
            jnp.where(side == 1, sines[1], 0.0),
        ]
    )
    y_twist = jnp.stack([cosines[2], sines[2]])
    which = side.astype(jnp.int32).reshape(1)

    occ = psi_occ.reshape(psi_occ.shape[0], 2, rows_x, rows_y)
    resp = psi_resp.reshape(bands, 2, rows_x, rows_y)
    guess = initial_guess.reshape(bands, 2, rows_x, rows_y)
    change = potential_change.reshape(2, rows_x, rows_y)

    guess_mid, occ_send = prep_call(which, x_rot, guess, occ)
    occ_other = exchange(occ_send)

    packed = jnp.stack(
        [
            projector,
            jnp.pad(atom_cells.astype(jnp.float32), ((0, 0), (0, projector.shape[1] - 3))),
        ],
        axis=1,
    )
    below = from_behind(packed, 1)
    above = from_behind(packed, -1)
    below, above, occ_first = lax.optimization_barrier((below, above, occ))
    cells = [atom_cells]
    for side_pack in (below, above):
        cells.append(side_pack[:, 1, :3].astype(jnp.int32))
    all_x = jnp.stack([c[:, 1] for c in cells])
    all_y = jnp.stack([c[:, 2] for c in cells])
    at_row = jnp.mod(all_x - RAD - side * half + EDGE, rows_x)
    inner = at_row % 8
    touching = at_row < half + EDGE
    put_starts = jnp.where(touching, at_row - inner, half + 2 * EDGE).astype(jnp.int32)
    get_starts = jnp.where(touching[0], at_row[0] - inner[0], 0).astype(jnp.int32)
    img = window_images(inner[0], all_y[0], offsets, projector, thetas[2], rows_y, (-1, 0, 1))
    low_img = window_images(inner[1], all_y[1], offsets, below[:, 0], thetas[2], rows_y, (1,))[:, 0]
    high_img = window_images(inner[2], all_y[2], offsets, above[:, 0], thetas[2], rows_y, (-1,))[:, 0]

    def local_part(mid):
        low = from_behind(mid, 1)
        high = from_behind(mid, -1)
        zsum, proj, up, down = gather(get_starts, z_rot, strength, mid, low, high, img)
        low_coef = from_behind(up, 1)
        high_coef = from_behind(down, -1)
        lap = stencil(which, band_energy, y_twist, put_starts, proj, mid, zsum, local_potential, img)
        return put_starts, low_coef, high_coef, lap

    first_sums = total(first_corr(which, occ_first, resp, change, guess))
    starts, low_coef, high_coef, lap = local_part(guess_mid)
    residual, edges, part = residual_call(
        weight, which, starts, low_coef, high_coef, first_sums, lap, low_img, high_img, occ, occ_other, resp, change
    )
    tot = total(part)
    norm0 = tot[2, :bands]
    residual = fill_call(x_rot, exchange(edges), residual)
    residual_other = exchange(residual)
    starts, low_coef, high_coef, lap = local_part(residual)
    image, edges, part = image_call(
        SHIFT_WEIGHT * weight, which, starts, low_coef, high_coef, tot, lap, low_img, high_img, residual, occ, occ_other
    )
    image = fill_call(x_rot, exchange(edges), image)
    image_other = exchange(image)
    starts, low_coef, high_coef, lap = local_part(image)
    image2, part = local_call(starts, low_coef, high_coef, lap, low_img, high_img, image, part)
    tot = total(part)
    sums = tot[0:2]
    cross = tot[2, :bands]
    square = tot[2, bands : 2 * bands]
    occ_square = jnp.sum((sums * sums).reshape(-1, bands, 2), axis=(0, 2))
    triple = tot[3, :bands] + SHIFT_WEIGHT * weight * occ_square
    step0 = norm0 / cross
    norm1 = norm0 - 2.0 * step0 * cross + step0 * step0 * square
    growth = norm1 / norm0
    lead = 1.0 + growth
    curvature = lead * lead * cross - 2.0 * lead * step0 * square + step0 * step0 * triple
    step1 = norm1 / curvature
    mix0 = -step0 - step1 * lead
    mix1 = step1 * step0
    per_lane = jnp.tile(jnp.repeat(mix1, 2), sums.shape[1] // fields)
    last_sums = SHIFT_WEIGHT * weight * sums * per_lane[None, :]
    mine = last_call(which, last_sums, jnp.stack([mix0, mix1]), residual, image, image2, occ, occ_other)
    theirs = exchange(mine)

    def join(own_half, other_half):
        lower = jnp.where(side == 0, own_half, other_half)
        upper = jnp.where(side == 0, other_half, own_half)
        return jnp.concatenate([lower, upper], axis=1).reshape(bands, 2, 1, rows_x, rows_y)

    inside = lambda v: v[:, EDGE : EDGE + half]
    wide = lambda v: v[:, None, None, None, None]
    response = (
        initial_guess
        + wide(step0 + step1 * lead) * join(inside(residual), inside(residual_other))
        - wide(step0 * step1) * join(inside(image), inside(image_other))
    )
    return response, join(mine, theirs)


def solution(mesh):
    return jax.shard_map(
        shards,
        mesh=mesh,
        in_specs=(
            P("occ", None, "space", None, None),
            P("resp", None, "space", None, None),
            P("resp", None, "space", None, None),
            P("space", None, None),
            P(None, "space", None, None),
            P("resp"),
            P(),
            P("space", None),
            P(),
            P("space", None),
            P("space"),
        ),
        out_specs=(P("resp", None, "space", None, None), P("resp", None, "space", None, None)),
        check_vma=False,
    )
```

```python
import functools
import math

import jax
import jax.numpy as jnp
from jax import lax
from jax.experimental import pallas as pl
from jax.experimental.pallas import tpu as pltpu
from jax.sharding import PartitionSpec as P

RAD = 4
QDIV = 8
EDGE = 8
WIN = 16
SHIFT_WEIGHT = 3.0
PRECISE = lax.Precision.HIGHEST
SWAP = [(0, 1), (1, 0)]

VMEM = pl.BlockSpec(memory_space=pltpu.VMEM)
SMEM = pl.BlockSpec(memory_space=pltpu.SMEM)
ANY = pl.BlockSpec(memory_space=pl.ANY)
HBM = pl.BlockSpec(memory_space=pltpu.HBM)


def params(mib):
    return pltpu.CompilerParams(vmem_limit_bytes=mib * 1024 * 1024)


def sum_rows(values):
    total = jnp.sum(values, axis=2, keepdims=True)
    row = lax.broadcasted_iota(jnp.int32, values.shape, 0)
    lane = lax.broadcasted_iota(jnp.int32, values.shape, 2)
    picked = jnp.sum(jnp.where(row == lane, total, 0.0), axis=0)
    return jnp.sum(picked, axis=0, keepdims=True)


def rows8(index):
    return pl.ds(pl.multiple_of(index * 8, 8), 8)


def prep_kernel(which_ref, rot_ref, guess_ref, occ_ref, out_ref, send_ref, middle, low, high, sems):
    fields, wide, _ = out_ref.shape
    half = wide - 2 * EDGE
    count = occ_ref.shape[0]
    side = which_ref[0]
    begin = pl.multiple_of(side * half, 8)
    away = pl.multiple_of((1 - side) * half, 8)
    under = pl.multiple_of((1 - side) * half + half - EDGE, 8)
    copies = []
    for j, (start, size, dst) in enumerate(((begin, half, middle), (under, EDGE, low), (away, EDGE, high))):
        copies.append(pltpu.make_async_copy(guess_ref.at[:, :, pl.ds(start, size)], dst, sems.at[j]))
    parts = sems.shape[0] - 3
    each = count // parts
    sends = []
    for j in range(parts):
        chosen = slice(j * each, (j + 1) * each)
        sends.append(
            pltpu.make_async_copy(occ_ref.at[chosen, :, pl.ds(away, half)], send_ref.at[chosen], sems.at[3 + j])
        )
    for copy in copies + sends:
        copy.start()
    for copy in copies:
        copy.wait()
    for n in range(fields // 2):
        for k in range(2):
            out_ref[2 * n + k, EDGE : EDGE + half] = middle[n, k]
        for src, spot, j in ((low, 0, 0), (high, EDGE + half, 2)):
            c, s = rot_ref[j], rot_ref[j + 1]
            re, im = src[n, 0], src[n, 1]
            out_ref[2 * n, spot : spot + EDGE] = re * c - im * s
            out_ref[2 * n + 1, spot : spot + EDGE] = re * s + im * c
    for copy in sends:
        copy.wait()


def prep_call(which, x_rot, guess, occ):
    bands, _, rows, cols = guess.shape
    half = rows // 2
    return pl.pallas_call(
        prep_kernel,
        out_shape=(
            jax.ShapeDtypeStruct((2 * bands, half + 2 * EDGE, cols), jnp.float32),
            jax.ShapeDtypeStruct((occ.shape[0], 2, half, cols), jnp.float32),
        ),
        in_specs=[SMEM, SMEM, HBM, HBM],
        out_specs=(VMEM, VMEM),
        scratch_shapes=[
            pltpu.VMEM((bands, 2, half, cols), jnp.float32),
            pltpu.VMEM((bands, 2, EDGE, cols), jnp.float32),
            pltpu.VMEM((bands, 2, EDGE, cols), jnp.float32),
            pltpu.SemaphoreType.DMA((7,)),
        ],
        compiler_params=params(60),
        name="prep",
    )(which, x_rot, guess, occ)


def fill_kernel(rot_ref, got_ref, ext_ref, out_ref, low, high, sems):
    fields, wide, _ = out_ref.shape
    for n in range(fields // 2):
        for dst, at, j in ((low, EDGE, 0), (high, 0, 2)):
            c, s = rot_ref[j], rot_ref[j + 1]
            re, im = got_ref[2 * n, at : at + EDGE], got_ref[2 * n + 1, at : at + EDGE]
            dst[2 * n] = re * c - im * s
            dst[2 * n + 1] = re * s + im * c
    one = pltpu.make_async_copy(low, out_ref.at[:, 0:EDGE], sems.at[0])
    two = pltpu.make_async_copy(high, out_ref.at[:, wide - EDGE : wide], sems.at[1])
    one.start()
    two.start()
    one.wait()
    two.wait()


def fill_call(x_rot, got, ext):
    shape = (ext.shape[0], EDGE, ext.shape[2])
    return pl.pallas_call(
        fill_kernel,
        out_shape=jax.ShapeDtypeStruct(ext.shape, jnp.float32),
        in_specs=[SMEM, VMEM, ANY],
        out_specs=ANY,
        scratch_shapes=[
            pltpu.VMEM(shape, jnp.float32),
            pltpu.VMEM(shape, jnp.float32),
            pltpu.SemaphoreType.DMA((2,)),
        ],
        input_output_aliases={2: 0},
        compiler_params=params(4),
        name="fill",
    )(x_rot, got, ext)


def first_corr_kernel(which_ref, occ_ref, resp_ref, pot_ref, guess_ref, out_ref, mixed, red):
    bands, _, rows, _ = resp_ref.shape
    group = occ_ref.shape[0]
    step = pl.program_id(0)

    @pl.when(step == 0)
    def _():
        for n in range(bands):
            re = resp_ref[n, 0]
            im = resp_ref[n, 1]
            mixed[2 * n] = pot_ref[0] * re - pot_ref[1] * im - SHIFT_WEIGHT * guess_ref[n, 0]
            mixed[2 * n + 1] = pot_ref[0] * im + pot_ref[1] * re - SHIFT_WEIGHT * guess_ref[n, 1]

    def row(i, accs):
        at = rows8(i)
        occ = [(occ_ref[k, 0, at], occ_ref[k, 1, at]) for k in range(group)]
        accs = list(accs)
        for n in range(bands):
            re, im = mixed[2 * n, at], mixed[2 * n + 1, at]
            for k, (pr, pi) in enumerate(occ):
                j = (k * bands + n) * 2
                accs[j] = accs[j] + (pr * re + pi * im)
                accs[j + 1] = accs[j + 1] + (pr * im - pi * re)
        return tuple(accs)

    zero = jnp.zeros((8, 128), jnp.float32)
    count = 2 * bands * group
    accs = lax.fori_loop(0, rows // 8, row, (zero,) * count, unroll=3)
    for j in range(count):
        red[step * count + j] = accs[j]

    @pl.when(step == pl.num_programs(0) - 1)
    def _():
        out_ref[...] = jnp.zeros(out_ref.shape, jnp.float32)
        total = sum_rows(red[...])
        side = which_ref[0]
        out_ref[0:1] = jnp.where(side == 0, total, 0.0)
        out_ref[1:2] = jnp.where(side == 0, 0.0, total)


def first_corr(which, psi_occ, psi_resp, pot, guess):
    group = 4
    count, _, rows, cols = psi_occ.shape
    fixed = lambda shape: pl.BlockSpec(shape, lambda i: (0,) * len(shape))
    return pl.pallas_call(
        first_corr_kernel,
        out_shape=jax.ShapeDtypeStruct((8, 128), jnp.float32),
        grid=(count // group,),
        in_specs=[
            SMEM,
            pl.BlockSpec((group, 2, rows, cols), lambda i: (i, 0, 0, 0)),
            fixed(psi_resp.shape),
            fixed(pot.shape),
            fixed(guess.shape),
        ],
        out_specs=fixed((8, 128)),
        scratch_shapes=[
            pltpu.VMEM((psi_resp.shape[0] * 2, rows, cols), jnp.float32),
            pltpu.VMEM((128, 8, 128), jnp.float32),
        ],
        compiler_params=params(60),
        name="first_corr",
    )(which, psi_occ, psi_resp, pot, guess)


def gather_kernel(start_ref, rot_ref, str_ref, mid_ref, low_ref, high_ref, img_ref,
                  zsum_ref, out_ref, up_ref, down_ref, low, high, red):
    fields = mid_ref.shape[0]
    half = zsum_ref.shape[1]
    for n in range(fields // 2):
        for src, dst, j in ((low_ref, low, 0), (high_ref, high, 2)):
            c, s = rot_ref[j], rot_ref[j + 1]
            re, im = src[2 * n], src[2 * n + 1]
            dst[2 * n] = re * c - im * s
            dst[2 * n + 1] = re * s + im * c
        for k in range(2):
            f = 2 * n + k
            zsum_ref[f] = low[f, EDGE : EDGE + half] + high[f, EDGE : EDGE + half]
    atoms = img_ref.shape[0]

    def atom(a, _):
        begin = pl.multiple_of(start_ref[a], 8)
        accs = [jnp.zeros((8, 128), jnp.float32)] * fields
        for z, src in enumerate((low, mid_ref, high)):
            for k in range(2):
                at = pl.ds(pl.multiple_of(begin + 8 * k, 8), 8)
                ire = img_ref[a, z, 0, 8 * k : 8 * k + 8]
                iim = img_ref[a, z, 1, 8 * k : 8 * k + 8]
                for n in range(fields // 2):
                    re, im = src[2 * n, at], src[2 * n + 1, at]
                    accs[2 * n] = accs[2 * n] + (re * ire - im * iim)
                    accs[2 * n + 1] = accs[2 * n + 1] + (re * iim + im * ire)
        for f in range(fields):
            red[a * fields + f] = accs[f] * str_ref[a]
        return 0

    lax.fori_loop(0, atoms, atom, 0)
    total = atoms * fields
    even = lax.broadcasted_iota(jnp.int32, (1, 128), 1) % 2 == 0
    for b in range(out_ref.shape[0]):
        stop = min(total, 128 * b + 128)
        value = sum_rows(red[128 * b : stop])
        times_i = jnp.where(even, -pltpu.roll(value, 127, 1), pltpu.roll(value, 1, 1))
        out_ref[b : b + 1] = value
        up_ref[b : b + 1] = value * rot_ref[4] + times_i * rot_ref[5]
        down_ref[b : b + 1] = value * rot_ref[6] + times_i * rot_ref[7]


def gather(starts, rot, strength, mid, low, high, img):
    fields, rows, cols = mid.shape
    atoms = img.shape[0]
    blocks = -(-atoms * fields // 128)
    coef = jax.ShapeDtypeStruct((blocks, 128), jnp.float32)
    return pl.pallas_call(
        gather_kernel,
        out_shape=(
            jax.ShapeDtypeStruct((fields, rows - 2 * EDGE, cols), jnp.float32),
            coef,
            coef,
            coef,
        ),
        in_specs=[SMEM] * 3 + [VMEM] * 4,
        out_specs=(VMEM,) * 4,
        scratch_shapes=[
            pltpu.VMEM(mid.shape, jnp.float32),
            pltpu.VMEM(mid.shape, jnp.float32),
            pltpu.VMEM((atoms * fields, 8, 128), jnp.float32),
        ],
        compiler_params=params(10),
        name="gather",
    )(starts, rot, strength, mid, low, high, img)


def spread_into(acc, start_of, coef_ref, image_of, atoms):
    fields = acc.shape[0]

    def atom(a, _):
        begin = pl.multiple_of(start_of(a), 8)
        line = lax.div(a * fields, 128)
        lane = lax.rem(a * fields, 128)
        for k in range(2):
            at = pl.ds(pl.multiple_of(begin + 8 * k, 8), 8)
            ire = image_of(a, 0, k)
            iim = image_of(a, 1, k)
            for n in range(fields // 2):
                pr = coef_ref[line, lane + 2 * n]
                pi = coef_ref[line, lane + 2 * n + 1]
                acc[2 * n, at] = acc[2 * n, at] + (pr * ire + pi * iim)
                acc[2 * n + 1, at] = acc[2 * n + 1, at] + (pi * ire - pr * iim)
        return 0

    lax.fori_loop(0, atoms, atom, 0)


def stencil_kernel(which_ref, energy_ref, twist_ref, starts_ref, coef_ref, mid_ref, zsum_ref, pot_ref, img_ref, out_ref):
    fields, half, cols = zsum_ref.shape
    lane = lax.broadcasted_iota(jnp.int32, (half, cols), 1)
    first, last = lane == 0, lane == cols - 1
    c, s = twist_ref[0], twist_ref[1]
    pot = pot_ref[0, pl.ds(pl.multiple_of(which_ref[0] * half, 8), half)] + 3.0
    for n in range(fields // 2):
        re = mid_ref[2 * n, EDGE : EDGE + half]
        im = mid_ref[2 * n + 1, EDGE : EDGE + half]
        re_next, im_next = pltpu.roll(re, cols - 1, 1), pltpu.roll(im, cols - 1, 1)
        re_prev, im_prev = pltpu.roll(re, 1, 1), pltpu.roll(im, 1, 1)
        y_re = jnp.where(last, re_next * c - im_next * s, re_next) + jnp.where(
            first, re_prev * c + im_prev * s, re_prev
        )
        y_im = jnp.where(last, re_next * s + im_next * c, im_next) + jnp.where(
            first, im_prev * c - re_prev * s, im_prev
        )
        scale = pot - energy_ref[n]
        for f, value, beside in ((2 * n, re, y_re), (2 * n + 1, im, y_im)):
            beside = beside + zsum_ref[f]
            beside = beside + mid_ref[f, EDGE - 1 : EDGE - 1 + half]
            beside = beside + mid_ref[f, EDGE + 1 : EDGE + 1 + half]
            out_ref[f, EDGE : EDGE + half] = scale * value - 0.5 * beside
            out_ref[f, 0:EDGE] = jnp.zeros((EDGE, cols), jnp.float32)
            out_ref[f, EDGE + half :] = jnp.zeros((EDGE + WIN, cols), jnp.float32)
    atoms = img_ref.shape[0]
    image = lambda a, part, k: img_ref[a, 1, part, 8 * k : 8 * k + 8]
    spread_into(out_ref, lambda a: starts_ref[0, a], coef_ref, image, atoms)


def stencil(which, energy, twist, starts, coef, mid, zsum, pot, img):
    fields, half, cols = zsum.shape
    return pl.pallas_call(
        stencil_kernel,
        out_shape=jax.ShapeDtypeStruct((fields, half + 2 * EDGE + WIN, cols), jnp.float32),
        in_specs=[SMEM] * 5 + [VMEM] * 4,
        out_specs=VMEM,
        compiler_params=params(10),
        name="stencil",
    )(which, energy, twist, starts, coef, mid, zsum, pot, img)


def spread_sides(acc, starts_ref, low_coef, high_coef, low_img, high_img):
    atoms = low_img.shape[0]
    for j, coef, img in ((1, low_coef, low_img), (2, high_coef, high_img)):
        image = lambda a, part, k, img=img: img[a, part, 8 * k : 8 * k + 8]
        spread_into(acc, lambda a, j=j: starts_ref[j, a], coef, image, atoms)


def occupied_into(store, half, fields, sums_ref, side, own_ref, other_ref, base, scale, block, copies_of):
    count = own_ref.shape[0]

    def rows_of(b, _):
        at = pl.ds(pl.multiple_of(b * block, 8), block)
        for copy in copies_of(b):
            copy.wait()

        def band(m, accs):
            accs = list(accs)
            for row, occ in ((side, own_ref), (1 - side, other_ref)):
                pr, pi = occ[m, 0, at], occ[m, 1, at]
                for n in range(fields // 2):
                    sr = sums_ref[row, m * fields + 2 * n]
                    si = sums_ref[row, m * fields + 2 * n + 1]
                    accs[2 * n] = accs[2 * n] + (pr * sr - pi * si)
                    accs[2 * n + 1] = accs[2 * n + 1] + (pr * si + pi * sr)
            return tuple(accs)

        zero = jnp.zeros((block, 128), jnp.float32)
        accs = lax.fori_loop(0, count, band, (zero,) * fields, unroll=2)
        for f in range(fields):
            store(f, b * block, base(f, b * block, block) + scale * accs[f])
        return 0

    lax.fori_loop(0, half // block, rows_of, 0)


def correlate_into(red, src, offset, half, own_ref, other_ref):
    fields = src.shape[0]
    count = own_ref.shape[0]
    bands = fields // 2

    def pair(g, _):
        def row(i, accs):
            at = rows8(i)
            moved = pl.ds(pl.multiple_of(i * 8 + offset, 8), 8)
            accs = list(accs)
            occ = []
            for ref in (own_ref, other_ref):
                for k in range(2):
                    occ.append((ref[2 * g + k, 0, at], ref[2 * g + k, 1, at]))
            for n in range(bands):
                re, im = src[2 * n, moved], src[2 * n + 1, moved]
                for q, (pr, pi) in enumerate(occ):
                    j = (q * bands + n) * 2
                    accs[j] = accs[j] + (pr * re + pi * im)
                    accs[j + 1] = accs[j + 1] + (pr * im - pi * re)
            return tuple(accs)

        zero = jnp.zeros((8, 128), jnp.float32)
        accs = lax.fori_loop(0, half // 8, row, (zero,) * (8 * bands), unroll=3)
        for q in range(4):
            for j in range(fields):
                red[q // 2, (2 * g + q % 2) * fields + j] = accs[q * fields + j]
        return 0

    lax.fori_loop(0, count // 2, pair, 0)


def dots_into(red_dot, half, fields, pairs):
    bands = fields // 2

    def row(i, accs):
        at = pl.ds(pl.multiple_of(i * 8 + EDGE, 8), 8)
        accs = list(accs)
        for p, (left, right) in enumerate(pairs):
            for n in range(bands):
                value = left[2 * n, at] * right[2 * n, at] + left[2 * n + 1, at] * right[2 * n + 1, at]
                accs[p * bands + n] = accs[p * bands + n] + value
        return tuple(accs)

    zero = jnp.zeros((8, 128), jnp.float32)
    accs = lax.fori_loop(0, half // 8, row, (zero,) * (bands * len(pairs)), unroll=3)
    for j in range(bands * len(pairs)):
        red_dot[j] = accs[j]


def pick_block(half):
    return next(b for b in (24, 16, 8) if half % b == 0)


def shift_rows(start, size):
    return pl.ds(pl.multiple_of(start + EDGE, 8), size)


def band_copies(which_ref, half, block, b, occ_ref, occ_other_ref, own, other, sems):
    begin = pl.multiple_of(which_ref[0] * half + b * block, 8)
    at = pl.ds(pl.multiple_of(b * block, 8), block)
    return (
        pltpu.make_async_copy(occ_ref.at[:, :, pl.ds(begin, block)], own.at[:, :, at], sems.at[0, b]),
        pltpu.make_async_copy(occ_other_ref.at[:, :, at], other.at[:, :, at], sems.at[1, b]),
    )


def start_bands(half, block, copies_of):
    for b in range(half // block):
        for copy in copies_of(b):
            copy.start()


def write_sums(sum_ref, side, red):
    mine, theirs = sum_rows(red[0]), sum_rows(red[1])
    sum_ref[...] = jnp.zeros(sum_ref.shape, jnp.float32)
    sum_ref[0:1] = jnp.where(side == 0, mine, theirs)
    sum_ref[1:2] = jnp.where(side == 0, theirs, mine)


def write_edges(edge_ref, out_ref, half):
    for f in range(out_ref.shape[0]):
        edge_ref[f, 0:EDGE] = out_ref[f, EDGE : 2 * EDGE]
        edge_ref[f, EDGE : 2 * EDGE] = out_ref[f, half : half + EDGE]


def residual_kernel(scale, which_ref, starts_ref, low_coef, high_coef, sums_ref, lap_ref, low_ref, high_ref,
                    occ_ref, occ_other_ref, resp_hbm, pot_hbm, out_ref, edge_ref, sum_ref,
                    acc, own, other, resp, pot, red, red_dot, sems, more_sems):
    fields, wide, cols = out_ref.shape
    half = wide - 2 * EDGE
    side = which_ref[0]
    block = pick_block(half)
    begin = pl.multiple_of(side * half, 8)
    copies = (
        pltpu.make_async_copy(resp_hbm.at[:, :, pl.ds(begin, half)], resp, more_sems.at[0]),
        pltpu.make_async_copy(pot_hbm.at[:, pl.ds(begin, half)], pot, more_sems.at[1]),
    )
    for copy in copies:
        copy.start()
    copies_of = lambda b: band_copies(which_ref, half, block, b, occ_ref, occ_other_ref, own, other, sems)
    start_bands(half, block, copies_of)
    acc[...] = lap_ref[...]
    spread_sides(acc, starts_ref, low_coef, high_coef, low_ref, high_ref)
    for copy in copies:
        copy.wait()

    def base(f, start, size):
        at = pl.ds(pl.multiple_of(start, 8), size)
        re, im = resp[f // 2, 0, at], resp[f // 2, 1, at]
        if f % 2 == 0:
            prod = pot[0, at] * re - pot[1, at] * im
        else:
            prod = pot[0, at] * im + pot[1, at] * re
        return -prod - acc[f, shift_rows(start, size)]

    def store(f, start, value):
        out_ref[f, shift_rows(start, block)] = value

    occupied_into(store, half, fields, sums_ref, side, own, other, base, scale, block, copies_of)
    write_edges(edge_ref, out_ref, half)
    correlate_into(red, out_ref, EDGE, half, own, other)
    dots_into(red_dot, half, fields, [(out_ref, out_ref)])
    write_sums(sum_ref, side, red)
    sum_ref[2:3] = sum_rows(red_dot[0 : fields // 2])


def field_outputs(fields, half, cols):
    return (
        jax.ShapeDtypeStruct((fields, half + 2 * EDGE, cols), jnp.float32),
        jax.ShapeDtypeStruct((fields, 2 * EDGE, cols), jnp.float32),
        jax.ShapeDtypeStruct((8, 128), jnp.float32),
    )


def residual_call(scale, which, starts, low_coef, high_coef, sums, lap, low_img, high_img, psi_occ, other, resp, pot):
    fields, long, cols = lap.shape
    half = long - 2 * EDGE - WIN
    return pl.pallas_call(
        functools.partial(residual_kernel, scale),
        out_shape=field_outputs(fields, half, cols),
        in_specs=[SMEM] * 5 + [VMEM] * 3 + [HBM] * 4,
        out_specs=(VMEM,) * 3,
        scratch_shapes=[
            pltpu.VMEM(lap.shape, jnp.float32),
            pltpu.VMEM(other.shape, jnp.float32),
            pltpu.VMEM(other.shape, jnp.float32),
            pltpu.VMEM(resp.shape[:2] + (half, cols), jnp.float32),
            pltpu.VMEM((2, half, cols), jnp.float32),
            pltpu.VMEM((2, 128, 8, 128), jnp.float32),
            pltpu.VMEM((16, 8, 128), jnp.float32),
            pltpu.SemaphoreType.DMA((2, half // pick_block(half))),
            pltpu.SemaphoreType.DMA((2,)),
        ],
        compiler_params=params(16),
        name="residual",
    )(which, starts, low_coef, high_coef, sums, lap, low_img, high_img, psi_occ, other, resp, pot)


def image_kernel(scale, which_ref, starts_ref, low_coef, high_coef, sums_ref, lap_ref, low_ref, high_ref,
                 res_ref, occ_ref, occ_other_ref, out_ref, edge_ref, sum_ref,
                 acc, own, other, red, red_dot, sems):
    fields, wide, cols = out_ref.shape
    half = wide - 2 * EDGE
    side = which_ref[0]
    block = pick_block(half)
    copies_of = lambda b: band_copies(which_ref, half, block, b, occ_ref, occ_other_ref, own, other, sems)
    start_bands(half, block, copies_of)
    acc[...] = lap_ref[...]
    spread_sides(acc, starts_ref, low_coef, high_coef, low_ref, high_ref)

    def base(f, start, size):
        return acc[f, shift_rows(start, size)]

    def store(f, start, value):
        out_ref[f, shift_rows(start, block)] = value

    occupied_into(store, half, fields, sums_ref, side, own, other, base, scale, block, copies_of)
    write_edges(edge_ref, out_ref, half)
    correlate_into(red, out_ref, EDGE, half, own, other)
    dots_into(red_dot, half, fields, [(res_ref, out_ref), (out_ref, out_ref)])
    write_sums(sum_ref, side, red)
    sum_ref[2:3] = sum_rows(red_dot[0:fields])


def image_call(scale, which, starts, low_coef, high_coef, sums, lap, low_img, high_img, res, psi_occ, other):
    fields, long, cols = lap.shape
    half = long - 2 * EDGE - WIN
    return pl.pallas_call(
        functools.partial(image_kernel, scale),
        out_shape=field_outputs(fields, half, cols),
        in_specs=[SMEM] * 5 + [VMEM] * 4 + [HBM] * 2,
        out_specs=(VMEM,) * 3,
        scratch_shapes=[
            pltpu.VMEM(lap.shape, jnp.float32),
            pltpu.VMEM(other.shape, jnp.float32),
            pltpu.VMEM(other.shape, jnp.float32),
            pltpu.VMEM((2, 128, 8, 128), jnp.float32),
            pltpu.VMEM((16, 8, 128), jnp.float32),
            pltpu.SemaphoreType.DMA((2, half // pick_block(half))),
        ],
        compiler_params=params(16),
        name="image",
    )(which, starts, low_coef, high_coef, sums, lap, low_img, high_img, res, psi_occ, other)


def local_kernel(starts_ref, low_coef, high_coef, lap_ref, low_ref, high_ref, field_ref, part_ref,
                 out_ref, sum_ref, red_dot):
    fields = out_ref.shape[0]
    half = field_ref.shape[1] - 2 * EDGE
    out_ref[...] = lap_ref[...]
    spread_sides(out_ref, starts_ref, low_coef, high_coef, low_ref, high_ref)
    dots_into(red_dot, half, fields, [(field_ref, out_ref)])
    sum_ref[...] = part_ref[...]
    sum_ref[3:4] = sum_rows(red_dot[0 : fields // 2])


def local_call(starts, low_coef, high_coef, lap, low_img, high_img, field, part):
    return pl.pallas_call(
        local_kernel,
        out_shape=(
            jax.ShapeDtypeStruct(lap.shape, jnp.float32),
            jax.ShapeDtypeStruct((8, 128), jnp.float32),
        ),
        in_specs=[SMEM] * 3 + [VMEM] * 5,
        out_specs=(VMEM, VMEM),
        scratch_shapes=[pltpu.VMEM((16, 8, 128), jnp.float32)],
        compiler_params=params(8),
        name="local",
    )(starts, low_coef, high_coef, lap, low_img, high_img, field, part)


def last_kernel(which_ref, sums_ref, mix_ref, res_hbm, first_hbm, second_hbm, occ_ref, occ_other_ref,
                out_ref, res, first, second, own, other, sems, more_sems):
    fields, half, cols = out_ref.shape
    side = which_ref[0]
    block = pick_block(half)

    def copies_of(b):
        at = pl.ds(pl.multiple_of(b * block, 8), block)
        moved = shift_rows(b * block, block)
        own_copies = tuple(
            pltpu.make_async_copy(src.at[:, moved], dst.at[:, at], more_sems.at[j, b])
            for j, (src, dst) in enumerate(((res_hbm, res), (first_hbm, first), (second_hbm, second)))
        )
        return own_copies + band_copies(which_ref, half, block, b, occ_ref, occ_other_ref, own, other, sems)

    start_bands(half, block, copies_of)

    def base(f, start, size):
        n = f // 2
        at = pl.ds(pl.multiple_of(start, 8), size)
        return res[f, at] + mix_ref[0, n] * first[f, at] + mix_ref[1, n] * second[f, at]

    def store(f, start, value):
        out_ref[f, pl.ds(pl.multiple_of(start, 8), block)] = value

    occupied_into(store, half, fields, sums_ref, side, own, other, base, 1.0, block, copies_of)


def last_call(which, sums, mix, res, first, second, psi_occ, other):
    fields, wide, cols = res.shape
    half = wide - 2 * EDGE
    blocks = half // pick_block(half)
    field = pltpu.VMEM((fields, half, cols), jnp.float32)
    return pl.pallas_call(
        last_kernel,
        out_shape=jax.ShapeDtypeStruct((fields, half, cols), jnp.float32),
        in_specs=[SMEM] * 3 + [HBM] * 5,
        out_specs=VMEM,
        scratch_shapes=[
            field,
            field,
            field,
            pltpu.VMEM(other.shape, jnp.float32),
            pltpu.VMEM(other.shape, jnp.float32),
            pltpu.SemaphoreType.DMA((2, blocks)),
            pltpu.SemaphoreType.DMA((3, blocks)),
        ],
        compiler_params=params(60),
        name="last",
    )(which, sums, mix, res, first, second, psi_occ, other)


def xor_sum(block, bits):
    count = lax.axis_size("space") * lax.axis_size("occ")
    masks = [0]
    for bit in bits:
        masks = masks + [mask | bit for mask in masks]
    parts = [block]
    for mask in masks[1:]:
        parts.append(lax.ppermute(block, ("space", "occ"), [(i, i ^ mask) for i in range(count)]))
    while len(parts) > 1:
        parts = [parts[j] + parts[j + 1] for j in range(0, len(parts), 2)]
    return parts[0]


def total(block):
    count = lax.axis_size("space")
    bit = 2
    while count > 1:
        if count % 4 == 0:
            block = xor_sum(block, (bit, 2 * bit))
            bit, count = 4 * bit, count // 4
        else:
            block = xor_sum(block, (bit,))
            bit, count = 2 * bit, count // 2
    return xor_sum(block, (1,))


def exchange(block):
    return lax.ppermute(block, "occ", SWAP)


def from_behind(block, distance):
    count = lax.axis_size("space")
    return lax.ppermute(block, "space", [((i - distance) % count, i) for i in range(count)])


def window_images(x_cell, y_cell, offsets, values, theta_y, rows_y, planes):
    y_raw = y_cell[:, None] + offsets[None, :, 2]
    y_wrap = jnp.floor_divide(y_raw, rows_y)
    y_at = y_raw - y_wrap * rows_y
    angles = theta_y * y_wrap.astype(jnp.float32)
    row = x_cell[:, None] + offsets[None, :, 1] + RAD
    slot = []
    for plane in planes:
        wanted = (row[:, None, :] == jnp.arange(WIN, dtype=jnp.int32)[None, :, None]) & (
            offsets[:, 0] == plane
        )[None, None, :]
        slot.append(wanted)
    slots = jnp.stack(slot, axis=1)
    weights = jnp.stack([values * jnp.cos(angles), values * jnp.sin(angles)], axis=1)
    left = jnp.where(slots[:, :, None], weights[:, None, :, None, :], 0.0)
    atoms = left.shape[0]
    left = left.reshape(atoms, len(planes) * 2 * WIN, -1)
    right = (y_at[:, :, None] == jnp.arange(rows_y, dtype=jnp.int32)[None, None, :]).astype(jnp.float32)
    image = jnp.einsum("apk,aky->apy", left, right, precision=PRECISE)
    return image.reshape(atoms, len(planes), 2, WIN, rows_y)


def shards(
    psi_occ,
    psi_resp,
    initial_guess,
    local_potential,
    potential_change,
    band_energy,
    q_index,
    atom_cells,
    offsets,
    projector,
    strength,
):
    slab_count = lax.axis_size("space")
    slab_index = lax.axis_index("space")
    side = lax.axis_index("occ")
    layers, rows_x, rows_y = local_potential.shape
    half = rows_x // 2
    atoms = atom_cells.shape[0]
    bands = psi_resp.shape[0]
    fields = 2 * bands
    weight = 1.0 / (layers * slab_count * rows_x * rows_y)
    thetas = q_index.astype(jnp.float32) * (2.0 * math.pi / QDIV)
    cosines = jnp.cos(thetas)
    sines = jnp.sin(thetas)
    at_first = slab_index == 0
    at_last = slab_index == slab_count - 1
    z_rot = jnp.stack(
        [
            jnp.where(at_first, cosines[0], 1.0),
            jnp.where(at_first, -sines[0], 0.0),
            jnp.where(at_last, cosines[0], 1.0),
            jnp.where(at_last, sines[0], 0.0),
            jnp.where(at_last, cosines[0], 1.0),
            jnp.where(at_last, -sines[0], 0.0),
            jnp.where(at_first, cosines[0], 1.0),
            jnp.where(at_first, sines[0], 0.0),
        ]
    )
    x_rot = jnp.stack(
        [
            jnp.where(side == 0, cosines[1], 1.0),
            jnp.where(side == 0, -sines[1], 0.0),
            jnp.where(side == 1, cosines[1], 1.0),
            jnp.where(side == 1, sines[1], 0.0),
        ]
    )
    y_twist = jnp.stack([cosines[2], sines[2]])
    which = side.astype(jnp.int32).reshape(1)

    occ = psi_occ.reshape(psi_occ.shape[0], 2, rows_x, rows_y)
    resp = psi_resp.reshape(bands, 2, rows_x, rows_y)
    guess = initial_guess.reshape(bands, 2, rows_x, rows_y)
    change = potential_change.reshape(2, rows_x, rows_y)

    guess_mid, occ_send = prep_call(which, x_rot, guess, occ)
    occ_other = exchange(occ_send)

    packed = jnp.stack(
        [
            projector,
            jnp.pad(atom_cells.astype(jnp.float32), ((0, 0), (0, projector.shape[1] - 3))),
        ],
        axis=1,
    )
    below = from_behind(packed, 1)
    above = from_behind(packed, -1)
    below, above, occ_first = lax.optimization_barrier((below, above, occ))
    cells = [atom_cells]
    for side_pack in (below, above):
        cells.append(side_pack[:, 1, :3].astype(jnp.int32))
    all_x = jnp.stack([c[:, 1] for c in cells])
    all_y = jnp.stack([c[:, 2] for c in cells])
    at_row = jnp.mod(all_x - RAD - side * half + EDGE, rows_x)
    inner = at_row % 8
    touching = at_row < half + EDGE
    put_starts = jnp.where(touching, at_row - inner, half + 2 * EDGE).astype(jnp.int32)
    get_starts = jnp.where(touching[0], at_row[0] - inner[0], 0).astype(jnp.int32)
    img = window_images(inner[0], all_y[0], offsets, projector, thetas[2], rows_y, (-1, 0, 1))
    low_img = window_images(inner[1], all_y[1], offsets, below[:, 0], thetas[2], rows_y, (1,))[:, 0]
    high_img = window_images(inner[2], all_y[2], offsets, above[:, 0], thetas[2], rows_y, (-1,))[:, 0]

    def local_part(mid):
        low = from_behind(mid, 1)
        high = from_behind(mid, -1)
        zsum, proj, up, down = gather(get_starts, z_rot, strength, mid, low, high, img)
        low_coef = from_behind(up, 1)
        high_coef = from_behind(down, -1)
        lap = stencil(which, band_energy, y_twist, put_starts, proj, mid, zsum, local_potential, img)
        return put_starts, low_coef, high_coef, lap

    first_sums = total(first_corr(which, occ_first, resp, change, guess))
    starts, low_coef, high_coef, lap = local_part(guess_mid)
    residual, edges, part = residual_call(
        weight, which, starts, low_coef, high_coef, first_sums, lap, low_img, high_img, occ, occ_other, resp, change
    )
    tot = total(part)
    norm0 = tot[2, :bands]
    residual = fill_call(x_rot, exchange(edges), residual)
    residual_other = exchange(residual)
    starts, low_coef, high_coef, lap = local_part(residual)
    image, edges, part = image_call(
        SHIFT_WEIGHT * weight, which, starts, low_coef, high_coef, tot, lap, low_img, high_img, residual, occ, occ_other
    )
    image = fill_call(x_rot, exchange(edges), image)
    image_other = exchange(image)
    starts, low_coef, high_coef, lap = local_part(image)
    image2, part = local_call(starts, low_coef, high_coef, lap, low_img, high_img, image, part)
    tot = total(part)
    sums = tot[0:2]
    cross = tot[2, :bands]
    square = tot[2, bands : 2 * bands]
    occ_square = jnp.sum((sums * sums).reshape(-1, bands, 2), axis=(0, 2))
    triple = tot[3, :bands] + SHIFT_WEIGHT * weight * occ_square
    step0 = norm0 / cross
    norm1 = norm0 - 2.0 * step0 * cross + step0 * step0 * square
    growth = norm1 / norm0
    lead = 1.0 + growth
    curvature = lead * lead * cross - 2.0 * lead * step0 * square + step0 * step0 * triple
    step1 = norm1 / curvature
    mix0 = -step0 - step1 * lead
    mix1 = step1 * step0
    per_lane = jnp.tile(jnp.repeat(mix1, 2), sums.shape[1] // fields)
    last_sums = SHIFT_WEIGHT * weight * sums * per_lane[None, :]
    mine = last_call(which, last_sums, jnp.stack([mix0, mix1]), residual, image, image2, occ, occ_other)
    theirs = exchange(mine)

    def join(own_half, other_half):
        lower = jnp.where(side == 0, own_half, other_half)
        upper = jnp.where(side == 0, other_half, own_half)
        return jnp.concatenate([lower, upper], axis=1).reshape(bands, 2, 1, rows_x, rows_y)

    inside = lambda v: v[:, EDGE : EDGE + half]
    wide = lambda v: v[:, None, None, None, None]
    response = (
        initial_guess
        + wide(step0 + step1 * lead) * join(inside(residual), inside(residual_other))
        - wide(step0 * step1) * join(inside(image), inside(image_other))
    )
    return response, join(mine, theirs)


def solution(mesh):
    return jax.shard_map(
        shards,
        mesh=mesh,
        in_specs=(
            P("occ", None, "space", None, None),
            P("resp", None, "space", None, None),
            P("resp", None, "space", None, None),
            P("space", None, None),
            P(None, "space", None, None),
            P("resp"),
            P(),
            P("space", None),
            P(),
            P("space", None),
            P("space"),
        ),
        out_specs=(P("resp", None, "space", None, None), P("resp", None, "space", None, None)),
        check_vma=False,
    )
```

```python
import functools
import math

import jax
import jax.numpy as jnp
from jax import lax
from jax.experimental import pallas as pl
from jax.experimental.pallas import tpu as pltpu
from jax.sharding import PartitionSpec as P

RAD = 4
QDIV = 8
EDGE = 8
WIN = 16
SHIFT_WEIGHT = 3.0
PRECISE = lax.Precision.HIGHEST
SWAP = [(0, 1), (1, 0)]

VMEM = pl.BlockSpec(memory_space=pltpu.VMEM)
SMEM = pl.BlockSpec(memory_space=pltpu.SMEM)
ANY = pl.BlockSpec(memory_space=pl.ANY)
HBM = pl.BlockSpec(memory_space=pltpu.HBM)


def params(mib):
    return pltpu.CompilerParams(vmem_limit_bytes=mib * 1024 * 1024)


def sum_rows(values):
    total = jnp.sum(values, axis=2, keepdims=True)
    row = lax.broadcasted_iota(jnp.int32, values.shape, 0)
    lane = lax.broadcasted_iota(jnp.int32, values.shape, 2)
    picked = jnp.sum(jnp.where(row == lane, total, 0.0), axis=0)
    return jnp.sum(picked, axis=0, keepdims=True)


def rows8(index):
    return pl.ds(pl.multiple_of(index * 8, 8), 8)


def prep_kernel(which_ref, rot_ref, guess_ref, occ_ref, out_ref, send_ref, middle, low, high, sems):
    fields, wide, _ = out_ref.shape
    half = wide - 2 * EDGE
    count = occ_ref.shape[0]
    side = which_ref[0]
    begin = pl.multiple_of(side * half, 8)
    away = pl.multiple_of((1 - side) * half, 8)
    under = pl.multiple_of((1 - side) * half + half - EDGE, 8)
    copies = []
    for j, (start, size, dst) in enumerate(((begin, half, middle), (under, EDGE, low), (away, EDGE, high))):
        copies.append(pltpu.make_async_copy(guess_ref.at[:, :, pl.ds(start, size)], dst, sems.at[j]))
    parts = sems.shape[0] - 3
    each = count // parts
    sends = []
    for j in range(parts):
        chosen = slice(j * each, (j + 1) * each)
        sends.append(
            pltpu.make_async_copy(occ_ref.at[chosen, :, pl.ds(away, half)], send_ref.at[chosen], sems.at[3 + j])
        )
    for copy in copies + sends:
        copy.start()
    for copy in copies:
        copy.wait()
    for n in range(fields // 2):
        for k in range(2):
            out_ref[2 * n + k, EDGE : EDGE + half] = middle[n, k]
        for src, spot, j in ((low, 0, 0), (high, EDGE + half, 2)):
            c, s = rot_ref[j], rot_ref[j + 1]
            re, im = src[n, 0], src[n, 1]
            out_ref[2 * n, spot : spot + EDGE] = re * c - im * s
            out_ref[2 * n + 1, spot : spot + EDGE] = re * s + im * c
    for copy in sends:
        copy.wait()


def prep_call(which, x_rot, guess, occ):
    bands, _, rows, cols = guess.shape
    half = rows // 2
    return pl.pallas_call(
        prep_kernel,
        out_shape=(
            jax.ShapeDtypeStruct((2 * bands, half + 2 * EDGE, cols), jnp.float32),
            jax.ShapeDtypeStruct((occ.shape[0], 2, half, cols), jnp.float32),
        ),
        in_specs=[SMEM, SMEM, HBM, HBM],
        out_specs=(VMEM, VMEM),
        scratch_shapes=[
            pltpu.VMEM((bands, 2, half, cols), jnp.float32),
            pltpu.VMEM((bands, 2, EDGE, cols), jnp.float32),
            pltpu.VMEM((bands, 2, EDGE, cols), jnp.float32),
            pltpu.SemaphoreType.DMA((7,)),
        ],
        compiler_params=params(60),
        name="prep",
    )(which, x_rot, guess, occ)


def fill_kernel(rot_ref, got_ref, ext_ref, out_ref, low, high, sems):
    fields, wide, _ = out_ref.shape
    for n in range(fields // 2):
        for dst, at, j in ((low, EDGE, 0), (high, 0, 2)):
            c, s = rot_ref[j], rot_ref[j + 1]
            re, im = got_ref[2 * n, at : at + EDGE], got_ref[2 * n + 1, at : at + EDGE]
            dst[2 * n] = re * c - im * s
            dst[2 * n + 1] = re * s + im * c
    one = pltpu.make_async_copy(low, out_ref.at[:, 0:EDGE], sems.at[0])
    two = pltpu.make_async_copy(high, out_ref.at[:, wide - EDGE : wide], sems.at[1])
    one.start()
    two.start()
    one.wait()
    two.wait()


def fill_call(x_rot, got, ext):
    shape = (ext.shape[0], EDGE, ext.shape[2])
    return pl.pallas_call(
        fill_kernel,
        out_shape=jax.ShapeDtypeStruct(ext.shape, jnp.float32),
        in_specs=[SMEM, VMEM, ANY],
        out_specs=ANY,
        scratch_shapes=[
            pltpu.VMEM(shape, jnp.float32),
            pltpu.VMEM(shape, jnp.float32),
            pltpu.SemaphoreType.DMA((2,)),
        ],
        input_output_aliases={2: 0},
        compiler_params=params(4),
        name="fill",
    )(x_rot, got, ext)


def first_corr_kernel(which_ref, occ_ref, resp_ref, pot_ref, guess_ref, out_ref, mixed, red):
    bands, _, rows, _ = resp_ref.shape
    group = occ_ref.shape[0]
    step = pl.program_id(0)

    @pl.when(step == 0)
    def _():
        for n in range(bands):
            re = resp_ref[n, 0]
            im = resp_ref[n, 1]
            mixed[2 * n] = pot_ref[0] * re - pot_ref[1] * im - SHIFT_WEIGHT * guess_ref[n, 0]
            mixed[2 * n + 1] = pot_ref[0] * im + pot_ref[1] * re - SHIFT_WEIGHT * guess_ref[n, 1]

    def row(i, accs):
        at = rows8(i)
        occ = [(occ_ref[k, 0, at], occ_ref[k, 1, at]) for k in range(group)]
        accs = list(accs)
        for n in range(bands):
            re, im = mixed[2 * n, at], mixed[2 * n + 1, at]
            for k, (pr, pi) in enumerate(occ):
                j = (k * bands + n) * 2
                accs[j] = accs[j] + (pr * re + pi * im)
                accs[j + 1] = accs[j + 1] + (pr * im - pi * re)
        return tuple(accs)

    zero = jnp.zeros((8, 128), jnp.float32)
    count = 2 * bands * group
    accs = lax.fori_loop(0, rows // 8, row, (zero,) * count, unroll=3)
    for j in range(count):
        red[step * count + j] = accs[j]

    @pl.when(step == pl.num_programs(0) - 1)
    def _():
        out_ref[...] = jnp.zeros(out_ref.shape, jnp.float32)
        total = sum_rows(red[...])
        side = which_ref[0]
        out_ref[0:1] = jnp.where(side == 0, total, 0.0)
        out_ref[1:2] = jnp.where(side == 0, 0.0, total)


def first_corr(which, psi_occ, psi_resp, pot, guess):
    group = 4
    count, _, rows, cols = psi_occ.shape
    fixed = lambda shape: pl.BlockSpec(shape, lambda i: (0,) * len(shape))
    return pl.pallas_call(
        first_corr_kernel,
        out_shape=jax.ShapeDtypeStruct((8, 128), jnp.float32),
        grid=(count // group,),
        in_specs=[
            SMEM,
            pl.BlockSpec((group, 2, rows, cols), lambda i: (i, 0, 0, 0)),
            fixed(psi_resp.shape),
            fixed(pot.shape),
            fixed(guess.shape),
        ],
        out_specs=fixed((8, 128)),
        scratch_shapes=[
            pltpu.VMEM((psi_resp.shape[0] * 2, rows, cols), jnp.float32),
            pltpu.VMEM((128, 8, 128), jnp.float32),
        ],
        compiler_params=params(60),
        name="first_corr",
    )(which, psi_occ, psi_resp, pot, guess)


def project(src, begin, image_of, accs):
    accs = list(accs)
    for k in range(2):
        at = pl.ds(pl.multiple_of(begin + 8 * k, 8), 8)
        ire, iim = image_of(0, k), image_of(1, k)
        for n in range(len(accs) // 2):
            re, im = src[2 * n, at], src[2 * n + 1, at]
            accs[2 * n] = accs[2 * n] + (re * ire - im * iim)
            accs[2 * n + 1] = accs[2 * n + 1] + (re * iim + im * ire)
    return accs


def lanes_of(red, total, blocks):
    return jnp.concatenate([sum_rows(red[128 * b : min(total, 128 * b + 128)]) for b in range(blocks)], axis=0)


def turn_lanes(value, cosine, sine_part):
    even = lax.broadcasted_iota(jnp.int32, value.shape, 1) % 2 == 0
    times_i = jnp.where(even, -pltpu.roll(value, 127, 1), pltpu.roll(value, 1, 1))
    return value * cosine + times_i * sine_part


def plane_kernel(which_ref, energy_ref, twist_ref, starts_ref, rot_ref, str_ref, mid_ref, pot_ref, low_img, high_img,
                 out_ref, low_ref, high_ref, down_ref, up_ref, red):
    fields, wide, cols = mid_ref.shape
    half = wide - 2 * EDGE
    atoms = low_img.shape[0]
    total = atoms * fields

    def atom(a, _):
        for j, img, z in ((1, low_img, 1), (2, high_img, 0)):
            begin = starts_ref[j, a]
            image = lambda part, k: img[a, z, part, 8 * k : 8 * k + 8]
            accs = project(mid_ref, begin, image, [jnp.zeros((8, 128), jnp.float32)] * fields)
            for f in range(fields):
                red[j - 1, a * fields + f] = accs[f] * str_ref[j, a]
        return 0

    lax.fori_loop(0, atoms, atom, 0)
    blocks = low_ref.shape[0]
    low = lanes_of(red.at[0], total, blocks)
    high = lanes_of(red.at[1], total, blocks)
    low_ref[...] = low
    high_ref[...] = high
    down_ref[...] = turn_lanes(low, rot_ref[4], rot_ref[5])
    up_ref[...] = turn_lanes(high, rot_ref[6], rot_ref[7])

    lane = lax.broadcasted_iota(jnp.int32, (half, cols), 1)
    first, last = lane == 0, lane == cols - 1
    c, s = twist_ref[0], twist_ref[1]
    pot = pot_ref[0, pl.ds(pl.multiple_of(which_ref[0] * half, 8), half)] + 3.0
    for n in range(fields // 2):
        re = mid_ref[2 * n, EDGE : EDGE + half]
        im = mid_ref[2 * n + 1, EDGE : EDGE + half]
        re_next, im_next = pltpu.roll(re, cols - 1, 1), pltpu.roll(im, cols - 1, 1)
        re_prev, im_prev = pltpu.roll(re, 1, 1), pltpu.roll(im, 1, 1)
        y_re = jnp.where(last, re_next * c - im_next * s, re_next) + jnp.where(
            first, re_prev * c + im_prev * s, re_prev
        )
        y_im = jnp.where(last, re_next * s + im_next * c, im_next) + jnp.where(
            first, im_prev * c - re_prev * s, im_prev
        )
        scale = pot - energy_ref[n]
        for f, value, beside in ((2 * n, re, y_re), (2 * n + 1, im, y_im)):
            beside = beside + mid_ref[f, EDGE - 1 : EDGE - 1 + half]
            beside = beside + mid_ref[f, EDGE + 1 : EDGE + 1 + half]
            out_ref[f, EDGE : EDGE + half] = scale * value - 0.5 * beside
            out_ref[f, 0:EDGE] = jnp.zeros((EDGE, cols), jnp.float32)
            out_ref[f, EDGE + half :] = jnp.zeros((EDGE + WIN, cols), jnp.float32)


def plane_call(which, energy, twist, starts, rot, strength, mid, pot, low_img, high_img):
    fields, wide, cols = mid.shape
    atoms = low_img.shape[0]
    blocks = -(-atoms * fields // 128)
    coef = jax.ShapeDtypeStruct((blocks, 128), jnp.float32)
    return pl.pallas_call(
        plane_kernel,
        out_shape=(jax.ShapeDtypeStruct((fields, wide + WIN, cols), jnp.float32), coef, coef, coef, coef),
        in_specs=[SMEM] * 6 + [VMEM] * 4,
        out_specs=(VMEM,) * 5,
        scratch_shapes=[pltpu.VMEM((2, atoms * fields, 8, 128), jnp.float32)],
        compiler_params=params(10),
        name="plane",
    )(which, energy, twist, starts, rot, strength, mid, pot, low_img, high_img)


def gather_kernel(starts_ref, rot_ref, str_ref, mid_ref, low_ref, high_ref, img_ref, low_img, high_img,
                  part_low, part_high, got_low, got_high, zsum_ref, out_ref, low, high, red):
    fields = mid_ref.shape[0]
    half = zsum_ref.shape[1]
    for n in range(fields // 2):
        for src, dst, j in ((low_ref, low, 0), (high_ref, high, 2)):
            c, s = rot_ref[j], rot_ref[j + 1]
            re, im = src[2 * n], src[2 * n + 1]
            dst[2 * n] = re * c - im * s
            dst[2 * n + 1] = re * s + im * c
        for k in range(2):
            f = 2 * n + k
            zsum_ref[f] = low[f, EDGE : EDGE + half] + high[f, EDGE : EDGE + half]
    atoms = img_ref.shape[0]
    groups = (
        (0, ((low, img_ref, 0), (mid_ref, img_ref, 1), (high, img_ref, 2))),
        (1, ((low, low_img, 0),)),
        (2, ((high, high_img, 1),)),
    )

    def atom(a, _):
        for j, planes in groups:
            begin = starts_ref[j, a]
            accs = [jnp.zeros((8, 128), jnp.float32)] * fields
            for src, img, z in planes:
                image = lambda part, k, img=img, z=z: img[a, z, part, 8 * k : 8 * k + 8]
                accs = project(src, begin, image, accs)
            for f in range(fields):
                red[j, a * fields + f] = accs[f] * str_ref[j, a]
        return 0

    lax.fori_loop(0, atoms, atom, 0)
    total = atoms * fields
    blocks = part_low.shape[0]
    out_ref[0:blocks] = lanes_of(red.at[0], total, blocks)
    out_ref[blocks : 2 * blocks] = lanes_of(red.at[1], total, blocks) + part_low[...] + got_low[...]
    out_ref[2 * blocks : 3 * blocks] = lanes_of(red.at[2], total, blocks) + part_high[...] + got_high[...]


def gather(starts, rot, strength, mid, low, high, img, low_img, high_img, parts, got):
    fields, rows, cols = mid.shape
    atoms = img.shape[0]
    blocks = -(-atoms * fields // 128)
    return pl.pallas_call(
        gather_kernel,
        out_shape=(
            jax.ShapeDtypeStruct((fields, rows - 2 * EDGE, cols), jnp.float32),
            jax.ShapeDtypeStruct((3 * blocks, 128), jnp.float32),
        ),
        in_specs=[SMEM] * 3 + [VMEM] * 10,
        out_specs=(VMEM,) * 2,
        scratch_shapes=[
            pltpu.VMEM(mid.shape, jnp.float32),
            pltpu.VMEM(mid.shape, jnp.float32),
            pltpu.VMEM((3, atoms * fields, 8, 128), jnp.float32),
        ],
        compiler_params=params(10),
        name="gather",
    )(starts, rot, strength, mid, low, high, img, low_img, high_img, *parts, *got)


def spread_into(acc, plane_ref, zsum_ref, starts_ref, coef_ref, images):
    fields = acc.shape[0]
    half = zsum_ref.shape[1]
    atoms = images[0][0].shape[0]
    blocks = coef_ref.shape[0] // 3
    inside = pl.ds(EDGE, half)
    if acc is not plane_ref:
        acc[:, 0:EDGE] = plane_ref[:, 0:EDGE]
        acc[:, EDGE + half :] = plane_ref[:, EDGE + half :]
    acc[:, inside] = plane_ref[:, inside] - 0.5 * zsum_ref[...]

    def atom(a, _):
        line = lax.div(a * fields, 128)
        lane = lax.rem(a * fields, 128)
        for j, (img, z) in enumerate(images):
            begin = pl.multiple_of(starts_ref[j, a], 8)
            for k in range(2):
                at = pl.ds(pl.multiple_of(begin + 8 * k, 8), 8)
                ire = img[a, z, 0, 8 * k : 8 * k + 8]
                iim = img[a, z, 1, 8 * k : 8 * k + 8]
                for n in range(fields // 2):
                    pr = coef_ref[j * blocks + line, lane + 2 * n]
                    pi = coef_ref[j * blocks + line, lane + 2 * n + 1]
                    acc[2 * n, at] = acc[2 * n, at] + (pr * ire + pi * iim)
                    acc[2 * n + 1, at] = acc[2 * n + 1, at] + (pi * ire - pr * iim)
        return 0

    lax.fori_loop(0, atoms, atom, 0)


def occupied_into(store, half, fields, sums_ref, side, own_ref, other_ref, base, scale, block, copies_of):
    count = own_ref.shape[0]

    def rows_of(b, _):
        at = pl.ds(pl.multiple_of(b * block, 8), block)
        for copy in copies_of(b):
            copy.wait()

        def band(m, accs):
            accs = list(accs)
            for row, occ in ((side, own_ref), (1 - side, other_ref)):
                pr, pi = occ[m, 0, at], occ[m, 1, at]
                for n in range(fields // 2):
                    sr = sums_ref[row, m * fields + 2 * n]
                    si = sums_ref[row, m * fields + 2 * n + 1]
                    accs[2 * n] = accs[2 * n] + (pr * sr - pi * si)
                    accs[2 * n + 1] = accs[2 * n + 1] + (pr * si + pi * sr)
            return tuple(accs)

        zero = jnp.zeros((block, 128), jnp.float32)
        accs = lax.fori_loop(0, count, band, (zero,) * fields, unroll=2)
        for f in range(fields):
            store(f, b * block, base(f, b * block, block) + scale * accs[f])
        return 0

    lax.fori_loop(0, half // block, rows_of, 0)


def correlate_into(red, src, offset, half, own_ref, other_ref):
    fields = src.shape[0]
    count = own_ref.shape[0]
    bands = fields // 2

    def pair(g, _):
        def row(i, accs):
            at = rows8(i)
            moved = pl.ds(pl.multiple_of(i * 8 + offset, 8), 8)
            accs = list(accs)
            occ = []
            for ref in (own_ref, other_ref):
                for k in range(2):
                    occ.append((ref[2 * g + k, 0, at], ref[2 * g + k, 1, at]))
            for n in range(bands):
                re, im = src[2 * n, moved], src[2 * n + 1, moved]
                for q, (pr, pi) in enumerate(occ):
                    j = (q * bands + n) * 2
                    accs[j] = accs[j] + (pr * re + pi * im)
                    accs[j + 1] = accs[j + 1] + (pr * im - pi * re)
            return tuple(accs)

        zero = jnp.zeros((8, 128), jnp.float32)
        accs = lax.fori_loop(0, half // 8, row, (zero,) * (8 * bands), unroll=3)
        for q in range(4):
            for j in range(fields):
                red[q // 2, (2 * g + q % 2) * fields + j] = accs[q * fields + j]
        return 0

    lax.fori_loop(0, count // 2, pair, 0)


def dots_into(red_dot, half, fields, pairs):
    bands = fields // 2

    def row(i, accs):
        at = pl.ds(pl.multiple_of(i * 8 + EDGE, 8), 8)
        accs = list(accs)
        for p, (left, right) in enumerate(pairs):
            for n in range(bands):
                value = left[2 * n, at] * right[2 * n, at] + left[2 * n + 1, at] * right[2 * n + 1, at]
                accs[p * bands + n] = accs[p * bands + n] + value
        return tuple(accs)

    zero = jnp.zeros((8, 128), jnp.float32)
    accs = lax.fori_loop(0, half // 8, row, (zero,) * (bands * len(pairs)), unroll=3)
    for j in range(bands * len(pairs)):
        red_dot[j] = accs[j]


def pick_block(half):
    return next(b for b in (24, 16, 8) if half % b == 0)


def shift_rows(start, size):
    return pl.ds(pl.multiple_of(start + EDGE, 8), size)


def band_copies(which_ref, half, block, b, occ_ref, occ_other_ref, own, other, sems):
    begin = pl.multiple_of(which_ref[0] * half + b * block, 8)
    at = pl.ds(pl.multiple_of(b * block, 8), block)
    return (
        pltpu.make_async_copy(occ_ref.at[:, :, pl.ds(begin, block)], own.at[:, :, at], sems.at[0, b]),
        pltpu.make_async_copy(occ_other_ref.at[:, :, at], other.at[:, :, at], sems.at[1, b]),
    )


def start_bands(half, block, copies_of):
    for b in range(half // block):
        for copy in copies_of(b):
            copy.start()


def write_sums(sum_ref, side, red):
    mine, theirs = sum_rows(red[0]), sum_rows(red[1])
    sum_ref[...] = jnp.zeros(sum_ref.shape, jnp.float32)
    sum_ref[0:1] = jnp.where(side == 0, mine, theirs)
    sum_ref[1:2] = jnp.where(side == 0, theirs, mine)


def write_edges(edge_ref, out_ref, half):
    for f in range(out_ref.shape[0]):
        edge_ref[f, 0:EDGE] = out_ref[f, EDGE : 2 * EDGE]
        edge_ref[f, EDGE : 2 * EDGE] = out_ref[f, half : half + EDGE]


def residual_kernel(scale, which_ref, starts_ref, coef_ref, sums_ref, plane_ref, zsum_ref, img_ref, low_ref, high_ref,
                    occ_ref, occ_other_ref, resp_hbm, pot_hbm, out_ref, edge_ref, sum_ref,
                    acc, own, other, resp, pot, red, red_dot, sems, more_sems):
    fields, wide, cols = out_ref.shape
    half = wide - 2 * EDGE
    side = which_ref[0]
    block = pick_block(half)
    begin = pl.multiple_of(side * half, 8)
    copies = (
        pltpu.make_async_copy(resp_hbm.at[:, :, pl.ds(begin, half)], resp, more_sems.at[0]),
        pltpu.make_async_copy(pot_hbm.at[:, pl.ds(begin, half)], pot, more_sems.at[1]),
    )
    for copy in copies:
        copy.start()
    copies_of = lambda b: band_copies(which_ref, half, block, b, occ_ref, occ_other_ref, own, other, sems)
    start_bands(half, block, copies_of)
    spread_into(acc, plane_ref, zsum_ref, starts_ref, coef_ref, ((img_ref, 1), (low_ref, 1), (high_ref, 0)))
    for copy in copies:
        copy.wait()

    def base(f, start, size):
        at = pl.ds(pl.multiple_of(start, 8), size)
        re, im = resp[f // 2, 0, at], resp[f // 2, 1, at]
        if f % 2 == 0:
            prod = pot[0, at] * re - pot[1, at] * im
        else:
            prod = pot[0, at] * im + pot[1, at] * re
        return -prod - acc[f, shift_rows(start, size)]

    def store(f, start, value):
        out_ref[f, shift_rows(start, block)] = value

    occupied_into(store, half, fields, sums_ref, side, own, other, base, scale, block, copies_of)
    write_edges(edge_ref, out_ref, half)
    correlate_into(red, out_ref, EDGE, half, own, other)
    dots_into(red_dot, half, fields, [(out_ref, out_ref)])
    write_sums(sum_ref, side, red)
    sum_ref[2:3] = sum_rows(red_dot[0 : fields // 2])


def field_outputs(fields, half, cols):
    return (
        jax.ShapeDtypeStruct((fields, half + 2 * EDGE, cols), jnp.float32),
        jax.ShapeDtypeStruct((fields, 2 * EDGE, cols), jnp.float32),
        jax.ShapeDtypeStruct((8, 128), jnp.float32),
    )


def residual_call(scale, which, starts, sums, local, images, psi_occ, other, resp, pot):
    coef, plane, zsum = local
    fields, half, cols = zsum.shape
    return pl.pallas_call(
        functools.partial(residual_kernel, scale),
        out_shape=field_outputs(fields, half, cols),
        in_specs=[SMEM] * 4 + [VMEM] * 5 + [HBM] * 4,
        out_specs=(VMEM,) * 3,
        scratch_shapes=[
            pltpu.VMEM(plane.shape, jnp.float32),
            pltpu.VMEM(other.shape, jnp.float32),
            pltpu.VMEM(other.shape, jnp.float32),
            pltpu.VMEM(resp.shape[:2] + (half, cols), jnp.float32),
            pltpu.VMEM((2, half, cols), jnp.float32),
            pltpu.VMEM((2, 128, 8, 128), jnp.float32),
            pltpu.VMEM((16, 8, 128), jnp.float32),
            pltpu.SemaphoreType.DMA((2, half // pick_block(half))),
            pltpu.SemaphoreType.DMA((2,)),
        ],
        compiler_params=params(16),
        name="residual",
    )(which, starts, coef, sums, plane, zsum, *images, psi_occ, other, resp, pot)


def image_kernel(scale, which_ref, starts_ref, coef_ref, sums_ref, plane_ref, zsum_ref, img_ref, low_ref, high_ref,
                 res_ref, occ_ref, occ_other_ref, out_ref, edge_ref, sum_ref,
                 acc, own, other, red, red_dot, sems):
    fields, wide, cols = out_ref.shape
    half = wide - 2 * EDGE
    side = which_ref[0]
    block = pick_block(half)
    copies_of = lambda b: band_copies(which_ref, half, block, b, occ_ref, occ_other_ref, own, other, sems)
    start_bands(half, block, copies_of)
    spread_into(acc, plane_ref, zsum_ref, starts_ref, coef_ref, ((img_ref, 1), (low_ref, 1), (high_ref, 0)))

    def base(f, start, size):
        return acc[f, shift_rows(start, size)]

    def store(f, start, value):
        out_ref[f, shift_rows(start, block)] = value

    occupied_into(store, half, fields, sums_ref, side, own, other, base, scale, block, copies_of)
    write_edges(edge_ref, out_ref, half)
    correlate_into(red, out_ref, EDGE, half, own, other)
    dots_into(red_dot, half, fields, [(res_ref, out_ref), (out_ref, out_ref)])
    write_sums(sum_ref, side, red)
    sum_ref[2:3] = sum_rows(red_dot[0:fields])


def image_call(scale, which, starts, sums, local, images, res, psi_occ, other):
    coef, plane, zsum = local
    fields, half, cols = zsum.shape
    return pl.pallas_call(
        functools.partial(image_kernel, scale),
        out_shape=field_outputs(fields, half, cols),
        in_specs=[SMEM] * 4 + [VMEM] * 6 + [HBM] * 2,
        out_specs=(VMEM,) * 3,
        scratch_shapes=[
            pltpu.VMEM(plane.shape, jnp.float32),
            pltpu.VMEM(other.shape, jnp.float32),
            pltpu.VMEM(other.shape, jnp.float32),
            pltpu.VMEM((2, 128, 8, 128), jnp.float32),
            pltpu.VMEM((16, 8, 128), jnp.float32),
            pltpu.SemaphoreType.DMA((2, half // pick_block(half))),
        ],
        compiler_params=params(16),
        name="image",
    )(which, starts, coef, sums, plane, zsum, *images, res, psi_occ, other)


def local_kernel(starts_ref, coef_ref, plane_ref, zsum_ref, img_ref, low_ref, high_ref, field_ref, part_ref,
                 out_ref, sum_ref, red_dot):
    fields = out_ref.shape[0]
    half = zsum_ref.shape[1]
    spread_into(out_ref, plane_ref, zsum_ref, starts_ref, coef_ref, ((img_ref, 1), (low_ref, 1), (high_ref, 0)))
    dots_into(red_dot, half, fields, [(field_ref, out_ref)])
    sum_ref[...] = part_ref[...]
    sum_ref[3:4] = sum_rows(red_dot[0 : fields // 2])


def local_call(starts, local, images, field, part):
    coef, plane, zsum = local
    return pl.pallas_call(
        local_kernel,
        out_shape=(
            jax.ShapeDtypeStruct(plane.shape, jnp.float32),
            jax.ShapeDtypeStruct((8, 128), jnp.float32),
        ),
        in_specs=[SMEM] * 2 + [VMEM] * 7,
        out_specs=(VMEM, VMEM),
        scratch_shapes=[pltpu.VMEM((16, 8, 128), jnp.float32)],
        compiler_params=params(10),
        name="local",
    )(starts, coef, plane, zsum, *images, field, part)


def last_kernel(which_ref, sums_ref, mix_ref, res_hbm, first_hbm, second_hbm, occ_ref, occ_other_ref,
                out_ref, res, first, second, own, other, sems, more_sems):
    fields, half, cols = out_ref.shape
    side = which_ref[0]
    block = pick_block(half)

    def copies_of(b):
        at = pl.ds(pl.multiple_of(b * block, 8), block)
        moved = shift_rows(b * block, block)
        own_copies = tuple(
            pltpu.make_async_copy(src.at[:, moved], dst.at[:, at], more_sems.at[j, b])
            for j, (src, dst) in enumerate(((res_hbm, res), (first_hbm, first), (second_hbm, second)))
        )
        return own_copies + band_copies(which_ref, half, block, b, occ_ref, occ_other_ref, own, other, sems)

    start_bands(half, block, copies_of)

    def base(f, start, size):
        n = f // 2
        at = pl.ds(pl.multiple_of(start, 8), size)
        return res[f, at] + mix_ref[0, n] * first[f, at] + mix_ref[1, n] * second[f, at]

    def store(f, start, value):
        out_ref[f, pl.ds(pl.multiple_of(start, 8), block)] = value

    occupied_into(store, half, fields, sums_ref, side, own, other, base, 1.0, block, copies_of)


def last_call(which, sums, mix, res, first, second, psi_occ, other):
    fields, wide, cols = res.shape
    half = wide - 2 * EDGE
    blocks = half // pick_block(half)
    field = pltpu.VMEM((fields, half, cols), jnp.float32)
    return pl.pallas_call(
        last_kernel,
        out_shape=jax.ShapeDtypeStruct((fields, half, cols), jnp.float32),
        in_specs=[SMEM] * 3 + [HBM] * 5,
        out_specs=VMEM,
        scratch_shapes=[
            field,
            field,
            field,
            pltpu.VMEM(other.shape, jnp.float32),
            pltpu.VMEM(other.shape, jnp.float32),
            pltpu.SemaphoreType.DMA((2, blocks)),
            pltpu.SemaphoreType.DMA((3, blocks)),
        ],
        compiler_params=params(60),
        name="last",
    )(which, sums, mix, res, first, second, psi_occ, other)


def xor_sum(block, bits):
    count = lax.axis_size("space") * lax.axis_size("occ")
    masks = [0]
    for bit in bits:
        masks = masks + [mask | bit for mask in masks]
    parts = [block]
    for mask in masks[1:]:
        parts.append(lax.ppermute(block, ("space", "occ"), [(i, i ^ mask) for i in range(count)]))
    while len(parts) > 1:
        parts = [parts[j] + parts[j + 1] for j in range(0, len(parts), 2)]
    return parts[0]


def total(block):
    count = lax.axis_size("space")
    bit = 2
    while count > 1:
        if count % 4 == 0:
            block = xor_sum(block, (bit, 2 * bit))
            bit, count = 4 * bit, count // 4
        else:
            block = xor_sum(block, (bit,))
            bit, count = 2 * bit, count // 2
    return xor_sum(block, (1,))


def exchange(block):
    return lax.ppermute(block, "occ", SWAP)


def from_behind(block, distance):
    count = lax.axis_size("space")
    return lax.ppermute(block, "space", [((i - distance) % count, i) for i in range(count)])


def window_images(x_cell, y_cell, offsets, values, theta_y, rows_y, planes):
    y_raw = y_cell[:, None] + offsets[None, :, 2]
    y_wrap = jnp.floor_divide(y_raw, rows_y)
    y_at = y_raw - y_wrap * rows_y
    angles = theta_y * y_wrap.astype(jnp.float32)
    row = x_cell[:, None] + offsets[None, :, 1] + RAD
    slot = []
    for plane in planes:
        wanted = (row[:, None, :] == jnp.arange(WIN, dtype=jnp.int32)[None, :, None]) & (
            offsets[:, 0] == plane
        )[None, None, :]
        slot.append(wanted)
    slots = jnp.stack(slot, axis=1)
    weights = jnp.stack([values * jnp.cos(angles), values * jnp.sin(angles)], axis=1)
    left = jnp.where(slots[:, :, None], weights[:, None, :, None, :], 0.0)
    atoms = left.shape[0]
    left = left.reshape(atoms, len(planes) * 2 * WIN, -1)
    right = (y_at[:, :, None] == jnp.arange(rows_y, dtype=jnp.int32)[None, None, :]).astype(jnp.float32)
    image = jnp.einsum("apk,aky->apy", left, right, precision=PRECISE)
    return image.reshape(atoms, len(planes), 2, WIN, rows_y)


def shards(
    psi_occ,
    psi_resp,
    initial_guess,
    local_potential,
    potential_change,
    band_energy,
    q_index,
    atom_cells,
    offsets,
    projector,
    strength,
):
    slab_count = lax.axis_size("space")
    slab_index = lax.axis_index("space")
    side = lax.axis_index("occ")
    layers, rows_x, rows_y = local_potential.shape
    half = rows_x // 2
    atoms = atom_cells.shape[0]
    bands = psi_resp.shape[0]
    fields = 2 * bands
    weight = 1.0 / (layers * slab_count * rows_x * rows_y)
    thetas = q_index.astype(jnp.float32) * (2.0 * math.pi / QDIV)
    cosines = jnp.cos(thetas)
    sines = jnp.sin(thetas)
    at_first = slab_index == 0
    at_last = slab_index == slab_count - 1
    z_rot = jnp.stack(
        [
            jnp.where(at_first, cosines[0], 1.0),
            jnp.where(at_first, -sines[0], 0.0),
            jnp.where(at_last, cosines[0], 1.0),
            jnp.where(at_last, sines[0], 0.0),
            jnp.where(slab_index < 2, cosines[0], 1.0),
            jnp.where(slab_index < 2, sines[0], 0.0),
            jnp.where(slab_index >= slab_count - 2, cosines[0], 1.0),
            jnp.where(slab_index >= slab_count - 2, -sines[0], 0.0),
        ]
    )
    x_rot = jnp.stack(
        [
            jnp.where(side == 0, cosines[1], 1.0),
            jnp.where(side == 0, -sines[1], 0.0),
            jnp.where(side == 1, cosines[1], 1.0),
            jnp.where(side == 1, sines[1], 0.0),
        ]
    )
    y_twist = jnp.stack([cosines[2], sines[2]])
    which = side.astype(jnp.int32).reshape(1)

    occ = psi_occ.reshape(psi_occ.shape[0], 2, rows_x, rows_y)
    resp = psi_resp.reshape(bands, 2, rows_x, rows_y)
    guess = initial_guess.reshape(bands, 2, rows_x, rows_y)
    change = potential_change.reshape(2, rows_x, rows_y)

    guess_mid, occ_send = prep_call(which, x_rot, guess, occ)
    occ_other = exchange(occ_send)

    packed = jnp.stack(
        [
            projector,
            jnp.pad(
                jnp.concatenate([atom_cells.astype(jnp.float32), strength[:, None]], axis=1),
                ((0, 0), (0, projector.shape[1] - 4)),
            ),
        ],
        axis=1,
    )
    below = from_behind(packed, 1)
    above = from_behind(packed, -1)
    below, above, occ_first = lax.optimization_barrier((below, above, occ))
    cells = [atom_cells]
    for side_pack in (below, above):
        cells.append(side_pack[:, 1, :3].astype(jnp.int32))
    all_x = jnp.stack([c[:, 1] for c in cells])
    all_y = jnp.stack([c[:, 2] for c in cells])
    at_row = jnp.mod(all_x - RAD - side * half + EDGE, rows_x)
    inner = at_row % 8
    touching = at_row < half + EDGE
    put_starts = jnp.where(touching, at_row - inner, half + 2 * EDGE).astype(jnp.int32)
    get_starts = jnp.where(touching, at_row - inner, 0).astype(jnp.int32)
    strengths = jnp.stack([strength, below[:, 1, 3], above[:, 1, 3]])
    img = window_images(inner[0], all_y[0], offsets, projector, thetas[2], rows_y, (-1, 0, 1))
    low_img = window_images(inner[1], all_y[1], offsets, below[:, 0], thetas[2], rows_y, (0, 1))
    high_img = window_images(inner[2], all_y[2], offsets, above[:, 0], thetas[2], rows_y, (-1, 0))
    images = (img, low_img, high_img)

    def local_part(mid):
        low = from_behind(mid, 1)
        high = from_behind(mid, -1)
        plane, part_low, part_high, down, up = plane_call(
            which, band_energy, y_twist, get_starts, z_rot, strengths, mid, local_potential, low_img, high_img
        )
        got = (from_behind(up, 2), from_behind(down, -2))
        zsum, coef = gather(get_starts, z_rot, strengths, mid, low, high, *images, (part_low, part_high), got)
        return coef, plane, zsum

    first_sums = total(first_corr(which, occ_first, resp, change, guess))
    residual, edges, part = residual_call(
        weight, which, put_starts, first_sums, local_part(guess_mid), images, occ, occ_other, resp, change
    )
    tot = total(part)
    norm0 = tot[2, :bands]
    residual = fill_call(x_rot, exchange(edges), residual)
    residual_other = exchange(residual)
    image, edges, part = image_call(
        SHIFT_WEIGHT * weight, which, put_starts, tot, local_part(residual), images, residual, occ, occ_other
    )
    image = fill_call(x_rot, exchange(edges), image)
    image_other = exchange(image)
    image2, part = local_call(put_starts, local_part(image), images, image, part)
    tot = total(part)
    sums = tot[0:2]
    cross = tot[2, :bands]
    square = tot[2, bands : 2 * bands]
    occ_square = jnp.sum((sums * sums).reshape(-1, bands, 2), axis=(0, 2))
    triple = tot[3, :bands] + SHIFT_WEIGHT * weight * occ_square
    step0 = norm0 / cross
    norm1 = norm0 - 2.0 * step0 * cross + step0 * step0 * square
    growth = norm1 / norm0
    lead = 1.0 + growth
    curvature = lead * lead * cross - 2.0 * lead * step0 * square + step0 * step0 * triple
    step1 = norm1 / curvature
    mix0 = -step0 - step1 * lead
    mix1 = step1 * step0
    per_lane = jnp.tile(jnp.repeat(mix1, 2), sums.shape[1] // fields)
    last_sums = SHIFT_WEIGHT * weight * sums * per_lane[None, :]
    mine = last_call(which, last_sums, jnp.stack([mix0, mix1]), residual, image, image2, occ, occ_other)
    theirs = exchange(mine)

    def join(own_half, other_half):
        lower = jnp.where(side == 0, own_half, other_half)
        upper = jnp.where(side == 0, other_half, own_half)
        return jnp.concatenate([lower, upper], axis=1).reshape(bands, 2, 1, rows_x, rows_y)

    inside = lambda v: v[:, EDGE : EDGE + half]
    wide = lambda v: v[:, None, None, None, None]
    response = (
        initial_guess
        + wide(step0 + step1 * lead) * join(inside(residual), inside(residual_other))
        - wide(step0 * step1) * join(inside(image), inside(image_other))
    )
    return response, join(mine, theirs)


def solution(mesh):
    return jax.shard_map(
        shards,
        mesh=mesh,
        in_specs=(
            P("occ", None, "space", None, None),
            P("resp", None, "space", None, None),
            P("resp", None, "space", None, None),
            P("space", None, None),
            P(None, "space", None, None),
            P("resp"),
            P(),
            P("space", None),
            P(),
            P("space", None),
            P("space"),
        ),
        out_specs=(P("resp", None, "space", None, None), P("resp", None, "space", None, None)),
        check_vma=False,
    )
```

```python
import functools
import math

import jax
import jax.numpy as jnp
from jax import lax
from jax.experimental import pallas as pl
from jax.experimental.pallas import tpu as pltpu
from jax.sharding import PartitionSpec as P

RAD = 4
QDIV = 8
EDGE = 8
WIN = 16
SHIFT_WEIGHT = 3.0
PRECISE = lax.Precision.HIGHEST
SWAP = [(0, 1), (1, 0)]

VMEM = pl.BlockSpec(memory_space=pltpu.VMEM)
SMEM = pl.BlockSpec(memory_space=pltpu.SMEM)
ANY = pl.BlockSpec(memory_space=pl.ANY)
HBM = pl.BlockSpec(memory_space=pltpu.HBM)


def params(mib):
    return pltpu.CompilerParams(vmem_limit_bytes=mib * 1024 * 1024)


def sum_rows(values):
    total = jnp.sum(values, axis=2, keepdims=True)
    row = lax.broadcasted_iota(jnp.int32, values.shape, 0)
    lane = lax.broadcasted_iota(jnp.int32, values.shape, 2)
    picked = jnp.sum(jnp.where(row == lane, total, 0.0), axis=0)
    return jnp.sum(picked, axis=0, keepdims=True)


def rows8(index):
    return pl.ds(pl.multiple_of(index * 8, 8), 8)


def extra_rows(count, fields):
    return -(-count // (8 * fields)) * 8


def prep_kernel(which_ref, cos_ref, sin_ref, guess_ref, occ_ref, atoms_ref, out_ref, send_ref, middle, low, high, sems):
    fields = out_ref.shape[0]
    half = send_ref.shape[2]
    wide = half + 2 * EDGE
    count = occ_ref.shape[0]
    side = which_ref[0]
    begin = pl.multiple_of(side * half, 8)
    away = pl.multiple_of((1 - side) * half, 8)
    under = pl.multiple_of((1 - side) * half + half - EDGE, 8)
    copies = []
    for j, (start, size, dst) in enumerate(((begin, half, middle), (under, EDGE, low), (away, EDGE, high))):
        copies.append(pltpu.make_async_copy(guess_ref.at[:, :, pl.ds(start, size)], dst, sems.at[j]))
    parts = sems.shape[0] - 3
    each = count // parts
    sends = []
    for j in range(parts):
        chosen = slice(j * each, (j + 1) * each)
        sends.append(
            pltpu.make_async_copy(occ_ref.at[chosen, :, pl.ds(away, half)], send_ref.at[chosen], sems.at[3 + j])
        )
    for copy in copies + sends:
        copy.start()
    for copy in copies:
        copy.wait()
    for n in range(fields // 2):
        for k in range(2):
            out_ref[2 * n + k, EDGE : EDGE + half] = middle[n, k]
        for src, spot, j in ((low, 0, 4), (high, EDGE + half, 5)):
            c, s = cos_ref[j], sin_ref[j]
            re, im = src[n, 0], src[n, 1]
            out_ref[2 * n, spot : spot + EDGE] = re * c - im * s
            out_ref[2 * n + 1, spot : spot + EDGE] = re * s + im * c
    for f in range(fields):
        for r in range(0, out_ref.shape[1] - wide, 8):
            at = f * (out_ref.shape[1] - wide) + r
            if at < atoms_ref.shape[0]:
                out_ref[f, wide + r : wide + r + 8] = atoms_ref[at : at + 8]
            else:
                out_ref[f, wide + r : wide + r + 8] = jnp.zeros((8, 128), jnp.float32)
    for copy in sends:
        copy.wait()


def prep_call(which, rot, guess, occ, atoms):
    bands, _, rows, cols = guess.shape
    half = rows // 2
    extra = extra_rows(atoms.shape[0], 2 * bands)
    return pl.pallas_call(
        prep_kernel,
        out_shape=(
            jax.ShapeDtypeStruct((2 * bands, half + 2 * EDGE + extra, cols), jnp.float32),
            jax.ShapeDtypeStruct((occ.shape[0], 2, half, cols), jnp.float32),
        ),
        in_specs=[SMEM, SMEM, SMEM, HBM, HBM, VMEM],
        out_specs=(VMEM, VMEM),
        scratch_shapes=[
            pltpu.VMEM((bands, 2, half, cols), jnp.float32),
            pltpu.VMEM((bands, 2, EDGE, cols), jnp.float32),
            pltpu.VMEM((bands, 2, EDGE, cols), jnp.float32),
            pltpu.SemaphoreType.DMA((7,)),
        ],
        compiler_params=params(60),
        name="prep",
    )(which, *rot, guess, occ, atoms)


def fill_kernel(cos_ref, sin_ref, got_ref, ext_ref, out_ref, low, high, sems):
    fields, wide, _ = out_ref.shape
    for n in range(fields // 2):
        for dst, at, j in ((low, EDGE, 4), (high, 0, 5)):
            c, s = cos_ref[j], sin_ref[j]
            re, im = got_ref[2 * n, at : at + EDGE], got_ref[2 * n + 1, at : at + EDGE]
            dst[2 * n] = re * c - im * s
            dst[2 * n + 1] = re * s + im * c
    one = pltpu.make_async_copy(low, out_ref.at[:, 0:EDGE], sems.at[0])
    two = pltpu.make_async_copy(high, out_ref.at[:, wide - EDGE : wide], sems.at[1])
    one.start()
    two.start()
    one.wait()
    two.wait()


def fill_call(rot, got, ext):
    shape = (ext.shape[0], EDGE, ext.shape[2])
    return pl.pallas_call(
        fill_kernel,
        out_shape=jax.ShapeDtypeStruct(ext.shape, jnp.float32),
        in_specs=[SMEM, SMEM, VMEM, ANY],
        out_specs=ANY,
        scratch_shapes=[
            pltpu.VMEM(shape, jnp.float32),
            pltpu.VMEM(shape, jnp.float32),
            pltpu.SemaphoreType.DMA((2,)),
        ],
        input_output_aliases={3: 0},
        compiler_params=params(4),
        name="fill",
    )(*rot, got, ext)


def first_corr_kernel(which_ref, occ_ref, resp_ref, pot_ref, guess_ref, out_ref, mixed, red):
    bands, _, rows, _ = resp_ref.shape
    group = occ_ref.shape[0]
    step = pl.program_id(0)

    @pl.when(step == 0)
    def _():
        for n in range(bands):
            re = resp_ref[n, 0]
            im = resp_ref[n, 1]
            mixed[2 * n] = pot_ref[0] * re - pot_ref[1] * im - SHIFT_WEIGHT * guess_ref[n, 0]
            mixed[2 * n + 1] = pot_ref[0] * im + pot_ref[1] * re - SHIFT_WEIGHT * guess_ref[n, 1]

    def row(i, accs):
        at = rows8(i)
        occ = [(occ_ref[k, 0, at], occ_ref[k, 1, at]) for k in range(group)]
        accs = list(accs)
        for n in range(bands):
            re, im = mixed[2 * n, at], mixed[2 * n + 1, at]
            for k, (pr, pi) in enumerate(occ):
                j = (k * bands + n) * 2
                accs[j] = accs[j] + (pr * re + pi * im)
                accs[j + 1] = accs[j + 1] + (pr * im - pi * re)
        return tuple(accs)

    zero = jnp.zeros((8, 128), jnp.float32)
    count = 2 * bands * group
    accs = lax.fori_loop(0, rows // 8, row, (zero,) * count, unroll=3)
    for j in range(count):
        red[step * count + j] = accs[j]

    @pl.when(step == pl.num_programs(0) - 1)
    def _():
        out_ref[...] = jnp.zeros(out_ref.shape, jnp.float32)
        total = sum_rows(red[...])
        side = which_ref[0]
        out_ref[0:1] = jnp.where(side == 0, total, 0.0)
        out_ref[1:2] = jnp.where(side == 0, 0.0, total)


def first_corr(which, psi_occ, psi_resp, pot, guess):
    group = 4
    count, _, rows, cols = psi_occ.shape
    fixed = lambda shape: pl.BlockSpec(shape, lambda i: (0,) * len(shape))
    return pl.pallas_call(
        first_corr_kernel,
        out_shape=jax.ShapeDtypeStruct((8, 128), jnp.float32),
        grid=(count // group,),
        in_specs=[
            SMEM,
            pl.BlockSpec((group, 2, rows, cols), lambda i: (i, 0, 0, 0)),
            fixed(psi_resp.shape),
            fixed(pot.shape),
            fixed(guess.shape),
        ],
        out_specs=fixed((8, 128)),
        scratch_shapes=[
            pltpu.VMEM((psi_resp.shape[0] * 2, rows, cols), jnp.float32),
            pltpu.VMEM((128, 8, 128), jnp.float32),
        ],
        compiler_params=params(60),
        name="first_corr",
    )(which, psi_occ, psi_resp, pot, guess)


def gather_kernel(start_ref, cos_ref, sin_ref, str_ref, mid_ref, low_ref, high_ref, img_ref,
                  zsum_ref, out_ref, up_ref, down_ref, low, high, red):
    fields = mid_ref.shape[0]
    half = zsum_ref.shape[1]
    wide = half + 2 * EDGE
    for n in range(fields // 2):
        for src, dst, j in ((low_ref, low, 0), (high_ref, high, 1)):
            c, s = cos_ref[j], sin_ref[j]
            re, im = src[2 * n, 0:wide], src[2 * n + 1, 0:wide]
            dst[2 * n] = re * c - im * s
            dst[2 * n + 1] = re * s + im * c
        for k in range(2):
            f = 2 * n + k
            zsum_ref[f] = low[f, EDGE : EDGE + half] + high[f, EDGE : EDGE + half]
    atoms = img_ref.shape[0]

    def atom(a, _):
        begin = pl.multiple_of(start_ref[a], 8)
        accs = [jnp.zeros((8, 128), jnp.float32)] * fields
        for z, src in enumerate((low, mid_ref, high)):
            for k in range(2):
                at = pl.ds(pl.multiple_of(begin + 8 * k, 8), 8)
                ire = img_ref[a, z, 0, 8 * k : 8 * k + 8]
                iim = img_ref[a, z, 1, 8 * k : 8 * k + 8]
                for n in range(fields // 2):
                    re, im = src[2 * n, at], src[2 * n + 1, at]
                    accs[2 * n] = accs[2 * n] + (re * ire - im * iim)
                    accs[2 * n + 1] = accs[2 * n + 1] + (re * iim + im * ire)
        for f in range(fields):
            red[a * fields + f] = accs[f] * str_ref[a]
        return 0

    lax.fori_loop(0, atoms, atom, 0)
    total = atoms * fields
    value = lanes_of(red, total, out_ref.shape[0])
    out_ref[...] = value
    up_ref[...] = turn_lanes(value, cos_ref[7], sin_ref[7])
    down_ref[...] = turn_lanes(value, cos_ref[8], sin_ref[8])


def gather(starts, rot, strength, mid, low, high, img, half):
    fields, _, cols = mid.shape
    rows = half + 2 * EDGE
    atoms = img.shape[0]
    blocks = -(-atoms * fields // 128)
    coef = jax.ShapeDtypeStruct((blocks, 128), jnp.float32)
    return pl.pallas_call(
        gather_kernel,
        out_shape=(
            jax.ShapeDtypeStruct((fields, rows - 2 * EDGE, cols), jnp.float32),
            coef,
            coef,
            coef,
        ),
        in_specs=[SMEM] * 4 + [VMEM] * 4,
        out_specs=(VMEM,) * 4,
        scratch_shapes=[
            pltpu.VMEM((fields, rows, cols), jnp.float32),
            pltpu.VMEM((fields, rows, cols), jnp.float32),
            pltpu.VMEM((atoms * fields, 8, 128), jnp.float32),
        ],
        compiler_params=params(10),
        name="gather",
    )(starts, *rot, strength, mid, low, high, img)


def spread_into(acc, start_of, coef_ref, image_of, atoms):
    fields = acc.shape[0]

    def atom(a, _):
        begin = pl.multiple_of(start_of(a), 8)
        line = lax.div(a * fields, 128)
        lane = lax.rem(a * fields, 128)
        for k in range(2):
            at = pl.ds(pl.multiple_of(begin + 8 * k, 8), 8)
            ire = image_of(a, 0, k)
            iim = image_of(a, 1, k)
            for n in range(fields // 2):
                pr = coef_ref[line, lane + 2 * n]
                pi = coef_ref[line, lane + 2 * n + 1]
                acc[2 * n, at] = acc[2 * n, at] + (pr * ire + pi * iim)
                acc[2 * n + 1, at] = acc[2 * n + 1, at] + (pi * ire - pr * iim)
        return 0

    lax.fori_loop(0, atoms, atom, 0)


def stencil_kernel(which_ref, energy_ref, cos_ref, sin_ref, starts_ref, coef_ref, mid_ref, zsum_ref, pot_ref, img_ref, out_ref):
    fields, half, cols = zsum_ref.shape
    lane = lax.broadcasted_iota(jnp.int32, (half, cols), 1)
    first, last = lane == 0, lane == cols - 1
    c, s = cos_ref[6], sin_ref[6]
    pot = pot_ref[0, pl.ds(pl.multiple_of(which_ref[0] * half, 8), half)] + 3.0
    for n in range(fields // 2):
        re = mid_ref[2 * n, EDGE : EDGE + half]
        im = mid_ref[2 * n + 1, EDGE : EDGE + half]
        re_next, im_next = pltpu.roll(re, cols - 1, 1), pltpu.roll(im, cols - 1, 1)
        re_prev, im_prev = pltpu.roll(re, 1, 1), pltpu.roll(im, 1, 1)
        y_re = jnp.where(last, re_next * c - im_next * s, re_next) + jnp.where(
            first, re_prev * c + im_prev * s, re_prev
        )
        y_im = jnp.where(last, re_next * s + im_next * c, im_next) + jnp.where(
            first, im_prev * c - re_prev * s, im_prev
        )
        scale = pot - energy_ref[n]
        for f, value, beside in ((2 * n, re, y_re), (2 * n + 1, im, y_im)):
            beside = beside + zsum_ref[f]
            beside = beside + mid_ref[f, EDGE - 1 : EDGE - 1 + half]
            beside = beside + mid_ref[f, EDGE + 1 : EDGE + 1 + half]
            out_ref[f, EDGE : EDGE + half] = scale * value - 0.5 * beside
            out_ref[f, 0:EDGE] = jnp.zeros((EDGE, cols), jnp.float32)
            out_ref[f, EDGE + half :] = jnp.zeros((EDGE + WIN, cols), jnp.float32)
    atoms = img_ref.shape[0]
    image = lambda a, part, k: img_ref[a, 1, part, 8 * k : 8 * k + 8]
    spread_into(out_ref, lambda a: starts_ref[0, a], coef_ref, image, atoms)


def stencil(which, energy, rot, starts, coef, mid, zsum, pot, img):
    fields, half, cols = zsum.shape
    return pl.pallas_call(
        stencil_kernel,
        out_shape=jax.ShapeDtypeStruct((fields, half + 2 * EDGE + WIN, cols), jnp.float32),
        in_specs=[SMEM] * 6 + [VMEM] * 4,
        out_specs=VMEM,
        compiler_params=params(10),
        name="stencil",
    )(which, energy, *rot, starts, coef, mid, zsum, pot, img)


def project(src, begin, image_of, accs):
    accs = list(accs)
    for k in range(2):
        at = pl.ds(pl.multiple_of(begin + 8 * k, 8), 8)
        ire, iim = image_of(0, k), image_of(1, k)
        for n in range(len(accs) // 2):
            re, im = src[2 * n, at], src[2 * n + 1, at]
            accs[2 * n] = accs[2 * n] + (re * ire - im * iim)
            accs[2 * n + 1] = accs[2 * n + 1] + (re * iim + im * ire)
    return accs


def lanes_of(red, total, blocks):
    return jnp.concatenate([sum_rows(red[128 * b : min(total, 128 * b + 128)]) for b in range(blocks)], axis=0)


def turn_lanes(value, cosine, sine_part):
    even = lax.broadcasted_iota(jnp.int32, value.shape, 1) % 2 == 0
    times_i = jnp.where(even, -pltpu.roll(value, 127, 1), pltpu.roll(value, 1, 1))
    return value * cosine + times_i * sine_part


def plane_kernel(which_ref, energy_ref, starts_ref, cos_ref, sin_ref, str_ref, mid_ref, pot_ref, low_img, high_img,
                 out_ref, low_ref, high_ref, down_ref, up_ref, red):
    fields, wide, cols = mid_ref.shape
    half = wide - 2 * EDGE
    atoms = low_img.shape[0]
    total = atoms * fields

    def atom(a, _):
        for j, img, z in ((1, low_img, 1), (2, high_img, 0)):
            begin = starts_ref[j, a]
            image = lambda part, k: img[a, z, part, 8 * k : 8 * k + 8]
            accs = project(mid_ref, begin, image, [jnp.zeros((8, 128), jnp.float32)] * fields)
            for f in range(fields):
                red[j - 1, a * fields + f] = accs[f] * str_ref[j, a]
        return 0

    lax.fori_loop(0, atoms, atom, 0)
    blocks = low_ref.shape[0]
    low = lanes_of(red.at[0], total, blocks)
    high = lanes_of(red.at[1], total, blocks)
    low_ref[...] = low
    high_ref[...] = high
    down_ref[...] = turn_lanes(low, cos_ref[2], sin_ref[2])
    up_ref[...] = turn_lanes(high, cos_ref[3], sin_ref[3])

    lane = lax.broadcasted_iota(jnp.int32, (half, cols), 1)
    first, last = lane == 0, lane == cols - 1
    c, s = cos_ref[6], sin_ref[6]
    pot = pot_ref[0, pl.ds(pl.multiple_of(which_ref[0] * half, 8), half)] + 3.0
    for n in range(fields // 2):
        re = mid_ref[2 * n, EDGE : EDGE + half]
        im = mid_ref[2 * n + 1, EDGE : EDGE + half]
        re_next, im_next = pltpu.roll(re, cols - 1, 1), pltpu.roll(im, cols - 1, 1)
        re_prev, im_prev = pltpu.roll(re, 1, 1), pltpu.roll(im, 1, 1)
        y_re = jnp.where(last, re_next * c - im_next * s, re_next) + jnp.where(
            first, re_prev * c + im_prev * s, re_prev
        )
        y_im = jnp.where(last, re_next * s + im_next * c, im_next) + jnp.where(
            first, im_prev * c - re_prev * s, im_prev
        )
        scale = pot - energy_ref[n]
        for f, value, beside in ((2 * n, re, y_re), (2 * n + 1, im, y_im)):
            beside = beside + mid_ref[f, EDGE - 1 : EDGE - 1 + half]
            beside = beside + mid_ref[f, EDGE + 1 : EDGE + 1 + half]
            out_ref[f, EDGE : EDGE + half] = scale * value - 0.5 * beside
            out_ref[f, 0:EDGE] = jnp.zeros((EDGE, cols), jnp.float32)
            out_ref[f, EDGE + half :] = jnp.zeros((EDGE + WIN, cols), jnp.float32)


def plane_call(which, energy, starts, rot, strength, mid, pot, low_img, high_img):
    fields, wide, cols = mid.shape
    atoms = low_img.shape[0]
    blocks = -(-atoms * fields // 128)
    coef = jax.ShapeDtypeStruct((blocks, 128), jnp.float32)
    return pl.pallas_call(
        plane_kernel,
        out_shape=(jax.ShapeDtypeStruct((fields, wide + WIN, cols), jnp.float32), coef, coef, coef, coef),
        in_specs=[SMEM] * 6 + [VMEM] * 4,
        out_specs=(VMEM,) * 5,
        scratch_shapes=[pltpu.VMEM((2, atoms * fields, 8, 128), jnp.float32)],
        compiler_params=params(10),
        name="plane",
    )(which, energy, starts, *rot, strength, mid, pot, low_img, high_img)


def gather_all_kernel(starts_ref, cos_ref, sin_ref, str_ref, mid_ref, low_ref, high_ref, img_ref, low_img, high_img,
                  part_low, part_high, got_low, got_high, zsum_ref, out_ref, low, high, red):
    fields = mid_ref.shape[0]
    half = zsum_ref.shape[1]
    wide = half + 2 * EDGE
    for n in range(fields // 2):
        for src, dst, j in ((low_ref, low, 0), (high_ref, high, 1)):
            c, s = cos_ref[j], sin_ref[j]
            re, im = src[2 * n, 0:wide], src[2 * n + 1, 0:wide]
            dst[2 * n] = re * c - im * s
            dst[2 * n + 1] = re * s + im * c
        for k in range(2):
            f = 2 * n + k
            zsum_ref[f] = low[f, EDGE : EDGE + half] + high[f, EDGE : EDGE + half]
    atoms = img_ref.shape[0]
    groups = (
        (0, ((low, img_ref, 0), (mid_ref, img_ref, 1), (high, img_ref, 2))),
        (1, ((low, low_img, 0),)),
        (2, ((high, high_img, 1),)),
    )

    def atom(a, _):
        for j, planes in groups:
            begin = starts_ref[j, a]
            accs = [jnp.zeros((8, 128), jnp.float32)] * fields
            for src, img, z in planes:
                image = lambda part, k, img=img, z=z: img[a, z, part, 8 * k : 8 * k + 8]
                accs = project(src, begin, image, accs)
            for f in range(fields):
                red[j, a * fields + f] = accs[f] * str_ref[j, a]
        return 0

    lax.fori_loop(0, atoms, atom, 0)
    total = atoms * fields
    blocks = part_low.shape[0]
    out_ref[0:blocks] = lanes_of(red.at[0], total, blocks)
    out_ref[blocks : 2 * blocks] = lanes_of(red.at[1], total, blocks) + part_low[...] + got_low[...]
    out_ref[2 * blocks : 3 * blocks] = lanes_of(red.at[2], total, blocks) + part_high[...] + got_high[...]


def gather_all(starts, rot, strength, mid, low, high, img, low_img, high_img, parts, got):
    fields, rows, cols = mid.shape
    atoms = img.shape[0]
    blocks = -(-atoms * fields // 128)
    return pl.pallas_call(
        gather_all_kernel,
        out_shape=(
            jax.ShapeDtypeStruct((fields, rows - 2 * EDGE, cols), jnp.float32),
            jax.ShapeDtypeStruct((3 * blocks, 128), jnp.float32),
        ),
        in_specs=[SMEM] * 4 + [VMEM] * 10,
        out_specs=(VMEM,) * 2,
        scratch_shapes=[
            pltpu.VMEM(mid.shape, jnp.float32),
            pltpu.VMEM(mid.shape, jnp.float32),
            pltpu.VMEM((3, atoms * fields, 8, 128), jnp.float32),
        ],
        compiler_params=params(10),
        name="gather_all",
    )(starts, *rot, strength, mid, low, high, img, low_img, high_img, *parts, *got)


def spread_sides(acc, starts_ref, low_coef, high_coef, low_img, high_img):
    atoms = low_img.shape[0]
    for j, coef, img, z in ((1, low_coef, low_img, 1), (2, high_coef, high_img, 0)):
        image = lambda a, part, k, img=img, z=z: img[a, z, part, 8 * k : 8 * k + 8]
        spread_into(acc, lambda a, j=j: starts_ref[j, a], coef, image, atoms)


def spread_all(acc, plane_ref, zsum_ref, starts_ref, coef_ref, images):
    fields = acc.shape[0]
    half = zsum_ref.shape[1]
    atoms = images[0][0].shape[0]
    blocks = coef_ref.shape[0] // 3
    inside = pl.ds(EDGE, half)
    if acc is not plane_ref:
        acc[:, 0:EDGE] = plane_ref[:, 0:EDGE]
        acc[:, EDGE + half :] = plane_ref[:, EDGE + half :]
    acc[:, inside] = plane_ref[:, inside] - 0.5 * zsum_ref[...]

    def atom(a, _):
        line = lax.div(a * fields, 128)
        lane = lax.rem(a * fields, 128)
        for j, (img, z) in enumerate(images):
            begin = pl.multiple_of(starts_ref[j, a], 8)
            for k in range(2):
                at = pl.ds(pl.multiple_of(begin + 8 * k, 8), 8)
                ire = img[a, z, 0, 8 * k : 8 * k + 8]
                iim = img[a, z, 1, 8 * k : 8 * k + 8]
                for n in range(fields // 2):
                    pr = coef_ref[j * blocks + line, lane + 2 * n]
                    pi = coef_ref[j * blocks + line, lane + 2 * n + 1]
                    acc[2 * n, at] = acc[2 * n, at] + (pr * ire + pi * iim)
                    acc[2 * n + 1, at] = acc[2 * n + 1, at] + (pi * ire - pr * iim)
        return 0

    lax.fori_loop(0, atoms, atom, 0)


def occupied_into(store, half, fields, sums_ref, side, own_ref, other_ref, base, scale, block, copies_of, start=None, ahead=0):
    count = own_ref.shape[0]

    def rows_of(b, _):
        at = pl.ds(pl.multiple_of(b * block, 8), block)
        for copy in copies_of(b):
            copy.wait()
        if start is not None:

            @pl.when(b + ahead < half // block)
            def _():
                start(b + ahead)

        def band(m, accs):
            accs = list(accs)
            for row, occ in ((side, own_ref), (1 - side, other_ref)):
                pr, pi = occ[m, 0, at], occ[m, 1, at]
                for n in range(fields // 2):
                    sr = sums_ref[row, m * fields + 2 * n]
                    si = sums_ref[row, m * fields + 2 * n + 1]
                    accs[2 * n] = accs[2 * n] + (pr * sr - pi * si)
                    accs[2 * n + 1] = accs[2 * n + 1] + (pr * si + pi * sr)
            return tuple(accs)

        zero = jnp.zeros((block, 128), jnp.float32)
        accs = lax.fori_loop(0, count, band, (zero,) * fields, unroll=2)
        for f in range(fields):
            store(f, b * block, base(f, b * block, block) + scale * accs[f])
        return 0

    lax.fori_loop(0, half // block, rows_of, 0)


def correlate_into(red, src, offset, half, own_ref, other_ref):
    fields = src.shape[0]
    count = own_ref.shape[0]
    bands = fields // 2

    def pair(g, _):
        def row(i, accs):
            at = rows8(i)
            moved = pl.ds(pl.multiple_of(i * 8 + offset, 8), 8)
            accs = list(accs)
            occ = []
            for ref in (own_ref, other_ref):
                for k in range(2):
                    occ.append((ref[2 * g + k, 0, at], ref[2 * g + k, 1, at]))
            for n in range(bands):
                re, im = src[2 * n, moved], src[2 * n + 1, moved]
                for q, (pr, pi) in enumerate(occ):
                    j = (q * bands + n) * 2
                    accs[j] = accs[j] + (pr * re + pi * im)
                    accs[j + 1] = accs[j + 1] + (pr * im - pi * re)
            return tuple(accs)

        zero = jnp.zeros((8, 128), jnp.float32)
        accs = lax.fori_loop(0, half // 8, row, (zero,) * (8 * bands), unroll=3)
        for q in range(4):
            for j in range(fields):
                red[q // 2, (2 * g + q % 2) * fields + j] = accs[q * fields + j]
        return 0

    lax.fori_loop(0, count // 2, pair, 0)


def dots_into(red_dot, half, fields, pairs):
    bands = fields // 2

    def row(i, accs):
        at = pl.ds(pl.multiple_of(i * 8 + EDGE, 8), 8)
        accs = list(accs)
        for p, (left, right) in enumerate(pairs):
            for n in range(bands):
                value = left[2 * n, at] * right[2 * n, at] + left[2 * n + 1, at] * right[2 * n + 1, at]
                accs[p * bands + n] = accs[p * bands + n] + value
        return tuple(accs)

    zero = jnp.zeros((8, 128), jnp.float32)
    accs = lax.fori_loop(0, half // 8, row, (zero,) * (bands * len(pairs)), unroll=3)
    for j in range(bands * len(pairs)):
        red_dot[j] = accs[j]


def pick_block(half):
    return next(b for b in (24, 16, 8) if half % b == 0)


def shift_rows(start, size):
    return pl.ds(pl.multiple_of(start + EDGE, 8), size)


def band_copies(which_ref, half, block, b, occ_ref, occ_other_ref, own, other, sems):
    begin = pl.multiple_of(which_ref[0] * half + b * block, 8)
    at = pl.ds(pl.multiple_of(b * block, 8), block)
    return (
        pltpu.make_async_copy(occ_ref.at[:, :, pl.ds(begin, block)], own.at[:, :, at], sems.at[0, b]),
        pltpu.make_async_copy(occ_other_ref.at[:, :, at], other.at[:, :, at], sems.at[1, b]),
    )


def start_bands(half, block, copies_of):
    for b in range(half // block):
        for copy in copies_of(b):
            copy.start()


def write_sums(sum_ref, side, red):
    mine, theirs = sum_rows(red[0]), sum_rows(red[1])
    sum_ref[...] = jnp.zeros(sum_ref.shape, jnp.float32)
    sum_ref[0:1] = jnp.where(side == 0, mine, theirs)
    sum_ref[1:2] = jnp.where(side == 0, theirs, mine)


def write_edges(edge_ref, out_ref, half):
    for f in range(out_ref.shape[0]):
        edge_ref[f, 0:EDGE] = out_ref[f, EDGE : 2 * EDGE]
        edge_ref[f, EDGE : 2 * EDGE] = out_ref[f, half : half + EDGE]


def residual_kernel(scale, which_ref, starts_ref, low_coef, high_coef, sums_ref, lap_ref, low_ref, high_ref,
                    occ_ref, occ_other_ref, resp_hbm, pot_hbm, out_ref, edge_ref, sum_ref,
                    acc, own, other, resp, pot, red, red_dot, sems, more_sems):
    fields, wide, cols = out_ref.shape
    half = wide - 2 * EDGE
    side = which_ref[0]
    block = pick_block(half)
    begin = pl.multiple_of(side * half, 8)
    copies = (
        pltpu.make_async_copy(resp_hbm.at[:, :, pl.ds(begin, half)], resp, more_sems.at[0]),
        pltpu.make_async_copy(pot_hbm.at[:, pl.ds(begin, half)], pot, more_sems.at[1]),
    )
    for copy in copies:
        copy.start()
    copies_of = lambda b: band_copies(which_ref, half, block, b, occ_ref, occ_other_ref, own, other, sems)
    start_bands(half, block, copies_of)
    acc[...] = lap_ref[...]
    spread_sides(acc, starts_ref, low_coef, high_coef, low_ref, high_ref)
    for copy in copies:
        copy.wait()

    def base(f, start, size):
        at = pl.ds(pl.multiple_of(start, 8), size)
        re, im = resp[f // 2, 0, at], resp[f // 2, 1, at]
        if f % 2 == 0:
            prod = pot[0, at] * re - pot[1, at] * im
        else:
            prod = pot[0, at] * im + pot[1, at] * re
        return -prod - acc[f, shift_rows(start, size)]

    def store(f, start, value):
        out_ref[f, shift_rows(start, block)] = value

    occupied_into(store, half, fields, sums_ref, side, own, other, base, scale, block, copies_of)
    write_edges(edge_ref, out_ref, half)
    correlate_into(red, out_ref, EDGE, half, own, other)
    dots_into(red_dot, half, fields, [(out_ref, out_ref)])
    write_sums(sum_ref, side, red)
    sum_ref[2:3] = sum_rows(red_dot[0 : fields // 2])


def field_outputs(fields, half, cols):
    return (
        jax.ShapeDtypeStruct((fields, half + 2 * EDGE, cols), jnp.float32),
        jax.ShapeDtypeStruct((fields, 2 * EDGE, cols), jnp.float32),
        jax.ShapeDtypeStruct((8, 128), jnp.float32),
    )


def residual_call(scale, which, starts, low_coef, high_coef, sums, lap, low_img, high_img, psi_occ, other, resp, pot):
    fields, long, cols = lap.shape
    half = long - 2 * EDGE - WIN
    return pl.pallas_call(
        functools.partial(residual_kernel, scale),
        out_shape=field_outputs(fields, half, cols),
        in_specs=[SMEM] * 5 + [VMEM] * 3 + [HBM] * 4,
        out_specs=(VMEM,) * 3,
        scratch_shapes=[
            pltpu.VMEM(lap.shape, jnp.float32),
            pltpu.VMEM(other.shape, jnp.float32),
            pltpu.VMEM(other.shape, jnp.float32),
            pltpu.VMEM(resp.shape[:2] + (half, cols), jnp.float32),
            pltpu.VMEM((2, half, cols), jnp.float32),
            pltpu.VMEM((2, 128, 8, 128), jnp.float32),
            pltpu.VMEM((16, 8, 128), jnp.float32),
            pltpu.SemaphoreType.DMA((2, half // pick_block(half))),
            pltpu.SemaphoreType.DMA((2,)),
        ],
        compiler_params=params(16),
        name="residual",
    )(which, starts, low_coef, high_coef, sums, lap, low_img, high_img, psi_occ, other, resp, pot)


def image_kernel(scale, which_ref, starts_ref, low_coef, high_coef, sums_ref, lap_ref, low_ref, high_ref,
                 res_ref, occ_ref, occ_other_ref, out_ref, edge_ref, sum_ref,
                 acc, own, other, red, red_dot, sems):
    fields, wide, cols = out_ref.shape
    half = wide - 2 * EDGE
    side = which_ref[0]
    block = pick_block(half)
    copies_of = lambda b: band_copies(which_ref, half, block, b, occ_ref, occ_other_ref, own, other, sems)
    start_bands(half, block, copies_of)
    acc[...] = lap_ref[...]
    spread_sides(acc, starts_ref, low_coef, high_coef, low_ref, high_ref)

    def base(f, start, size):
        return acc[f, shift_rows(start, size)]

    def store(f, start, value):
        out_ref[f, shift_rows(start, block)] = value

    occupied_into(store, half, fields, sums_ref, side, own, other, base, scale, block, copies_of)
    write_edges(edge_ref, out_ref, half)
    correlate_into(red, out_ref, EDGE, half, own, other)
    dots_into(red_dot, half, fields, [(res_ref, out_ref), (out_ref, out_ref)])
    write_sums(sum_ref, side, red)
    sum_ref[2:3] = sum_rows(red_dot[0:fields])


def image_call(scale, which, starts, low_coef, high_coef, sums, lap, low_img, high_img, res, psi_occ, other):
    fields, long, cols = lap.shape
    half = long - 2 * EDGE - WIN
    return pl.pallas_call(
        functools.partial(image_kernel, scale),
        out_shape=field_outputs(fields, half, cols),
        in_specs=[SMEM] * 5 + [VMEM] * 4 + [HBM] * 2,
        out_specs=(VMEM,) * 3,
        scratch_shapes=[
            pltpu.VMEM(lap.shape, jnp.float32),
            pltpu.VMEM(other.shape, jnp.float32),
            pltpu.VMEM(other.shape, jnp.float32),
            pltpu.VMEM((2, 128, 8, 128), jnp.float32),
            pltpu.VMEM((16, 8, 128), jnp.float32),
            pltpu.SemaphoreType.DMA((2, half // pick_block(half))),
        ],
        compiler_params=params(16),
        name="image",
    )(which, starts, low_coef, high_coef, sums, lap, low_img, high_img, res, psi_occ, other)


def local_kernel(starts_ref, coef_ref, plane_ref, zsum_ref, img_ref, low_ref, high_ref, field_ref, part_ref,
                 out_ref, sum_ref, red_dot):
    fields = out_ref.shape[0]
    half = zsum_ref.shape[1]
    spread_all(out_ref, plane_ref, zsum_ref, starts_ref, coef_ref, ((img_ref, 1), (low_ref, 1), (high_ref, 0)))
    dots_into(red_dot, half, fields, [(field_ref, out_ref)])
    sum_ref[...] = part_ref[...]
    sum_ref[3:4] = sum_rows(red_dot[0 : fields // 2])


def local_call(starts, local, images, field, part):
    coef, plane, zsum = local
    return pl.pallas_call(
        local_kernel,
        out_shape=(
            jax.ShapeDtypeStruct(plane.shape, jnp.float32),
            jax.ShapeDtypeStruct((8, 128), jnp.float32),
        ),
        in_specs=[SMEM] * 2 + [VMEM] * 7,
        out_specs=(VMEM, VMEM),
        scratch_shapes=[pltpu.VMEM((16, 8, 128), jnp.float32)],
        compiler_params=params(10),
        name="local",
    )(starts, coef, plane, zsum, *images, field, part)


def last_kernel(which_ref, sums_ref, mix_ref, res_hbm, first_hbm, second_hbm, occ_ref, occ_other_ref,
                out_ref, res, first, second, own, other, sems, more_sems):
    fields, half, cols = out_ref.shape
    side = which_ref[0]
    block = pick_block(half)

    def copies_of(b):
        at = pl.ds(pl.multiple_of(b * block, 8), block)
        moved = shift_rows(b * block, block)
        own_copies = tuple(
            pltpu.make_async_copy(src.at[:, moved], dst.at[:, at], more_sems.at[j, b])
            for j, (src, dst) in enumerate(((res_hbm, res), (first_hbm, first), (second_hbm, second)))
        )
        return own_copies + band_copies(which_ref, half, block, b, occ_ref, occ_other_ref, own, other, sems)

    ahead = 2

    def start(b):
        for copy in copies_of(b):
            copy.start()

    for b in range(ahead):
        start(b)

    def base(f, start, size):
        n = f // 2
        at = pl.ds(pl.multiple_of(start, 8), size)
        return res[f, at] + mix_ref[0, n] * first[f, at] + mix_ref[1, n] * second[f, at]

    def store(f, start, value):
        out_ref[f, pl.ds(pl.multiple_of(start, 8), block)] = value

    occupied_into(store, half, fields, sums_ref, side, own, other, base, 1.0, block, copies_of, start, ahead)


def last_call(which, sums, mix, res, first, second, psi_occ, other):
    fields, wide, cols = res.shape
    half = wide - 2 * EDGE
    blocks = half // pick_block(half)
    field = pltpu.VMEM((fields, half, cols), jnp.float32)
    return pl.pallas_call(
        last_kernel,
        out_shape=jax.ShapeDtypeStruct((fields, half, cols), jnp.float32),
        in_specs=[SMEM] * 3 + [HBM] * 5,
        out_specs=VMEM,
        scratch_shapes=[
            field,
            field,
            field,
            pltpu.VMEM(other.shape, jnp.float32),
            pltpu.VMEM(other.shape, jnp.float32),
            pltpu.SemaphoreType.DMA((2, blocks)),
            pltpu.SemaphoreType.DMA((3, blocks)),
        ],
        compiler_params=params(60),
        name="last",
    )(which, sums, mix, res, first, second, psi_occ, other)


def xor_sum(block, bits):
    count = lax.axis_size("space") * lax.axis_size("occ")
    masks = [0]
    for bit in bits:
        masks = masks + [mask | bit for mask in masks]
    parts = [block]
    for mask in masks[1:]:
        parts.append(lax.ppermute(block, ("space", "occ"), [(i, i ^ mask) for i in range(count)]))
    while len(parts) > 1:
        parts = [parts[j] + parts[j + 1] for j in range(0, len(parts), 2)]
    return parts[0]


def total(block, groups=None):
    count = lax.axis_size("space")
    bit = 2
    steps = []
    while count > 1:
        wide = count % 4 == 0
        steps.append((bit, 2 * bit) if wide else (bit,))
        bit, count = (4 * bit, count // 4) if wide else (2 * bit, count // 2)
    steps.append((1,))
    for bits in steps[groups] if groups is not None else steps:
        block = xor_sum(block, bits)
    return block


def exchange(block):
    return lax.ppermute(block, "occ", SWAP)


def from_behind(block, distance):
    count = lax.axis_size("space")
    return lax.ppermute(block, "space", [((i - distance) % count, i) for i in range(count)])


def window_images(x_cell, y_cell, offsets, values, theta_y, rows_y, planes):
    y_raw = y_cell[:, None] + offsets[None, :, 2]
    y_wrap = jnp.floor_divide(y_raw, rows_y)
    y_at = y_raw - y_wrap * rows_y
    angles = theta_y * y_wrap.astype(jnp.float32)
    row = x_cell[:, None] + offsets[None, :, 1] + RAD
    slot = []
    for plane in planes:
        wanted = (row[:, None, :] == jnp.arange(WIN, dtype=jnp.int32)[None, :, None]) & (
            offsets[:, 0] == plane
        )[None, None, :]
        slot.append(wanted)
    slots = jnp.stack(slot, axis=1)
    weights = jnp.stack([values * jnp.cos(angles), values * jnp.sin(angles)], axis=1)
    left = jnp.where(slots[:, :, None], weights[:, None, :, None, :], 0.0)
    atoms = left.shape[0]
    left = left.reshape(atoms, len(planes) * 2 * WIN, -1)
    right = (y_at[:, :, None] == jnp.arange(rows_y, dtype=jnp.int32)[None, None, :]).astype(jnp.float32)
    image = jnp.einsum("apk,aky->apy", left, right, precision=PRECISE)
    return image.reshape(atoms, len(planes), 2, WIN, rows_y)


def shards(
    psi_occ,
    psi_resp,
    initial_guess,
    local_potential,
    potential_change,
    band_energy,
    q_index,
    atom_cells,
    offsets,
    projector,
    strength,
):
    slab_count = lax.axis_size("space")
    slab_index = lax.axis_index("space")
    side = lax.axis_index("occ")
    layers, rows_x, rows_y = local_potential.shape
    half = rows_x // 2
    atoms = atom_cells.shape[0]
    bands = psi_resp.shape[0]
    fields = 2 * bands
    weight = 1.0 / (layers * slab_count * rows_x * rows_y)
    thetas = q_index.astype(jnp.float32) * (2.0 * math.pi / QDIV)
    at_first, at_last = slab_index == 0, slab_index == slab_count - 1
    near_first, near_last = slab_index < 2, slab_index >= slab_count - 2
    flags = (at_first, at_last, near_first, near_last, side == 0, side == 1, None, at_last, at_first)
    signs = (-1.0, 1.0, 1.0, -1.0, -1.0, 1.0, 1.0, -1.0, 1.0)
    axes = (0, 0, 0, 0, 1, 1, 2, 0, 0)
    kind = jnp.arange(16, dtype=jnp.int32)
    angle = jnp.zeros(16, jnp.float32)
    for j, (flag, sign, axis) in enumerate(zip(flags, signs, axes)):
        chosen = kind == j
        if flag is not None:
            chosen = chosen & flag
        angle = jnp.where(chosen, sign * thetas[axis], angle)
    rot = (jnp.cos(angle), jnp.sin(angle))
    which = side.astype(jnp.int32).reshape(1)

    occ = psi_occ.reshape(psi_occ.shape[0], 2, rows_x, rows_y)
    resp = psi_resp.reshape(bands, 2, rows_x, rows_y)
    guess = initial_guess.reshape(bands, 2, rows_x, rows_y)
    change = potential_change.reshape(2, rows_x, rows_y)

    cell_rows = jnp.pad(
        jnp.concatenate([atom_cells.astype(jnp.float32), strength[:, None]], axis=1),
        ((0, 0), (0, projector.shape[1] - 4)),
    )
    packed = jnp.concatenate([projector, cell_rows], axis=0)
    guess_mid, occ_send = prep_call(which, rot, guess, occ, packed)
    occ_other = exchange(occ_send)
    first_sums = total(first_corr(which, occ, resp, change, guess), slice(0, 2))
    first_sums, guess_mid = lax.optimization_barrier((first_sums, guess_mid))
    first_sums = total(first_sums, slice(2, None))
    guess_low = from_behind(guess_mid, 1)
    guess_high = from_behind(guess_mid, -1)

    def unpack(block):
        rows = block[:, half + 2 * EDGE :].reshape(-1, rows_y)
        return rows[:atoms], rows[atoms : 2 * atoms]

    below, below_cells = unpack(guess_low)
    above, above_cells = unpack(guess_high)
    cells = [atom_cells]
    for rows in (below_cells, above_cells):
        cells.append(rows[:, :3].astype(jnp.int32))
    all_x = jnp.stack([c[:, 1] for c in cells])
    all_y = jnp.stack([c[:, 2] for c in cells])
    at_row = jnp.mod(all_x - RAD - side * half + EDGE, rows_x)
    inner = at_row % 8
    touching = at_row < half + EDGE
    put_starts = jnp.where(touching, at_row - inner, half + 2 * EDGE).astype(jnp.int32)
    get_starts = jnp.where(touching, at_row - inner, 0).astype(jnp.int32)
    own_row = jnp.mod(atom_cells[:, 1] - RAD - side * half + EDGE, rows_x)
    own_inner = own_row % 8
    own_starts = jnp.where(own_row < half + EDGE, own_row - own_inner, 0).astype(jnp.int32)
    strengths = jnp.stack([strength, below_cells[:, 3], above_cells[:, 3]])
    img = window_images(own_inner, atom_cells[:, 2], offsets, projector, thetas[2], rows_y, (-1, 0, 1))
    low_img = window_images(inner[1], all_y[1], offsets, below, thetas[2], rows_y, (0, 1))
    high_img = window_images(inner[2], all_y[2], offsets, above, thetas[2], rows_y, (-1, 0))
    images = (img, low_img, high_img)

    def local_part(mid, low, high):
        zsum, proj, up, down = gather(own_starts, rot, strength, mid, low, high, img, half)
        low_coef = from_behind(up, 1)
        high_coef = from_behind(down, -1)
        lap = stencil(which, band_energy, rot, put_starts, proj, mid, zsum, local_potential, img)
        return put_starts, low_coef, high_coef, lap

    def far_part(mid):
        low = from_behind(mid, 1)
        high = from_behind(mid, -1)
        plane, part_low, part_high, down, up = plane_call(
            which, band_energy, get_starts, rot, strengths, mid, local_potential, low_img, high_img
        )
        got = (from_behind(up, 2), from_behind(down, -2))
        zsum, coef = gather_all(get_starts, rot, strengths, mid, low, high, *images, (part_low, part_high), got)
        return coef, plane, zsum

    starts, low_coef, high_coef, lap = local_part(guess_mid, guess_low, guess_high)
    residual, edges, part = residual_call(
        weight, which, starts, low_coef, high_coef, first_sums, lap, low_img, high_img, occ, occ_other, resp, change
    )
    tot = total(part)
    norm0 = tot[2, :bands]
    residual = fill_call(rot, exchange(edges), residual)
    residual_other = exchange(residual)
    starts, low_coef, high_coef, lap = local_part(residual, from_behind(residual, 1), from_behind(residual, -1))
    image, edges, part = image_call(
        SHIFT_WEIGHT * weight, which, starts, low_coef, high_coef, tot, lap, low_img, high_img, residual, occ, occ_other
    )
    image = fill_call(rot, exchange(edges), image)
    image_other = exchange(image)
    image2, part = local_call(put_starts, far_part(image), images, image, part)
    tot = total(part)
    sums = tot[0:2]
    cross = tot[2, :bands]
    square = tot[2, bands : 2 * bands]
    occ_square = jnp.sum((sums * sums).reshape(-1, bands, 2), axis=(0, 2))
    triple = tot[3, :bands] + SHIFT_WEIGHT * weight * occ_square
    step0 = norm0 / cross
    norm1 = norm0 - 2.0 * step0 * cross + step0 * step0 * square
    growth = norm1 / norm0
    lead = 1.0 + growth
    curvature = lead * lead * cross - 2.0 * lead * step0 * square + step0 * step0 * triple
    step1 = norm1 / curvature
    mix0 = -step0 - step1 * lead
    mix1 = step1 * step0
    per_lane = jnp.tile(jnp.repeat(mix1, 2), sums.shape[1] // fields)
    last_sums = SHIFT_WEIGHT * weight * sums * per_lane[None, :]
    mine = last_call(which, last_sums, jnp.stack([mix0, mix1]), residual, image, image2, occ, occ_other)
    theirs = exchange(mine)

    def join(own_half, other_half):
        lower = jnp.where(side == 0, own_half, other_half)
        upper = jnp.where(side == 0, other_half, own_half)
        return jnp.concatenate([lower, upper], axis=1).reshape(bands, 2, 1, rows_x, rows_y)

    inside = lambda v: v[:, EDGE : EDGE + half]
    wide = lambda v: v[:, None, None, None, None]
    response = (
        initial_guess
        + wide(step0 + step1 * lead) * join(inside(residual), inside(residual_other))
        - wide(step0 * step1) * join(inside(image), inside(image_other))
    )
    return response, join(mine, theirs)


def solution(mesh):
    return jax.shard_map(
        shards,
        mesh=mesh,
        in_specs=(
            P("occ", None, "space", None, None),
            P("resp", None, "space", None, None),
            P("resp", None, "space", None, None),
            P("space", None, None),
            P(None, "space", None, None),
            P("resp"),
            P(),
            P("space", None),
            P(),
            P("space", None),
            P("space"),
        ),
        out_specs=(P("resp", None, "space", None, None), P("resp", None, "space", None, None)),
        check_vma=False,
    )
```

```python
import functools
import math

import jax
import jax.numpy as jnp
from jax import lax
from jax.experimental import pallas as pl
from jax.experimental.pallas import tpu as pltpu
from jax.sharding import PartitionSpec as P

RAD = 4
QDIV = 8
EDGE = 8
WIN = 16
SHIFT_WEIGHT = 3.0
PRECISE = lax.Precision.HIGHEST
SWAP = [(0, 1), (1, 0)]

VMEM = pl.BlockSpec(memory_space=pltpu.VMEM)
SMEM = pl.BlockSpec(memory_space=pltpu.SMEM)
ANY = pl.BlockSpec(memory_space=pl.ANY)
HBM = pl.BlockSpec(memory_space=pltpu.HBM)


def params(mib):
    return pltpu.CompilerParams(vmem_limit_bytes=mib * 1024 * 1024)


def sum_rows(values):
    total = jnp.sum(values, axis=2, keepdims=True)
    row = lax.broadcasted_iota(jnp.int32, values.shape, 0)
    lane = lax.broadcasted_iota(jnp.int32, values.shape, 2)
    picked = jnp.sum(jnp.where(row == lane, total, 0.0), axis=0)
    return jnp.sum(picked, axis=0, keepdims=True)


def rows8(index):
    return pl.ds(pl.multiple_of(index * 8, 8), 8)


def extra_rows(count, fields):
    return -(-count // (8 * fields)) * 8


AXES = (0, 0, 0, 0, 1, 1, 2, 0, 0)
SIGNS = (-1, 1, 1, -1, -1, 1, 1, -1, 1)
TURNS = [2.0 * math.pi * k / QDIV for k in range(QDIV)]


def prep_kernel(slab_count, where_ref, q_ref, guess_ref, atoms_ref, out_ref, cos_ref, sin_ref, middle, low, high, sems):
    fields = out_ref.shape[0]
    half = middle.shape[2]
    wide = half + 2 * EDGE
    side, slab = where_ref[0], where_ref[1]
    begin = pl.multiple_of(side * half, 8)
    away = pl.multiple_of((1 - side) * half, 8)
    under = pl.multiple_of((1 - side) * half + half - EDGE, 8)
    copies = []
    for j, (start, size, dst) in enumerate(((begin, half, middle), (under, EDGE, low), (away, EDGE, high))):
        copies.append(pltpu.make_async_copy(guess_ref.at[:, :, pl.ds(start, size)], dst, sems.at[j]))
    for copy in copies:
        copy.start()

    first, last = slab == 0, slab == slab_count - 1
    flags = (first, last, slab < 2, slab >= slab_count - 2, side == 0, side == 1, slab >= 0, last, first)
    for j, (flag, sign, axis) in enumerate(zip(flags, SIGNS, AXES)):
        step = jnp.where(flag, jnp.bitwise_and(sign * q_ref[axis], QDIV - 1), 0)
        cosine, sine = jnp.float32(1.0), jnp.float32(0.0)
        for k in range(1, QDIV):
            cosine = jnp.where(step == k, jnp.float32(math.cos(TURNS[k])), cosine)
            sine = jnp.where(step == k, jnp.float32(math.sin(TURNS[k])), sine)
        cos_ref[j] = cosine
        sin_ref[j] = sine

    for f in range(fields):
        for r in range(0, out_ref.shape[1] - wide, 8):
            at = f * (out_ref.shape[1] - wide) + r
            if at < atoms_ref.shape[0]:
                out_ref[f, wide + r : wide + r + 8] = atoms_ref[at : at + 8]
            else:
                out_ref[f, wide + r : wide + r + 8] = jnp.zeros((8, 128), jnp.float32)
    for copy in copies:
        copy.wait()
    for n in range(fields // 2):
        for k in range(2):
            out_ref[2 * n + k, EDGE : EDGE + half] = middle[n, k]
        for src, spot, j in ((low, 0, 4), (high, EDGE + half, 5)):
            c, s = cos_ref[j], sin_ref[j]
            re, im = src[n, 0], src[n, 1]
            out_ref[2 * n, spot : spot + EDGE] = re * c - im * s
            out_ref[2 * n + 1, spot : spot + EDGE] = re * s + im * c


def prep_call(slab_count, where, q_index, guess, atoms):
    bands, _, rows, cols = guess.shape
    half = rows // 2
    extra = extra_rows(atoms.shape[0], 2 * bands)
    table = jax.ShapeDtypeStruct((len(AXES),), jnp.float32)
    return pl.pallas_call(
        functools.partial(prep_kernel, slab_count),
        out_shape=(
            jax.ShapeDtypeStruct((2 * bands, half + 2 * EDGE + extra, cols), jnp.float32),
            table,
            table,
        ),
        in_specs=[SMEM, SMEM, HBM, VMEM],
        out_specs=(VMEM, SMEM, SMEM),
        scratch_shapes=[
            pltpu.VMEM((bands, 2, half, cols), jnp.float32),
            pltpu.VMEM((bands, 2, EDGE, cols), jnp.float32),
            pltpu.VMEM((bands, 2, EDGE, cols), jnp.float32),
            pltpu.SemaphoreType.DMA((3,)),
        ],
        compiler_params=params(8),
        name="prep",
    )(where, q_index, guess, atoms)


def fill_kernel(cos_ref, sin_ref, got_ref, ext_ref, out_ref, low, high, sems):
    fields, wide, _ = out_ref.shape
    for n in range(fields // 2):
        for dst, at, j in ((low, EDGE, 4), (high, 0, 5)):
            c, s = cos_ref[j], sin_ref[j]
            re, im = got_ref[2 * n, at : at + EDGE], got_ref[2 * n + 1, at : at + EDGE]
            dst[2 * n] = re * c - im * s
            dst[2 * n + 1] = re * s + im * c
    one = pltpu.make_async_copy(low, out_ref.at[:, 0:EDGE], sems.at[0])
    two = pltpu.make_async_copy(high, out_ref.at[:, wide - EDGE : wide], sems.at[1])
    one.start()
    two.start()
    one.wait()
    two.wait()


def fill_call(rot, got, ext):
    shape = (ext.shape[0], EDGE, ext.shape[2])
    return pl.pallas_call(
        fill_kernel,
        out_shape=jax.ShapeDtypeStruct(ext.shape, jnp.float32),
        in_specs=[SMEM, SMEM, VMEM, ANY],
        out_specs=ANY,
        scratch_shapes=[
            pltpu.VMEM(shape, jnp.float32),
            pltpu.VMEM(shape, jnp.float32),
            pltpu.SemaphoreType.DMA((2,)),
        ],
        input_output_aliases={3: 0},
        compiler_params=params(4),
        name="fill",
    )(*rot, got, ext)


def first_corr_kernel(which_ref, occ_ref, resp_ref, pot_ref, guess_ref, out_ref, send_a, send_b, mixed, red):
    bands, _, rows, _ = resp_ref.shape
    group = occ_ref.shape[0]
    step = pl.program_id(0)
    half = send_a.shape[2]
    middle = pl.num_programs(0) // 2
    away = pl.ds(pl.multiple_of((1 - which_ref[0]) * half, 8), half)

    @pl.when(step < middle)
    def _():
        send_a[...] = occ_ref[:, :, away]

    @pl.when(step >= middle)
    def _():
        send_b[...] = occ_ref[:, :, away]

    @pl.when(step == 0)
    def _():
        for n in range(bands):
            re = resp_ref[n, 0]
            im = resp_ref[n, 1]
            mixed[2 * n] = pot_ref[0] * re - pot_ref[1] * im - SHIFT_WEIGHT * guess_ref[n, 0]
            mixed[2 * n + 1] = pot_ref[0] * im + pot_ref[1] * re - SHIFT_WEIGHT * guess_ref[n, 1]

    def row(i, accs):
        at = rows8(i)
        occ = [(occ_ref[k, 0, at], occ_ref[k, 1, at]) for k in range(group)]
        accs = list(accs)
        for n in range(bands):
            re, im = mixed[2 * n, at], mixed[2 * n + 1, at]
            for k, (pr, pi) in enumerate(occ):
                j = (k * bands + n) * 2
                accs[j] = accs[j] + (pr * re + pi * im)
                accs[j + 1] = accs[j + 1] + (pr * im - pi * re)
        return tuple(accs)

    zero = jnp.zeros((8, 128), jnp.float32)
    count = 2 * bands * group
    accs = lax.fori_loop(0, rows // 8, row, (zero,) * count, unroll=3)
    for j in range(count):
        red[step * count + j] = accs[j]

    @pl.when(step == pl.num_programs(0) - 1)
    def _():
        out_ref[...] = jnp.zeros(out_ref.shape, jnp.float32)
        total = sum_rows(red[...])
        side = which_ref[0]
        out_ref[0:1] = jnp.where(side == 0, total, 0.0)
        out_ref[1:2] = jnp.where(side == 0, 0.0, total)


def first_corr(which, psi_occ, psi_resp, pot, guess):
    group = 4
    count, _, rows, cols = psi_occ.shape
    fixed = lambda shape: pl.BlockSpec(shape, lambda i: (0,) * len(shape))
    middle = count // group // 2
    send = jax.ShapeDtypeStruct((count // 2, 2, rows // 2, cols), jnp.float32)
    shape = (group, 2, rows // 2, cols)
    return pl.pallas_call(
        first_corr_kernel,
        out_shape=(
            jax.ShapeDtypeStruct((8, 128), jnp.float32),
            send,
            send,
        ),
        grid=(count // group,),
        in_specs=[
            SMEM,
            pl.BlockSpec((group, 2, rows, cols), lambda i: (i, 0, 0, 0)),
            fixed(psi_resp.shape),
            fixed(pot.shape),
            fixed(guess.shape),
        ],
        out_specs=(
            fixed((8, 128)),
            pl.BlockSpec(shape, lambda i: (jnp.minimum(i, middle - 1), 0, 0, 0)),
            pl.BlockSpec(shape, lambda i: (jnp.maximum(i - middle, 0), 0, 0, 0)),
        ),
        scratch_shapes=[
            pltpu.VMEM((psi_resp.shape[0] * 2, rows, cols), jnp.float32),
            pltpu.VMEM((128, 8, 128), jnp.float32),
        ],
        compiler_params=params(60),
        name="first_corr",
    )(which, psi_occ, psi_resp, pot, guess)


def gather_kernel(start_ref, cos_ref, sin_ref, str_ref, mid_ref, low_ref, high_ref, img_ref,
                  zsum_ref, out_ref, up_ref, down_ref, low, high, red):
    fields = mid_ref.shape[0]
    half = zsum_ref.shape[1]
    wide = half + 2 * EDGE
    for n in range(fields // 2):
        for src, dst, j in ((low_ref, low, 0), (high_ref, high, 1)):
            c, s = cos_ref[j], sin_ref[j]
            re, im = src[2 * n, 0:wide], src[2 * n + 1, 0:wide]
            dst[2 * n] = re * c - im * s
            dst[2 * n + 1] = re * s + im * c
        for k in range(2):
            f = 2 * n + k
            zsum_ref[f] = low[f, EDGE : EDGE + half] + high[f, EDGE : EDGE + half]
    atoms = img_ref.shape[0]

    def atom(a, _):
        begin = pl.multiple_of(start_ref[a], 8)
        accs = [jnp.zeros((8, 128), jnp.float32)] * fields
        for z, src in enumerate((low, mid_ref, high)):
            for k in range(2):
                at = pl.ds(pl.multiple_of(begin + 8 * k, 8), 8)
                ire = img_ref[a, z, 0, 8 * k : 8 * k + 8]
                iim = img_ref[a, z, 1, 8 * k : 8 * k + 8]
                for n in range(fields // 2):
                    re, im = src[2 * n, at], src[2 * n + 1, at]
                    accs[2 * n] = accs[2 * n] + (re * ire - im * iim)
                    accs[2 * n + 1] = accs[2 * n + 1] + (re * iim + im * ire)
        for f in range(fields):
            red[a * fields + f] = accs[f] * str_ref[a]
        return 0

    lax.fori_loop(0, atoms, atom, 0)
    total = atoms * fields
    value = lanes_of(red, total, out_ref.shape[0])
    out_ref[...] = value
    up_ref[...] = turn_lanes(value, cos_ref[7], sin_ref[7])
    down_ref[...] = turn_lanes(value, cos_ref[8], sin_ref[8])


def gather(starts, rot, strength, mid, low, high, img, half):
    fields, _, cols = mid.shape
    rows = half + 2 * EDGE
    atoms = img.shape[0]
    blocks = -(-atoms * fields // 128)
    coef = jax.ShapeDtypeStruct((blocks, 128), jnp.float32)
    return pl.pallas_call(
        gather_kernel,
        out_shape=(
            jax.ShapeDtypeStruct((fields, rows - 2 * EDGE, cols), jnp.float32),
            coef,
            coef,
            coef,
        ),
        in_specs=[SMEM] * 4 + [VMEM] * 4,
        out_specs=(VMEM,) * 4,
        scratch_shapes=[
            pltpu.VMEM((fields, rows, cols), jnp.float32),
            pltpu.VMEM((fields, rows, cols), jnp.float32),
            pltpu.VMEM((atoms * fields, 8, 128), jnp.float32),
        ],
        compiler_params=params(10),
        name="gather",
    )(starts, *rot, strength, mid, low, high, img)


def spread_into(acc, start_of, coef_ref, image_of, atoms):
    fields = acc.shape[0]

    def atom(a, _):
        begin = pl.multiple_of(start_of(a), 8)
        line = lax.div(a * fields, 128)
        lane = lax.rem(a * fields, 128)
        for k in range(2):
            at = pl.ds(pl.multiple_of(begin + 8 * k, 8), 8)
            ire = image_of(a, 0, k)
            iim = image_of(a, 1, k)
            for n in range(fields // 2):
                pr = coef_ref[line, lane + 2 * n]
                pi = coef_ref[line, lane + 2 * n + 1]
                acc[2 * n, at] = acc[2 * n, at] + (pr * ire + pi * iim)
                acc[2 * n + 1, at] = acc[2 * n + 1, at] + (pi * ire - pr * iim)
        return 0

    lax.fori_loop(0, atoms, atom, 0)


def stencil_kernel(which_ref, energy_ref, cos_ref, sin_ref, starts_ref, coef_ref, mid_ref, zsum_ref, pot_ref, img_ref, out_ref):
    fields, half, cols = zsum_ref.shape
    lane = lax.broadcasted_iota(jnp.int32, (half, cols), 1)
    first, last = lane == 0, lane == cols - 1
    c, s = cos_ref[6], sin_ref[6]
    pot = pot_ref[0, pl.ds(pl.multiple_of(which_ref[0] * half, 8), half)] + 3.0
    for n in range(fields // 2):
        re = mid_ref[2 * n, EDGE : EDGE + half]
        im = mid_ref[2 * n + 1, EDGE : EDGE + half]
        re_next, im_next = pltpu.roll(re, cols - 1, 1), pltpu.roll(im, cols - 1, 1)
        re_prev, im_prev = pltpu.roll(re, 1, 1), pltpu.roll(im, 1, 1)
        y_re = jnp.where(last, re_next * c - im_next * s, re_next) + jnp.where(
            first, re_prev * c + im_prev * s, re_prev
        )
        y_im = jnp.where(last, re_next * s + im_next * c, im_next) + jnp.where(
            first, im_prev * c - re_prev * s, im_prev
        )
        scale = pot - energy_ref[n]
        for f, value, beside in ((2 * n, re, y_re), (2 * n + 1, im, y_im)):
            beside = beside + zsum_ref[f]
            beside = beside + mid_ref[f, EDGE - 1 : EDGE - 1 + half]
            beside = beside + mid_ref[f, EDGE + 1 : EDGE + 1 + half]
            out_ref[f, EDGE : EDGE + half] = scale * value - 0.5 * beside
            out_ref[f, 0:EDGE] = jnp.zeros((EDGE, cols), jnp.float32)
            out_ref[f, EDGE + half :] = jnp.zeros((EDGE + WIN, cols), jnp.float32)
    atoms = img_ref.shape[0]
    image = lambda a, part, k: img_ref[a, 1, part, 8 * k : 8 * k + 8]
    spread_into(out_ref, lambda a: starts_ref[0, a], coef_ref, image, atoms)


def stencil(which, energy, rot, starts, coef, mid, zsum, pot, img):
    fields, half, cols = zsum.shape
    return pl.pallas_call(
        stencil_kernel,
        out_shape=jax.ShapeDtypeStruct((fields, half + 2 * EDGE + WIN, cols), jnp.float32),
        in_specs=[SMEM] * 6 + [VMEM] * 4,
        out_specs=VMEM,
        compiler_params=params(10),
        name="stencil",
    )(which, energy, *rot, starts, coef, mid, zsum, pot, img)


def project(src, begin, image_of, accs):
    accs = list(accs)
    for k in range(2):
        at = pl.ds(pl.multiple_of(begin + 8 * k, 8), 8)
        ire, iim = image_of(0, k), image_of(1, k)
        for n in range(len(accs) // 2):
            re, im = src[2 * n, at], src[2 * n + 1, at]
            accs[2 * n] = accs[2 * n] + (re * ire - im * iim)
            accs[2 * n + 1] = accs[2 * n + 1] + (re * iim + im * ire)
    return accs


def lanes_of(red, total, blocks):
    return jnp.concatenate([sum_rows(red[128 * b : min(total, 128 * b + 128)]) for b in range(blocks)], axis=0)


def turn_lanes(value, cosine, sine_part):
    even = lax.broadcasted_iota(jnp.int32, value.shape, 1) % 2 == 0
    times_i = jnp.where(even, -pltpu.roll(value, 127, 1), pltpu.roll(value, 1, 1))
    return value * cosine + times_i * sine_part


def plane_kernel(which_ref, energy_ref, starts_ref, cos_ref, sin_ref, str_ref, mid_ref, pot_ref, low_img, high_img,
                 out_ref, low_ref, high_ref, down_ref, up_ref, red):
    fields, wide, cols = mid_ref.shape
    half = wide - 2 * EDGE
    atoms = low_img.shape[0]
    total = atoms * fields

    def atom(a, _):
        for j, img, z in ((1, low_img, 1), (2, high_img, 0)):
            begin = starts_ref[j, a]
            image = lambda part, k: img[a, z, part, 8 * k : 8 * k + 8]
            accs = project(mid_ref, begin, image, [jnp.zeros((8, 128), jnp.float32)] * fields)
            for f in range(fields):
                red[j - 1, a * fields + f] = accs[f] * str_ref[j, a]
        return 0

    lax.fori_loop(0, atoms, atom, 0)
    blocks = low_ref.shape[0]
    low = lanes_of(red.at[0], total, blocks)
    high = lanes_of(red.at[1], total, blocks)
    low_ref[...] = low
    high_ref[...] = high
    down_ref[...] = turn_lanes(low, cos_ref[2], sin_ref[2])
    up_ref[...] = turn_lanes(high, cos_ref[3], sin_ref[3])

    lane = lax.broadcasted_iota(jnp.int32, (half, cols), 1)
    first, last = lane == 0, lane == cols - 1
    c, s = cos_ref[6], sin_ref[6]
    pot = pot_ref[0, pl.ds(pl.multiple_of(which_ref[0] * half, 8), half)] + 3.0
    for n in range(fields // 2):
        re = mid_ref[2 * n, EDGE : EDGE + half]
        im = mid_ref[2 * n + 1, EDGE : EDGE + half]
        re_next, im_next = pltpu.roll(re, cols - 1, 1), pltpu.roll(im, cols - 1, 1)
        re_prev, im_prev = pltpu.roll(re, 1, 1), pltpu.roll(im, 1, 1)
        y_re = jnp.where(last, re_next * c - im_next * s, re_next) + jnp.where(
            first, re_prev * c + im_prev * s, re_prev
        )
        y_im = jnp.where(last, re_next * s + im_next * c, im_next) + jnp.where(
            first, im_prev * c - re_prev * s, im_prev
        )
        scale = pot - energy_ref[n]
        for f, value, beside in ((2 * n, re, y_re), (2 * n + 1, im, y_im)):
            beside = beside + mid_ref[f, EDGE - 1 : EDGE - 1 + half]
            beside = beside + mid_ref[f, EDGE + 1 : EDGE + 1 + half]
            out_ref[f, EDGE : EDGE + half] = scale * value - 0.5 * beside
            out_ref[f, 0:EDGE] = jnp.zeros((EDGE, cols), jnp.float32)
            out_ref[f, EDGE + half :] = jnp.zeros((EDGE + WIN, cols), jnp.float32)


def plane_call(which, energy, starts, rot, strength, mid, pot, low_img, high_img):
    fields, wide, cols = mid.shape
    atoms = low_img.shape[0]
    blocks = -(-atoms * fields // 128)
    coef = jax.ShapeDtypeStruct((blocks, 128), jnp.float32)
    return pl.pallas_call(
        plane_kernel,
        out_shape=(jax.ShapeDtypeStruct((fields, wide + WIN, cols), jnp.float32), coef, coef, coef, coef),
        in_specs=[SMEM] * 6 + [VMEM] * 4,
        out_specs=(VMEM,) * 5,
        scratch_shapes=[pltpu.VMEM((2, atoms * fields, 8, 128), jnp.float32)],
        compiler_params=params(10),
        name="plane",
    )(which, energy, starts, *rot, strength, mid, pot, low_img, high_img)


def gather_all_kernel(starts_ref, cos_ref, sin_ref, str_ref, mid_ref, low_ref, high_ref, img_ref, low_img, high_img,
                  part_low, part_high, got_low, got_high, zsum_ref, out_ref, low, high, red):
    fields = mid_ref.shape[0]
    half = zsum_ref.shape[1]
    wide = half + 2 * EDGE
    for n in range(fields // 2):
        for src, dst, j in ((low_ref, low, 0), (high_ref, high, 1)):
            c, s = cos_ref[j], sin_ref[j]
            re, im = src[2 * n, 0:wide], src[2 * n + 1, 0:wide]
            dst[2 * n] = re * c - im * s
            dst[2 * n + 1] = re * s + im * c
        for k in range(2):
            f = 2 * n + k
            zsum_ref[f] = low[f, EDGE : EDGE + half] + high[f, EDGE : EDGE + half]
    atoms = img_ref.shape[0]
    groups = (
        (0, ((low, img_ref, 0), (mid_ref, img_ref, 1), (high, img_ref, 2))),
        (1, ((low, low_img, 0),)),
        (2, ((high, high_img, 1),)),
    )

    def atom(a, _):
        for j, planes in groups:
            begin = starts_ref[j, a]
            accs = [jnp.zeros((8, 128), jnp.float32)] * fields
            for src, img, z in planes:
                image = lambda part, k, img=img, z=z: img[a, z, part, 8 * k : 8 * k + 8]
                accs = project(src, begin, image, accs)
            for f in range(fields):
                red[j, a * fields + f] = accs[f] * str_ref[j, a]
        return 0

    lax.fori_loop(0, atoms, atom, 0)
    total = atoms * fields
    blocks = part_low.shape[0]
    out_ref[0:blocks] = lanes_of(red.at[0], total, blocks)
    out_ref[blocks : 2 * blocks] = lanes_of(red.at[1], total, blocks) + part_low[...] + got_low[...]
    out_ref[2 * blocks : 3 * blocks] = lanes_of(red.at[2], total, blocks) + part_high[...] + got_high[...]


def gather_all(starts, rot, strength, mid, low, high, img, low_img, high_img, parts, got):
    fields, rows, cols = mid.shape
    atoms = img.shape[0]
    blocks = -(-atoms * fields // 128)
    return pl.pallas_call(
        gather_all_kernel,
        out_shape=(
            jax.ShapeDtypeStruct((fields, rows - 2 * EDGE, cols), jnp.float32),
            jax.ShapeDtypeStruct((3 * blocks, 128), jnp.float32),
        ),
        in_specs=[SMEM] * 4 + [VMEM] * 10,
        out_specs=(VMEM,) * 2,
        scratch_shapes=[
            pltpu.VMEM(mid.shape, jnp.float32),
            pltpu.VMEM(mid.shape, jnp.float32),
            pltpu.VMEM((3, atoms * fields, 8, 128), jnp.float32),
        ],
        compiler_params=params(10),
        name="gather_all",
    )(starts, *rot, strength, mid, low, high, img, low_img, high_img, *parts, *got)


def spread_sides(acc, starts_ref, low_coef, high_coef, low_img, high_img):
    atoms = low_img.shape[0]
    for j, coef, img, z in ((1, low_coef, low_img, 1), (2, high_coef, high_img, 0)):
        image = lambda a, part, k, img=img, z=z: img[a, z, part, 8 * k : 8 * k + 8]
        spread_into(acc, lambda a, j=j: starts_ref[j, a], coef, image, atoms)


def spread_all(acc, plane_ref, zsum_ref, starts_ref, coef_ref, images):
    fields = acc.shape[0]
    half = zsum_ref.shape[1]
    atoms = images[0][0].shape[0]
    blocks = coef_ref.shape[0] // 3
    inside = pl.ds(EDGE, half)
    if acc is not plane_ref:
        acc[:, 0:EDGE] = plane_ref[:, 0:EDGE]
        acc[:, EDGE + half :] = plane_ref[:, EDGE + half :]
    acc[:, inside] = plane_ref[:, inside] - 0.5 * zsum_ref[...]

    def atom(a, _):
        line = lax.div(a * fields, 128)
        lane = lax.rem(a * fields, 128)
        for j, (img, z) in enumerate(images):
            begin = pl.multiple_of(starts_ref[j, a], 8)
            for k in range(2):
                at = pl.ds(pl.multiple_of(begin + 8 * k, 8), 8)
                ire = img[a, z, 0, 8 * k : 8 * k + 8]
                iim = img[a, z, 1, 8 * k : 8 * k + 8]
                for n in range(fields // 2):
                    pr = coef_ref[j * blocks + line, lane + 2 * n]
                    pi = coef_ref[j * blocks + line, lane + 2 * n + 1]
                    acc[2 * n, at] = acc[2 * n, at] + (pr * ire + pi * iim)
                    acc[2 * n + 1, at] = acc[2 * n + 1, at] + (pi * ire - pr * iim)
        return 0

    lax.fori_loop(0, atoms, atom, 0)


def occupied_into(store, half, fields, sums_ref, side, own_ref, other_ref, base, scale, block, copies_of, start=None, ahead=0):
    count = own_ref.shape[0]

    def rows_of(b, _):
        at = pl.ds(pl.multiple_of(b * block, 8), block)
        for copy in copies_of(b):
            copy.wait()
        if start is not None:

            @pl.when(b + ahead < half // block)
            def _():
                start(b + ahead)

        def band(m, accs):
            accs = list(accs)
            for row, occ in ((side, own_ref), (1 - side, other_ref)):
                pr, pi = occ[m, 0, at], occ[m, 1, at]
                for n in range(fields // 2):
                    sr = sums_ref[row, m * fields + 2 * n]
                    si = sums_ref[row, m * fields + 2 * n + 1]
                    accs[2 * n] = accs[2 * n] + (pr * sr - pi * si)
                    accs[2 * n + 1] = accs[2 * n + 1] + (pr * si + pi * sr)
            return tuple(accs)

        zero = jnp.zeros((block, 128), jnp.float32)
        accs = lax.fori_loop(0, count, band, (zero,) * fields, unroll=2)
        for f in range(fields):
            store(f, b * block, base(f, b * block, block) + scale * accs[f])
        return 0

    lax.fori_loop(0, half // block, rows_of, 0)


def correlate_into(red, src, offset, half, own_ref, other_ref):
    fields = src.shape[0]
    count = own_ref.shape[0]
    bands = fields // 2

    def pair(g, _):
        def row(i, accs):
            at = rows8(i)
            moved = pl.ds(pl.multiple_of(i * 8 + offset, 8), 8)
            accs = list(accs)
            occ = []
            for ref in (own_ref, other_ref):
                for k in range(2):
                    occ.append((ref[2 * g + k, 0, at], ref[2 * g + k, 1, at]))
            for n in range(bands):
                re, im = src[2 * n, moved], src[2 * n + 1, moved]
                for q, (pr, pi) in enumerate(occ):
                    j = (q * bands + n) * 2
                    accs[j] = accs[j] + (pr * re + pi * im)
                    accs[j + 1] = accs[j + 1] + (pr * im - pi * re)
            return tuple(accs)

        zero = jnp.zeros((8, 128), jnp.float32)
        accs = lax.fori_loop(0, half // 8, row, (zero,) * (8 * bands), unroll=3)
        for q in range(4):
            for j in range(fields):
                red[q // 2, (2 * g + q % 2) * fields + j] = accs[q * fields + j]
        return 0

    lax.fori_loop(0, count // 2, pair, 0)


def dots_into(red_dot, half, fields, pairs):
    bands = fields // 2

    def row(i, accs):
        at = pl.ds(pl.multiple_of(i * 8 + EDGE, 8), 8)
        accs = list(accs)
        for p, (left, right) in enumerate(pairs):
            for n in range(bands):
                value = left[2 * n, at] * right[2 * n, at] + left[2 * n + 1, at] * right[2 * n + 1, at]
                accs[p * bands + n] = accs[p * bands + n] + value
        return tuple(accs)

    zero = jnp.zeros((8, 128), jnp.float32)
    accs = lax.fori_loop(0, half // 8, row, (zero,) * (bands * len(pairs)), unroll=3)
    for j in range(bands * len(pairs)):
        red_dot[j] = accs[j]


def pick_block(half):
    return next(b for b in (24, 16, 8) if half % b == 0)


def shift_rows(start, size):
    return pl.ds(pl.multiple_of(start + EDGE, 8), size)


def band_copies(which_ref, half, block, b, occ_ref, other_refs, own, other, sems):
    begin = pl.multiple_of(which_ref[0] * half + b * block, 8)
    at = pl.ds(pl.multiple_of(b * block, 8), block)
    copies = [pltpu.make_async_copy(occ_ref.at[:, :, pl.ds(begin, block)], own.at[:, :, at], sems.at[0, b])]
    first = 0
    for j, ref in enumerate(other_refs):
        last = first + ref.shape[0]
        copies.append(pltpu.make_async_copy(ref.at[:, :, at], other.at[first:last, :, at], sems.at[1 + j, b]))
        first = last
    return tuple(copies)


def start_bands(half, block, copies_of):
    for b in range(half // block):
        for copy in copies_of(b):
            copy.start()


def write_sums(sum_ref, side, red):
    mine, theirs = sum_rows(red[0]), sum_rows(red[1])
    sum_ref[...] = jnp.zeros(sum_ref.shape, jnp.float32)
    sum_ref[0:1] = jnp.where(side == 0, mine, theirs)
    sum_ref[1:2] = jnp.where(side == 0, theirs, mine)


def write_edges(edge_ref, out_ref, half):
    for f in range(out_ref.shape[0]):
        edge_ref[f, 0:EDGE] = out_ref[f, EDGE : 2 * EDGE]
        edge_ref[f, EDGE : 2 * EDGE] = out_ref[f, half : half + EDGE]


def residual_kernel(scale, which_ref, starts_ref, low_coef, high_coef, sums_ref, lap_ref, low_ref, high_ref,
                    occ_ref, other_a, other_b, resp_hbm, pot_hbm, out_ref, edge_ref, sum_ref,
                    acc, own, other, resp, pot, red, red_dot, sems, more_sems):
    fields, wide, cols = out_ref.shape
    half = wide - 2 * EDGE
    side = which_ref[0]
    block = pick_block(half)
    begin = pl.multiple_of(side * half, 8)
    copies = (
        pltpu.make_async_copy(resp_hbm.at[:, :, pl.ds(begin, half)], resp, more_sems.at[0]),
        pltpu.make_async_copy(pot_hbm.at[:, pl.ds(begin, half)], pot, more_sems.at[1]),
    )
    for copy in copies:
        copy.start()
    copies_of = lambda b: band_copies(which_ref, half, block, b, occ_ref, (other_a, other_b), own, other, sems)
    start_bands(half, block, copies_of)
    acc[...] = lap_ref[...]
    spread_sides(acc, starts_ref, low_coef, high_coef, low_ref, high_ref)
    for copy in copies:
        copy.wait()

    def base(f, start, size):
        at = pl.ds(pl.multiple_of(start, 8), size)
        re, im = resp[f // 2, 0, at], resp[f // 2, 1, at]
        if f % 2 == 0:
            prod = pot[0, at] * re - pot[1, at] * im
        else:
            prod = pot[0, at] * im + pot[1, at] * re
        return -prod - acc[f, shift_rows(start, size)]

    def store(f, start, value):
        out_ref[f, shift_rows(start, block)] = value

    occupied_into(store, half, fields, sums_ref, side, own, other, base, scale, block, copies_of)
    write_edges(edge_ref, out_ref, half)
    correlate_into(red, out_ref, EDGE, half, own, other)
    dots_into(red_dot, half, fields, [(out_ref, out_ref)])
    write_sums(sum_ref, side, red)
    sum_ref[2:3] = sum_rows(red_dot[0 : fields // 2])


def field_outputs(fields, half, cols):
    return (
        jax.ShapeDtypeStruct((fields, half + 2 * EDGE, cols), jnp.float32),
        jax.ShapeDtypeStruct((fields, 2 * EDGE, cols), jnp.float32),
        jax.ShapeDtypeStruct((8, 128), jnp.float32),
    )


def residual_call(scale, which, starts, low_coef, high_coef, sums, lap, low_img, high_img, psi_occ, other, resp, pot):
    fields, long, cols = lap.shape
    half = long - 2 * EDGE - WIN
    return pl.pallas_call(
        functools.partial(residual_kernel, scale),
        out_shape=field_outputs(fields, half, cols),
        in_specs=[SMEM] * 5 + [VMEM] * 3 + [HBM] * 5,
        out_specs=(VMEM,) * 3,
        scratch_shapes=[
            pltpu.VMEM(lap.shape, jnp.float32),
            pltpu.VMEM(psi_occ.shape[:2] + (half, cols), jnp.float32),
            pltpu.VMEM(psi_occ.shape[:2] + (half, cols), jnp.float32),
            pltpu.VMEM(resp.shape[:2] + (half, cols), jnp.float32),
            pltpu.VMEM((2, half, cols), jnp.float32),
            pltpu.VMEM((2, 128, 8, 128), jnp.float32),
            pltpu.VMEM((16, 8, 128), jnp.float32),
            pltpu.SemaphoreType.DMA((3, half // pick_block(half))),
            pltpu.SemaphoreType.DMA((2,)),
        ],
        compiler_params=params(16),
        name="residual",
    )(which, starts, low_coef, high_coef, sums, lap, low_img, high_img, psi_occ, *other, resp, pot)


def image_kernel(scale, which_ref, starts_ref, low_coef, high_coef, sums_ref, lap_ref, low_ref, high_ref,
                 res_ref, occ_ref, other_a, other_b, out_ref, edge_ref, sum_ref,
                 acc, own, other, red, red_dot, sems):
    fields, wide, cols = out_ref.shape
    half = wide - 2 * EDGE
    side = which_ref[0]
    block = pick_block(half)
    copies_of = lambda b: band_copies(which_ref, half, block, b, occ_ref, (other_a, other_b), own, other, sems)
    start_bands(half, block, copies_of)
    acc[...] = lap_ref[...]
    spread_sides(acc, starts_ref, low_coef, high_coef, low_ref, high_ref)

    def base(f, start, size):
        return acc[f, shift_rows(start, size)]

    def store(f, start, value):
        out_ref[f, shift_rows(start, block)] = value

    occupied_into(store, half, fields, sums_ref, side, own, other, base, scale, block, copies_of)
    write_edges(edge_ref, out_ref, half)
    correlate_into(red, out_ref, EDGE, half, own, other)
    dots_into(red_dot, half, fields, [(res_ref, out_ref), (out_ref, out_ref)])
    write_sums(sum_ref, side, red)
    sum_ref[2:3] = sum_rows(red_dot[0:fields])


def image_call(scale, which, starts, low_coef, high_coef, sums, lap, low_img, high_img, res, psi_occ, other):
    fields, long, cols = lap.shape
    half = long - 2 * EDGE - WIN
    return pl.pallas_call(
        functools.partial(image_kernel, scale),
        out_shape=field_outputs(fields, half, cols),
        in_specs=[SMEM] * 5 + [VMEM] * 4 + [HBM] * 3,
        out_specs=(VMEM,) * 3,
        scratch_shapes=[
            pltpu.VMEM(lap.shape, jnp.float32),
            pltpu.VMEM(psi_occ.shape[:2] + (half, cols), jnp.float32),
            pltpu.VMEM(psi_occ.shape[:2] + (half, cols), jnp.float32),
            pltpu.VMEM((2, 128, 8, 128), jnp.float32),
            pltpu.VMEM((16, 8, 128), jnp.float32),
            pltpu.SemaphoreType.DMA((3, half // pick_block(half))),
        ],
        compiler_params=params(16),
        name="image",
    )(which, starts, low_coef, high_coef, sums, lap, low_img, high_img, res, psi_occ, *other)


def local_kernel(starts_ref, coef_ref, plane_ref, zsum_ref, img_ref, low_ref, high_ref, field_ref, part_ref,
                 out_ref, sum_ref, red_dot):
    fields = out_ref.shape[0]
    half = zsum_ref.shape[1]
    spread_all(out_ref, plane_ref, zsum_ref, starts_ref, coef_ref, ((img_ref, 1), (low_ref, 1), (high_ref, 0)))
    dots_into(red_dot, half, fields, [(field_ref, out_ref)])
    sum_ref[...] = part_ref[...]
    sum_ref[3:4] = sum_rows(red_dot[0 : fields // 2])


def local_call(starts, local, images, field, part):
    coef, plane, zsum = local
    return pl.pallas_call(
        local_kernel,
        out_shape=(
            jax.ShapeDtypeStruct(plane.shape, jnp.float32),
            jax.ShapeDtypeStruct((8, 128), jnp.float32),
        ),
        in_specs=[SMEM] * 2 + [VMEM] * 7,
        out_specs=(VMEM, VMEM),
        scratch_shapes=[pltpu.VMEM((16, 8, 128), jnp.float32)],
        compiler_params=params(10),
        name="local",
    )(starts, coef, plane, zsum, *images, field, part)


def last_kernel(which_ref, sums_ref, mix_ref, res_hbm, first_hbm, second_hbm, occ_ref, other_a, other_b,
                out_ref, res, first, second, own, other, sems, more_sems):
    fields, half, cols = out_ref.shape
    side = which_ref[0]
    block = pick_block(half)

    def copies_of(b):
        at = pl.ds(pl.multiple_of(b * block, 8), block)
        moved = shift_rows(b * block, block)
        own_copies = tuple(
            pltpu.make_async_copy(src.at[:, moved], dst.at[:, at], more_sems.at[j, b])
            for j, (src, dst) in enumerate(((res_hbm, res), (first_hbm, first), (second_hbm, second)))
        )
        return own_copies + band_copies(which_ref, half, block, b, occ_ref, (other_a, other_b), own, other, sems)

    ahead = 2

    def start(b):
        for copy in copies_of(b):
            copy.start()

    for b in range(ahead):
        start(b)

    def base(f, start, size):
        n = f // 2
        at = pl.ds(pl.multiple_of(start, 8), size)
        return res[f, at] + mix_ref[0, n] * first[f, at] + mix_ref[1, n] * second[f, at]

    def store(f, start, value):
        out_ref[f, pl.ds(pl.multiple_of(start, 8), block)] = value

    occupied_into(store, half, fields, sums_ref, side, own, other, base, 1.0, block, copies_of, start, ahead)


def last_call(which, sums, mix, res, first, second, psi_occ, other):
    fields, wide, cols = res.shape
    half = wide - 2 * EDGE
    blocks = half // pick_block(half)
    field = pltpu.VMEM((fields, half, cols), jnp.float32)
    return pl.pallas_call(
        last_kernel,
        out_shape=jax.ShapeDtypeStruct((fields, half, cols), jnp.float32),
        in_specs=[SMEM] * 3 + [HBM] * 6,
        out_specs=VMEM,
        scratch_shapes=[
            field,
            field,
            field,
            pltpu.VMEM(psi_occ.shape[:2] + (half, cols), jnp.float32),
            pltpu.VMEM(psi_occ.shape[:2] + (half, cols), jnp.float32),
            pltpu.SemaphoreType.DMA((3, blocks)),
            pltpu.SemaphoreType.DMA((3, blocks)),
        ],
        compiler_params=params(52),
        name="last",
    )(which, sums, mix, res, first, second, psi_occ, *other)


def xor_sum(block, bits):
    count = lax.axis_size("space") * lax.axis_size("occ")
    masks = [0]
    for bit in bits:
        masks = masks + [mask | bit for mask in masks]
    parts = [block]
    for mask in masks[1:]:
        parts.append(lax.ppermute(block, ("space", "occ"), [(i, i ^ mask) for i in range(count)]))
    while len(parts) > 1:
        parts = [parts[j] + parts[j + 1] for j in range(0, len(parts), 2)]
    return parts[0]


def total(block, groups=None):
    count = lax.axis_size("space")
    bit = 2
    steps = []
    while count > 1:
        wide = count % 4 == 0
        steps.append((bit, 2 * bit) if wide else (bit,))
        bit, count = (4 * bit, count // 4) if wide else (2 * bit, count // 2)
    steps.append((1,))
    for bits in steps[groups] if groups is not None else steps:
        block = xor_sum(block, bits)
    return block


def exchange(block):
    return lax.ppermute(block, "occ", SWAP)


def from_behind(block, distance):
    count = lax.axis_size("space")
    return lax.ppermute(block, "space", [((i - distance) % count, i) for i in range(count)])


def window_images(x_cell, y_cell, offsets, values, theta_y, rows_y, planes):
    y_raw = y_cell[:, None] + offsets[None, :, 2]
    y_wrap = jnp.floor_divide(y_raw, rows_y)
    y_at = y_raw - y_wrap * rows_y
    angles = theta_y * y_wrap.astype(jnp.float32)
    row = x_cell[:, None] + offsets[None, :, 1] + RAD
    slot = []
    for plane in planes:
        wanted = (row[:, None, :] == jnp.arange(WIN, dtype=jnp.int32)[None, :, None]) & (
            offsets[:, 0] == plane
        )[None, None, :]
        slot.append(wanted)
    slots = jnp.stack(slot, axis=1)
    weights = jnp.stack([values * jnp.cos(angles), values * jnp.sin(angles)], axis=1)
    left = jnp.where(slots[:, :, None], weights[:, None, :, None, :], 0.0)
    atoms = left.shape[0]
    left = left.reshape(atoms, len(planes) * 2 * WIN, -1)
    right = (y_at[:, :, None] == jnp.arange(rows_y, dtype=jnp.int32)[None, None, :]).astype(jnp.float32)
    image = jnp.einsum("apk,aky->apy", left, right, precision=PRECISE)
    return image.reshape(atoms, len(planes), 2, WIN, rows_y)


def shards(
    psi_occ,
    psi_resp,
    initial_guess,
    local_potential,
    potential_change,
    band_energy,
    q_index,
    atom_cells,
    offsets,
    projector,
    strength,
):
    slab_count = lax.axis_size("space")
    slab_index = lax.axis_index("space")
    side = lax.axis_index("occ")
    layers, rows_x, rows_y = local_potential.shape
    half = rows_x // 2
    atoms = atom_cells.shape[0]
    bands = psi_resp.shape[0]
    fields = 2 * bands
    weight = 1.0 / (layers * slab_count * rows_x * rows_y)
    thetas = q_index.astype(jnp.float32) * (2.0 * math.pi / QDIV)
    which = side.astype(jnp.int32).reshape(1)
    where = jnp.stack([side, slab_index]).astype(jnp.int32)

    occ = psi_occ.reshape(psi_occ.shape[0], 2, rows_x, rows_y)
    resp = psi_resp.reshape(bands, 2, rows_x, rows_y)
    guess = initial_guess.reshape(bands, 2, rows_x, rows_y)
    change = potential_change.reshape(2, rows_x, rows_y)

    cell_rows = jnp.pad(
        jnp.concatenate([atom_cells.astype(jnp.float32), strength[:, None]], axis=1),
        ((0, 0), (0, projector.shape[1] - 4)),
    )
    packed = jnp.concatenate([projector, cell_rows], axis=0)
    guess_mid, *rot = prep_call(slab_count, where, q_index, guess, packed)
    first_sums, *occ_send = first_corr(which, occ, resp, change, guess)
    first_sums = total(first_sums, slice(-1, None))
    first_sums, occ_send = lax.optimization_barrier((first_sums, occ_send))
    occ_other = [exchange(block) for block in occ_send]
    first_sums = total(first_sums, slice(0, 2))
    first_sums, guess_mid, occ_other[0] = lax.optimization_barrier((first_sums, guess_mid, occ_other[0]))
    first_sums = total(first_sums, slice(2, -1))
    guess_low = from_behind(guess_mid, 1)
    guess_high = from_behind(guess_mid, -1)

    def unpack(block):
        rows = block[:, half + 2 * EDGE :].reshape(-1, rows_y)
        return rows[:atoms], rows[atoms : 2 * atoms]

    below, below_cells = unpack(guess_low)
    above, above_cells = unpack(guess_high)
    cells = [atom_cells]
    for rows in (below_cells, above_cells):
        cells.append(rows[:, :3].astype(jnp.int32))
    all_x = jnp.stack([c[:, 1] for c in cells])
    all_y = jnp.stack([c[:, 2] for c in cells])
    at_row = jnp.mod(all_x - RAD - side * half + EDGE, rows_x)
    inner = at_row % 8
    touching = at_row < half + EDGE
    put_starts = jnp.where(touching, at_row - inner, half + 2 * EDGE).astype(jnp.int32)
    get_starts = jnp.where(touching, at_row - inner, 0).astype(jnp.int32)
    own_row = jnp.mod(atom_cells[:, 1] - RAD - side * half + EDGE, rows_x)
    own_inner = own_row % 8
    own_starts = jnp.where(own_row < half + EDGE, own_row - own_inner, 0).astype(jnp.int32)
    strengths = jnp.stack([strength, below_cells[:, 3], above_cells[:, 3]])
    img = window_images(own_inner, atom_cells[:, 2], offsets, projector, thetas[2], rows_y, (-1, 0, 1))
    low_img = window_images(inner[1], all_y[1], offsets, below, thetas[2], rows_y, (0, 1))
    high_img = window_images(inner[2], all_y[2], offsets, above, thetas[2], rows_y, (-1, 0))
    images = (img, low_img, high_img)

    def local_part(mid, low, high):
        zsum, proj, up, down = gather(own_starts, rot, strength, mid, low, high, img, half)
        low_coef = from_behind(up, 1)
        high_coef = from_behind(down, -1)
        lap = stencil(which, band_energy, rot, put_starts, proj, mid, zsum, local_potential, img)
        return put_starts, low_coef, high_coef, lap

    def far_part(mid):
        low = from_behind(mid, 1)
        high = from_behind(mid, -1)
        plane, part_low, part_high, down, up = plane_call(
            which, band_energy, get_starts, rot, strengths, mid, local_potential, low_img, high_img
        )
        got = (from_behind(up, 2), from_behind(down, -2))
        zsum, coef = gather_all(get_starts, rot, strengths, mid, low, high, *images, (part_low, part_high), got)
        return coef, plane, zsum

    starts, low_coef, high_coef, lap = local_part(guess_mid, guess_low, guess_high)
    residual, edges, part = residual_call(
        weight, which, starts, low_coef, high_coef, first_sums, lap, low_img, high_img, occ, occ_other, resp, change
    )
    tot = total(part)
    norm0 = tot[2, :bands]
    residual = fill_call(rot, exchange(edges), residual)
    starts, low_coef, high_coef, lap = local_part(residual, from_behind(residual, 1), from_behind(residual, -1))
    image, edges, part = image_call(
        SHIFT_WEIGHT * weight, which, starts, low_coef, high_coef, tot, lap, low_img, high_img, residual, occ, occ_other
    )
    image = fill_call(rot, exchange(edges), image)
    image_other = exchange(image)
    image2, part = local_call(put_starts, far_part(image), images, image, part)
    part, image_other, residual_send = lax.optimization_barrier((part, image_other, residual))
    residual_other = exchange(residual_send)
    tot = total(part, slice(0, 2))
    tot, residual_other = lax.optimization_barrier((tot, residual_other))
    tot = total(tot, slice(2, None))
    sums = tot[0:2]
    cross = tot[2, :bands]
    square = tot[2, bands : 2 * bands]
    occ_square = jnp.sum((sums * sums).reshape(-1, bands, 2), axis=(0, 2))
    triple = tot[3, :bands] + SHIFT_WEIGHT * weight * occ_square
    step0 = norm0 / cross
    norm1 = norm0 - 2.0 * step0 * cross + step0 * step0 * square
    growth = norm1 / norm0
    lead = 1.0 + growth
    curvature = lead * lead * cross - 2.0 * lead * step0 * square + step0 * step0 * triple
    step1 = norm1 / curvature
    mix0 = -step0 - step1 * lead
    mix1 = step1 * step0
    per_lane = jnp.tile(jnp.repeat(mix1, 2), sums.shape[1] // fields)
    last_sums = SHIFT_WEIGHT * weight * sums * per_lane[None, :]
    mine = last_call(which, last_sums, jnp.stack([mix0, mix1]), residual, image, image2, occ, occ_other)
    mine, residual_other, image_other = lax.optimization_barrier((mine, residual_other, image_other))
    theirs = exchange(mine)

    def join(own_half, other_half):
        lower = jnp.where(side == 0, own_half, other_half)
        upper = jnp.where(side == 0, other_half, own_half)
        return jnp.concatenate([lower, upper], axis=1).reshape(bands, 2, 1, rows_x, rows_y)

    inside = lambda v: v[:, EDGE : EDGE + half]
    wide = lambda v: v[:, None, None, None, None]
    response = (
        initial_guess
        + wide(step0 + step1 * lead) * join(inside(residual), inside(residual_other))
        - wide(step0 * step1) * join(inside(image), inside(image_other))
    )
    return response, join(mine, theirs)


def solution(mesh):
    return jax.shard_map(
        shards,
        mesh=mesh,
        in_specs=(
            P("occ", None, "space", None, None),
            P("resp", None, "space", None, None),
            P("resp", None, "space", None, None),
            P("space", None, None),
            P(None, "space", None, None),
            P("resp"),
            P(),
            P("space", None),
            P(),
            P("space", None),
            P("space"),
        ),
        out_specs=(P("resp", None, "space", None, None), P("resp", None, "space", None, None)),
        check_vma=False,
    )
```

```python
import functools
import math

import jax
import jax.numpy as jnp
from jax import lax
from jax.experimental import pallas as pl
from jax.experimental.pallas import tpu as pltpu
from jax.sharding import PartitionSpec as P

RAD = 4
QDIV = 8
EDGE = 8
WIN = 16
SHIFT_WEIGHT = 3.0
PRECISE = lax.Precision.HIGHEST
SWAP = [(0, 1), (1, 0)]

VMEM = pl.BlockSpec(memory_space=pltpu.VMEM)
SMEM = pl.BlockSpec(memory_space=pltpu.SMEM)
ANY = pl.BlockSpec(memory_space=pl.ANY)
HBM = pl.BlockSpec(memory_space=pltpu.HBM)


def params(mib):
    return pltpu.CompilerParams(vmem_limit_bytes=mib * 1024 * 1024)


def sum_rows(values):
    total = jnp.sum(values, axis=2, keepdims=True)
    row = lax.broadcasted_iota(jnp.int32, values.shape, 0)
    lane = lax.broadcasted_iota(jnp.int32, values.shape, 2)
    picked = jnp.sum(jnp.where(row == lane, total, 0.0), axis=0)
    return jnp.sum(picked, axis=0, keepdims=True)


def rows8(index):
    return pl.ds(pl.multiple_of(index * 8, 8), 8)


def extra_rows(count, fields):
    return -(-count // (8 * fields)) * 8


AXES = (0, 0, 0, 0, 1, 1, 2, 0, 0)
SIGNS = (-1, 1, 1, -1, -1, 1, 1, -1, 1)
TURNS = [2.0 * math.pi * k / QDIV for k in range(QDIV)]


def prep_kernel(slab_count, where_ref, q_ref, guess_ref, atoms_ref, out_ref, cos_ref, sin_ref, middle, low, high, sems):
    fields = out_ref.shape[0]
    half = middle.shape[2]
    wide = half + 2 * EDGE
    side, slab = where_ref[0], where_ref[1]
    begin = pl.multiple_of(side * half, 8)
    away = pl.multiple_of((1 - side) * half, 8)
    under = pl.multiple_of((1 - side) * half + half - EDGE, 8)
    copies = []
    for j, (start, size, dst) in enumerate(((begin, half, middle), (under, EDGE, low), (away, EDGE, high))):
        copies.append(pltpu.make_async_copy(guess_ref.at[:, :, pl.ds(start, size)], dst, sems.at[j]))
    for copy in copies:
        copy.start()

    first, last = slab == 0, slab == slab_count - 1
    flags = (first, last, slab < 2, slab >= slab_count - 2, side == 0, side == 1, slab >= 0, last, first)
    for j, (flag, sign, axis) in enumerate(zip(flags, SIGNS, AXES)):
        step = jnp.where(flag, jnp.bitwise_and(sign * q_ref[axis], QDIV - 1), 0)
        cosine, sine = jnp.float32(1.0), jnp.float32(0.0)
        for k in range(1, QDIV):
            cosine = jnp.where(step == k, jnp.float32(math.cos(TURNS[k])), cosine)
            sine = jnp.where(step == k, jnp.float32(math.sin(TURNS[k])), sine)
        cos_ref[j] = cosine
        sin_ref[j] = sine

    for f in range(fields):
        for r in range(0, out_ref.shape[1] - wide, 8):
            at = f * (out_ref.shape[1] - wide) + r
            if at < atoms_ref.shape[0]:
                out_ref[f, wide + r : wide + r + 8] = atoms_ref[at : at + 8]
            else:
                out_ref[f, wide + r : wide + r + 8] = jnp.zeros((8, 128), jnp.float32)
    for copy in copies:
        copy.wait()
    for n in range(fields // 2):
        for k in range(2):
            out_ref[2 * n + k, EDGE : EDGE + half] = middle[n, k]
        for src, spot, j in ((low, 0, 4), (high, EDGE + half, 5)):
            c, s = cos_ref[j], sin_ref[j]
            re, im = src[n, 0], src[n, 1]
            out_ref[2 * n, spot : spot + EDGE] = re * c - im * s
            out_ref[2 * n + 1, spot : spot + EDGE] = re * s + im * c


def prep_call(slab_count, where, q_index, guess, atoms):
    bands, _, rows, cols = guess.shape
    half = rows // 2
    extra = extra_rows(atoms.shape[0], 2 * bands)
    table = jax.ShapeDtypeStruct((len(AXES),), jnp.float32)
    return pl.pallas_call(
        functools.partial(prep_kernel, slab_count),
        out_shape=(
            jax.ShapeDtypeStruct((2 * bands, half + 2 * EDGE + extra, cols), jnp.float32),
            table,
            table,
        ),
        in_specs=[SMEM, SMEM, HBM, VMEM],
        out_specs=(VMEM, SMEM, SMEM),
        scratch_shapes=[
            pltpu.VMEM((bands, 2, half, cols), jnp.float32),
            pltpu.VMEM((bands, 2, EDGE, cols), jnp.float32),
            pltpu.VMEM((bands, 2, EDGE, cols), jnp.float32),
            pltpu.SemaphoreType.DMA((3,)),
        ],
        compiler_params=params(8),
        name="prep",
    )(where, q_index, guess, atoms)


def fill_kernel(cos_ref, sin_ref, got_ref, ext_ref, out_ref, low, high, sems):
    fields, wide, _ = out_ref.shape
    for n in range(fields // 2):
        for dst, at, j in ((low, EDGE, 4), (high, 0, 5)):
            c, s = cos_ref[j], sin_ref[j]
            re, im = got_ref[2 * n, at : at + EDGE], got_ref[2 * n + 1, at : at + EDGE]
            dst[2 * n] = re * c - im * s
            dst[2 * n + 1] = re * s + im * c
    one = pltpu.make_async_copy(low, out_ref.at[:, 0:EDGE], sems.at[0])
    two = pltpu.make_async_copy(high, out_ref.at[:, wide - EDGE : wide], sems.at[1])
    one.start()
    two.start()
    one.wait()
    two.wait()


def fill_call(rot, got, ext):
    shape = (ext.shape[0], EDGE, ext.shape[2])
    return pl.pallas_call(
        fill_kernel,
        out_shape=jax.ShapeDtypeStruct(ext.shape, jnp.float32),
        in_specs=[SMEM, SMEM, VMEM, ANY],
        out_specs=ANY,
        scratch_shapes=[
            pltpu.VMEM(shape, jnp.float32),
            pltpu.VMEM(shape, jnp.float32),
            pltpu.SemaphoreType.DMA((2,)),
        ],
        input_output_aliases={3: 0},
        compiler_params=params(4),
        name="fill",
    )(*rot, got, ext)


def first_corr_kernel(which_ref, occ_ref, resp_ref, pot_ref, guess_ref, out_ref, send_a, send_b, mixed, red):
    bands, _, rows, _ = resp_ref.shape
    group = occ_ref.shape[0]
    step = pl.program_id(0)
    half = send_a.shape[2]
    middle = pl.num_programs(0) // 2
    away = pl.ds(pl.multiple_of((1 - which_ref[0]) * half, 8), half)

    @pl.when(step < middle)
    def _():
        send_a[...] = occ_ref[:, :, away]

    @pl.when(step >= middle)
    def _():
        send_b[...] = occ_ref[:, :, away]

    @pl.when(step == 0)
    def _():
        for n in range(bands):
            re = resp_ref[n, 0]
            im = resp_ref[n, 1]
            mixed[2 * n] = pot_ref[0] * re - pot_ref[1] * im - SHIFT_WEIGHT * guess_ref[n, 0]
            mixed[2 * n + 1] = pot_ref[0] * im + pot_ref[1] * re - SHIFT_WEIGHT * guess_ref[n, 1]

    def row(i, accs):
        at = rows8(i)
        occ = [(occ_ref[k, 0, at], occ_ref[k, 1, at]) for k in range(group)]
        accs = list(accs)
        for n in range(bands):
            re, im = mixed[2 * n, at], mixed[2 * n + 1, at]
            for k, (pr, pi) in enumerate(occ):
                j = (k * bands + n) * 2
                accs[j] = accs[j] + (pr * re + pi * im)
                accs[j + 1] = accs[j + 1] + (pr * im - pi * re)
        return tuple(accs)

    zero = jnp.zeros((8, 128), jnp.float32)
    count = 2 * bands * group
    accs = lax.fori_loop(0, rows // 8, row, (zero,) * count, unroll=3)
    for j in range(count):
        red[step * count + j] = accs[j]

    @pl.when(step == pl.num_programs(0) - 1)
    def _():
        out_ref[...] = jnp.zeros(out_ref.shape, jnp.float32)
        total = sum_rows(red[...])
        side = which_ref[0]
        out_ref[0:1] = jnp.where(side == 0, total, 0.0)
        out_ref[1:2] = jnp.where(side == 0, 0.0, total)


def first_corr(which, psi_occ, psi_resp, pot, guess):
    group = 4
    count, _, rows, cols = psi_occ.shape
    fixed = lambda shape: pl.BlockSpec(shape, lambda i: (0,) * len(shape))
    middle = count // group // 2
    send = jax.ShapeDtypeStruct((count // 2, 2, rows // 2, cols), jnp.float32)
    shape = (group, 2, rows // 2, cols)
    return pl.pallas_call(
        first_corr_kernel,
        out_shape=(
            jax.ShapeDtypeStruct((8, 128), jnp.float32),
            send,
            send,
        ),
        grid=(count // group,),
        in_specs=[
            SMEM,
            pl.BlockSpec((group, 2, rows, cols), lambda i: (i, 0, 0, 0)),
            fixed(psi_resp.shape),
            fixed(pot.shape),
            fixed(guess.shape),
        ],
        out_specs=(
            fixed((8, 128)),
            pl.BlockSpec(shape, lambda i: (jnp.minimum(i, middle - 1), 0, 0, 0)),
            pl.BlockSpec(shape, lambda i: (jnp.maximum(i - middle, 0), 0, 0, 0)),
        ),
        scratch_shapes=[
            pltpu.VMEM((psi_resp.shape[0] * 2, rows, cols), jnp.float32),
            pltpu.VMEM((128, 8, 128), jnp.float32),
        ],
        compiler_params=params(60),
        name="first_corr",
    )(which, psi_occ, psi_resp, pot, guess)


def gather_kernel(start_ref, cos_ref, sin_ref, str_ref, mid_ref, low_ref, high_ref, img_ref,
                  zsum_ref, out_ref, up_ref, down_ref, low, high, red):
    fields = mid_ref.shape[0]
    half = zsum_ref.shape[1]
    wide = half + 2 * EDGE
    for n in range(fields // 2):
        for src, dst, j in ((low_ref, low, 0), (high_ref, high, 1)):
            c, s = cos_ref[j], sin_ref[j]
            re, im = src[2 * n, 0:wide], src[2 * n + 1, 0:wide]
            dst[2 * n] = re * c - im * s
            dst[2 * n + 1] = re * s + im * c
        for k in range(2):
            f = 2 * n + k
            zsum_ref[f] = low[f, EDGE : EDGE + half] + high[f, EDGE : EDGE + half]
    atoms = img_ref.shape[0]

    def atom(a, _):
        begin = pl.multiple_of(start_ref[a], 8)
        accs = [jnp.zeros((8, 128), jnp.float32)] * fields
        for z, src in enumerate((low, mid_ref, high)):
            for k in range(2):
                at = pl.ds(pl.multiple_of(begin + 8 * k, 8), 8)
                ire = img_ref[a, z, 0, 8 * k : 8 * k + 8]
                iim = img_ref[a, z, 1, 8 * k : 8 * k + 8]
                for n in range(fields // 2):
                    re, im = src[2 * n, at], src[2 * n + 1, at]
                    accs[2 * n] = accs[2 * n] + (re * ire - im * iim)
                    accs[2 * n + 1] = accs[2 * n + 1] + (re * iim + im * ire)
        for f in range(fields):
            red[a * fields + f] = accs[f] * str_ref[a]
        return 0

    lax.fori_loop(0, atoms, atom, 0)
    total = atoms * fields
    value = lanes_of(red, total, out_ref.shape[0])
    out_ref[...] = value
    up_ref[...] = turn_lanes(value, cos_ref[7], sin_ref[7])
    down_ref[...] = turn_lanes(value, cos_ref[8], sin_ref[8])


def gather(starts, rot, strength, mid, low, high, img, half):
    fields, _, cols = mid.shape
    rows = half + 2 * EDGE
    atoms = img.shape[0]
    blocks = -(-atoms * fields // 128)
    coef = jax.ShapeDtypeStruct((blocks, 128), jnp.float32)
    return pl.pallas_call(
        gather_kernel,
        out_shape=(
            jax.ShapeDtypeStruct((fields, rows - 2 * EDGE, cols), jnp.float32),
            coef,
            coef,
            coef,
        ),
        in_specs=[SMEM] * 4 + [VMEM] * 4,
        out_specs=(VMEM,) * 4,
        scratch_shapes=[
            pltpu.VMEM((fields, rows, cols), jnp.float32),
            pltpu.VMEM((fields, rows, cols), jnp.float32),
            pltpu.VMEM((atoms * fields, 8, 128), jnp.float32),
        ],
        compiler_params=params(10),
        name="gather",
    )(starts, *rot, strength, mid, low, high, img)


def spread_into(acc, start_of, coef_ref, image_of, atoms):
    fields = acc.shape[0]

    def atom(a, _):
        begin = pl.multiple_of(start_of(a), 8)
        line = lax.div(a * fields, 128)
        lane = lax.rem(a * fields, 128)
        for k in range(2):
            at = pl.ds(pl.multiple_of(begin + 8 * k, 8), 8)
            ire = image_of(a, 0, k)
            iim = image_of(a, 1, k)
            for n in range(fields // 2):
                pr = coef_ref[line, lane + 2 * n]
                pi = coef_ref[line, lane + 2 * n + 1]
                acc[2 * n, at] = acc[2 * n, at] + (pr * ire + pi * iim)
                acc[2 * n + 1, at] = acc[2 * n + 1, at] + (pi * ire - pr * iim)
        return 0

    lax.fori_loop(0, atoms, atom, 0)


def stencil_kernel(which_ref, energy_ref, cos_ref, sin_ref, starts_ref, coef_ref, mid_ref, zsum_ref, pot_ref, img_ref, out_ref):
    fields, half, cols = zsum_ref.shape
    lane = lax.broadcasted_iota(jnp.int32, (half, cols), 1)
    first, last = lane == 0, lane == cols - 1
    c, s = cos_ref[6], sin_ref[6]
    pot = pot_ref[0, pl.ds(pl.multiple_of(which_ref[0] * half, 8), half)] + 3.0
    for n in range(fields // 2):
        re = mid_ref[2 * n, EDGE : EDGE + half]
        im = mid_ref[2 * n + 1, EDGE : EDGE + half]
        re_next, im_next = pltpu.roll(re, cols - 1, 1), pltpu.roll(im, cols - 1, 1)
        re_prev, im_prev = pltpu.roll(re, 1, 1), pltpu.roll(im, 1, 1)
        y_re = jnp.where(last, re_next * c - im_next * s, re_next) + jnp.where(
            first, re_prev * c + im_prev * s, re_prev
        )
        y_im = jnp.where(last, re_next * s + im_next * c, im_next) + jnp.where(
            first, im_prev * c - re_prev * s, im_prev
        )
        scale = pot - energy_ref[n]
        for f, value, beside in ((2 * n, re, y_re), (2 * n + 1, im, y_im)):
            beside = beside + zsum_ref[f]
            beside = beside + mid_ref[f, EDGE - 1 : EDGE - 1 + half]
            beside = beside + mid_ref[f, EDGE + 1 : EDGE + 1 + half]
            out_ref[f, EDGE : EDGE + half] = scale * value - 0.5 * beside
            out_ref[f, 0:EDGE] = jnp.zeros((EDGE, cols), jnp.float32)
            out_ref[f, EDGE + half :] = jnp.zeros((EDGE + WIN, cols), jnp.float32)
    atoms = img_ref.shape[0]
    image = lambda a, part, k: img_ref[a, 1, part, 8 * k : 8 * k + 8]
    spread_into(out_ref, lambda a: starts_ref[0, a], coef_ref, image, atoms)


def stencil(which, energy, rot, starts, coef, mid, zsum, pot, img):
    fields, half, cols = zsum.shape
    return pl.pallas_call(
        stencil_kernel,
        out_shape=jax.ShapeDtypeStruct((fields, half + 2 * EDGE + WIN, cols), jnp.float32),
        in_specs=[SMEM] * 6 + [VMEM] * 4,
        out_specs=VMEM,
        compiler_params=params(10),
        name="stencil",
    )(which, energy, *rot, starts, coef, mid, zsum, pot, img)


def project(src, begin, image_of, accs):
    accs = list(accs)
    for k in range(2):
        at = pl.ds(pl.multiple_of(begin + 8 * k, 8), 8)
        ire, iim = image_of(0, k), image_of(1, k)
        for n in range(len(accs) // 2):
            re, im = src[2 * n, at], src[2 * n + 1, at]
            accs[2 * n] = accs[2 * n] + (re * ire - im * iim)
            accs[2 * n + 1] = accs[2 * n + 1] + (re * iim + im * ire)
    return accs


def lanes_of(red, total, blocks):
    return jnp.concatenate([sum_rows(red[128 * b : min(total, 128 * b + 128)]) for b in range(blocks)], axis=0)


def turn_lanes(value, cosine, sine_part):
    even = lax.broadcasted_iota(jnp.int32, value.shape, 1) % 2 == 0
    times_i = jnp.where(even, -pltpu.roll(value, 127, 1), pltpu.roll(value, 1, 1))
    return value * cosine + times_i * sine_part


def plane_kernel(which_ref, energy_ref, starts_ref, cos_ref, sin_ref, str_ref, mid_ref, pot_ref, low_img, high_img,
                 out_ref, low_ref, high_ref, down_ref, up_ref, red):
    fields, wide, cols = mid_ref.shape
    half = wide - 2 * EDGE
    atoms = low_img.shape[0]
    total = atoms * fields

    def atom(a, _):
        for j, img, z in ((1, low_img, 1), (2, high_img, 0)):
            begin = starts_ref[j, a]
            image = lambda part, k: img[a, z, part, 8 * k : 8 * k + 8]
            accs = project(mid_ref, begin, image, [jnp.zeros((8, 128), jnp.float32)] * fields)
            for f in range(fields):
                red[j - 1, a * fields + f] = accs[f] * str_ref[j, a]
        return 0

    lax.fori_loop(0, atoms, atom, 0)
    blocks = low_ref.shape[0]
    low = lanes_of(red.at[0], total, blocks)
    high = lanes_of(red.at[1], total, blocks)
    low_ref[...] = low
    high_ref[...] = high
    down_ref[...] = turn_lanes(low, cos_ref[2], sin_ref[2])
    up_ref[...] = turn_lanes(high, cos_ref[3], sin_ref[3])

    lane = lax.broadcasted_iota(jnp.int32, (half, cols), 1)
    first, last = lane == 0, lane == cols - 1
    c, s = cos_ref[6], sin_ref[6]
    pot = pot_ref[0, pl.ds(pl.multiple_of(which_ref[0] * half, 8), half)] + 3.0
    for n in range(fields // 2):
        re = mid_ref[2 * n, EDGE : EDGE + half]
        im = mid_ref[2 * n + 1, EDGE : EDGE + half]
        re_next, im_next = pltpu.roll(re, cols - 1, 1), pltpu.roll(im, cols - 1, 1)
        re_prev, im_prev = pltpu.roll(re, 1, 1), pltpu.roll(im, 1, 1)
        y_re = jnp.where(last, re_next * c - im_next * s, re_next) + jnp.where(
            first, re_prev * c + im_prev * s, re_prev
        )
        y_im = jnp.where(last, re_next * s + im_next * c, im_next) + jnp.where(
            first, im_prev * c - re_prev * s, im_prev
        )
        scale = pot - energy_ref[n]
        for f, value, beside in ((2 * n, re, y_re), (2 * n + 1, im, y_im)):
            beside = beside + mid_ref[f, EDGE - 1 : EDGE - 1 + half]
            beside = beside + mid_ref[f, EDGE + 1 : EDGE + 1 + half]
            out_ref[f, EDGE : EDGE + half] = scale * value - 0.5 * beside
            out_ref[f, 0:EDGE] = jnp.zeros((EDGE, cols), jnp.float32)
            out_ref[f, EDGE + half :] = jnp.zeros((EDGE + WIN, cols), jnp.float32)


def plane_call(which, energy, starts, rot, strength, mid, pot, low_img, high_img):
    fields, wide, cols = mid.shape
    atoms = low_img.shape[0]
    blocks = -(-atoms * fields // 128)
    coef = jax.ShapeDtypeStruct((blocks, 128), jnp.float32)
    return pl.pallas_call(
        plane_kernel,
        out_shape=(jax.ShapeDtypeStruct((fields, wide + WIN, cols), jnp.float32), coef, coef, coef, coef),
        in_specs=[SMEM] * 6 + [VMEM] * 4,
        out_specs=(VMEM,) * 5,
        scratch_shapes=[pltpu.VMEM((2, atoms * fields, 8, 128), jnp.float32)],
        compiler_params=params(10),
        name="plane",
    )(which, energy, starts, *rot, strength, mid, pot, low_img, high_img)


def gather_all_kernel(starts_ref, cos_ref, sin_ref, str_ref, mid_ref, low_ref, high_ref, img_ref, low_img, high_img,
                  part_low, part_high, got_low, got_high, zsum_ref, out_ref, low, high, red):
    fields = mid_ref.shape[0]
    half = zsum_ref.shape[1]
    wide = half + 2 * EDGE
    for n in range(fields // 2):
        for src, dst, j in ((low_ref, low, 0), (high_ref, high, 1)):
            c, s = cos_ref[j], sin_ref[j]
            re, im = src[2 * n, 0:wide], src[2 * n + 1, 0:wide]
            dst[2 * n] = re * c - im * s
            dst[2 * n + 1] = re * s + im * c
        for k in range(2):
            f = 2 * n + k
            zsum_ref[f] = low[f, EDGE : EDGE + half] + high[f, EDGE : EDGE + half]
    atoms = img_ref.shape[0]
    groups = (
        (0, ((low, img_ref, 0), (mid_ref, img_ref, 1), (high, img_ref, 2))),
        (1, ((low, low_img, 0),)),
        (2, ((high, high_img, 1),)),
    )

    def atom(a, _):
        for j, planes in groups:
            begin = starts_ref[j, a]
            accs = [jnp.zeros((8, 128), jnp.float32)] * fields
            for src, img, z in planes:
                image = lambda part, k, img=img, z=z: img[a, z, part, 8 * k : 8 * k + 8]
                accs = project(src, begin, image, accs)
            for f in range(fields):
                red[j, a * fields + f] = accs[f] * str_ref[j, a]
        return 0

    lax.fori_loop(0, atoms, atom, 0)
    total = atoms * fields
    blocks = part_low.shape[0]
    out_ref[0:blocks] = lanes_of(red.at[0], total, blocks)
    out_ref[blocks : 2 * blocks] = lanes_of(red.at[1], total, blocks) + part_low[...] + got_low[...]
    out_ref[2 * blocks : 3 * blocks] = lanes_of(red.at[2], total, blocks) + part_high[...] + got_high[...]


def gather_all(starts, rot, strength, mid, low, high, img, low_img, high_img, parts, got):
    fields, rows, cols = mid.shape
    atoms = img.shape[0]
    blocks = -(-atoms * fields // 128)
    return pl.pallas_call(
        gather_all_kernel,
        out_shape=(
            jax.ShapeDtypeStruct((fields, rows - 2 * EDGE, cols), jnp.float32),
            jax.ShapeDtypeStruct((3 * blocks, 128), jnp.float32),
        ),
        in_specs=[SMEM] * 4 + [VMEM] * 10,
        out_specs=(VMEM,) * 2,
        scratch_shapes=[
            pltpu.VMEM(mid.shape, jnp.float32),
            pltpu.VMEM(mid.shape, jnp.float32),
            pltpu.VMEM((3, atoms * fields, 8, 128), jnp.float32),
        ],
        compiler_params=params(10),
        name="gather_all",
    )(starts, *rot, strength, mid, low, high, img, low_img, high_img, *parts, *got)


def spread_sides(acc, starts_ref, low_coef, high_coef, low_img, high_img):
    atoms = low_img.shape[0]
    for j, coef, img, z in ((1, low_coef, low_img, 1), (2, high_coef, high_img, 0)):
        image = lambda a, part, k, img=img, z=z: img[a, z, part, 8 * k : 8 * k + 8]
        spread_into(acc, lambda a, j=j: starts_ref[j, a], coef, image, atoms)


def spread_all(acc, plane_ref, zsum_ref, starts_ref, coef_ref, images):
    fields = acc.shape[0]
    half = zsum_ref.shape[1]
    atoms = images[0][0].shape[0]
    blocks = coef_ref.shape[0] // 3
    inside = pl.ds(EDGE, half)
    if acc is not plane_ref:
        acc[:, 0:EDGE] = plane_ref[:, 0:EDGE]
        acc[:, EDGE + half :] = plane_ref[:, EDGE + half :]
    acc[:, inside] = plane_ref[:, inside] - 0.5 * zsum_ref[...]

    def atom(a, _):
        line = lax.div(a * fields, 128)
        lane = lax.rem(a * fields, 128)
        for j, (img, z) in enumerate(images):
            begin = pl.multiple_of(starts_ref[j, a], 8)
            for k in range(2):
                at = pl.ds(pl.multiple_of(begin + 8 * k, 8), 8)
                ire = img[a, z, 0, 8 * k : 8 * k + 8]
                iim = img[a, z, 1, 8 * k : 8 * k + 8]
                for n in range(fields // 2):
                    pr = coef_ref[j * blocks + line, lane + 2 * n]
                    pi = coef_ref[j * blocks + line, lane + 2 * n + 1]
                    acc[2 * n, at] = acc[2 * n, at] + (pr * ire + pi * iim)
                    acc[2 * n + 1, at] = acc[2 * n + 1, at] + (pi * ire - pr * iim)
        return 0

    lax.fori_loop(0, atoms, atom, 0)


def occupied_into(store, half, fields, sums_ref, side, own_ref, other_ref, base, scale, block, copies_of, start=None, ahead=0):
    count = own_ref.shape[0]

    def rows_of(b, _):
        at = pl.ds(pl.multiple_of(b * block, 8), block)
        for copy in copies_of(b):
            copy.wait()
        if start is not None:

            @pl.when(b + ahead < half // block)
            def _():
                start(b + ahead)

        def band(m, accs):
            accs = list(accs)
            for row, occ in ((side, own_ref), (1 - side, other_ref)):
                pr, pi = occ[m, 0, at], occ[m, 1, at]
                for n in range(fields // 2):
                    sr = sums_ref[row, m * fields + 2 * n]
                    si = sums_ref[row, m * fields + 2 * n + 1]
                    accs[2 * n] = accs[2 * n] + (pr * sr - pi * si)
                    accs[2 * n + 1] = accs[2 * n + 1] + (pr * si + pi * sr)
            return tuple(accs)

        zero = jnp.zeros((block, 128), jnp.float32)
        accs = lax.fori_loop(0, count, band, (zero,) * fields, unroll=2)
        for f in range(fields):
            store(f, b * block, base(f, b * block, block) + scale * accs[f])
        return 0

    lax.fori_loop(0, half // block, rows_of, 0)


def correlate_into(red, src, offset, half, own_ref, other_ref):
    fields = src.shape[0]
    count = own_ref.shape[0]
    bands = fields // 2

    def pair(g, _):
        def row(i, accs):
            at = rows8(i)
            moved = pl.ds(pl.multiple_of(i * 8 + offset, 8), 8)
            accs = list(accs)
            occ = []
            for ref in (own_ref, other_ref):
                for k in range(2):
                    occ.append((ref[2 * g + k, 0, at], ref[2 * g + k, 1, at]))
            for n in range(bands):
                re, im = src[2 * n, moved], src[2 * n + 1, moved]
                for q, (pr, pi) in enumerate(occ):
                    j = (q * bands + n) * 2
                    accs[j] = accs[j] + (pr * re + pi * im)
                    accs[j + 1] = accs[j + 1] + (pr * im - pi * re)
            return tuple(accs)

        zero = jnp.zeros((8, 128), jnp.float32)
        accs = lax.fori_loop(0, half // 8, row, (zero,) * (8 * bands), unroll=3)
        for q in range(4):
            for j in range(fields):
                red[q // 2, (2 * g + q % 2) * fields + j] = accs[q * fields + j]
        return 0

    lax.fori_loop(0, count // 2, pair, 0)


def dots_into(red_dot, half, fields, pairs):
    bands = fields // 2

    def row(i, accs):
        at = pl.ds(pl.multiple_of(i * 8 + EDGE, 8), 8)
        accs = list(accs)
        for p, (left, right) in enumerate(pairs):
            for n in range(bands):
                value = left[2 * n, at] * right[2 * n, at] + left[2 * n + 1, at] * right[2 * n + 1, at]
                accs[p * bands + n] = accs[p * bands + n] + value
        return tuple(accs)

    zero = jnp.zeros((8, 128), jnp.float32)
    accs = lax.fori_loop(0, half // 8, row, (zero,) * (bands * len(pairs)), unroll=3)
    for j in range(bands * len(pairs)):
        red_dot[j] = accs[j]


def pick_block(half):
    return next(b for b in (24, 16, 8) if half % b == 0)


def shift_rows(start, size):
    return pl.ds(pl.multiple_of(start + EDGE, 8), size)


def band_copies(which_ref, half, block, b, occ_ref, other_refs, own, other, sems):
    begin = pl.multiple_of(which_ref[0] * half + b * block, 8)
    at = pl.ds(pl.multiple_of(b * block, 8), block)
    copies = [pltpu.make_async_copy(occ_ref.at[:, :, pl.ds(begin, block)], own.at[:, :, at], sems.at[0, b])]
    first = 0
    for j, ref in enumerate(other_refs):
        last = first + ref.shape[0]
        copies.append(pltpu.make_async_copy(ref.at[:, :, at], other.at[first:last, :, at], sems.at[1 + j, b]))
        first = last
    return tuple(copies)


def start_bands(half, block, copies_of):
    for b in range(half // block):
        for copy in copies_of(b):
            copy.start()


def write_sums(sum_ref, side, red):
    mine, theirs = sum_rows(red[0]), sum_rows(red[1])
    sum_ref[...] = jnp.zeros(sum_ref.shape, jnp.float32)
    sum_ref[0:1] = jnp.where(side == 0, mine, theirs)
    sum_ref[1:2] = jnp.where(side == 0, theirs, mine)


def write_edges(edge_ref, out_ref, half):
    for f in range(out_ref.shape[0]):
        edge_ref[f, 0:EDGE] = out_ref[f, EDGE : 2 * EDGE]
        edge_ref[f, EDGE : 2 * EDGE] = out_ref[f, half : half + EDGE]


def residual_kernel(scale, which_ref, starts_ref, low_coef, high_coef, sums_ref, lap_ref, low_ref, high_ref,
                    occ_ref, other_a, other_b, resp_hbm, pot_hbm, out_ref, edge_ref, sum_ref,
                    acc, own, other, resp, pot, red, red_dot, sems, more_sems):
    fields, wide, cols = out_ref.shape
    half = wide - 2 * EDGE
    side = which_ref[0]
    block = pick_block(half)
    begin = pl.multiple_of(side * half, 8)
    copies = (
        pltpu.make_async_copy(resp_hbm.at[:, :, pl.ds(begin, half)], resp, more_sems.at[0]),
        pltpu.make_async_copy(pot_hbm.at[:, pl.ds(begin, half)], pot, more_sems.at[1]),
    )
    for copy in copies:
        copy.start()
    copies_of = lambda b: band_copies(which_ref, half, block, b, occ_ref, (other_a, other_b), own, other, sems)
    start_bands(half, block, copies_of)
    acc[...] = lap_ref[...]
    spread_sides(acc, starts_ref, low_coef, high_coef, low_ref, high_ref)
    for copy in copies:
        copy.wait()

    def base(f, start, size):
        at = pl.ds(pl.multiple_of(start, 8), size)
        re, im = resp[f // 2, 0, at], resp[f // 2, 1, at]
        if f % 2 == 0:
            prod = pot[0, at] * re - pot[1, at] * im
        else:
            prod = pot[0, at] * im + pot[1, at] * re
        return -prod - acc[f, shift_rows(start, size)]

    def store(f, start, value):
        out_ref[f, shift_rows(start, block)] = value

    occupied_into(store, half, fields, sums_ref, side, own, other, base, scale, block, copies_of)
    write_edges(edge_ref, out_ref, half)
    correlate_into(red, out_ref, EDGE, half, own, other)
    dots_into(red_dot, half, fields, [(out_ref, out_ref)])
    write_sums(sum_ref, side, red)
    sum_ref[2:3] = sum_rows(red_dot[0 : fields // 2])


def field_outputs(fields, half, cols):
    return (
        jax.ShapeDtypeStruct((fields, half + 2 * EDGE, cols), jnp.float32),
        jax.ShapeDtypeStruct((fields, 2 * EDGE, cols), jnp.float32),
        jax.ShapeDtypeStruct((8, 128), jnp.float32),
    )


def residual_call(scale, which, starts, low_coef, high_coef, sums, lap, low_img, high_img, psi_occ, other, resp, pot):
    fields, long, cols = lap.shape
    half = long - 2 * EDGE - WIN
    return pl.pallas_call(
        functools.partial(residual_kernel, scale),
        out_shape=field_outputs(fields, half, cols),
        in_specs=[SMEM] * 5 + [VMEM] * 3 + [HBM] * 5,
        out_specs=(VMEM,) * 3,
        scratch_shapes=[
            pltpu.VMEM(lap.shape, jnp.float32),
            pltpu.VMEM(psi_occ.shape[:2] + (half, cols), jnp.float32),
            pltpu.VMEM(psi_occ.shape[:2] + (half, cols), jnp.float32),
            pltpu.VMEM(resp.shape[:2] + (half, cols), jnp.float32),
            pltpu.VMEM((2, half, cols), jnp.float32),
            pltpu.VMEM((2, 128, 8, 128), jnp.float32),
            pltpu.VMEM((16, 8, 128), jnp.float32),
            pltpu.SemaphoreType.DMA((3, half // pick_block(half))),
            pltpu.SemaphoreType.DMA((2,)),
        ],
        compiler_params=params(16),
        name="residual",
    )(which, starts, low_coef, high_coef, sums, lap, low_img, high_img, psi_occ, *other, resp, pot)


def image_kernel(scale, which_ref, starts_ref, low_coef, high_coef, sums_ref, lap_ref, low_ref, high_ref,
                 res_ref, occ_ref, other_a, other_b, out_ref, edge_ref, sum_ref,
                 acc, own, other, red, red_dot, sems):
    fields, wide, cols = out_ref.shape
    half = wide - 2 * EDGE
    side = which_ref[0]
    block = pick_block(half)
    copies_of = lambda b: band_copies(which_ref, half, block, b, occ_ref, (other_a, other_b), own, other, sems)
    start_bands(half, block, copies_of)
    acc[...] = lap_ref[...]
    spread_sides(acc, starts_ref, low_coef, high_coef, low_ref, high_ref)

    def base(f, start, size):
        return acc[f, shift_rows(start, size)]

    def store(f, start, value):
        out_ref[f, shift_rows(start, block)] = value

    occupied_into(store, half, fields, sums_ref, side, own, other, base, scale, block, copies_of)
    write_edges(edge_ref, out_ref, half)
    correlate_into(red, out_ref, EDGE, half, own, other)
    dots_into(red_dot, half, fields, [(res_ref, out_ref), (out_ref, out_ref)])
    write_sums(sum_ref, side, red)
    sum_ref[2:3] = sum_rows(red_dot[0:fields])


def image_call(scale, which, starts, low_coef, high_coef, sums, lap, low_img, high_img, res, psi_occ, other):
    fields, long, cols = lap.shape
    half = long - 2 * EDGE - WIN
    return pl.pallas_call(
        functools.partial(image_kernel, scale),
        out_shape=field_outputs(fields, half, cols),
        in_specs=[SMEM] * 5 + [VMEM] * 4 + [HBM] * 3,
        out_specs=(VMEM,) * 3,
        scratch_shapes=[
            pltpu.VMEM(lap.shape, jnp.float32),
            pltpu.VMEM(psi_occ.shape[:2] + (half, cols), jnp.float32),
            pltpu.VMEM(psi_occ.shape[:2] + (half, cols), jnp.float32),
            pltpu.VMEM((2, 128, 8, 128), jnp.float32),
            pltpu.VMEM((16, 8, 128), jnp.float32),
            pltpu.SemaphoreType.DMA((3, half // pick_block(half))),
        ],
        compiler_params=params(16),
        name="image",
    )(which, starts, low_coef, high_coef, sums, lap, low_img, high_img, res, psi_occ, *other)


def local_kernel(starts_ref, coef_ref, plane_ref, zsum_ref, img_ref, low_ref, high_ref, field_ref, part_ref,
                 out_ref, sum_ref, red_dot):
    fields = out_ref.shape[0]
    half = zsum_ref.shape[1]
    spread_all(out_ref, plane_ref, zsum_ref, starts_ref, coef_ref, ((img_ref, 1), (low_ref, 1), (high_ref, 0)))
    dots_into(red_dot, half, fields, [(field_ref, out_ref)])
    sum_ref[...] = part_ref[...]
    sum_ref[3:4] = sum_rows(red_dot[0 : fields // 2])


def local_call(starts, local, images, field, part):
    coef, plane, zsum = local
    return pl.pallas_call(
        local_kernel,
        out_shape=(
            jax.ShapeDtypeStruct(plane.shape, jnp.float32),
            jax.ShapeDtypeStruct((8, 128), jnp.float32),
        ),
        in_specs=[SMEM] * 2 + [VMEM] * 7,
        out_specs=(VMEM, VMEM),
        scratch_shapes=[pltpu.VMEM((16, 8, 128), jnp.float32)],
        compiler_params=params(10),
        name="local",
    )(starts, coef, plane, zsum, *images, field, part)


def last_kernel(which_ref, sums_ref, mix_ref, res_hbm, first_hbm, second_hbm, occ_ref, other_a, other_b,
                out_ref, res, first, second, own, other, sems, more_sems):
    fields, half, cols = out_ref.shape
    side = which_ref[0]
    block = pick_block(half)

    def copies_of(b):
        at = pl.ds(pl.multiple_of(b * block, 8), block)
        moved = shift_rows(b * block, block)
        own_copies = tuple(
            pltpu.make_async_copy(src.at[:, moved], dst.at[:, at], more_sems.at[j, b])
            for j, (src, dst) in enumerate(((res_hbm, res), (first_hbm, first), (second_hbm, second)))
        )
        return own_copies + band_copies(which_ref, half, block, b, occ_ref, (other_a, other_b), own, other, sems)

    ahead = 2

    def start(b):
        for copy in copies_of(b):
            copy.start()

    for b in range(ahead):
        start(b)

    def base(f, start, size):
        n = f // 2
        at = pl.ds(pl.multiple_of(start, 8), size)
        return res[f, at] + mix_ref[0, n] * first[f, at] + mix_ref[1, n] * second[f, at]

    def store(f, start, value):
        out_ref[f, pl.ds(pl.multiple_of(start, 8), block)] = value

    occupied_into(store, half, fields, sums_ref, side, own, other, base, 1.0, block, copies_of, start, ahead)


def last_call(which, sums, mix, res, first, second, psi_occ, other):
    fields, wide, cols = res.shape
    half = wide - 2 * EDGE
    blocks = half // pick_block(half)
    field = pltpu.VMEM((fields, half, cols), jnp.float32)
    return pl.pallas_call(
        last_kernel,
        out_shape=jax.ShapeDtypeStruct((fields, half, cols), jnp.float32),
        in_specs=[SMEM] * 3 + [HBM] * 6,
        out_specs=VMEM,
        scratch_shapes=[
            field,
            field,
            field,
            pltpu.VMEM(psi_occ.shape[:2] + (half, cols), jnp.float32),
            pltpu.VMEM(psi_occ.shape[:2] + (half, cols), jnp.float32),
            pltpu.SemaphoreType.DMA((3, blocks)),
            pltpu.SemaphoreType.DMA((3, blocks)),
        ],
        compiler_params=params(52),
        name="last",
    )(which, sums, mix, res, first, second, psi_occ, *other)


def xor_sum(block, bits):
    count = lax.axis_size("space") * lax.axis_size("occ")
    masks = [0]
    for bit in bits:
        masks = masks + [mask | bit for mask in masks]
    parts = [block]
    for mask in masks[1:]:
        parts.append(lax.ppermute(block, ("space", "occ"), [(i, i ^ mask) for i in range(count)]))
    while len(parts) > 1:
        parts = [parts[j] + parts[j + 1] for j in range(0, len(parts), 2)]
    return parts[0]


def total(block, groups=None):
    count = lax.axis_size("space")
    bit = 2
    steps = []
    while count > 1:
        wide = count % 4 == 0
        steps.append((bit, 2 * bit) if wide else (bit,))
        bit, count = (4 * bit, count // 4) if wide else (2 * bit, count // 2)
    steps.append((1,))
    for bits in steps[groups] if groups is not None else steps:
        block = xor_sum(block, bits)
    return block


def exchange(block):
    return lax.ppermute(block, "occ", SWAP)


def from_behind(block, distance):
    count = lax.axis_size("space")
    return lax.ppermute(block, "space", [((i - distance) % count, i) for i in range(count)])


def window_images(x_cell, y_cell, offsets, values, theta_y, rows_y, planes):
    y_raw = y_cell[:, None] + offsets[None, :, 2]
    y_wrap = jnp.floor_divide(y_raw, rows_y)
    y_at = y_raw - y_wrap * rows_y
    angles = theta_y * y_wrap.astype(jnp.float32)
    row = x_cell[:, None] + offsets[None, :, 1] + RAD
    slot = []
    for plane in planes:
        wanted = (row[:, None, :] == jnp.arange(WIN, dtype=jnp.int32)[None, :, None]) & (
            offsets[:, 0] == plane
        )[None, None, :]
        slot.append(wanted)
    slots = jnp.stack(slot, axis=1)
    weights = jnp.stack([values * jnp.cos(angles), values * jnp.sin(angles)], axis=1)
    left = jnp.where(slots[:, :, None], weights[:, None, :, None, :], 0.0)
    atoms = left.shape[0]
    left = left.reshape(atoms, len(planes) * 2 * WIN, -1)
    right = (y_at[:, :, None] == jnp.arange(rows_y, dtype=jnp.int32)[None, None, :]).astype(jnp.float32)
    image = jnp.einsum("apk,aky->apy", left, right, precision=PRECISE)
    return image.reshape(atoms, len(planes), 2, WIN, rows_y)


def shards(
    psi_occ,
    psi_resp,
    initial_guess,
    local_potential,
    potential_change,
    band_energy,
    q_index,
    atom_cells,
    offsets,
    projector,
    strength,
):
    slab_count = lax.axis_size("space")
    slab_index = lax.axis_index("space")
    side = lax.axis_index("occ")
    layers, rows_x, rows_y = local_potential.shape
    half = rows_x // 2
    atoms = atom_cells.shape[0]
    bands = psi_resp.shape[0]
    fields = 2 * bands
    weight = 1.0 / (layers * slab_count * rows_x * rows_y)
    thetas = q_index.astype(jnp.float32) * (2.0 * math.pi / QDIV)
    which = side.astype(jnp.int32).reshape(1)
    where = jnp.stack([side, slab_index]).astype(jnp.int32)

    occ = psi_occ.reshape(psi_occ.shape[0], 2, rows_x, rows_y)
    resp = psi_resp.reshape(bands, 2, rows_x, rows_y)
    guess = initial_guess.reshape(bands, 2, rows_x, rows_y)
    change = potential_change.reshape(2, rows_x, rows_y)

    cell_rows = jnp.pad(
        jnp.concatenate([atom_cells.astype(jnp.float32), strength[:, None]], axis=1),
        ((0, 0), (0, projector.shape[1] - 4)),
    )
    packed = jnp.concatenate([projector, cell_rows], axis=0)
    guess_mid, *rot = prep_call(slab_count, where, q_index, guess, packed)
    first_sums, *occ_send = first_corr(which, occ, resp, change, guess)
    occ_other = [exchange(block) for block in occ_send]
    first_sums = total(first_sums, slice(0, 1))
    first_sums, guess_mid = lax.optimization_barrier((first_sums, guess_mid))
    first_sums = total(first_sums, slice(1, 2))
    first_sums, occ_other[0] = lax.optimization_barrier((first_sums, occ_other[0]))
    first_sums = total(first_sums, slice(2, -1))
    guess_low = from_behind(guess_mid, 1)
    guess_high = from_behind(guess_mid, -1)

    def unpack(block):
        rows = block[:, half + 2 * EDGE :].reshape(-1, rows_y)
        return rows[:atoms], rows[atoms : 2 * atoms]

    below, below_cells = unpack(guess_low)
    above, above_cells = unpack(guess_high)
    cells = [atom_cells]
    for rows in (below_cells, above_cells):
        cells.append(rows[:, :3].astype(jnp.int32))
    all_x = jnp.stack([c[:, 1] for c in cells])
    all_y = jnp.stack([c[:, 2] for c in cells])
    at_row = jnp.mod(all_x - RAD - side * half + EDGE, rows_x)
    inner = at_row % 8
    touching = at_row < half + EDGE
    put_starts = jnp.where(touching, at_row - inner, half + 2 * EDGE).astype(jnp.int32)
    get_starts = jnp.where(touching, at_row - inner, 0).astype(jnp.int32)
    own_row = jnp.mod(atom_cells[:, 1] - RAD - side * half + EDGE, rows_x)
    own_inner = own_row % 8
    own_starts = jnp.where(own_row < half + EDGE, own_row - own_inner, 0).astype(jnp.int32)
    strengths = jnp.stack([strength, below_cells[:, 3], above_cells[:, 3]])
    img = window_images(own_inner, atom_cells[:, 2], offsets, projector, thetas[2], rows_y, (-1, 0, 1))
    low_img = window_images(inner[1], all_y[1], offsets, below, thetas[2], rows_y, (0, 1))
    high_img = window_images(inner[2], all_y[2], offsets, above, thetas[2], rows_y, (-1, 0))
    images = (img, low_img, high_img)

    def local_part(mid, low, high):
        zsum, proj, up, down = gather(own_starts, rot, strength, mid, low, high, img, half)
        low_coef = from_behind(up, 1)
        high_coef = from_behind(down, -1)
        lap = stencil(which, band_energy, rot, put_starts, proj, mid, zsum, local_potential, img)
        return put_starts, low_coef, high_coef, lap

    def far_part(mid):
        low = from_behind(mid, 1)
        high = from_behind(mid, -1)
        plane, part_low, part_high, down, up = plane_call(
            which, band_energy, get_starts, rot, strengths, mid, local_potential, low_img, high_img
        )
        got = (from_behind(up, 2), from_behind(down, -2))
        zsum, coef = gather_all(get_starts, rot, strengths, mid, low, high, *images, (part_low, part_high), got)
        return coef, plane, zsum

    starts, low_coef, high_coef, lap = local_part(guess_mid, guess_low, guess_high)
    first_sums, lap = lax.optimization_barrier((first_sums, lap))
    first_sums = total(first_sums, slice(-1, None))
    residual, edges, part = residual_call(
        weight, which, starts, low_coef, high_coef, first_sums, lap, low_img, high_img, occ, occ_other, resp, change
    )
    tot = total(part)
    norm0 = tot[2, :bands]
    residual = fill_call(rot, exchange(edges), residual)
    starts, low_coef, high_coef, lap = local_part(residual, from_behind(residual, 1), from_behind(residual, -1))
    image, edges, part = image_call(
        SHIFT_WEIGHT * weight, which, starts, low_coef, high_coef, tot, lap, low_img, high_img, residual, occ, occ_other
    )
    image = fill_call(rot, exchange(edges), image)
    image_other = exchange(image)
    image2, part = local_call(put_starts, far_part(image), images, image, part)
    part, image_other, residual_send = lax.optimization_barrier((part, image_other, residual))
    residual_other = exchange(residual_send)
    tot = total(part, slice(0, 2))
    tot, residual_other = lax.optimization_barrier((tot, residual_other))
    tot = total(tot, slice(2, None))
    sums = tot[0:2]
    cross = tot[2, :bands]
    square = tot[2, bands : 2 * bands]
    occ_square = jnp.sum((sums * sums).reshape(-1, bands, 2), axis=(0, 2))
    triple = tot[3, :bands] + SHIFT_WEIGHT * weight * occ_square
    step0 = norm0 / cross
    norm1 = norm0 - 2.0 * step0 * cross + step0 * step0 * square
    growth = norm1 / norm0
    lead = 1.0 + growth
    curvature = lead * lead * cross - 2.0 * lead * step0 * square + step0 * step0 * triple
    step1 = norm1 / curvature
    mix0 = -step0 - step1 * lead
    mix1 = step1 * step0
    per_lane = jnp.tile(jnp.repeat(mix1, 2), sums.shape[1] // fields)
    last_sums = SHIFT_WEIGHT * weight * sums * per_lane[None, :]
    mine = last_call(which, last_sums, jnp.stack([mix0, mix1]), residual, image, image2, occ, occ_other)
    mine, residual_other, image_other = lax.optimization_barrier((mine, residual_other, image_other))
    theirs = exchange(mine)

    def join(own_half, other_half):
        lower = jnp.where(side == 0, own_half, other_half)
        upper = jnp.where(side == 0, other_half, own_half)
        return jnp.concatenate([lower, upper], axis=1).reshape(bands, 2, 1, rows_x, rows_y)

    inside = lambda v: v[:, EDGE : EDGE + half]
    wide = lambda v: v[:, None, None, None, None]
    response = (
        initial_guess
        + wide(step0 + step1 * lead) * join(inside(residual), inside(residual_other))
        - wide(step0 * step1) * join(inside(image), inside(image_other))
    )
    return response, join(mine, theirs)


def solution(mesh):
    return jax.shard_map(
        shards,
        mesh=mesh,
        in_specs=(
            P("occ", None, "space", None, None),
            P("resp", None, "space", None, None),
            P("resp", None, "space", None, None),
            P("space", None, None),
            P(None, "space", None, None),
            P("resp"),
            P(),
            P("space", None),
            P(),
            P("space", None),
            P("space"),
        ),
        out_specs=(P("resp", None, "space", None, None), P("resp", None, "space", None, None)),
        check_vma=False,
    )
```

```python
import functools
import math

import jax
import jax.numpy as jnp
from jax import lax
from jax.experimental import pallas as pl
from jax.experimental.pallas import tpu as pltpu
from jax.sharding import PartitionSpec as P

RAD = 4
QDIV = 8
EDGE = 8
WIN = 16
SHIFT_WEIGHT = 3.0
PRECISE = lax.Precision.HIGHEST
SWAP = [(0, 1), (1, 0)]

VMEM = pl.BlockSpec(memory_space=pltpu.VMEM)
SMEM = pl.BlockSpec(memory_space=pltpu.SMEM)
ANY = pl.BlockSpec(memory_space=pl.ANY)
HBM = pl.BlockSpec(memory_space=pltpu.HBM)


def params(mib):
    return pltpu.CompilerParams(vmem_limit_bytes=mib * 1024 * 1024)


def sum_rows(values):
    total = jnp.sum(values, axis=2, keepdims=True)
    row = lax.broadcasted_iota(jnp.int32, values.shape, 0)
    lane = lax.broadcasted_iota(jnp.int32, values.shape, 2)
    picked = jnp.sum(jnp.where(row == lane, total, 0.0), axis=0)
    return jnp.sum(picked, axis=0, keepdims=True)


def rows8(index):
    return pl.ds(pl.multiple_of(index * 8, 8), 8)


def extra_rows(count, fields):
    return -(-count // (8 * fields)) * 8


AXES = (0, 0, 0, 0, 1, 1, 2, 0, 0)
SIGNS = (-1, 1, 1, -1, -1, 1, 1, -1, 1)
TURNS = [2.0 * math.pi * k / QDIV for k in range(QDIV)]


def prep_kernel(slab_count, where_ref, q_ref, guess_ref, atoms_ref, out_ref, cos_ref, sin_ref, middle, low, high, sems):
    fields = out_ref.shape[0]
    half = middle.shape[2]
    wide = half + 2 * EDGE
    side, slab = where_ref[0], where_ref[1]
    begin = pl.multiple_of(side * half, 8)
    away = pl.multiple_of((1 - side) * half, 8)
    under = pl.multiple_of((1 - side) * half + half - EDGE, 8)
    copies = []
    for j, (start, size, dst) in enumerate(((begin, half, middle), (under, EDGE, low), (away, EDGE, high))):
        copies.append(pltpu.make_async_copy(guess_ref.at[:, :, pl.ds(start, size)], dst, sems.at[j]))
    for copy in copies:
        copy.start()

    first, last = slab == 0, slab == slab_count - 1
    flags = (first, last, slab < 2, slab >= slab_count - 2, side == 0, side == 1, slab >= 0, last, first)
    for j, (flag, sign, axis) in enumerate(zip(flags, SIGNS, AXES)):
        step = jnp.where(flag, jnp.bitwise_and(sign * q_ref[axis], QDIV - 1), 0)
        cosine, sine = jnp.float32(1.0), jnp.float32(0.0)
        for k in range(1, QDIV):
            cosine = jnp.where(step == k, jnp.float32(math.cos(TURNS[k])), cosine)
            sine = jnp.where(step == k, jnp.float32(math.sin(TURNS[k])), sine)
        cos_ref[j] = cosine
        sin_ref[j] = sine

    for f in range(fields):
        for r in range(0, out_ref.shape[1] - wide, 8):
            at = f * (out_ref.shape[1] - wide) + r
            if at < atoms_ref.shape[0]:
                out_ref[f, wide + r : wide + r + 8] = atoms_ref[at : at + 8]
            else:
                out_ref[f, wide + r : wide + r + 8] = jnp.zeros((8, 128), jnp.float32)
    for copy in copies:
        copy.wait()
    for n in range(fields // 2):
        for k in range(2):
            out_ref[2 * n + k, EDGE : EDGE + half] = middle[n, k]
        for src, spot, j in ((low, 0, 4), (high, EDGE + half, 5)):
            c, s = cos_ref[j], sin_ref[j]
            re, im = src[n, 0], src[n, 1]
            out_ref[2 * n, spot : spot + EDGE] = re * c - im * s
            out_ref[2 * n + 1, spot : spot + EDGE] = re * s + im * c


def prep_call(slab_count, where, q_index, guess, atoms):
    bands, _, rows, cols = guess.shape
    half = rows // 2
    extra = extra_rows(atoms.shape[0], 2 * bands)
    table = jax.ShapeDtypeStruct((len(AXES),), jnp.float32)
    return pl.pallas_call(
        functools.partial(prep_kernel, slab_count),
        out_shape=(
            jax.ShapeDtypeStruct((2 * bands, half + 2 * EDGE + extra, cols), jnp.float32),
            table,
            table,
        ),
        in_specs=[SMEM, SMEM, HBM, VMEM],
        out_specs=(VMEM, SMEM, SMEM),
        scratch_shapes=[
            pltpu.VMEM((bands, 2, half, cols), jnp.float32),
            pltpu.VMEM((bands, 2, EDGE, cols), jnp.float32),
            pltpu.VMEM((bands, 2, EDGE, cols), jnp.float32),
            pltpu.SemaphoreType.DMA((3,)),
        ],
        compiler_params=params(8),
        name="prep",
    )(where, q_index, guess, atoms)


def fill_kernel(cos_ref, sin_ref, got_ref, ext_ref, out_ref, low, high, sems):
    fields, wide, _ = out_ref.shape
    for n in range(fields // 2):
        for dst, at, j in ((low, EDGE, 4), (high, 0, 5)):
            c, s = cos_ref[j], sin_ref[j]
            re, im = got_ref[2 * n, at : at + EDGE], got_ref[2 * n + 1, at : at + EDGE]
            dst[2 * n] = re * c - im * s
            dst[2 * n + 1] = re * s + im * c
    one = pltpu.make_async_copy(low, out_ref.at[:, 0:EDGE], sems.at[0])
    two = pltpu.make_async_copy(high, out_ref.at[:, wide - EDGE : wide], sems.at[1])
    one.start()
    two.start()
    one.wait()
    two.wait()


def fill_call(rot, got, ext):
    shape = (ext.shape[0], EDGE, ext.shape[2])
    return pl.pallas_call(
        fill_kernel,
        out_shape=jax.ShapeDtypeStruct(ext.shape, jnp.float32),
        in_specs=[SMEM, SMEM, VMEM, ANY],
        out_specs=ANY,
        scratch_shapes=[
            pltpu.VMEM(shape, jnp.float32),
            pltpu.VMEM(shape, jnp.float32),
            pltpu.SemaphoreType.DMA((2,)),
        ],
        input_output_aliases={3: 0},
        compiler_params=params(4),
        name="fill",
    )(*rot, got, ext)


def first_corr_kernel(which_ref, occ_ref, resp_ref, pot_ref, guess_ref, out_ref, send_a, send_b, mixed, red):
    bands, _, rows, _ = resp_ref.shape
    group = occ_ref.shape[0]
    step = pl.program_id(0)
    half = send_a.shape[2]
    middle = pl.num_programs(0) // 2
    away = pl.ds(pl.multiple_of((1 - which_ref[0]) * half, 8), half)

    @pl.when(step < middle)
    def _():
        send_a[...] = occ_ref[:, :, away]

    @pl.when(step >= middle)
    def _():
        send_b[...] = occ_ref[:, :, away]

    @pl.when(step == 0)
    def _():
        for n in range(bands):
            re = resp_ref[n, 0]
            im = resp_ref[n, 1]
            mixed[2 * n] = pot_ref[0] * re - pot_ref[1] * im - SHIFT_WEIGHT * guess_ref[n, 0]
            mixed[2 * n + 1] = pot_ref[0] * im + pot_ref[1] * re - SHIFT_WEIGHT * guess_ref[n, 1]

    def row(i, accs):
        at = rows8(i)
        occ = [(occ_ref[k, 0, at], occ_ref[k, 1, at]) for k in range(group)]
        accs = list(accs)
        for n in range(bands):
            re, im = mixed[2 * n, at], mixed[2 * n + 1, at]
            for k, (pr, pi) in enumerate(occ):
                j = (k * bands + n) * 2
                accs[j] = accs[j] + (pr * re + pi * im)
                accs[j + 1] = accs[j + 1] + (pr * im - pi * re)
        return tuple(accs)

    zero = jnp.zeros((8, 128), jnp.float32)
    count = 2 * bands * group
    accs = lax.fori_loop(0, rows // 8, row, (zero,) * count, unroll=3)
    for j in range(count):
        red[step * count + j] = accs[j]

    @pl.when(step == pl.num_programs(0) - 1)
    def _():
        out_ref[...] = jnp.zeros(out_ref.shape, jnp.float32)
        total = sum_rows(red[...])
        side = which_ref[0]
        out_ref[0:1] = jnp.where(side == 0, total, 0.0)
        out_ref[1:2] = jnp.where(side == 0, 0.0, total)


def first_corr(which, psi_occ, psi_resp, pot, guess):
    group = 4
    count, _, rows, cols = psi_occ.shape
    fixed = lambda shape: pl.BlockSpec(shape, lambda i: (0,) * len(shape))
    middle = count // group // 2
    send = jax.ShapeDtypeStruct((count // 2, 2, rows // 2, cols), jnp.float32)
    shape = (group, 2, rows // 2, cols)
    return pl.pallas_call(
        first_corr_kernel,
        out_shape=(
            jax.ShapeDtypeStruct((8, 128), jnp.float32),
            send,
            send,
        ),
        grid=(count // group,),
        in_specs=[
            SMEM,
            pl.BlockSpec((group, 2, rows, cols), lambda i: (i, 0, 0, 0)),
            fixed(psi_resp.shape),
            fixed(pot.shape),
            fixed(guess.shape),
        ],
        out_specs=(
            fixed((8, 128)),
            pl.BlockSpec(shape, lambda i: (jnp.minimum(i, middle - 1), 0, 0, 0)),
            pl.BlockSpec(shape, lambda i: (jnp.maximum(i - middle, 0), 0, 0, 0)),
        ),
        scratch_shapes=[
            pltpu.VMEM((psi_resp.shape[0] * 2, rows, cols), jnp.float32),
            pltpu.VMEM((128, 8, 128), jnp.float32),
        ],
        compiler_params=params(60),
        name="first_corr",
    )(which, psi_occ, psi_resp, pot, guess)


def gather_kernel(start_ref, cos_ref, sin_ref, str_ref, mid_ref, low_ref, high_ref, img_ref,
                  zsum_ref, out_ref, up_ref, down_ref, low, high, red):
    fields = mid_ref.shape[0]
    half = zsum_ref.shape[1]
    wide = half + 2 * EDGE
    for n in range(fields // 2):
        for src, dst, j in ((low_ref, low, 0), (high_ref, high, 1)):
            c, s = cos_ref[j], sin_ref[j]
            re, im = src[2 * n, 0:wide], src[2 * n + 1, 0:wide]
            dst[2 * n] = re * c - im * s
            dst[2 * n + 1] = re * s + im * c
        for k in range(2):
            f = 2 * n + k
            zsum_ref[f] = low[f, EDGE : EDGE + half] + high[f, EDGE : EDGE + half]
    atoms = img_ref.shape[0]

    def atom(a, _):
        begin = pl.multiple_of(start_ref[a], 8)
        accs = [jnp.zeros((8, 128), jnp.float32)] * fields
        for z, src in enumerate((low, mid_ref, high)):
            for k in range(2):
                at = pl.ds(pl.multiple_of(begin + 8 * k, 8), 8)
                ire = img_ref[a, z, 0, 8 * k : 8 * k + 8]
                iim = img_ref[a, z, 1, 8 * k : 8 * k + 8]
                for n in range(fields // 2):
                    re, im = src[2 * n, at], src[2 * n + 1, at]
                    accs[2 * n] = accs[2 * n] + (re * ire - im * iim)
                    accs[2 * n + 1] = accs[2 * n + 1] + (re * iim + im * ire)
        for f in range(fields):
            red[a * fields + f] = accs[f] * str_ref[a]
        return 0

    lax.fori_loop(0, atoms, atom, 0)
    total = atoms * fields
    value = lanes_of(red, total, out_ref.shape[0])
    out_ref[...] = value
    up_ref[...] = turn_lanes(value, cos_ref[7], sin_ref[7])
    down_ref[...] = turn_lanes(value, cos_ref[8], sin_ref[8])


def gather(starts, rot, strength, mid, low, high, img, half):
    fields, _, cols = mid.shape
    rows = half + 2 * EDGE
    atoms = img.shape[0]
    blocks = -(-atoms * fields // 128)
    coef = jax.ShapeDtypeStruct((blocks, 128), jnp.float32)
    return pl.pallas_call(
        gather_kernel,
        out_shape=(
            jax.ShapeDtypeStruct((fields, rows - 2 * EDGE, cols), jnp.float32),
            coef,
            coef,
            coef,
        ),
        in_specs=[SMEM] * 4 + [VMEM] * 4,
        out_specs=(VMEM,) * 4,
        scratch_shapes=[
            pltpu.VMEM((fields, rows, cols), jnp.float32),
            pltpu.VMEM((fields, rows, cols), jnp.float32),
            pltpu.VMEM((atoms * fields, 8, 128), jnp.float32),
        ],
        compiler_params=params(10),
        name="gather",
    )(starts, *rot, strength, mid, low, high, img)


def spread_into(acc, start_of, coef_ref, image_of, atoms):
    fields = acc.shape[0]

    def atom(a, _):
        begin = pl.multiple_of(start_of(a), 8)
        line = lax.div(a * fields, 128)
        lane = lax.rem(a * fields, 128)
        for k in range(2):
            at = pl.ds(pl.multiple_of(begin + 8 * k, 8), 8)
            ire = image_of(a, 0, k)
            iim = image_of(a, 1, k)
            for n in range(fields // 2):
                pr = coef_ref[line, lane + 2 * n]
                pi = coef_ref[line, lane + 2 * n + 1]
                acc[2 * n, at] = acc[2 * n, at] + (pr * ire + pi * iim)
                acc[2 * n + 1, at] = acc[2 * n + 1, at] + (pi * ire - pr * iim)
        return 0

    lax.fori_loop(0, atoms, atom, 0)


def stencil_kernel(which_ref, energy_ref, cos_ref, sin_ref, starts_ref, coef_ref, mid_ref, zsum_ref, pot_ref, img_ref, out_ref):
    fields, half, cols = zsum_ref.shape
    lane = lax.broadcasted_iota(jnp.int32, (half, cols), 1)
    first, last = lane == 0, lane == cols - 1
    c, s = cos_ref[6], sin_ref[6]
    pot = pot_ref[0, pl.ds(pl.multiple_of(which_ref[0] * half, 8), half)] + 3.0
    for n in range(fields // 2):
        re = mid_ref[2 * n, EDGE : EDGE + half]
        im = mid_ref[2 * n + 1, EDGE : EDGE + half]
        re_next, im_next = pltpu.roll(re, cols - 1, 1), pltpu.roll(im, cols - 1, 1)
        re_prev, im_prev = pltpu.roll(re, 1, 1), pltpu.roll(im, 1, 1)
        y_re = jnp.where(last, re_next * c - im_next * s, re_next) + jnp.where(
            first, re_prev * c + im_prev * s, re_prev
        )
        y_im = jnp.where(last, re_next * s + im_next * c, im_next) + jnp.where(
            first, im_prev * c - re_prev * s, im_prev
        )
        scale = pot - energy_ref[n]
        for f, value, beside in ((2 * n, re, y_re), (2 * n + 1, im, y_im)):
            beside = beside + zsum_ref[f]
            beside = beside + mid_ref[f, EDGE - 1 : EDGE - 1 + half]
            beside = beside + mid_ref[f, EDGE + 1 : EDGE + 1 + half]
            out_ref[f, EDGE : EDGE + half] = scale * value - 0.5 * beside
            out_ref[f, 0:EDGE] = jnp.zeros((EDGE, cols), jnp.float32)
            out_ref[f, EDGE + half :] = jnp.zeros((EDGE + WIN, cols), jnp.float32)
    atoms = img_ref.shape[0]
    image = lambda a, part, k: img_ref[a, 1, part, 8 * k : 8 * k + 8]
    spread_into(out_ref, lambda a: starts_ref[0, a], coef_ref, image, atoms)


def stencil(which, energy, rot, starts, coef, mid, zsum, pot, img):
    fields, half, cols = zsum.shape
    return pl.pallas_call(
        stencil_kernel,
        out_shape=jax.ShapeDtypeStruct((fields, half + 2 * EDGE + WIN, cols), jnp.float32),
        in_specs=[SMEM] * 6 + [VMEM] * 4,
        out_specs=VMEM,
        compiler_params=params(10),
        name="stencil",
    )(which, energy, *rot, starts, coef, mid, zsum, pot, img)


def project(src, begin, image_of, accs):
    accs = list(accs)
    for k in range(2):
        at = pl.ds(pl.multiple_of(begin + 8 * k, 8), 8)
        ire, iim = image_of(0, k), image_of(1, k)
        for n in range(len(accs) // 2):
            re, im = src[2 * n, at], src[2 * n + 1, at]
            accs[2 * n] = accs[2 * n] + (re * ire - im * iim)
            accs[2 * n + 1] = accs[2 * n + 1] + (re * iim + im * ire)
    return accs


def lanes_of(red, total, blocks):
    return jnp.concatenate([sum_rows(red[128 * b : min(total, 128 * b + 128)]) for b in range(blocks)], axis=0)


def turn_lanes(value, cosine, sine_part):
    even = lax.broadcasted_iota(jnp.int32, value.shape, 1) % 2 == 0
    times_i = jnp.where(even, -pltpu.roll(value, 127, 1), pltpu.roll(value, 1, 1))
    return value * cosine + times_i * sine_part


def plane_kernel(which_ref, energy_ref, starts_ref, cos_ref, sin_ref, str_ref, mid_ref, pot_ref, low_img, high_img,
                 out_ref, low_ref, high_ref, down_ref, up_ref, red):
    fields, wide, cols = mid_ref.shape
    half = wide - 2 * EDGE
    atoms = low_img.shape[0]
    total = atoms * fields

    def atom(a, _):
        for j, img, z in ((1, low_img, 1), (2, high_img, 0)):
            begin = starts_ref[j, a]
            image = lambda part, k: img[a, z, part, 8 * k : 8 * k + 8]
            accs = project(mid_ref, begin, image, [jnp.zeros((8, 128), jnp.float32)] * fields)
            for f in range(fields):
                red[j - 1, a * fields + f] = accs[f] * str_ref[j, a]
        return 0

    lax.fori_loop(0, atoms, atom, 0)
    blocks = low_ref.shape[0]
    low = lanes_of(red.at[0], total, blocks)
    high = lanes_of(red.at[1], total, blocks)
    low_ref[...] = low
    high_ref[...] = high
    down_ref[...] = turn_lanes(low, cos_ref[2], sin_ref[2])
    up_ref[...] = turn_lanes(high, cos_ref[3], sin_ref[3])

    lane = lax.broadcasted_iota(jnp.int32, (half, cols), 1)
    first, last = lane == 0, lane == cols - 1
    c, s = cos_ref[6], sin_ref[6]
    pot = pot_ref[0, pl.ds(pl.multiple_of(which_ref[0] * half, 8), half)] + 3.0
    for n in range(fields // 2):
        re = mid_ref[2 * n, EDGE : EDGE + half]
        im = mid_ref[2 * n + 1, EDGE : EDGE + half]
        re_next, im_next = pltpu.roll(re, cols - 1, 1), pltpu.roll(im, cols - 1, 1)
        re_prev, im_prev = pltpu.roll(re, 1, 1), pltpu.roll(im, 1, 1)
        y_re = jnp.where(last, re_next * c - im_next * s, re_next) + jnp.where(
            first, re_prev * c + im_prev * s, re_prev
        )
        y_im = jnp.where(last, re_next * s + im_next * c, im_next) + jnp.where(
            first, im_prev * c - re_prev * s, im_prev
        )
        scale = pot - energy_ref[n]
        for f, value, beside in ((2 * n, re, y_re), (2 * n + 1, im, y_im)):
            beside = beside + mid_ref[f, EDGE - 1 : EDGE - 1 + half]
            beside = beside + mid_ref[f, EDGE + 1 : EDGE + 1 + half]
            out_ref[f, EDGE : EDGE + half] = scale * value - 0.5 * beside
            out_ref[f, 0:EDGE] = jnp.zeros((EDGE, cols), jnp.float32)
            out_ref[f, EDGE + half :] = jnp.zeros((EDGE + WIN, cols), jnp.float32)


def plane_call(which, energy, starts, rot, strength, mid, pot, low_img, high_img):
    fields, wide, cols = mid.shape
    atoms = low_img.shape[0]
    blocks = -(-atoms * fields // 128)
    coef = jax.ShapeDtypeStruct((blocks, 128), jnp.float32)
    return pl.pallas_call(
        plane_kernel,
        out_shape=(jax.ShapeDtypeStruct((fields, wide + WIN, cols), jnp.float32), coef, coef, coef, coef),
        in_specs=[SMEM] * 6 + [VMEM] * 4,
        out_specs=(VMEM,) * 5,
        scratch_shapes=[pltpu.VMEM((2, atoms * fields, 8, 128), jnp.float32)],
        compiler_params=params(10),
        name="plane",
    )(which, energy, starts, *rot, strength, mid, pot, low_img, high_img)


def gather_all_kernel(starts_ref, cos_ref, sin_ref, str_ref, mid_ref, low_ref, high_ref, img_ref, low_img, high_img,
                  part_low, part_high, got_low, got_high, zsum_ref, out_ref, low, high, red):
    fields = mid_ref.shape[0]
    half = zsum_ref.shape[1]
    wide = half + 2 * EDGE
    for n in range(fields // 2):
        for src, dst, j in ((low_ref, low, 0), (high_ref, high, 1)):
            c, s = cos_ref[j], sin_ref[j]
            re, im = src[2 * n, 0:wide], src[2 * n + 1, 0:wide]
            dst[2 * n] = re * c - im * s
            dst[2 * n + 1] = re * s + im * c
        for k in range(2):
            f = 2 * n + k
            zsum_ref[f] = low[f, EDGE : EDGE + half] + high[f, EDGE : EDGE + half]
    atoms = img_ref.shape[0]
    groups = (
        (0, ((low, img_ref, 0), (mid_ref, img_ref, 1), (high, img_ref, 2))),
        (1, ((low, low_img, 0),)),
        (2, ((high, high_img, 1),)),
    )

    def atom(a, _):
        for j, planes in groups:
            begin = starts_ref[j, a]
            accs = [jnp.zeros((8, 128), jnp.float32)] * fields
            for src, img, z in planes:
                image = lambda part, k, img=img, z=z: img[a, z, part, 8 * k : 8 * k + 8]
                accs = project(src, begin, image, accs)
            for f in range(fields):
                red[j, a * fields + f] = accs[f] * str_ref[j, a]
        return 0

    lax.fori_loop(0, atoms, atom, 0)
    total = atoms * fields
    blocks = part_low.shape[0]
    out_ref[0:blocks] = lanes_of(red.at[0], total, blocks)
    out_ref[blocks : 2 * blocks] = lanes_of(red.at[1], total, blocks) + part_low[...] + got_low[...]
    out_ref[2 * blocks : 3 * blocks] = lanes_of(red.at[2], total, blocks) + part_high[...] + got_high[...]


def gather_all(starts, rot, strength, mid, low, high, img, low_img, high_img, parts, got):
    fields, rows, cols = mid.shape
    atoms = img.shape[0]
    blocks = -(-atoms * fields // 128)
    return pl.pallas_call(
        gather_all_kernel,
        out_shape=(
            jax.ShapeDtypeStruct((fields, rows - 2 * EDGE, cols), jnp.float32),
            jax.ShapeDtypeStruct((3 * blocks, 128), jnp.float32),
        ),
        in_specs=[SMEM] * 4 + [VMEM] * 10,
        out_specs=(VMEM,) * 2,
        scratch_shapes=[
            pltpu.VMEM(mid.shape, jnp.float32),
            pltpu.VMEM(mid.shape, jnp.float32),
            pltpu.VMEM((3, atoms * fields, 8, 128), jnp.float32),
        ],
        compiler_params=params(10),
        name="gather_all",
    )(starts, *rot, strength, mid, low, high, img, low_img, high_img, *parts, *got)


def spread_sides(acc, starts_ref, low_coef, high_coef, low_img, high_img):
    atoms = low_img.shape[0]
    for j, coef, img, z in ((1, low_coef, low_img, 1), (2, high_coef, high_img, 0)):
        image = lambda a, part, k, img=img, z=z: img[a, z, part, 8 * k : 8 * k + 8]
        spread_into(acc, lambda a, j=j: starts_ref[j, a], coef, image, atoms)


def spread_all(acc, plane_ref, zsum_ref, starts_ref, coef_ref, images):
    fields = acc.shape[0]
    half = zsum_ref.shape[1]
    atoms = images[0][0].shape[0]
    blocks = coef_ref.shape[0] // 3
    inside = pl.ds(EDGE, half)
    if acc is not plane_ref:
        acc[:, 0:EDGE] = plane_ref[:, 0:EDGE]
        acc[:, EDGE + half :] = plane_ref[:, EDGE + half :]
    acc[:, inside] = plane_ref[:, inside] - 0.5 * zsum_ref[...]

    def atom(a, _):
        line = lax.div(a * fields, 128)
        lane = lax.rem(a * fields, 128)
        for j, (img, z) in enumerate(images):
            begin = pl.multiple_of(starts_ref[j, a], 8)
            for k in range(2):
                at = pl.ds(pl.multiple_of(begin + 8 * k, 8), 8)
                ire = img[a, z, 0, 8 * k : 8 * k + 8]
                iim = img[a, z, 1, 8 * k : 8 * k + 8]
                for n in range(fields // 2):
                    pr = coef_ref[j * blocks + line, lane + 2 * n]
                    pi = coef_ref[j * blocks + line, lane + 2 * n + 1]
                    acc[2 * n, at] = acc[2 * n, at] + (pr * ire + pi * iim)
                    acc[2 * n + 1, at] = acc[2 * n + 1, at] + (pi * ire - pr * iim)
        return 0

    lax.fori_loop(0, atoms, atom, 0)


def occupied_into(store, half, fields, sums_ref, side, own_ref, other_ref, base, scale, block, copies_of, start=None, ahead=0):
    count = own_ref.shape[0]

    def rows_of(b, _):
        at = pl.ds(pl.multiple_of(b * block, 8), block)
        for copy in copies_of(b):
            copy.wait()
        if start is not None:

            @pl.when(b + ahead < half // block)
            def _():
                start(b + ahead)

        def band(m, accs):
            accs = list(accs)
            for row, occ in ((side, own_ref), (1 - side, other_ref)):
                pr, pi = occ[m, 0, at], occ[m, 1, at]
                for n in range(fields // 2):
                    sr = sums_ref[row, m * fields + 2 * n]
                    si = sums_ref[row, m * fields + 2 * n + 1]
                    accs[2 * n] = accs[2 * n] + (pr * sr - pi * si)
                    accs[2 * n + 1] = accs[2 * n + 1] + (pr * si + pi * sr)
            return tuple(accs)

        zero = jnp.zeros((block, 128), jnp.float32)
        accs = lax.fori_loop(0, count, band, (zero,) * fields, unroll=2)
        for f in range(fields):
            store(f, b * block, base(f, b * block, block) + scale * accs[f])
        return 0

    lax.fori_loop(0, half // block, rows_of, 0)


def correlate_into(red, src, offset, half, own_ref, other_ref):
    fields = src.shape[0]
    count = own_ref.shape[0]
    bands = fields // 2

    def pair(g, _):
        def row(i, accs):
            at = rows8(i)
            moved = pl.ds(pl.multiple_of(i * 8 + offset, 8), 8)
            accs = list(accs)
            occ = []
            for ref in (own_ref, other_ref):
                for k in range(2):
                    occ.append((ref[2 * g + k, 0, at], ref[2 * g + k, 1, at]))
            for n in range(bands):
                re, im = src[2 * n, moved], src[2 * n + 1, moved]
                for q, (pr, pi) in enumerate(occ):
                    j = (q * bands + n) * 2
                    accs[j] = accs[j] + (pr * re + pi * im)
                    accs[j + 1] = accs[j + 1] + (pr * im - pi * re)
            return tuple(accs)

        zero = jnp.zeros((8, 128), jnp.float32)
        accs = lax.fori_loop(0, half // 8, row, (zero,) * (8 * bands), unroll=3)
        for q in range(4):
            for j in range(fields):
                red[q // 2, (2 * g + q % 2) * fields + j] = accs[q * fields + j]
        return 0

    lax.fori_loop(0, count // 2, pair, 0)


def dots_into(red_dot, half, fields, pairs):
    bands = fields // 2

    def row(i, accs):
        at = pl.ds(pl.multiple_of(i * 8 + EDGE, 8), 8)
        accs = list(accs)
        for p, (left, right) in enumerate(pairs):
            for n in range(bands):
                value = left[2 * n, at] * right[2 * n, at] + left[2 * n + 1, at] * right[2 * n + 1, at]
                accs[p * bands + n] = accs[p * bands + n] + value
        return tuple(accs)

    zero = jnp.zeros((8, 128), jnp.float32)
    accs = lax.fori_loop(0, half // 8, row, (zero,) * (bands * len(pairs)), unroll=3)
    for j in range(bands * len(pairs)):
        red_dot[j] = accs[j]


def pick_block(half):
    return next(b for b in (24, 16, 8) if half % b == 0)


def shift_rows(start, size):
    return pl.ds(pl.multiple_of(start + EDGE, 8), size)


def band_copies(which_ref, half, block, b, occ_ref, other_refs, own, other, sems):
    begin = pl.multiple_of(which_ref[0] * half + b * block, 8)
    at = pl.ds(pl.multiple_of(b * block, 8), block)
    copies = [pltpu.make_async_copy(occ_ref.at[:, :, pl.ds(begin, block)], own.at[:, :, at], sems.at[0, b])]
    first = 0
    for j, ref in enumerate(other_refs):
        last = first + ref.shape[0]
        copies.append(pltpu.make_async_copy(ref.at[:, :, at], other.at[first:last, :, at], sems.at[1 + j, b]))
        first = last
    return tuple(copies)


def start_bands(half, block, copies_of):
    for b in range(half // block):
        for copy in copies_of(b):
            copy.start()


def write_sums(sum_ref, side, red):
    mine, theirs = sum_rows(red[0]), sum_rows(red[1])
    sum_ref[...] = jnp.zeros(sum_ref.shape, jnp.float32)
    sum_ref[0:1] = jnp.where(side == 0, mine, theirs)
    sum_ref[1:2] = jnp.where(side == 0, theirs, mine)


def write_edges(edge_ref, out_ref, half):
    for f in range(out_ref.shape[0]):
        edge_ref[f, 0:EDGE] = out_ref[f, EDGE : 2 * EDGE]
        edge_ref[f, EDGE : 2 * EDGE] = out_ref[f, half : half + EDGE]


def residual_kernel(scale, which_ref, starts_ref, low_coef, high_coef, sums_ref, lap_ref, low_ref, high_ref,
                    occ_ref, other_a, other_b, resp_hbm, pot_hbm, out_ref, edge_ref, sum_ref,
                    acc, own, other, resp, pot, red, red_dot, sems, more_sems):
    fields, wide, cols = out_ref.shape
    half = wide - 2 * EDGE
    side = which_ref[0]
    block = pick_block(half)
    begin = pl.multiple_of(side * half, 8)
    copies = (
        pltpu.make_async_copy(resp_hbm.at[:, :, pl.ds(begin, half)], resp, more_sems.at[0]),
        pltpu.make_async_copy(pot_hbm.at[:, pl.ds(begin, half)], pot, more_sems.at[1]),
    )
    for copy in copies:
        copy.start()
    copies_of = lambda b: band_copies(which_ref, half, block, b, occ_ref, (other_a, other_b), own, other, sems)
    start_bands(half, block, copies_of)
    acc[...] = lap_ref[...]
    spread_sides(acc, starts_ref, low_coef, high_coef, low_ref, high_ref)
    for copy in copies:
        copy.wait()

    def base(f, start, size):
        at = pl.ds(pl.multiple_of(start, 8), size)
        re, im = resp[f // 2, 0, at], resp[f // 2, 1, at]
        if f % 2 == 0:
            prod = pot[0, at] * re - pot[1, at] * im
        else:
            prod = pot[0, at] * im + pot[1, at] * re
        return -prod - acc[f, shift_rows(start, size)]

    def store(f, start, value):
        out_ref[f, shift_rows(start, block)] = value

    occupied_into(store, half, fields, sums_ref, side, own, other, base, scale, block, copies_of)
    write_edges(edge_ref, out_ref, half)
    correlate_into(red, out_ref, EDGE, half, own, other)
    dots_into(red_dot, half, fields, [(out_ref, out_ref)])
    write_sums(sum_ref, side, red)
    sum_ref[2:3] = sum_rows(red_dot[0 : fields // 2])


def field_outputs(fields, half, cols):
    return (
        jax.ShapeDtypeStruct((fields, half + 2 * EDGE, cols), jnp.float32),
        jax.ShapeDtypeStruct((fields, 2 * EDGE, cols), jnp.float32),
        jax.ShapeDtypeStruct((8, 128), jnp.float32),
    )


def residual_call(scale, which, starts, low_coef, high_coef, sums, lap, low_img, high_img, psi_occ, other, resp, pot):
    fields, long, cols = lap.shape
    half = long - 2 * EDGE - WIN
    return pl.pallas_call(
        functools.partial(residual_kernel, scale),
        out_shape=field_outputs(fields, half, cols),
        in_specs=[SMEM] * 5 + [VMEM] * 3 + [HBM] * 5,
        out_specs=(VMEM,) * 3,
        scratch_shapes=[
            pltpu.VMEM(lap.shape, jnp.float32),
            pltpu.VMEM(psi_occ.shape[:2] + (half, cols), jnp.float32),
            pltpu.VMEM(psi_occ.shape[:2] + (half, cols), jnp.float32),
            pltpu.VMEM(resp.shape[:2] + (half, cols), jnp.float32),
            pltpu.VMEM((2, half, cols), jnp.float32),
            pltpu.VMEM((2, 128, 8, 128), jnp.float32),
            pltpu.VMEM((16, 8, 128), jnp.float32),
            pltpu.SemaphoreType.DMA((3, half // pick_block(half))),
            pltpu.SemaphoreType.DMA((2,)),
        ],
        compiler_params=params(16),
        name="residual",
    )(which, starts, low_coef, high_coef, sums, lap, low_img, high_img, psi_occ, *other, resp, pot)


def image_kernel(scale, which_ref, starts_ref, low_coef, high_coef, sums_ref, lap_ref, low_ref, high_ref,
                 res_ref, occ_ref, other_a, other_b, out_ref, edge_ref, sum_ref,
                 acc, own, other, red, red_dot, sems):
    fields, wide, cols = out_ref.shape
    half = wide - 2 * EDGE
    side = which_ref[0]
    block = pick_block(half)
    copies_of = lambda b: band_copies(which_ref, half, block, b, occ_ref, (other_a, other_b), own, other, sems)
    start_bands(half, block, copies_of)
    acc[...] = lap_ref[...]
    spread_sides(acc, starts_ref, low_coef, high_coef, low_ref, high_ref)

    def base(f, start, size):
        return acc[f, shift_rows(start, size)]

    def store(f, start, value):
        out_ref[f, shift_rows(start, block)] = value

    occupied_into(store, half, fields, sums_ref, side, own, other, base, scale, block, copies_of)
    write_edges(edge_ref, out_ref, half)
    correlate_into(red, out_ref, EDGE, half, own, other)
    dots_into(red_dot, half, fields, [(res_ref, out_ref), (out_ref, out_ref)])
    write_sums(sum_ref, side, red)
    sum_ref[2:3] = sum_rows(red_dot[0:fields])


def image_call(scale, which, starts, low_coef, high_coef, sums, lap, low_img, high_img, res, psi_occ, other):
    fields, long, cols = lap.shape
    half = long - 2 * EDGE - WIN
    return pl.pallas_call(
        functools.partial(image_kernel, scale),
        out_shape=field_outputs(fields, half, cols),
        in_specs=[SMEM] * 5 + [VMEM] * 4 + [HBM] * 3,
        out_specs=(VMEM,) * 3,
        scratch_shapes=[
            pltpu.VMEM(lap.shape, jnp.float32),
            pltpu.VMEM(psi_occ.shape[:2] + (half, cols), jnp.float32),
            pltpu.VMEM(psi_occ.shape[:2] + (half, cols), jnp.float32),
            pltpu.VMEM((2, 128, 8, 128), jnp.float32),
            pltpu.VMEM((16, 8, 128), jnp.float32),
            pltpu.SemaphoreType.DMA((3, half // pick_block(half))),
        ],
        compiler_params=params(16),
        name="image",
    )(which, starts, low_coef, high_coef, sums, lap, low_img, high_img, res, psi_occ, *other)


def local_kernel(starts_ref, coef_ref, plane_ref, zsum_ref, img_ref, low_ref, high_ref, field_ref, part_ref,
                 out_ref, sum_ref, red_dot):
    fields = out_ref.shape[0]
    half = zsum_ref.shape[1]
    spread_all(out_ref, plane_ref, zsum_ref, starts_ref, coef_ref, ((img_ref, 1), (low_ref, 1), (high_ref, 0)))
    dots_into(red_dot, half, fields, [(field_ref, out_ref)])
    sum_ref[...] = part_ref[...]
    sum_ref[3:4] = sum_rows(red_dot[0 : fields // 2])


def local_call(starts, local, images, field, part):
    coef, plane, zsum = local
    return pl.pallas_call(
        local_kernel,
        out_shape=(
            jax.ShapeDtypeStruct(plane.shape, jnp.float32),
            jax.ShapeDtypeStruct((8, 128), jnp.float32),
        ),
        in_specs=[SMEM] * 2 + [VMEM] * 7,
        out_specs=(VMEM, VMEM),
        scratch_shapes=[pltpu.VMEM((16, 8, 128), jnp.float32)],
        compiler_params=params(10),
        name="local",
    )(starts, coef, plane, zsum, *images, field, part)


def last_kernel(which_ref, sums_ref, mix_ref, res_hbm, first_hbm, second_hbm, occ_ref, other_a, other_b,
                out_ref, res, first, second, own, other, sems, more_sems):
    fields, half, cols = out_ref.shape
    side = which_ref[0]
    block = pick_block(half)

    def copies_of(b):
        at = pl.ds(pl.multiple_of(b * block, 8), block)
        moved = shift_rows(b * block, block)
        own_copies = tuple(
            pltpu.make_async_copy(src.at[:, moved], dst.at[:, at], more_sems.at[j, b])
            for j, (src, dst) in enumerate(((res_hbm, res), (first_hbm, first), (second_hbm, second)))
        )
        return own_copies + band_copies(which_ref, half, block, b, occ_ref, (other_a, other_b), own, other, sems)

    ahead = 2

    def start(b):
        for copy in copies_of(b):
            copy.start()

    for b in range(ahead):
        start(b)

    def base(f, start, size):
        n = f // 2
        at = pl.ds(pl.multiple_of(start, 8), size)
        return res[f, at] + mix_ref[0, n] * first[f, at] + mix_ref[1, n] * second[f, at]

    def store(f, start, value):
        out_ref[f, pl.ds(pl.multiple_of(start, 8), block)] = value

    occupied_into(store, half, fields, sums_ref, side, own, other, base, 1.0, block, copies_of, start, ahead)


def last_call(which, sums, mix, res, first, second, psi_occ, other):
    fields, wide, cols = res.shape
    half = wide - 2 * EDGE
    blocks = half // pick_block(half)
    field = pltpu.VMEM((fields, half, cols), jnp.float32)
    return pl.pallas_call(
        last_kernel,
        out_shape=jax.ShapeDtypeStruct((fields, half, cols), jnp.float32),
        in_specs=[SMEM] * 3 + [HBM] * 6,
        out_specs=VMEM,
        scratch_shapes=[
            field,
            field,
            field,
            pltpu.VMEM(psi_occ.shape[:2] + (half, cols), jnp.float32),
            pltpu.VMEM(psi_occ.shape[:2] + (half, cols), jnp.float32),
            pltpu.SemaphoreType.DMA((3, blocks)),
            pltpu.SemaphoreType.DMA((3, blocks)),
        ],
        compiler_params=params(52),
        name="last",
    )(which, sums, mix, res, first, second, psi_occ, *other)


def xor_sum(block, bits):
    count = lax.axis_size("space") * lax.axis_size("occ")
    masks = [0]
    for bit in bits:
        masks = masks + [mask | bit for mask in masks]
    parts = [block]
    for mask in masks[1:]:
        parts.append(lax.ppermute(block, ("space", "occ"), [(i, i ^ mask) for i in range(count)]))
    while len(parts) > 1:
        parts = [parts[j] + parts[j + 1] for j in range(0, len(parts), 2)]
    return parts[0]


def total(block, groups=None):
    count = lax.axis_size("space")
    bit = 2
    steps = []
    while count > 1:
        wide = count % 4 == 0
        steps.append((bit, 2 * bit) if wide else (bit,))
        bit, count = (4 * bit, count // 4) if wide else (2 * bit, count // 2)
    steps.append((1,))
    for bits in steps[groups] if groups is not None else steps:
        block = xor_sum(block, bits)
    return block


def exchange(block):
    return lax.ppermute(block, "occ", SWAP)


def from_behind(block, distance):
    count = lax.axis_size("space")
    return lax.ppermute(block, "space", [((i - distance) % count, i) for i in range(count)])


def window_images(x_cell, y_cell, offsets, values, theta_y, rows_y, planes):
    y_raw = y_cell[:, None] + offsets[None, :, 2]
    y_wrap = jnp.floor_divide(y_raw, rows_y)
    y_at = y_raw - y_wrap * rows_y
    angles = theta_y * y_wrap.astype(jnp.float32)
    row = x_cell[:, None] + offsets[None, :, 1] + RAD
    slot = []
    for plane in planes:
        wanted = (row[:, None, :] == jnp.arange(WIN, dtype=jnp.int32)[None, :, None]) & (
            offsets[:, 0] == plane
        )[None, None, :]
        slot.append(wanted)
    slots = jnp.stack(slot, axis=1)
    weights = jnp.stack([values * jnp.cos(angles), values * jnp.sin(angles)], axis=1)
    left = jnp.where(slots[:, :, None], weights[:, None, :, None, :], 0.0)
    atoms = left.shape[0]
    left = left.reshape(atoms, len(planes) * 2 * WIN, -1)
    right = (y_at[:, :, None] == jnp.arange(rows_y, dtype=jnp.int32)[None, None, :]).astype(jnp.float32)
    image = jnp.einsum("apk,aky->apy", left, right, precision=PRECISE)
    return image.reshape(atoms, len(planes), 2, WIN, rows_y)


def shards(
    psi_occ,
    psi_resp,
    initial_guess,
    local_potential,
    potential_change,
    band_energy,
    q_index,
    atom_cells,
    offsets,
    projector,
    strength,
):
    slab_count = lax.axis_size("space")
    slab_index = lax.axis_index("space")
    side = lax.axis_index("occ")
    layers, rows_x, rows_y = local_potential.shape
    half = rows_x // 2
    atoms = atom_cells.shape[0]
    bands = psi_resp.shape[0]
    fields = 2 * bands
    weight = 1.0 / (layers * slab_count * rows_x * rows_y)
    thetas = q_index.astype(jnp.float32) * (2.0 * math.pi / QDIV)
    which = side.astype(jnp.int32).reshape(1)
    where = jnp.stack([side, slab_index]).astype(jnp.int32)

    occ = psi_occ.reshape(psi_occ.shape[0], 2, rows_x, rows_y)
    resp = psi_resp.reshape(bands, 2, rows_x, rows_y)
    guess = initial_guess.reshape(bands, 2, rows_x, rows_y)
    change = potential_change.reshape(2, rows_x, rows_y)

    cell_rows = jnp.pad(
        jnp.concatenate([atom_cells.astype(jnp.float32), strength[:, None]], axis=1),
        ((0, 0), (0, projector.shape[1] - 4)),
    )
    packed = jnp.concatenate([projector, cell_rows], axis=0)
    guess_mid, *rot = prep_call(slab_count, where, q_index, guess, packed)
    first_sums, *occ_send = first_corr(which, occ, resp, change, guess)
    occ_other = [exchange(block) for block in occ_send]
    first_sums = total(first_sums, slice(0, 1))
    first_sums, guess_mid = lax.optimization_barrier((first_sums, guess_mid))
    first_sums = xor_sum(xor_sum(first_sums, (8,)), (16,))
    first_sums = xor_sum(first_sums, (32,))
    first_sums, occ_other[0] = lax.optimization_barrier((first_sums, occ_other[0]))
    first_sums = xor_sum(first_sums, (64,))
    guess_low = from_behind(guess_mid, 1)
    guess_high = from_behind(guess_mid, -1)

    def unpack(block):
        rows = block[:, half + 2 * EDGE :].reshape(-1, rows_y)
        return rows[:atoms], rows[atoms : 2 * atoms]

    below, below_cells = unpack(guess_low)
    above, above_cells = unpack(guess_high)
    cells = [atom_cells]
    for rows in (below_cells, above_cells):
        cells.append(rows[:, :3].astype(jnp.int32))
    all_x = jnp.stack([c[:, 1] for c in cells])
    all_y = jnp.stack([c[:, 2] for c in cells])
    at_row = jnp.mod(all_x - RAD - side * half + EDGE, rows_x)
    inner = at_row % 8
    touching = at_row < half + EDGE
    put_starts = jnp.where(touching, at_row - inner, half + 2 * EDGE).astype(jnp.int32)
    get_starts = jnp.where(touching, at_row - inner, 0).astype(jnp.int32)
    own_row = jnp.mod(atom_cells[:, 1] - RAD - side * half + EDGE, rows_x)
    own_inner = own_row % 8
    own_starts = jnp.where(own_row < half + EDGE, own_row - own_inner, 0).astype(jnp.int32)
    strengths = jnp.stack([strength, below_cells[:, 3], above_cells[:, 3]])
    img = window_images(own_inner, atom_cells[:, 2], offsets, projector, thetas[2], rows_y, (-1, 0, 1))
    low_img = window_images(inner[1], all_y[1], offsets, below, thetas[2], rows_y, (0, 1))
    high_img = window_images(inner[2], all_y[2], offsets, above, thetas[2], rows_y, (-1, 0))
    images = (img, low_img, high_img)

    def local_part(mid, low, high):
        zsum, proj, up, down = gather(own_starts, rot, strength, mid, low, high, img, half)
        low_coef = from_behind(up, 1)
        high_coef = from_behind(down, -1)
        lap = stencil(which, band_energy, rot, put_starts, proj, mid, zsum, local_potential, img)
        return put_starts, low_coef, high_coef, lap

    def far_part(mid):
        low = from_behind(mid, 1)
        high = from_behind(mid, -1)
        plane, part_low, part_high, down, up = plane_call(
            which, band_energy, get_starts, rot, strengths, mid, local_potential, low_img, high_img
        )
        got = (from_behind(up, 2), from_behind(down, -2))
        zsum, coef = gather_all(get_starts, rot, strengths, mid, low, high, *images, (part_low, part_high), got)
        return coef, plane, zsum

    starts, low_coef, high_coef, lap = local_part(guess_mid, guess_low, guess_high)
    first_sums, lap = lax.optimization_barrier((first_sums, lap))
    first_sums = total(first_sums, slice(-1, None))
    residual, edges, part = residual_call(
        weight, which, starts, low_coef, high_coef, first_sums, lap, low_img, high_img, occ, occ_other, resp, change
    )
    tot = total(part)
    norm0 = tot[2, :bands]
    residual = fill_call(rot, exchange(edges), residual)
    starts, low_coef, high_coef, lap = local_part(residual, from_behind(residual, 1), from_behind(residual, -1))
    image, edges, part = image_call(
        SHIFT_WEIGHT * weight, which, starts, low_coef, high_coef, tot, lap, low_img, high_img, residual, occ, occ_other
    )
    image = fill_call(rot, exchange(edges), image)
    image_other = exchange(image)
    image2, part = local_call(put_starts, far_part(image), images, image, part)
    part, image_other, residual_send = lax.optimization_barrier((part, image_other, residual))
    residual_other = exchange(residual_send)
    tot = total(part, slice(0, 2))
    tot, residual_other = lax.optimization_barrier((tot, residual_other))
    tot = total(tot, slice(2, None))
    sums = tot[0:2]
    cross = tot[2, :bands]
    square = tot[2, bands : 2 * bands]
    occ_square = jnp.sum((sums * sums).reshape(-1, bands, 2), axis=(0, 2))
    triple = tot[3, :bands] + SHIFT_WEIGHT * weight * occ_square
    step0 = norm0 / cross
    norm1 = norm0 - 2.0 * step0 * cross + step0 * step0 * square
    growth = norm1 / norm0
    lead = 1.0 + growth
    curvature = lead * lead * cross - 2.0 * lead * step0 * square + step0 * step0 * triple
    step1 = norm1 / curvature
    mix0 = -step0 - step1 * lead
    mix1 = step1 * step0
    per_lane = jnp.tile(jnp.repeat(mix1, 2), sums.shape[1] // fields)
    last_sums = SHIFT_WEIGHT * weight * sums * per_lane[None, :]
    mine = last_call(which, last_sums, jnp.stack([mix0, mix1]), residual, image, image2, occ, occ_other)
    mine, residual_other, image_other = lax.optimization_barrier((mine, residual_other, image_other))
    theirs = exchange(mine)

    def join(own_half, other_half):
        lower = jnp.where(side == 0, own_half, other_half)
        upper = jnp.where(side == 0, other_half, own_half)
        return jnp.concatenate([lower, upper], axis=1).reshape(bands, 2, 1, rows_x, rows_y)

    inside = lambda v: v[:, EDGE : EDGE + half]
    wide = lambda v: v[:, None, None, None, None]
    response = (
        initial_guess
        + wide(step0 + step1 * lead) * join(inside(residual), inside(residual_other))
        - wide(step0 * step1) * join(inside(image), inside(image_other))
    )
    return response, join(mine, theirs)


def solution(mesh):
    return jax.shard_map(
        shards,
        mesh=mesh,
        in_specs=(
            P("occ", None, "space", None, None),
            P("resp", None, "space", None, None),
            P("resp", None, "space", None, None),
            P("space", None, None),
            P(None, "space", None, None),
            P("resp"),
            P(),
            P("space", None),
            P(),
            P("space", None),
            P("space"),
        ),
        out_specs=(P("resp", None, "space", None, None), P("resp", None, "space", None, None)),
        check_vma=False,
    )
```

```python
import functools
import math

import jax
import jax.numpy as jnp
from jax import lax
from jax.experimental import pallas as pl
from jax.experimental.pallas import tpu as pltpu
from jax.sharding import PartitionSpec as P

RAD = 4
QDIV = 8
EDGE = 8
WIN = 16
SHIFT_WEIGHT = 3.0
PRECISE = lax.Precision.HIGHEST
SWAP = [(0, 1), (1, 0)]

VMEM = pl.BlockSpec(memory_space=pltpu.VMEM)
SMEM = pl.BlockSpec(memory_space=pltpu.SMEM)
ANY = pl.BlockSpec(memory_space=pl.ANY)
HBM = pl.BlockSpec(memory_space=pltpu.HBM)


def params(mib):
    return pltpu.CompilerParams(vmem_limit_bytes=mib * 1024 * 1024)


def sum_rows(values):
    total = jnp.sum(values, axis=2, keepdims=True)
    row = lax.broadcasted_iota(jnp.int32, values.shape, 0)
    lane = lax.broadcasted_iota(jnp.int32, values.shape, 2)
    picked = jnp.sum(jnp.where(row == lane, total, 0.0), axis=0)
    return jnp.sum(picked, axis=0, keepdims=True)


def rows8(index):
    return pl.ds(pl.multiple_of(index * 8, 8), 8)


def extra_rows(count, fields):
    return -(-count // (8 * fields)) * 8


AXES = (0, 0, 0, 0, 1, 1, 2, 0, 0)
SIGNS = (-1, 1, 1, -1, -1, 1, 1, -1, 1)
TURNS = [2.0 * math.pi * k / QDIV for k in range(QDIV)]


def prep_kernel(slab_count, where_ref, q_ref, guess_ref, atoms_ref, out_ref, cos_ref, sin_ref, middle, low, high, sems):
    fields = out_ref.shape[0]
    half = middle.shape[2]
    wide = half + 2 * EDGE
    side, slab = where_ref[0], where_ref[1]
    begin = pl.multiple_of(side * half, 8)
    away = pl.multiple_of((1 - side) * half, 8)
    under = pl.multiple_of((1 - side) * half + half - EDGE, 8)
    copies = []
    for j, (start, size, dst) in enumerate(((begin, half, middle), (under, EDGE, low), (away, EDGE, high))):
        copies.append(pltpu.make_async_copy(guess_ref.at[:, :, pl.ds(start, size)], dst, sems.at[j]))
    for copy in copies:
        copy.start()

    first, last = slab == 0, slab == slab_count - 1
    flags = (first, last, slab < 2, slab >= slab_count - 2, side == 0, side == 1, slab >= 0, last, first)
    for j, (flag, sign, axis) in enumerate(zip(flags, SIGNS, AXES)):
        step = jnp.where(flag, jnp.bitwise_and(sign * q_ref[axis], QDIV - 1), 0)
        cosine, sine = jnp.float32(1.0), jnp.float32(0.0)
        for k in range(1, QDIV):
            cosine = jnp.where(step == k, jnp.float32(math.cos(TURNS[k])), cosine)
            sine = jnp.where(step == k, jnp.float32(math.sin(TURNS[k])), sine)
        cos_ref[j] = cosine
        sin_ref[j] = sine

    for f in range(fields):
        for r in range(0, out_ref.shape[1] - wide, 8):
            at = f * (out_ref.shape[1] - wide) + r
            if at < atoms_ref.shape[0]:
                out_ref[f, wide + r : wide + r + 8] = atoms_ref[at : at + 8]
            else:
                out_ref[f, wide + r : wide + r + 8] = jnp.zeros((8, 128), jnp.float32)
    for copy in copies:
        copy.wait()
    for n in range(fields // 2):
        for k in range(2):
            out_ref[2 * n + k, EDGE : EDGE + half] = middle[n, k]
        for src, spot, j in ((low, 0, 4), (high, EDGE + half, 5)):
            c, s = cos_ref[j], sin_ref[j]
            re, im = src[n, 0], src[n, 1]
            out_ref[2 * n, spot : spot + EDGE] = re * c - im * s
            out_ref[2 * n + 1, spot : spot + EDGE] = re * s + im * c


def prep_call(slab_count, where, q_index, guess, atoms):
    bands, _, rows, cols = guess.shape
    half = rows // 2
    extra = extra_rows(atoms.shape[0], 2 * bands)
    table = jax.ShapeDtypeStruct((len(AXES),), jnp.float32)
    return pl.pallas_call(
        functools.partial(prep_kernel, slab_count),
        out_shape=(
            jax.ShapeDtypeStruct((2 * bands, half + 2 * EDGE + extra, cols), jnp.float32),
            table,
            table,
        ),
        in_specs=[SMEM, SMEM, HBM, VMEM],
        out_specs=(VMEM, SMEM, SMEM),
        scratch_shapes=[
            pltpu.VMEM((bands, 2, half, cols), jnp.float32),
            pltpu.VMEM((bands, 2, EDGE, cols), jnp.float32),
            pltpu.VMEM((bands, 2, EDGE, cols), jnp.float32),
            pltpu.SemaphoreType.DMA((3,)),
        ],
        compiler_params=params(8),
        name="prep",
    )(where, q_index, guess, atoms)


def fill_kernel(cos_ref, sin_ref, got_ref, ext_ref, out_ref, low, high, sems):
    fields, wide, _ = out_ref.shape
    for n in range(fields // 2):
        for dst, at, j in ((low, EDGE, 4), (high, 0, 5)):
            c, s = cos_ref[j], sin_ref[j]
            re, im = got_ref[2 * n, at : at + EDGE], got_ref[2 * n + 1, at : at + EDGE]
            dst[2 * n] = re * c - im * s
            dst[2 * n + 1] = re * s + im * c
    one = pltpu.make_async_copy(low, out_ref.at[:, 0:EDGE], sems.at[0])
    two = pltpu.make_async_copy(high, out_ref.at[:, wide - EDGE : wide], sems.at[1])
    one.start()
    two.start()
    one.wait()
    two.wait()


def fill_call(rot, got, ext):
    shape = (ext.shape[0], EDGE, ext.shape[2])
    return pl.pallas_call(
        fill_kernel,
        out_shape=jax.ShapeDtypeStruct(ext.shape, jnp.float32),
        in_specs=[SMEM, SMEM, VMEM, ANY],
        out_specs=ANY,
        scratch_shapes=[
            pltpu.VMEM(shape, jnp.float32),
            pltpu.VMEM(shape, jnp.float32),
            pltpu.SemaphoreType.DMA((2,)),
        ],
        input_output_aliases={3: 0},
        compiler_params=params(4),
        name="fill",
    )(*rot, got, ext)


def first_corr_kernel(which_ref, occ_ref, resp_ref, pot_ref, guess_ref, out_ref, send_a, send_b, mixed, red):
    bands, _, rows, _ = resp_ref.shape
    group = occ_ref.shape[0]
    step = pl.program_id(0)
    half = send_a.shape[2]
    middle = pl.num_programs(0) // 2
    away = pl.ds(pl.multiple_of((1 - which_ref[0]) * half, 8), half)

    @pl.when(step < middle)
    def _():
        send_a[...] = occ_ref[:, :, away]

    @pl.when(step >= middle)
    def _():
        send_b[...] = occ_ref[:, :, away]

    @pl.when(step == 0)
    def _():
        for n in range(bands):
            re = resp_ref[n, 0]
            im = resp_ref[n, 1]
            mixed[2 * n] = pot_ref[0] * re - pot_ref[1] * im - SHIFT_WEIGHT * guess_ref[n, 0]
            mixed[2 * n + 1] = pot_ref[0] * im + pot_ref[1] * re - SHIFT_WEIGHT * guess_ref[n, 1]

    def row(i, accs):
        at = rows8(i)
        occ = [(occ_ref[k, 0, at], occ_ref[k, 1, at]) for k in range(group)]
        accs = list(accs)
        for n in range(bands):
            re, im = mixed[2 * n, at], mixed[2 * n + 1, at]
            for k, (pr, pi) in enumerate(occ):
                j = (k * bands + n) * 2
                accs[j] = accs[j] + (pr * re + pi * im)
                accs[j + 1] = accs[j + 1] + (pr * im - pi * re)
        return tuple(accs)

    zero = jnp.zeros((8, 128), jnp.float32)
    count = 2 * bands * group
    accs = lax.fori_loop(0, rows // 8, row, (zero,) * count, unroll=3)
    for j in range(count):
        red[step * count + j] = accs[j]

    @pl.when(step == pl.num_programs(0) - 1)
    def _():
        out_ref[...] = jnp.zeros(out_ref.shape, jnp.float32)
        total = sum_rows(red[...])
        side = which_ref[0]
        out_ref[0:1] = jnp.where(side == 0, total, 0.0)
        out_ref[1:2] = jnp.where(side == 0, 0.0, total)


def first_corr(which, psi_occ, psi_resp, pot, guess):
    group = 4
    count, _, rows, cols = psi_occ.shape
    fixed = lambda shape: pl.BlockSpec(shape, lambda i: (0,) * len(shape))
    middle = count // group // 2
    send = jax.ShapeDtypeStruct((count // 2, 2, rows // 2, cols), jnp.float32)
    shape = (group, 2, rows // 2, cols)
    return pl.pallas_call(
        first_corr_kernel,
        out_shape=(
            jax.ShapeDtypeStruct((8, 128), jnp.float32),
            send,
            send,
        ),
        grid=(count // group,),
        in_specs=[
            SMEM,
            pl.BlockSpec((group, 2, rows, cols), lambda i: (i, 0, 0, 0)),
            fixed(psi_resp.shape),
            fixed(pot.shape),
            fixed(guess.shape),
        ],
        out_specs=(
            fixed((8, 128)),
            pl.BlockSpec(shape, lambda i: (jnp.minimum(i, middle - 1), 0, 0, 0)),
            pl.BlockSpec(shape, lambda i: (jnp.maximum(i - middle, 0), 0, 0, 0)),
        ),
        scratch_shapes=[
            pltpu.VMEM((psi_resp.shape[0] * 2, rows, cols), jnp.float32),
            pltpu.VMEM((128, 8, 128), jnp.float32),
        ],
        compiler_params=params(60),
        name="first_corr",
    )(which, psi_occ, psi_resp, pot, guess)


def gather_kernel(start_ref, cos_ref, sin_ref, str_ref, mid_ref, low_ref, high_ref, img_ref,
                  zsum_ref, out_ref, up_ref, down_ref, low, high, red):
    fields = mid_ref.shape[0]
    half = zsum_ref.shape[1]
    wide = half + 2 * EDGE
    for n in range(fields // 2):
        for src, dst, j in ((low_ref, low, 0), (high_ref, high, 1)):
            c, s = cos_ref[j], sin_ref[j]
            re, im = src[2 * n, 0:wide], src[2 * n + 1, 0:wide]
            dst[2 * n] = re * c - im * s
            dst[2 * n + 1] = re * s + im * c
        for k in range(2):
            f = 2 * n + k
            zsum_ref[f] = low[f, EDGE : EDGE + half] + high[f, EDGE : EDGE + half]
    atoms = img_ref.shape[0]

    def atom(a, _):
        begin = pl.multiple_of(start_ref[a], 8)
        accs = [jnp.zeros((8, 128), jnp.float32)] * fields
        for z, src in enumerate((low, mid_ref, high)):
            for k in range(2):
                at = pl.ds(pl.multiple_of(begin + 8 * k, 8), 8)
                ire = img_ref[a, z, 0, 8 * k : 8 * k + 8]
                iim = img_ref[a, z, 1, 8 * k : 8 * k + 8]
                for n in range(fields // 2):
                    re, im = src[2 * n, at], src[2 * n + 1, at]
                    accs[2 * n] = accs[2 * n] + (re * ire - im * iim)
                    accs[2 * n + 1] = accs[2 * n + 1] + (re * iim + im * ire)
        for f in range(fields):
            red[a * fields + f] = accs[f] * str_ref[a]
        return 0

    lax.fori_loop(0, atoms, atom, 0)
    total = atoms * fields
    value = lanes_of(red, total, out_ref.shape[0])
    out_ref[...] = value
    up_ref[...] = turn_lanes(value, cos_ref[7], sin_ref[7])
    down_ref[...] = turn_lanes(value, cos_ref[8], sin_ref[8])


def gather(starts, rot, strength, mid, low, high, img, half):
    fields, _, cols = mid.shape
    rows = half + 2 * EDGE
    atoms = img.shape[0]
    blocks = -(-atoms * fields // 128)
    coef = jax.ShapeDtypeStruct((blocks, 128), jnp.float32)
    return pl.pallas_call(
        gather_kernel,
        out_shape=(
            jax.ShapeDtypeStruct((fields, rows - 2 * EDGE, cols), jnp.float32),
            coef,
            coef,
            coef,
        ),
        in_specs=[SMEM] * 4 + [VMEM] * 4,
        out_specs=(VMEM,) * 4,
        scratch_shapes=[
            pltpu.VMEM((fields, rows, cols), jnp.float32),
            pltpu.VMEM((fields, rows, cols), jnp.float32),
            pltpu.VMEM((atoms * fields, 8, 128), jnp.float32),
        ],
        compiler_params=params(10),
        name="gather",
    )(starts, *rot, strength, mid, low, high, img)


def spread_into(acc, start_of, coef_ref, image_of, atoms):
    fields = acc.shape[0]

    def atom(a, _):
        begin = pl.multiple_of(start_of(a), 8)
        line = lax.div(a * fields, 128)
        lane = lax.rem(a * fields, 128)
        for k in range(2):
            at = pl.ds(pl.multiple_of(begin + 8 * k, 8), 8)
            ire = image_of(a, 0, k)
            iim = image_of(a, 1, k)
            for n in range(fields // 2):
                pr = coef_ref[line, lane + 2 * n]
                pi = coef_ref[line, lane + 2 * n + 1]
                acc[2 * n, at] = acc[2 * n, at] + (pr * ire + pi * iim)
                acc[2 * n + 1, at] = acc[2 * n + 1, at] + (pi * ire - pr * iim)
        return 0

    lax.fori_loop(0, atoms, atom, 0)


def stencil_kernel(which_ref, energy_ref, cos_ref, sin_ref, starts_ref, coef_ref, mid_ref, zsum_ref, pot_ref, img_ref, out_ref):
    fields, half, cols = zsum_ref.shape
    lane = lax.broadcasted_iota(jnp.int32, (half, cols), 1)
    first, last = lane == 0, lane == cols - 1
    c, s = cos_ref[6], sin_ref[6]
    pot = pot_ref[0, pl.ds(pl.multiple_of(which_ref[0] * half, 8), half)] + 3.0
    for n in range(fields // 2):
        re = mid_ref[2 * n, EDGE : EDGE + half]
        im = mid_ref[2 * n + 1, EDGE : EDGE + half]
        re_next, im_next = pltpu.roll(re, cols - 1, 1), pltpu.roll(im, cols - 1, 1)
        re_prev, im_prev = pltpu.roll(re, 1, 1), pltpu.roll(im, 1, 1)
        y_re = jnp.where(last, re_next * c - im_next * s, re_next) + jnp.where(
            first, re_prev * c + im_prev * s, re_prev
        )
        y_im = jnp.where(last, re_next * s + im_next * c, im_next) + jnp.where(
            first, im_prev * c - re_prev * s, im_prev
        )
        scale = pot - energy_ref[n]
        for f, value, beside in ((2 * n, re, y_re), (2 * n + 1, im, y_im)):
            beside = beside + zsum_ref[f]
            beside = beside + mid_ref[f, EDGE - 1 : EDGE - 1 + half]
            beside = beside + mid_ref[f, EDGE + 1 : EDGE + 1 + half]
            out_ref[f, EDGE : EDGE + half] = scale * value - 0.5 * beside
            out_ref[f, 0:EDGE] = jnp.zeros((EDGE, cols), jnp.float32)
            out_ref[f, EDGE + half :] = jnp.zeros((EDGE + WIN, cols), jnp.float32)
    atoms = img_ref.shape[0]
    image = lambda a, part, k: img_ref[a, 1, part, 8 * k : 8 * k + 8]
    spread_into(out_ref, lambda a: starts_ref[0, a], coef_ref, image, atoms)


def stencil(which, energy, rot, starts, coef, mid, zsum, pot, img):
    fields, half, cols = zsum.shape
    return pl.pallas_call(
        stencil_kernel,
        out_shape=jax.ShapeDtypeStruct((fields, half + 2 * EDGE + WIN, cols), jnp.float32),
        in_specs=[SMEM] * 6 + [VMEM] * 4,
        out_specs=VMEM,
        compiler_params=params(10),
        name="stencil",
    )(which, energy, *rot, starts, coef, mid, zsum, pot, img)


def project(src, begin, image_of, accs):
    accs = list(accs)
    for k in range(2):
        at = pl.ds(pl.multiple_of(begin + 8 * k, 8), 8)
        ire, iim = image_of(0, k), image_of(1, k)
        for n in range(len(accs) // 2):
            re, im = src[2 * n, at], src[2 * n + 1, at]
            accs[2 * n] = accs[2 * n] + (re * ire - im * iim)
            accs[2 * n + 1] = accs[2 * n + 1] + (re * iim + im * ire)
    return accs


def lanes_of(red, total, blocks):
    return jnp.concatenate([sum_rows(red[128 * b : min(total, 128 * b + 128)]) for b in range(blocks)], axis=0)


def turn_lanes(value, cosine, sine_part):
    even = lax.broadcasted_iota(jnp.int32, value.shape, 1) % 2 == 0
    times_i = jnp.where(even, -pltpu.roll(value, 127, 1), pltpu.roll(value, 1, 1))
    return value * cosine + times_i * sine_part


def plane_kernel(which_ref, energy_ref, starts_ref, cos_ref, sin_ref, str_ref, mid_ref, pot_ref, low_img, high_img,
                 out_ref, low_ref, high_ref, down_ref, up_ref, red):
    fields, wide, cols = mid_ref.shape
    half = wide - 2 * EDGE
    atoms = low_img.shape[0]
    total = atoms * fields

    def atom(a, _):
        for j, img, z in ((1, low_img, 1), (2, high_img, 0)):
            begin = starts_ref[j, a]
            image = lambda part, k: img[a, z, part, 8 * k : 8 * k + 8]
            accs = project(mid_ref, begin, image, [jnp.zeros((8, 128), jnp.float32)] * fields)
            for f in range(fields):
                red[j - 1, a * fields + f] = accs[f] * str_ref[j, a]
        return 0

    lax.fori_loop(0, atoms, atom, 0)
    blocks = low_ref.shape[0]
    low = lanes_of(red.at[0], total, blocks)
    high = lanes_of(red.at[1], total, blocks)
    low_ref[...] = low
    high_ref[...] = high
    down_ref[...] = turn_lanes(low, cos_ref[2], sin_ref[2])
    up_ref[...] = turn_lanes(high, cos_ref[3], sin_ref[3])

    lane = lax.broadcasted_iota(jnp.int32, (half, cols), 1)
    first, last = lane == 0, lane == cols - 1
    c, s = cos_ref[6], sin_ref[6]
    pot = pot_ref[0, pl.ds(pl.multiple_of(which_ref[0] * half, 8), half)] + 3.0
    for n in range(fields // 2):
        re = mid_ref[2 * n, EDGE : EDGE + half]
        im = mid_ref[2 * n + 1, EDGE : EDGE + half]
        re_next, im_next = pltpu.roll(re, cols - 1, 1), pltpu.roll(im, cols - 1, 1)
        re_prev, im_prev = pltpu.roll(re, 1, 1), pltpu.roll(im, 1, 1)
        y_re = jnp.where(last, re_next * c - im_next * s, re_next) + jnp.where(
            first, re_prev * c + im_prev * s, re_prev
        )
        y_im = jnp.where(last, re_next * s + im_next * c, im_next) + jnp.where(
            first, im_prev * c - re_prev * s, im_prev
        )
        scale = pot - energy_ref[n]
        for f, value, beside in ((2 * n, re, y_re), (2 * n + 1, im, y_im)):
            beside = beside + mid_ref[f, EDGE - 1 : EDGE - 1 + half]
            beside = beside + mid_ref[f, EDGE + 1 : EDGE + 1 + half]
            out_ref[f, EDGE : EDGE + half] = scale * value - 0.5 * beside
            out_ref[f, 0:EDGE] = jnp.zeros((EDGE, cols), jnp.float32)
            out_ref[f, EDGE + half :] = jnp.zeros((EDGE + WIN, cols), jnp.float32)


def plane_call(which, energy, starts, rot, strength, mid, pot, low_img, high_img):
    fields, wide, cols = mid.shape
    atoms = low_img.shape[0]
    blocks = -(-atoms * fields // 128)
    coef = jax.ShapeDtypeStruct((blocks, 128), jnp.float32)
    return pl.pallas_call(
        plane_kernel,
        out_shape=(jax.ShapeDtypeStruct((fields, wide + WIN, cols), jnp.float32), coef, coef, coef, coef),
        in_specs=[SMEM] * 6 + [VMEM] * 4,
        out_specs=(VMEM,) * 5,
        scratch_shapes=[pltpu.VMEM((2, atoms * fields, 8, 128), jnp.float32)],
        compiler_params=params(10),
        name="plane",
    )(which, energy, starts, *rot, strength, mid, pot, low_img, high_img)


def gather_all_kernel(starts_ref, cos_ref, sin_ref, str_ref, mid_ref, low_ref, high_ref, img_ref, low_img, high_img,
                  part_low, part_high, got_low, got_high, zsum_ref, out_ref, low, high, red):
    fields = mid_ref.shape[0]
    half = zsum_ref.shape[1]
    wide = half + 2 * EDGE
    for n in range(fields // 2):
        for src, dst, j in ((low_ref, low, 0), (high_ref, high, 1)):
            c, s = cos_ref[j], sin_ref[j]
            re, im = src[2 * n, 0:wide], src[2 * n + 1, 0:wide]
            dst[2 * n] = re * c - im * s
            dst[2 * n + 1] = re * s + im * c
        for k in range(2):
            f = 2 * n + k
            zsum_ref[f] = low[f, EDGE : EDGE + half] + high[f, EDGE : EDGE + half]
    atoms = img_ref.shape[0]
    groups = (
        (0, ((low, img_ref, 0), (mid_ref, img_ref, 1), (high, img_ref, 2))),
        (1, ((low, low_img, 0),)),
        (2, ((high, high_img, 1),)),
    )

    def atom(a, _):
        for j, planes in groups:
            begin = starts_ref[j, a]
            accs = [jnp.zeros((8, 128), jnp.float32)] * fields
            for src, img, z in planes:
                image = lambda part, k, img=img, z=z: img[a, z, part, 8 * k : 8 * k + 8]
                accs = project(src, begin, image, accs)
            for f in range(fields):
                red[j, a * fields + f] = accs[f] * str_ref[j, a]
        return 0

    lax.fori_loop(0, atoms, atom, 0)
    total = atoms * fields
    blocks = part_low.shape[0]
    out_ref[0:blocks] = lanes_of(red.at[0], total, blocks)
    out_ref[blocks : 2 * blocks] = lanes_of(red.at[1], total, blocks) + part_low[...] + got_low[...]
    out_ref[2 * blocks : 3 * blocks] = lanes_of(red.at[2], total, blocks) + part_high[...] + got_high[...]


def gather_all(starts, rot, strength, mid, low, high, img, low_img, high_img, parts, got):
    fields, rows, cols = mid.shape
    atoms = img.shape[0]
    blocks = -(-atoms * fields // 128)
    return pl.pallas_call(
        gather_all_kernel,
        out_shape=(
            jax.ShapeDtypeStruct((fields, rows - 2 * EDGE, cols), jnp.float32),
            jax.ShapeDtypeStruct((3 * blocks, 128), jnp.float32),
        ),
        in_specs=[SMEM] * 4 + [VMEM] * 10,
        out_specs=(VMEM,) * 2,
        scratch_shapes=[
            pltpu.VMEM(mid.shape, jnp.float32),
            pltpu.VMEM(mid.shape, jnp.float32),
            pltpu.VMEM((3, atoms * fields, 8, 128), jnp.float32),
        ],
        compiler_params=params(10),
        name="gather_all",
    )(starts, *rot, strength, mid, low, high, img, low_img, high_img, *parts, *got)


def spread_sides(acc, starts_ref, low_coef, high_coef, low_img, high_img):
    atoms = low_img.shape[0]
    for j, coef, img, z in ((1, low_coef, low_img, 1), (2, high_coef, high_img, 0)):
        image = lambda a, part, k, img=img, z=z: img[a, z, part, 8 * k : 8 * k + 8]
        spread_into(acc, lambda a, j=j: starts_ref[j, a], coef, image, atoms)


def spread_all(acc, plane_ref, zsum_ref, starts_ref, coef_ref, images):
    fields = acc.shape[0]
    half = zsum_ref.shape[1]
    atoms = images[0][0].shape[0]
    blocks = coef_ref.shape[0] // 3
    inside = pl.ds(EDGE, half)
    if acc is not plane_ref:
        acc[:, 0:EDGE] = plane_ref[:, 0:EDGE]
        acc[:, EDGE + half :] = plane_ref[:, EDGE + half :]
    acc[:, inside] = plane_ref[:, inside] - 0.5 * zsum_ref[...]

    def atom(a, _):
        line = lax.div(a * fields, 128)
        lane = lax.rem(a * fields, 128)
        for j, (img, z) in enumerate(images):
            begin = pl.multiple_of(starts_ref[j, a], 8)
            for k in range(2):
                at = pl.ds(pl.multiple_of(begin + 8 * k, 8), 8)
                ire = img[a, z, 0, 8 * k : 8 * k + 8]
                iim = img[a, z, 1, 8 * k : 8 * k + 8]
                for n in range(fields // 2):
                    pr = coef_ref[j * blocks + line, lane + 2 * n]
                    pi = coef_ref[j * blocks + line, lane + 2 * n + 1]
                    acc[2 * n, at] = acc[2 * n, at] + (pr * ire + pi * iim)
                    acc[2 * n + 1, at] = acc[2 * n + 1, at] + (pi * ire - pr * iim)
        return 0

    lax.fori_loop(0, atoms, atom, 0)


def occupied_into(store, half, fields, sums_ref, side, own_ref, other_ref, base, scale, block, copies_of, start=None, ahead=0):
    count = own_ref.shape[0]

    def rows_of(b, _):
        at = pl.ds(pl.multiple_of(b * block, 8), block)
        for copy in copies_of(b):
            copy.wait()
        if start is not None:

            @pl.when(b + ahead < half // block)
            def _():
                start(b + ahead)

        def band(m, accs):
            accs = list(accs)
            for row, occ in ((side, own_ref), (1 - side, other_ref)):
                pr, pi = occ[m, 0, at], occ[m, 1, at]
                for n in range(fields // 2):
                    sr = sums_ref[row, m * fields + 2 * n]
                    si = sums_ref[row, m * fields + 2 * n + 1]
                    accs[2 * n] = accs[2 * n] + (pr * sr - pi * si)
                    accs[2 * n + 1] = accs[2 * n + 1] + (pr * si + pi * sr)
            return tuple(accs)

        zero = jnp.zeros((block, 128), jnp.float32)
        accs = lax.fori_loop(0, count, band, (zero,) * fields, unroll=4)
        for f in range(fields):
            store(f, b * block, base(f, b * block, block) + scale * accs[f])
        return 0

    lax.fori_loop(0, half // block, rows_of, 0)


def correlate_into(red, src, offset, half, own_ref, other_ref):
    fields = src.shape[0]
    count = own_ref.shape[0]
    bands = fields // 2

    def pair(g, _):
        def row(i, accs):
            at = rows8(i)
            moved = pl.ds(pl.multiple_of(i * 8 + offset, 8), 8)
            accs = list(accs)
            occ = []
            for ref in (own_ref, other_ref):
                for k in range(2):
                    occ.append((ref[2 * g + k, 0, at], ref[2 * g + k, 1, at]))
            for n in range(bands):
                re, im = src[2 * n, moved], src[2 * n + 1, moved]
                for q, (pr, pi) in enumerate(occ):
                    j = (q * bands + n) * 2
                    accs[j] = accs[j] + (pr * re + pi * im)
                    accs[j + 1] = accs[j + 1] + (pr * im - pi * re)
            return tuple(accs)

        zero = jnp.zeros((8, 128), jnp.float32)
        accs = lax.fori_loop(0, half // 8, row, (zero,) * (8 * bands), unroll=5)
        for q in range(4):
            for j in range(fields):
                red[q // 2, (2 * g + q % 2) * fields + j] = accs[q * fields + j]
        return 0

    lax.fori_loop(0, count // 2, pair, 0)


def dots_into(red_dot, half, fields, pairs):
    bands = fields // 2

    def row(i, accs):
        at = pl.ds(pl.multiple_of(i * 8 + EDGE, 8), 8)
        accs = list(accs)
        for p, (left, right) in enumerate(pairs):
            for n in range(bands):
                value = left[2 * n, at] * right[2 * n, at] + left[2 * n + 1, at] * right[2 * n + 1, at]
                accs[p * bands + n] = accs[p * bands + n] + value
        return tuple(accs)

    zero = jnp.zeros((8, 128), jnp.float32)
    accs = lax.fori_loop(0, half // 8, row, (zero,) * (bands * len(pairs)), unroll=3)
    for j in range(bands * len(pairs)):
        red_dot[j] = accs[j]


def pick_block(half):
    return next(b for b in (24, 16, 8) if half % b == 0)


def shift_rows(start, size):
    return pl.ds(pl.multiple_of(start + EDGE, 8), size)


def band_copies(which_ref, half, block, b, occ_ref, other_refs, own, other, sems):
    begin = pl.multiple_of(which_ref[0] * half + b * block, 8)
    at = pl.ds(pl.multiple_of(b * block, 8), block)
    copies = [pltpu.make_async_copy(occ_ref.at[:, :, pl.ds(begin, block)], own.at[:, :, at], sems.at[0, b])]
    first = 0
    for j, ref in enumerate(other_refs):
        last = first + ref.shape[0]
        copies.append(pltpu.make_async_copy(ref.at[:, :, at], other.at[first:last, :, at], sems.at[1 + j, b]))
        first = last
    return tuple(copies)


def start_bands(half, block, copies_of):
    for b in range(half // block):
        for copy in copies_of(b):
            copy.start()


def write_sums(sum_ref, side, red):
    mine, theirs = sum_rows(red[0]), sum_rows(red[1])
    sum_ref[...] = jnp.zeros(sum_ref.shape, jnp.float32)
    sum_ref[0:1] = jnp.where(side == 0, mine, theirs)
    sum_ref[1:2] = jnp.where(side == 0, theirs, mine)


def write_edges(edge_ref, out_ref, half):
    for f in range(out_ref.shape[0]):
        edge_ref[f, 0:EDGE] = out_ref[f, EDGE : 2 * EDGE]
        edge_ref[f, EDGE : 2 * EDGE] = out_ref[f, half : half + EDGE]


def residual_kernel(scale, which_ref, starts_ref, low_coef, high_coef, sums_ref, lap_ref, low_ref, high_ref,
                    occ_ref, other_a, other_b, resp_hbm, pot_hbm, out_ref, edge_ref, sum_ref,
                    acc, own, other, resp, pot, red, red_dot, sems, more_sems):
    fields, wide, cols = out_ref.shape
    half = wide - 2 * EDGE
    side = which_ref[0]
    block = pick_block(half)
    begin = pl.multiple_of(side * half, 8)
    copies = (
        pltpu.make_async_copy(resp_hbm.at[:, :, pl.ds(begin, half)], resp, more_sems.at[0]),
        pltpu.make_async_copy(pot_hbm.at[:, pl.ds(begin, half)], pot, more_sems.at[1]),
    )
    for copy in copies:
        copy.start()
    copies_of = lambda b: band_copies(which_ref, half, block, b, occ_ref, (other_a, other_b), own, other, sems)
    start_bands(half, block, copies_of)
    acc[...] = lap_ref[...]
    spread_sides(acc, starts_ref, low_coef, high_coef, low_ref, high_ref)
    for copy in copies:
        copy.wait()

    def base(f, start, size):
        at = pl.ds(pl.multiple_of(start, 8), size)
        re, im = resp[f // 2, 0, at], resp[f // 2, 1, at]
        if f % 2 == 0:
            prod = pot[0, at] * re - pot[1, at] * im
        else:
            prod = pot[0, at] * im + pot[1, at] * re
        return -prod - acc[f, shift_rows(start, size)]

    def store(f, start, value):
        out_ref[f, shift_rows(start, block)] = value

    occupied_into(store, half, fields, sums_ref, side, own, other, base, scale, block, copies_of)
    write_edges(edge_ref, out_ref, half)
    correlate_into(red, out_ref, EDGE, half, own, other)
    dots_into(red_dot, half, fields, [(out_ref, out_ref)])
    write_sums(sum_ref, side, red)
    sum_ref[2:3] = sum_rows(red_dot[0 : fields // 2])


def field_outputs(fields, half, cols):
    return (
        jax.ShapeDtypeStruct((fields, half + 2 * EDGE, cols), jnp.float32),
        jax.ShapeDtypeStruct((fields, 2 * EDGE, cols), jnp.float32),
        jax.ShapeDtypeStruct((8, 128), jnp.float32),
    )


def residual_call(scale, which, starts, low_coef, high_coef, sums, lap, low_img, high_img, psi_occ, other, resp, pot):
    fields, long, cols = lap.shape
    half = long - 2 * EDGE - WIN
    return pl.pallas_call(
        functools.partial(residual_kernel, scale),
        out_shape=field_outputs(fields, half, cols),
        in_specs=[SMEM] * 5 + [VMEM] * 3 + [HBM] * 5,
        out_specs=(VMEM,) * 3,
        scratch_shapes=[
            pltpu.VMEM(lap.shape, jnp.float32),
            pltpu.VMEM(psi_occ.shape[:2] + (half, cols), jnp.float32),
            pltpu.VMEM(psi_occ.shape[:2] + (half, cols), jnp.float32),
            pltpu.VMEM(resp.shape[:2] + (half, cols), jnp.float32),
            pltpu.VMEM((2, half, cols), jnp.float32),
            pltpu.VMEM((2, 128, 8, 128), jnp.float32),
            pltpu.VMEM((16, 8, 128), jnp.float32),
            pltpu.SemaphoreType.DMA((3, half // pick_block(half))),
            pltpu.SemaphoreType.DMA((2,)),
        ],
        compiler_params=params(16),
        name="residual",
    )(which, starts, low_coef, high_coef, sums, lap, low_img, high_img, psi_occ, *other, resp, pot)


def image_kernel(scale, which_ref, starts_ref, low_coef, high_coef, sums_ref, lap_ref, low_ref, high_ref,
                 res_ref, occ_ref, other_a, other_b, out_ref, edge_ref, sum_ref,
                 acc, own, other, red, red_dot, sems):
    fields, wide, cols = out_ref.shape
    half = wide - 2 * EDGE
    side = which_ref[0]
    block = pick_block(half)
    copies_of = lambda b: band_copies(which_ref, half, block, b, occ_ref, (other_a, other_b), own, other, sems)
    start_bands(half, block, copies_of)
    acc[...] = lap_ref[...]
    spread_sides(acc, starts_ref, low_coef, high_coef, low_ref, high_ref)

    def base(f, start, size):
        return acc[f, shift_rows(start, size)]

    def store(f, start, value):
        out_ref[f, shift_rows(start, block)] = value

    occupied_into(store, half, fields, sums_ref, side, own, other, base, scale, block, copies_of)
    write_edges(edge_ref, out_ref, half)
    correlate_into(red, out_ref, EDGE, half, own, other)
    dots_into(red_dot, half, fields, [(res_ref, out_ref), (out_ref, out_ref)])
    write_sums(sum_ref, side, red)
    sum_ref[2:3] = sum_rows(red_dot[0:fields])


def image_call(scale, which, starts, low_coef, high_coef, sums, lap, low_img, high_img, res, psi_occ, other):
    fields, long, cols = lap.shape
    half = long - 2 * EDGE - WIN
    return pl.pallas_call(
        functools.partial(image_kernel, scale),
        out_shape=field_outputs(fields, half, cols),
        in_specs=[SMEM] * 5 + [VMEM] * 4 + [HBM] * 3,
        out_specs=(VMEM,) * 3,
        scratch_shapes=[
            pltpu.VMEM(lap.shape, jnp.float32),
            pltpu.VMEM(psi_occ.shape[:2] + (half, cols), jnp.float32),
            pltpu.VMEM(psi_occ.shape[:2] + (half, cols), jnp.float32),
            pltpu.VMEM((2, 128, 8, 128), jnp.float32),
            pltpu.VMEM((16, 8, 128), jnp.float32),
            pltpu.SemaphoreType.DMA((3, half // pick_block(half))),
        ],
        compiler_params=params(16),
        name="image",
    )(which, starts, low_coef, high_coef, sums, lap, low_img, high_img, res, psi_occ, *other)


def local_kernel(starts_ref, coef_ref, plane_ref, zsum_ref, img_ref, low_ref, high_ref, field_ref, part_ref,
                 out_ref, sum_ref, acc, red_dot, sem):
    fields = acc.shape[0]
    half = zsum_ref.shape[1]
    spread_all(acc, plane_ref, zsum_ref, starts_ref, coef_ref, ((img_ref, 1), (low_ref, 1), (high_ref, 0)))
    copy = pltpu.make_async_copy(acc, out_ref, sem)
    copy.start()
    dots_into(red_dot, half, fields, [(field_ref, acc)])
    sum_ref[...] = part_ref[...]
    sum_ref[3:4] = sum_rows(red_dot[0 : fields // 2])
    copy.wait()


def local_call(starts, local, images, field, part):
    coef, plane, zsum = local
    return pl.pallas_call(
        local_kernel,
        out_shape=(
            jax.ShapeDtypeStruct(plane.shape, jnp.float32),
            jax.ShapeDtypeStruct((8, 128), jnp.float32),
        ),
        in_specs=[SMEM] * 2 + [VMEM] * 7,
        out_specs=(HBM, VMEM),
        scratch_shapes=[
            pltpu.VMEM(plane.shape, jnp.float32),
            pltpu.VMEM((16, 8, 128), jnp.float32),
            pltpu.SemaphoreType.DMA,
        ],
        compiler_params=params(10),
        name="local",
    )(starts, coef, plane, zsum, *images, field, part)


def last_kernel(which_ref, sums_ref, mix_ref, res_hbm, first_hbm, second_hbm, occ_ref, other_a, other_b,
                out_ref, res, first, second, own, other, sems, more_sems):
    fields, half, cols = out_ref.shape
    side = which_ref[0]
    block = pick_block(half)

    def copies_of(b):
        at = pl.ds(pl.multiple_of(b * block, 8), block)
        moved = shift_rows(b * block, block)
        own_copies = tuple(
            pltpu.make_async_copy(src.at[:, moved], dst.at[:, at], more_sems.at[j, b])
            for j, (src, dst) in enumerate(((res_hbm, res), (first_hbm, first), (second_hbm, second)))
        )
        return own_copies + band_copies(which_ref, half, block, b, occ_ref, (other_a, other_b), own, other, sems)

    ahead = 2

    def start(b):
        for copy in copies_of(b):
            copy.start()

    for b in range(ahead):
        start(b)

    def base(f, start, size):
        n = f // 2
        at = pl.ds(pl.multiple_of(start, 8), size)
        return res[f, at] + mix_ref[0, n] * first[f, at] + mix_ref[1, n] * second[f, at]

    def store(f, start, value):
        out_ref[f, pl.ds(pl.multiple_of(start, 8), block)] = value

    occupied_into(store, half, fields, sums_ref, side, own, other, base, 1.0, block, copies_of, start, ahead)


def last_call(which, sums, mix, res, first, second, psi_occ, other):
    fields, wide, cols = res.shape
    half = wide - 2 * EDGE
    blocks = half // pick_block(half)
    field = pltpu.VMEM((fields, half, cols), jnp.float32)
    return pl.pallas_call(
        last_kernel,
        out_shape=jax.ShapeDtypeStruct((fields, half, cols), jnp.float32),
        in_specs=[SMEM] * 3 + [HBM] * 6,
        out_specs=VMEM,
        scratch_shapes=[
            field,
            field,
            field,
            pltpu.VMEM(psi_occ.shape[:2] + (half, cols), jnp.float32),
            pltpu.VMEM(psi_occ.shape[:2] + (half, cols), jnp.float32),
            pltpu.SemaphoreType.DMA((3, blocks)),
            pltpu.SemaphoreType.DMA((3, blocks)),
        ],
        compiler_params=params(52),
        name="last",
    )(which, sums, mix, res, first, second, psi_occ, *other)


def xor_sum(block, bits):
    count = lax.axis_size("space") * lax.axis_size("occ")
    masks = [0]
    for bit in bits:
        masks = masks + [mask | bit for mask in masks]
    parts = [block]
    for mask in masks[1:]:
        parts.append(lax.ppermute(block, ("space", "occ"), [(i, i ^ mask) for i in range(count)]))
    while len(parts) > 1:
        parts = [parts[j] + parts[j + 1] for j in range(0, len(parts), 2)]
    return parts[0]


def total(block, groups=None):
    count = lax.axis_size("space")
    bit = 2
    steps = []
    while count > 1:
        wide = count % 4 == 0
        steps.append((bit, 2 * bit) if wide else (bit,))
        bit, count = (4 * bit, count // 4) if wide else (2 * bit, count // 2)
    steps.append((1,))
    for bits in steps[groups] if groups is not None else steps:
        block = xor_sum(block, bits)
    return block


def exchange(block):
    return lax.ppermute(block, "occ", SWAP)


def from_behind(block, distance):
    count = lax.axis_size("space")
    return lax.ppermute(block, "space", [((i - distance) % count, i) for i in range(count)])


def window_images(x_cell, y_cell, offsets, values, theta_y, rows_y, planes):
    y_raw = y_cell[:, None] + offsets[None, :, 2]
    y_wrap = jnp.floor_divide(y_raw, rows_y)
    y_at = y_raw - y_wrap * rows_y
    angles = theta_y * y_wrap.astype(jnp.float32)
    row = x_cell[:, None] + offsets[None, :, 1] + RAD
    slot = []
    for plane in planes:
        wanted = (row[:, None, :] == jnp.arange(WIN, dtype=jnp.int32)[None, :, None]) & (
            offsets[:, 0] == plane
        )[None, None, :]
        slot.append(wanted)
    slots = jnp.stack(slot, axis=1)
    weights = jnp.stack([values * jnp.cos(angles), values * jnp.sin(angles)], axis=1)
    left = jnp.where(slots[:, :, None], weights[:, None, :, None, :], 0.0)
    atoms = left.shape[0]
    left = left.reshape(atoms, len(planes) * 2 * WIN, -1)
    right = (y_at[:, :, None] == jnp.arange(rows_y, dtype=jnp.int32)[None, None, :]).astype(jnp.float32)
    image = jnp.einsum("apk,aky->apy", left, right, precision=PRECISE)
    return image.reshape(atoms, len(planes), 2, WIN, rows_y)


def shards(
    psi_occ,
    psi_resp,
    initial_guess,
    local_potential,
    potential_change,
    band_energy,
    q_index,
    atom_cells,
    offsets,
    projector,
    strength,
):
    slab_count = lax.axis_size("space")
    slab_index = lax.axis_index("space")
    side = lax.axis_index("occ")
    layers, rows_x, rows_y = local_potential.shape
    half = rows_x // 2
    atoms = atom_cells.shape[0]
    bands = psi_resp.shape[0]
    fields = 2 * bands
    weight = 1.0 / (layers * slab_count * rows_x * rows_y)
    thetas = q_index.astype(jnp.float32) * (2.0 * math.pi / QDIV)
    which = side.astype(jnp.int32).reshape(1)
    where = jnp.stack([side, slab_index]).astype(jnp.int32)

    occ = psi_occ.reshape(psi_occ.shape[0], 2, rows_x, rows_y)
    resp = psi_resp.reshape(bands, 2, rows_x, rows_y)
    guess = initial_guess.reshape(bands, 2, rows_x, rows_y)
    change = potential_change.reshape(2, rows_x, rows_y)

    cell_rows = jnp.pad(
        jnp.concatenate([atom_cells.astype(jnp.float32), strength[:, None]], axis=1),
        ((0, 0), (0, projector.shape[1] - 4)),
    )
    packed = jnp.concatenate([projector, cell_rows], axis=0)
    guess_mid, *rot = prep_call(slab_count, where, q_index, guess, packed)
    first_sums, *occ_send = first_corr(which, occ, resp, change, guess)
    occ_other = [exchange(block) for block in occ_send]
    first_sums = total(first_sums, slice(0, 1))
    first_sums, guess_mid = lax.optimization_barrier((first_sums, guess_mid))
    first_sums = xor_sum(xor_sum(first_sums, (8,)), (16,))
    first_sums = xor_sum(first_sums, (32,))
    first_sums, occ_other[0] = lax.optimization_barrier((first_sums, occ_other[0]))
    first_sums = xor_sum(first_sums, (64,))
    guess_low = from_behind(guess_mid, 1)
    guess_high = from_behind(guess_mid, -1)

    def unpack(block):
        rows = block[:, half + 2 * EDGE :].reshape(-1, rows_y)
        return rows[:atoms], rows[atoms : 2 * atoms]

    below, below_cells = unpack(guess_low)
    above, above_cells = unpack(guess_high)
    cells = [atom_cells]
    for rows in (below_cells, above_cells):
        cells.append(rows[:, :3].astype(jnp.int32))
    all_x = jnp.stack([c[:, 1] for c in cells])
    all_y = jnp.stack([c[:, 2] for c in cells])
    at_row = jnp.mod(all_x - RAD - side * half + EDGE, rows_x)
    inner = at_row % 8
    touching = at_row < half + EDGE
    put_starts = jnp.where(touching, at_row - inner, half + 2 * EDGE).astype(jnp.int32)
    get_starts = jnp.where(touching, at_row - inner, 0).astype(jnp.int32)
    own_row = jnp.mod(atom_cells[:, 1] - RAD - side * half + EDGE, rows_x)
    own_inner = own_row % 8
    own_starts = jnp.where(own_row < half + EDGE, own_row - own_inner, 0).astype(jnp.int32)
    strengths = jnp.stack([strength, below_cells[:, 3], above_cells[:, 3]])
    img = window_images(own_inner, atom_cells[:, 2], offsets, projector, thetas[2], rows_y, (-1, 0, 1))
    low_img = window_images(inner[1], all_y[1], offsets, below, thetas[2], rows_y, (0, 1))
    high_img = window_images(inner[2], all_y[2], offsets, above, thetas[2], rows_y, (-1, 0))
    images = (img, low_img, high_img)

    def local_part(mid, low, high):
        zsum, proj, up, down = gather(own_starts, rot, strength, mid, low, high, img, half)
        low_coef = from_behind(up, 1)
        high_coef = from_behind(down, -1)
        lap = stencil(which, band_energy, rot, put_starts, proj, mid, zsum, local_potential, img)
        return put_starts, low_coef, high_coef, lap

    def far_part(mid):
        low = from_behind(mid, 1)
        high = from_behind(mid, -1)
        plane, part_low, part_high, down, up = plane_call(
            which, band_energy, get_starts, rot, strengths, mid, local_potential, low_img, high_img
        )
        got = (from_behind(up, 2), from_behind(down, -2))
        zsum, coef = gather_all(get_starts, rot, strengths, mid, low, high, *images, (part_low, part_high), got)
        return coef, plane, zsum

    starts, low_coef, high_coef, lap = local_part(guess_mid, guess_low, guess_high)
    first_sums, lap = lax.optimization_barrier((first_sums, lap))
    first_sums = total(first_sums, slice(-1, None))
    residual, edges, part = residual_call(
        weight, which, starts, low_coef, high_coef, first_sums, lap, low_img, high_img, occ, occ_other, resp, change
    )
    tot = total(part)
    norm0 = tot[2, :bands]
    residual = fill_call(rot, exchange(edges), residual)
    starts, low_coef, high_coef, lap = local_part(residual, from_behind(residual, 1), from_behind(residual, -1))
    image, edges, part = image_call(
        SHIFT_WEIGHT * weight, which, starts, low_coef, high_coef, tot, lap, low_img, high_img, residual, occ, occ_other
    )
    image = fill_call(rot, exchange(edges), image)
    image_other = exchange(image)
    image2, part = local_call(put_starts, far_part(image), images, image, part)
    part, image_other, residual_send = lax.optimization_barrier((part, image_other, residual))
    residual_other = exchange(residual_send)
    tot = total(part, slice(0, 2))
    tot, residual_other = lax.optimization_barrier((tot, residual_other))
    tot = total(tot, slice(2, None))
    sums = tot[0:2]
    cross = tot[2, :bands]
    square = tot[2, bands : 2 * bands]
    occ_square = jnp.sum((sums * sums).reshape(-1, bands, 2), axis=(0, 2))
    triple = tot[3, :bands] + SHIFT_WEIGHT * weight * occ_square
    step0 = norm0 / cross
    norm1 = norm0 - 2.0 * step0 * cross + step0 * step0 * square
    growth = norm1 / norm0
    lead = 1.0 + growth
    curvature = lead * lead * cross - 2.0 * lead * step0 * square + step0 * step0 * triple
    step1 = norm1 / curvature
    mix0 = -step0 - step1 * lead
    mix1 = step1 * step0
    per_lane = jnp.tile(jnp.repeat(mix1, 2), sums.shape[1] // fields)
    last_sums = SHIFT_WEIGHT * weight * sums * per_lane[None, :]
    mine = last_call(which, last_sums, jnp.stack([mix0, mix1]), residual, image, image2, occ, occ_other)
    mine, residual_other, image_other = lax.optimization_barrier((mine, residual_other, image_other))
    theirs = exchange(mine)

    def join(own_half, other_half):
        lower = jnp.where(side == 0, own_half, other_half)
        upper = jnp.where(side == 0, other_half, own_half)
        return jnp.concatenate([lower, upper], axis=1).reshape(bands, 2, 1, rows_x, rows_y)

    inside = lambda v: v[:, EDGE : EDGE + half]
    wide = lambda v: v[:, None, None, None, None]
    response = (
        initial_guess
        + wide(step0 + step1 * lead) * join(inside(residual), inside(residual_other))
        - wide(step0 * step1) * join(inside(image), inside(image_other))
    )
    return response, join(mine, theirs)


def solution(mesh):
    return jax.shard_map(
        shards,
        mesh=mesh,
        in_specs=(
            P("occ", None, "space", None, None),
            P("resp", None, "space", None, None),
            P("resp", None, "space", None, None),
            P("space", None, None),
            P(None, "space", None, None),
            P("resp"),
            P(),
            P("space", None),
            P(),
            P("space", None),
            P("space"),
        ),
        out_specs=(P("resp", None, "space", None, None), P("resp", None, "space", None, None)),
        check_vma=False,
    )
```

```python
import functools
import math

import jax
import jax.numpy as jnp
from jax import lax
from jax.experimental import pallas as pl
from jax.experimental.pallas import tpu as pltpu
from jax.sharding import PartitionSpec as P

RAD = 4
QDIV = 8
EDGE = 8
WIN = 16
SHIFT_WEIGHT = 3.0
PRECISE = lax.Precision.HIGHEST
SWAP = [(0, 1), (1, 0)]

VMEM = pl.BlockSpec(memory_space=pltpu.VMEM)
SMEM = pl.BlockSpec(memory_space=pltpu.SMEM)
ANY = pl.BlockSpec(memory_space=pl.ANY)
HBM = pl.BlockSpec(memory_space=pltpu.HBM)


def params(mib):
    return pltpu.CompilerParams(vmem_limit_bytes=mib * 1024 * 1024)


def sum_rows(values):
    total = jnp.sum(values, axis=2, keepdims=True)
    row = lax.broadcasted_iota(jnp.int32, values.shape, 0)
    lane = lax.broadcasted_iota(jnp.int32, values.shape, 2)
    picked = jnp.sum(jnp.where(row == lane, total, 0.0), axis=0)
    return jnp.sum(picked, axis=0, keepdims=True)


def rows8(index):
    return pl.ds(pl.multiple_of(index * 8, 8), 8)


def extra_rows(count, fields):
    return -(-count // (8 * fields)) * 8


AXES = (0, 0, 0, 0, 1, 1, 2, 0, 0)
SIGNS = (-1, 1, 1, -1, -1, 1, 1, -1, 1)
TURNS = [2.0 * math.pi * k / QDIV for k in range(QDIV)]


def prep_kernel(slab_count, where_ref, q_ref, guess_ref, atoms_ref, out_ref, cos_ref, sin_ref, middle, low, high, sems):
    fields = out_ref.shape[0]
    half = middle.shape[2]
    wide = half + 2 * EDGE
    side, slab = where_ref[0], where_ref[1]
    begin = pl.multiple_of(side * half, 8)
    away = pl.multiple_of((1 - side) * half, 8)
    under = pl.multiple_of((1 - side) * half + half - EDGE, 8)
    copies = []
    for j, (start, size, dst) in enumerate(((begin, half, middle), (under, EDGE, low), (away, EDGE, high))):
        copies.append(pltpu.make_async_copy(guess_ref.at[:, :, pl.ds(start, size)], dst, sems.at[j]))
    for copy in copies:
        copy.start()

    first, last = slab == 0, slab == slab_count - 1
    flags = (first, last, slab < 2, slab >= slab_count - 2, side == 0, side == 1, slab >= 0, last, first)
    for j, (flag, sign, axis) in enumerate(zip(flags, SIGNS, AXES)):
        step = jnp.where(flag, jnp.bitwise_and(sign * q_ref[axis], QDIV - 1), 0)
        cosine, sine = jnp.float32(1.0), jnp.float32(0.0)
        for k in range(1, QDIV):
            cosine = jnp.where(step == k, jnp.float32(math.cos(TURNS[k])), cosine)
            sine = jnp.where(step == k, jnp.float32(math.sin(TURNS[k])), sine)
        cos_ref[j] = cosine
        sin_ref[j] = sine

    for f in range(fields):
        for r in range(0, out_ref.shape[1] - wide, 8):
            at = f * (out_ref.shape[1] - wide) + r
            if at < atoms_ref.shape[0]:
                out_ref[f, wide + r : wide + r + 8] = atoms_ref[at : at + 8]
            else:
                out_ref[f, wide + r : wide + r + 8] = jnp.zeros((8, 128), jnp.float32)
    for copy in copies:
        copy.wait()
    for n in range(fields // 2):
        for k in range(2):
            out_ref[2 * n + k, EDGE : EDGE + half] = middle[n, k]
        for src, spot, j in ((low, 0, 4), (high, EDGE + half, 5)):
            c, s = cos_ref[j], sin_ref[j]
            re, im = src[n, 0], src[n, 1]
            out_ref[2 * n, spot : spot + EDGE] = re * c - im * s
            out_ref[2 * n + 1, spot : spot + EDGE] = re * s + im * c


def prep_call(slab_count, where, q_index, guess, atoms):
    bands, _, rows, cols = guess.shape
    half = rows // 2
    extra = extra_rows(atoms.shape[0], 2 * bands)
    table = jax.ShapeDtypeStruct((len(AXES),), jnp.float32)
    return pl.pallas_call(
        functools.partial(prep_kernel, slab_count),
        out_shape=(
            jax.ShapeDtypeStruct((2 * bands, half + 2 * EDGE + extra, cols), jnp.float32),
            table,
            table,
        ),
        in_specs=[SMEM, SMEM, HBM, VMEM],
        out_specs=(VMEM, SMEM, SMEM),
        scratch_shapes=[
            pltpu.VMEM((bands, 2, half, cols), jnp.float32),
            pltpu.VMEM((bands, 2, EDGE, cols), jnp.float32),
            pltpu.VMEM((bands, 2, EDGE, cols), jnp.float32),
            pltpu.SemaphoreType.DMA((3,)),
        ],
        compiler_params=params(8),
        name="prep",
    )(where, q_index, guess, atoms)


def fill_kernel(cos_ref, sin_ref, got_ref, ext_ref, out_ref, low, high, sems):
    fields, wide, _ = out_ref.shape
    for n in range(fields // 2):
        for dst, at, j in ((low, EDGE, 4), (high, 0, 5)):
            c, s = cos_ref[j], sin_ref[j]
            re, im = got_ref[2 * n, at : at + EDGE], got_ref[2 * n + 1, at : at + EDGE]
            dst[2 * n] = re * c - im * s
            dst[2 * n + 1] = re * s + im * c
    one = pltpu.make_async_copy(low, out_ref.at[:, 0:EDGE], sems.at[0])
    two = pltpu.make_async_copy(high, out_ref.at[:, wide - EDGE : wide], sems.at[1])
    one.start()
    two.start()
    one.wait()
    two.wait()


def fill_call(rot, got, ext):
    shape = (ext.shape[0], EDGE, ext.shape[2])
    return pl.pallas_call(
        fill_kernel,
        out_shape=jax.ShapeDtypeStruct(ext.shape, jnp.float32),
        in_specs=[SMEM, SMEM, VMEM, ANY],
        out_specs=ANY,
        scratch_shapes=[
            pltpu.VMEM(shape, jnp.float32),
            pltpu.VMEM(shape, jnp.float32),
            pltpu.SemaphoreType.DMA((2,)),
        ],
        input_output_aliases={3: 0},
        compiler_params=params(4),
        name="fill",
    )(*rot, got, ext)


def first_corr_kernel(which_ref, occ_ref, resp_ref, pot_ref, guess_ref, out_ref, send_a, send_b, mixed, red):
    bands, _, rows, _ = resp_ref.shape
    group = occ_ref.shape[0]
    step = pl.program_id(0)
    half = send_a.shape[2]
    middle = pl.num_programs(0) // 2
    away = pl.ds(pl.multiple_of((1 - which_ref[0]) * half, 8), half)

    @pl.when(step < middle)
    def _():
        send_a[...] = occ_ref[:, :, away]

    @pl.when(step >= middle)
    def _():
        send_b[...] = occ_ref[:, :, away]

    @pl.when(step == 0)
    def _():
        for n in range(bands):
            re = resp_ref[n, 0]
            im = resp_ref[n, 1]
            mixed[2 * n] = pot_ref[0] * re - pot_ref[1] * im - SHIFT_WEIGHT * guess_ref[n, 0]
            mixed[2 * n + 1] = pot_ref[0] * im + pot_ref[1] * re - SHIFT_WEIGHT * guess_ref[n, 1]

    def row(i, accs):
        at = rows8(i)
        occ = [(occ_ref[k, 0, at], occ_ref[k, 1, at]) for k in range(group)]
        accs = list(accs)
        for n in range(bands):
            re, im = mixed[2 * n, at], mixed[2 * n + 1, at]
            for k, (pr, pi) in enumerate(occ):
                j = (k * bands + n) * 2
                accs[j] = accs[j] + (pr * re + pi * im)
                accs[j + 1] = accs[j + 1] + (pr * im - pi * re)
        return tuple(accs)

    zero = jnp.zeros((8, 128), jnp.float32)
    count = 2 * bands * group
    accs = lax.fori_loop(0, rows // 8, row, (zero,) * count, unroll=6)
    for j in range(count):
        red[step * count + j] = accs[j]

    @pl.when(step == pl.num_programs(0) - 1)
    def _():
        out_ref[...] = jnp.zeros(out_ref.shape, jnp.float32)
        total = sum_rows(red[...])
        side = which_ref[0]
        out_ref[0:1] = jnp.where(side == 0, total, 0.0)
        out_ref[1:2] = jnp.where(side == 0, 0.0, total)


def first_corr(which, psi_occ, psi_resp, pot, guess):
    group = 4
    count, _, rows, cols = psi_occ.shape
    fixed = lambda shape: pl.BlockSpec(shape, lambda i: (0,) * len(shape))
    middle = count // group // 2
    send = jax.ShapeDtypeStruct((count // 2, 2, rows // 2, cols), jnp.float32)
    shape = (group, 2, rows // 2, cols)
    return pl.pallas_call(
        first_corr_kernel,
        out_shape=(
            jax.ShapeDtypeStruct((8, 128), jnp.float32),
            send,
            send,
        ),
        grid=(count // group,),
        in_specs=[
            SMEM,
            pl.BlockSpec((group, 2, rows, cols), lambda i: (i, 0, 0, 0)),
            fixed(psi_resp.shape),
            fixed(pot.shape),
            fixed(guess.shape),
        ],
        out_specs=(
            fixed((8, 128)),
            pl.BlockSpec(shape, lambda i: (jnp.minimum(i, middle - 1), 0, 0, 0)),
            pl.BlockSpec(shape, lambda i: (jnp.maximum(i - middle, 0), 0, 0, 0)),
        ),
        scratch_shapes=[
            pltpu.VMEM((psi_resp.shape[0] * 2, rows, cols), jnp.float32),
            pltpu.VMEM((128, 8, 128), jnp.float32),
        ],
        compiler_params=params(60),
        name="first_corr",
    )(which, psi_occ, psi_resp, pot, guess)


def gather_kernel(start_ref, cos_ref, sin_ref, str_ref, mid_ref, low_ref, high_ref, img_ref,
                  zsum_ref, out_ref, up_ref, down_ref, low, high, red):
    fields = mid_ref.shape[0]
    half = zsum_ref.shape[1]
    wide = half + 2 * EDGE
    for n in range(fields // 2):
        for src, dst, j in ((low_ref, low, 0), (high_ref, high, 1)):
            c, s = cos_ref[j], sin_ref[j]
            re, im = src[2 * n, 0:wide], src[2 * n + 1, 0:wide]
            dst[2 * n] = re * c - im * s
            dst[2 * n + 1] = re * s + im * c
        for k in range(2):
            f = 2 * n + k
            zsum_ref[f] = low[f, EDGE : EDGE + half] + high[f, EDGE : EDGE + half]
    atoms = img_ref.shape[0]

    def atom(a, _):
        begin = pl.multiple_of(start_ref[a], 8)
        accs = [jnp.zeros((8, 128), jnp.float32)] * fields
        for z, src in enumerate((low, mid_ref, high)):
            for k in range(2):
                at = pl.ds(pl.multiple_of(begin + 8 * k, 8), 8)
                ire = img_ref[a, z, 0, 8 * k : 8 * k + 8]
                iim = img_ref[a, z, 1, 8 * k : 8 * k + 8]
                for n in range(fields // 2):
                    re, im = src[2 * n, at], src[2 * n + 1, at]
                    accs[2 * n] = accs[2 * n] + (re * ire - im * iim)
                    accs[2 * n + 1] = accs[2 * n + 1] + (re * iim + im * ire)
        for f in range(fields):
            red[a * fields + f] = accs[f] * str_ref[a]
        return 0

    lax.fori_loop(0, atoms, atom, 0)
    total = atoms * fields
    value = lanes_of(red, total, out_ref.shape[0])
    out_ref[...] = value
    up_ref[...] = turn_lanes(value, cos_ref[7], sin_ref[7])
    down_ref[...] = turn_lanes(value, cos_ref[8], sin_ref[8])


def gather(starts, rot, strength, mid, low, high, img, half):
    fields, _, cols = mid.shape
    rows = half + 2 * EDGE
    atoms = img.shape[0]
    blocks = -(-atoms * fields // 128)
    coef = jax.ShapeDtypeStruct((blocks, 128), jnp.float32)
    return pl.pallas_call(
        gather_kernel,
        out_shape=(
            jax.ShapeDtypeStruct((fields, rows - 2 * EDGE, cols), jnp.float32),
            coef,
            coef,
            coef,
        ),
        in_specs=[SMEM] * 4 + [VMEM] * 4,
        out_specs=(VMEM,) * 4,
        scratch_shapes=[
            pltpu.VMEM((fields, rows, cols), jnp.float32),
            pltpu.VMEM((fields, rows, cols), jnp.float32),
            pltpu.VMEM((atoms * fields, 8, 128), jnp.float32),
        ],
        compiler_params=params(10),
        name="gather",
    )(starts, *rot, strength, mid, low, high, img)


def spread_into(acc, start_of, coef_ref, image_of, atoms):
    fields = acc.shape[0]

    def atom(a, _):
        begin = pl.multiple_of(start_of(a), 8)
        line = lax.div(a * fields, 128)
        lane = lax.rem(a * fields, 128)
        for k in range(2):
            at = pl.ds(pl.multiple_of(begin + 8 * k, 8), 8)
            ire = image_of(a, 0, k)
            iim = image_of(a, 1, k)
            for n in range(fields // 2):
                pr = coef_ref[line, lane + 2 * n]
                pi = coef_ref[line, lane + 2 * n + 1]
                acc[2 * n, at] = acc[2 * n, at] + (pr * ire + pi * iim)
                acc[2 * n + 1, at] = acc[2 * n + 1, at] + (pi * ire - pr * iim)
        return 0

    lax.fori_loop(0, atoms, atom, 0)


def stencil_kernel(which_ref, energy_ref, cos_ref, sin_ref, starts_ref, coef_ref, mid_ref, zsum_ref, pot_ref, img_ref, out_ref):
    fields, half, cols = zsum_ref.shape
    lane = lax.broadcasted_iota(jnp.int32, (half, cols), 1)
    first, last = lane == 0, lane == cols - 1
    c, s = cos_ref[6], sin_ref[6]
    pot = pot_ref[0, pl.ds(pl.multiple_of(which_ref[0] * half, 8), half)] + 3.0
    for n in range(fields // 2):
        re = mid_ref[2 * n, EDGE : EDGE + half]
        im = mid_ref[2 * n + 1, EDGE : EDGE + half]
        re_next, im_next = pltpu.roll(re, cols - 1, 1), pltpu.roll(im, cols - 1, 1)
        re_prev, im_prev = pltpu.roll(re, 1, 1), pltpu.roll(im, 1, 1)
        y_re = jnp.where(last, re_next * c - im_next * s, re_next) + jnp.where(
            first, re_prev * c + im_prev * s, re_prev
        )
        y_im = jnp.where(last, re_next * s + im_next * c, im_next) + jnp.where(
            first, im_prev * c - re_prev * s, im_prev
        )
        scale = pot - energy_ref[n]
        for f, value, beside in ((2 * n, re, y_re), (2 * n + 1, im, y_im)):
            beside = beside + zsum_ref[f]
            beside = beside + mid_ref[f, EDGE - 1 : EDGE - 1 + half]
            beside = beside + mid_ref[f, EDGE + 1 : EDGE + 1 + half]
            out_ref[f, EDGE : EDGE + half] = scale * value - 0.5 * beside
            out_ref[f, 0:EDGE] = jnp.zeros((EDGE, cols), jnp.float32)
            out_ref[f, EDGE + half :] = jnp.zeros((EDGE + WIN, cols), jnp.float32)
    atoms = img_ref.shape[0]
    image = lambda a, part, k: img_ref[a, 1, part, 8 * k : 8 * k + 8]
    spread_into(out_ref, lambda a: starts_ref[0, a], coef_ref, image, atoms)


def stencil(which, energy, rot, starts, coef, mid, zsum, pot, img):
    fields, half, cols = zsum.shape
    return pl.pallas_call(
        stencil_kernel,
        out_shape=jax.ShapeDtypeStruct((fields, half + 2 * EDGE + WIN, cols), jnp.float32),
        in_specs=[SMEM] * 6 + [VMEM] * 4,
        out_specs=VMEM,
        compiler_params=params(10),
        name="stencil",
    )(which, energy, *rot, starts, coef, mid, zsum, pot, img)


def project(src, begin, image_of, accs):
    accs = list(accs)
    for k in range(2):
        at = pl.ds(pl.multiple_of(begin + 8 * k, 8), 8)
        ire, iim = image_of(0, k), image_of(1, k)
        for n in range(len(accs) // 2):
            re, im = src[2 * n, at], src[2 * n + 1, at]
            accs[2 * n] = accs[2 * n] + (re * ire - im * iim)
            accs[2 * n + 1] = accs[2 * n + 1] + (re * iim + im * ire)
    return accs


def lanes_of(red, total, blocks):
    return jnp.concatenate([sum_rows(red[128 * b : min(total, 128 * b + 128)]) for b in range(blocks)], axis=0)


def turn_lanes(value, cosine, sine_part):
    even = lax.broadcasted_iota(jnp.int32, value.shape, 1) % 2 == 0
    times_i = jnp.where(even, -pltpu.roll(value, 127, 1), pltpu.roll(value, 1, 1))
    return value * cosine + times_i * sine_part


def plane_kernel(which_ref, energy_ref, starts_ref, cos_ref, sin_ref, str_ref, mid_ref, pot_ref, low_img, high_img,
                 out_ref, low_ref, high_ref, down_ref, up_ref, red):
    fields, wide, cols = mid_ref.shape
    half = wide - 2 * EDGE
    atoms = low_img.shape[0]
    total = atoms * fields

    def atom(a, _):
        for j, img, z in ((1, low_img, 1), (2, high_img, 0)):
            begin = starts_ref[j, a]
            image = lambda part, k: img[a, z, part, 8 * k : 8 * k + 8]
            accs = project(mid_ref, begin, image, [jnp.zeros((8, 128), jnp.float32)] * fields)
            for f in range(fields):
                red[j - 1, a * fields + f] = accs[f] * str_ref[j, a]
        return 0

    lax.fori_loop(0, atoms, atom, 0)
    blocks = low_ref.shape[0]
    low = lanes_of(red.at[0], total, blocks)
    high = lanes_of(red.at[1], total, blocks)
    low_ref[...] = low
    high_ref[...] = high
    down_ref[...] = turn_lanes(low, cos_ref[2], sin_ref[2])
    up_ref[...] = turn_lanes(high, cos_ref[3], sin_ref[3])

    lane = lax.broadcasted_iota(jnp.int32, (half, cols), 1)
    first, last = lane == 0, lane == cols - 1
    c, s = cos_ref[6], sin_ref[6]
    pot = pot_ref[0, pl.ds(pl.multiple_of(which_ref[0] * half, 8), half)] + 3.0
    for n in range(fields // 2):
        re = mid_ref[2 * n, EDGE : EDGE + half]
        im = mid_ref[2 * n + 1, EDGE : EDGE + half]
        re_next, im_next = pltpu.roll(re, cols - 1, 1), pltpu.roll(im, cols - 1, 1)
        re_prev, im_prev = pltpu.roll(re, 1, 1), pltpu.roll(im, 1, 1)
        y_re = jnp.where(last, re_next * c - im_next * s, re_next) + jnp.where(
            first, re_prev * c + im_prev * s, re_prev
        )
        y_im = jnp.where(last, re_next * s + im_next * c, im_next) + jnp.where(
            first, im_prev * c - re_prev * s, im_prev
        )
        scale = pot - energy_ref[n]
        for f, value, beside in ((2 * n, re, y_re), (2 * n + 1, im, y_im)):
            beside = beside + mid_ref[f, EDGE - 1 : EDGE - 1 + half]
            beside = beside + mid_ref[f, EDGE + 1 : EDGE + 1 + half]
            out_ref[f, EDGE : EDGE + half] = scale * value - 0.5 * beside
            out_ref[f, 0:EDGE] = jnp.zeros((EDGE, cols), jnp.float32)
            out_ref[f, EDGE + half :] = jnp.zeros((EDGE + WIN, cols), jnp.float32)


def plane_call(which, energy, starts, rot, strength, mid, pot, low_img, high_img):
    fields, wide, cols = mid.shape
    atoms = low_img.shape[0]
    blocks = -(-atoms * fields // 128)
    coef = jax.ShapeDtypeStruct((blocks, 128), jnp.float32)
    return pl.pallas_call(
        plane_kernel,
        out_shape=(jax.ShapeDtypeStruct((fields, wide + WIN, cols), jnp.float32), coef, coef, coef, coef),
        in_specs=[SMEM] * 6 + [VMEM] * 4,
        out_specs=(VMEM,) * 5,
        scratch_shapes=[pltpu.VMEM((2, atoms * fields, 8, 128), jnp.float32)],
        compiler_params=params(10),
        name="plane",
    )(which, energy, starts, *rot, strength, mid, pot, low_img, high_img)


def gather_all_kernel(starts_ref, cos_ref, sin_ref, str_ref, mid_ref, low_ref, high_ref, img_ref, low_img, high_img,
                  part_low, part_high, got_low, got_high, zsum_ref, out_ref, low, high, red):
    fields = mid_ref.shape[0]
    half = zsum_ref.shape[1]
    wide = half + 2 * EDGE
    for n in range(fields // 2):
        for src, dst, j in ((low_ref, low, 0), (high_ref, high, 1)):
            c, s = cos_ref[j], sin_ref[j]
            re, im = src[2 * n, 0:wide], src[2 * n + 1, 0:wide]
            dst[2 * n] = re * c - im * s
            dst[2 * n + 1] = re * s + im * c
        for k in range(2):
            f = 2 * n + k
            zsum_ref[f] = low[f, EDGE : EDGE + half] + high[f, EDGE : EDGE + half]
    atoms = img_ref.shape[0]
    groups = (
        (0, ((low, img_ref, 0), (mid_ref, img_ref, 1), (high, img_ref, 2))),
        (1, ((low, low_img, 0),)),
        (2, ((high, high_img, 1),)),
    )

    def atom(a, _):
        for j, planes in groups:
            begin = starts_ref[j, a]
            accs = [jnp.zeros((8, 128), jnp.float32)] * fields
            for src, img, z in planes:
                image = lambda part, k, img=img, z=z: img[a, z, part, 8 * k : 8 * k + 8]
                accs = project(src, begin, image, accs)
            for f in range(fields):
                red[j, a * fields + f] = accs[f] * str_ref[j, a]
        return 0

    lax.fori_loop(0, atoms, atom, 0)
    total = atoms * fields
    blocks = part_low.shape[0]
    out_ref[0:blocks] = lanes_of(red.at[0], total, blocks)
    out_ref[blocks : 2 * blocks] = lanes_of(red.at[1], total, blocks) + part_low[...] + got_low[...]
    out_ref[2 * blocks : 3 * blocks] = lanes_of(red.at[2], total, blocks) + part_high[...] + got_high[...]


def gather_all(starts, rot, strength, mid, low, high, img, low_img, high_img, parts, got):
    fields, rows, cols = mid.shape
    atoms = img.shape[0]
    blocks = -(-atoms * fields // 128)
    return pl.pallas_call(
        gather_all_kernel,
        out_shape=(
            jax.ShapeDtypeStruct((fields, rows - 2 * EDGE, cols), jnp.float32),
            jax.ShapeDtypeStruct((3 * blocks, 128), jnp.float32),
        ),
        in_specs=[SMEM] * 4 + [VMEM] * 10,
        out_specs=(VMEM,) * 2,
        scratch_shapes=[
            pltpu.VMEM(mid.shape, jnp.float32),
            pltpu.VMEM(mid.shape, jnp.float32),
            pltpu.VMEM((3, atoms * fields, 8, 128), jnp.float32),
        ],
        compiler_params=params(10),
        name="gather_all",
    )(starts, *rot, strength, mid, low, high, img, low_img, high_img, *parts, *got)


def spread_sides(acc, starts_ref, low_coef, high_coef, low_img, high_img):
    atoms = low_img.shape[0]
    for j, coef, img, z in ((1, low_coef, low_img, 1), (2, high_coef, high_img, 0)):
        image = lambda a, part, k, img=img, z=z: img[a, z, part, 8 * k : 8 * k + 8]
        spread_into(acc, lambda a, j=j: starts_ref[j, a], coef, image, atoms)


def spread_all(acc, plane_ref, zsum_ref, starts_ref, coef_ref, images):
    fields = acc.shape[0]
    half = zsum_ref.shape[1]
    atoms = images[0][0].shape[0]
    blocks = coef_ref.shape[0] // 3
    inside = pl.ds(EDGE, half)
    if acc is not plane_ref:
        acc[:, 0:EDGE] = plane_ref[:, 0:EDGE]
        acc[:, EDGE + half :] = plane_ref[:, EDGE + half :]
    acc[:, inside] = plane_ref[:, inside] - 0.5 * zsum_ref[...]

    def atom(a, _):
        line = lax.div(a * fields, 128)
        lane = lax.rem(a * fields, 128)
        for j, (img, z) in enumerate(images):
            begin = pl.multiple_of(starts_ref[j, a], 8)
            for k in range(2):
                at = pl.ds(pl.multiple_of(begin + 8 * k, 8), 8)
                ire = img[a, z, 0, 8 * k : 8 * k + 8]
                iim = img[a, z, 1, 8 * k : 8 * k + 8]
                for n in range(fields // 2):
                    pr = coef_ref[j * blocks + line, lane + 2 * n]
                    pi = coef_ref[j * blocks + line, lane + 2 * n + 1]
                    acc[2 * n, at] = acc[2 * n, at] + (pr * ire + pi * iim)
                    acc[2 * n + 1, at] = acc[2 * n + 1, at] + (pi * ire - pr * iim)
        return 0

    lax.fori_loop(0, atoms, atom, 0)


def occupied_into(store, half, fields, sums_ref, side, own_ref, other_ref, base, scale, block, copies_of, start=None, ahead=0):
    count = own_ref.shape[0]

    def rows_of(b, _):
        at = pl.ds(pl.multiple_of(b * block, 8), block)
        for copy in copies_of(b):
            copy.wait()
        if start is not None:

            @pl.when(b + ahead < half // block)
            def _():
                start(b + ahead)

        def band(m, accs):
            accs = list(accs)
            for row, occ in ((side, own_ref), (1 - side, other_ref)):
                pr, pi = occ[m, 0, at], occ[m, 1, at]
                for n in range(fields // 2):
                    sr = sums_ref[row, m * fields + 2 * n]
                    si = sums_ref[row, m * fields + 2 * n + 1]
                    accs[2 * n] = accs[2 * n] + (pr * sr - pi * si)
                    accs[2 * n + 1] = accs[2 * n + 1] + (pr * si + pi * sr)
            return tuple(accs)

        zero = jnp.zeros((block, 128), jnp.float32)
        accs = lax.fori_loop(0, count, band, (zero,) * fields, unroll=8)
        for f in range(fields):
            store(f, b * block, base(f, b * block, block) + scale * accs[f])
        return 0

    lax.fori_loop(0, half // block, rows_of, 0)


def correlate_into(red, src, offset, half, own_ref, other_ref):
    fields = src.shape[0]
    count = own_ref.shape[0]
    bands = fields // 2

    def pair(g, _):
        def row(i, accs):
            at = rows8(i)
            moved = pl.ds(pl.multiple_of(i * 8 + offset, 8), 8)
            accs = list(accs)
            occ = []
            for ref in (own_ref, other_ref):
                for k in range(2):
                    occ.append((ref[2 * g + k, 0, at], ref[2 * g + k, 1, at]))
            for n in range(bands):
                re, im = src[2 * n, moved], src[2 * n + 1, moved]
                for q, (pr, pi) in enumerate(occ):
                    j = (q * bands + n) * 2
                    accs[j] = accs[j] + (pr * re + pi * im)
                    accs[j + 1] = accs[j + 1] + (pr * im - pi * re)
            return tuple(accs)

        zero = jnp.zeros((8, 128), jnp.float32)
        accs = lax.fori_loop(0, half // 8, row, (zero,) * (8 * bands), unroll=5)
        for q in range(4):
            for j in range(fields):
                red[q // 2, (2 * g + q % 2) * fields + j] = accs[q * fields + j]
        return 0

    lax.fori_loop(0, count // 2, pair, 0)


def dots_into(red_dot, half, fields, pairs):
    bands = fields // 2

    def row(i, accs):
        at = pl.ds(pl.multiple_of(i * 8 + EDGE, 8), 8)
        accs = list(accs)
        for p, (left, right) in enumerate(pairs):
            for n in range(bands):
                value = left[2 * n, at] * right[2 * n, at] + left[2 * n + 1, at] * right[2 * n + 1, at]
                accs[p * bands + n] = accs[p * bands + n] + value
        return tuple(accs)

    zero = jnp.zeros((8, 128), jnp.float32)
    accs = lax.fori_loop(0, half // 8, row, (zero,) * (bands * len(pairs)), unroll=3)
    for j in range(bands * len(pairs)):
        red_dot[j] = accs[j]


def pick_block(half):
    return next(b for b in (24, 16, 8) if half % b == 0)


def shift_rows(start, size):
    return pl.ds(pl.multiple_of(start + EDGE, 8), size)


def band_copies(which_ref, half, block, b, occ_ref, other_refs, own, other, sems):
    begin = pl.multiple_of(which_ref[0] * half + b * block, 8)
    at = pl.ds(pl.multiple_of(b * block, 8), block)
    copies = [pltpu.make_async_copy(occ_ref.at[:, :, pl.ds(begin, block)], own.at[:, :, at], sems.at[0, b])]
    first = 0
    for j, ref in enumerate(other_refs):
        last = first + ref.shape[0]
        copies.append(pltpu.make_async_copy(ref.at[:, :, at], other.at[first:last, :, at], sems.at[1 + j, b]))
        first = last
    return tuple(copies)


def start_bands(half, block, copies_of):
    for b in range(half // block):
        for copy in copies_of(b):
            copy.start()


def write_sums(sum_ref, side, red):
    mine, theirs = sum_rows(red[0]), sum_rows(red[1])
    sum_ref[...] = jnp.zeros(sum_ref.shape, jnp.float32)
    sum_ref[0:1] = jnp.where(side == 0, mine, theirs)
    sum_ref[1:2] = jnp.where(side == 0, theirs, mine)


def write_edges(edge_ref, out_ref, half):
    for f in range(out_ref.shape[0]):
        edge_ref[f, 0:EDGE] = out_ref[f, EDGE : 2 * EDGE]
        edge_ref[f, EDGE : 2 * EDGE] = out_ref[f, half : half + EDGE]


def residual_kernel(scale, which_ref, starts_ref, low_coef, high_coef, sums_ref, lap_ref, low_ref, high_ref,
                    occ_ref, other_a, other_b, resp_hbm, pot_hbm, out_ref, edge_ref, sum_ref,
                    acc, own, other, resp, pot, red, red_dot, sems, more_sems):
    fields, wide, cols = out_ref.shape
    half = wide - 2 * EDGE
    side = which_ref[0]
    block = pick_block(half)
    begin = pl.multiple_of(side * half, 8)
    copies = (
        pltpu.make_async_copy(resp_hbm.at[:, :, pl.ds(begin, half)], resp, more_sems.at[0]),
        pltpu.make_async_copy(pot_hbm.at[:, pl.ds(begin, half)], pot, more_sems.at[1]),
    )
    for copy in copies:
        copy.start()
    copies_of = lambda b: band_copies(which_ref, half, block, b, occ_ref, (other_a, other_b), own, other, sems)
    start_bands(half, block, copies_of)
    acc[...] = lap_ref[...]
    spread_sides(acc, starts_ref, low_coef, high_coef, low_ref, high_ref)
    for copy in copies:
        copy.wait()

    def base(f, start, size):
        at = pl.ds(pl.multiple_of(start, 8), size)
        re, im = resp[f // 2, 0, at], resp[f // 2, 1, at]
        if f % 2 == 0:
            prod = pot[0, at] * re - pot[1, at] * im
        else:
            prod = pot[0, at] * im + pot[1, at] * re
        return -prod - acc[f, shift_rows(start, size)]

    def store(f, start, value):
        out_ref[f, shift_rows(start, block)] = value

    occupied_into(store, half, fields, sums_ref, side, own, other, base, scale, block, copies_of)
    write_edges(edge_ref, out_ref, half)
    correlate_into(red, out_ref, EDGE, half, own, other)
    dots_into(red_dot, half, fields, [(out_ref, out_ref)])
    write_sums(sum_ref, side, red)
    sum_ref[2:3] = sum_rows(red_dot[0 : fields // 2])


def field_outputs(fields, half, cols):
    return (
        jax.ShapeDtypeStruct((fields, half + 2 * EDGE, cols), jnp.float32),
        jax.ShapeDtypeStruct((fields, 2 * EDGE, cols), jnp.float32),
        jax.ShapeDtypeStruct((8, 128), jnp.float32),
    )


def residual_call(scale, which, starts, low_coef, high_coef, sums, lap, low_img, high_img, psi_occ, other, resp, pot):
    fields, long, cols = lap.shape
    half = long - 2 * EDGE - WIN
    return pl.pallas_call(
        functools.partial(residual_kernel, scale),
        out_shape=field_outputs(fields, half, cols),
        in_specs=[SMEM] * 5 + [VMEM] * 3 + [HBM] * 5,
        out_specs=(VMEM,) * 3,
        scratch_shapes=[
            pltpu.VMEM(lap.shape, jnp.float32),
            pltpu.VMEM(psi_occ.shape[:2] + (half, cols), jnp.float32),
            pltpu.VMEM(psi_occ.shape[:2] + (half, cols), jnp.float32),
            pltpu.VMEM(resp.shape[:2] + (half, cols), jnp.float32),
            pltpu.VMEM((2, half, cols), jnp.float32),
            pltpu.VMEM((2, 128, 8, 128), jnp.float32),
            pltpu.VMEM((16, 8, 128), jnp.float32),
            pltpu.SemaphoreType.DMA((3, half // pick_block(half))),
            pltpu.SemaphoreType.DMA((2,)),
        ],
        compiler_params=params(16),
        name="residual",
    )(which, starts, low_coef, high_coef, sums, lap, low_img, high_img, psi_occ, *other, resp, pot)


def image_kernel(scale, which_ref, starts_ref, low_coef, high_coef, sums_ref, lap_ref, low_ref, high_ref,
                 res_ref, occ_ref, other_a, other_b, out_ref, edge_ref, sum_ref,
                 acc, own, other, red, red_dot, sems):
    fields, wide, cols = out_ref.shape
    half = wide - 2 * EDGE
    side = which_ref[0]
    block = pick_block(half)
    copies_of = lambda b: band_copies(which_ref, half, block, b, occ_ref, (other_a, other_b), own, other, sems)
    start_bands(half, block, copies_of)
    acc[...] = lap_ref[...]
    spread_sides(acc, starts_ref, low_coef, high_coef, low_ref, high_ref)

    def base(f, start, size):
        return acc[f, shift_rows(start, size)]

    def store(f, start, value):
        out_ref[f, shift_rows(start, block)] = value

    occupied_into(store, half, fields, sums_ref, side, own, other, base, scale, block, copies_of)
    write_edges(edge_ref, out_ref, half)
    correlate_into(red, out_ref, EDGE, half, own, other)
    dots_into(red_dot, half, fields, [(res_ref, out_ref), (out_ref, out_ref)])
    write_sums(sum_ref, side, red)
    sum_ref[2:3] = sum_rows(red_dot[0:fields])


def image_call(scale, which, starts, low_coef, high_coef, sums, lap, low_img, high_img, res, psi_occ, other):
    fields, long, cols = lap.shape
    half = long - 2 * EDGE - WIN
    return pl.pallas_call(
        functools.partial(image_kernel, scale),
        out_shape=field_outputs(fields, half, cols),
        in_specs=[SMEM] * 5 + [VMEM] * 4 + [HBM] * 3,
        out_specs=(VMEM,) * 3,
        scratch_shapes=[
            pltpu.VMEM(lap.shape, jnp.float32),
            pltpu.VMEM(psi_occ.shape[:2] + (half, cols), jnp.float32),
            pltpu.VMEM(psi_occ.shape[:2] + (half, cols), jnp.float32),
            pltpu.VMEM((2, 128, 8, 128), jnp.float32),
            pltpu.VMEM((16, 8, 128), jnp.float32),
            pltpu.SemaphoreType.DMA((3, half // pick_block(half))),
        ],
        compiler_params=params(16),
        name="image",
    )(which, starts, low_coef, high_coef, sums, lap, low_img, high_img, res, psi_occ, *other)


def local_kernel(starts_ref, coef_ref, plane_ref, zsum_ref, img_ref, low_ref, high_ref, field_ref, part_ref,
                 out_ref, sum_ref, acc, red_dot, sem):
    fields = acc.shape[0]
    half = zsum_ref.shape[1]
    spread_all(acc, plane_ref, zsum_ref, starts_ref, coef_ref, ((img_ref, 1), (low_ref, 1), (high_ref, 0)))
    copy = pltpu.make_async_copy(acc, out_ref, sem)
    copy.start()
    dots_into(red_dot, half, fields, [(field_ref, acc)])
    sum_ref[...] = part_ref[...]
    sum_ref[3:4] = sum_rows(red_dot[0 : fields // 2])
    copy.wait()


def local_call(starts, local, images, field, part):
    coef, plane, zsum = local
    return pl.pallas_call(
        local_kernel,
        out_shape=(
            jax.ShapeDtypeStruct(plane.shape, jnp.float32),
            jax.ShapeDtypeStruct((8, 128), jnp.float32),
        ),
        in_specs=[SMEM] * 2 + [VMEM] * 7,
        out_specs=(HBM, VMEM),
        scratch_shapes=[
            pltpu.VMEM(plane.shape, jnp.float32),
            pltpu.VMEM((16, 8, 128), jnp.float32),
            pltpu.SemaphoreType.DMA,
        ],
        compiler_params=params(10),
        name="local",
    )(starts, coef, plane, zsum, *images, field, part)


def last_kernel(which_ref, sums_ref, mix_ref, res_hbm, first_hbm, second_hbm, occ_ref, other_a, other_b,
                out_ref, res, first, second, own, other, sems, more_sems):
    fields, half, cols = out_ref.shape
    side = which_ref[0]
    block = pick_block(half)

    def copies_of(b):
        at = pl.ds(pl.multiple_of(b * block, 8), block)
        moved = shift_rows(b * block, block)
        own_copies = tuple(
            pltpu.make_async_copy(src.at[:, moved], dst.at[:, at], more_sems.at[j, b])
            for j, (src, dst) in enumerate(((res_hbm, res), (first_hbm, first), (second_hbm, second)))
        )
        return own_copies + band_copies(which_ref, half, block, b, occ_ref, (other_a, other_b), own, other, sems)

    ahead = 2

    def start(b):
        for copy in copies_of(b):
            copy.start()

    for b in range(ahead):
        start(b)

    def base(f, start, size):
        n = f // 2
        at = pl.ds(pl.multiple_of(start, 8), size)
        return res[f, at] + mix_ref[0, n] * first[f, at] + mix_ref[1, n] * second[f, at]

    def store(f, start, value):
        out_ref[f, pl.ds(pl.multiple_of(start, 8), block)] = value

    occupied_into(store, half, fields, sums_ref, side, own, other, base, 1.0, block, copies_of, start, ahead)


def last_call(which, sums, mix, res, first, second, psi_occ, other):
    fields, wide, cols = res.shape
    half = wide - 2 * EDGE
    blocks = half // pick_block(half)
    field = pltpu.VMEM((fields, half, cols), jnp.float32)
    return pl.pallas_call(
        last_kernel,
        out_shape=jax.ShapeDtypeStruct((fields, half, cols), jnp.float32),
        in_specs=[SMEM] * 3 + [HBM] * 6,
        out_specs=VMEM,
        scratch_shapes=[
            field,
            field,
            field,
            pltpu.VMEM(psi_occ.shape[:2] + (half, cols), jnp.float32),
            pltpu.VMEM(psi_occ.shape[:2] + (half, cols), jnp.float32),
            pltpu.SemaphoreType.DMA((3, blocks)),
            pltpu.SemaphoreType.DMA((3, blocks)),
        ],
        compiler_params=params(52),
        name="last",
    )(which, sums, mix, res, first, second, psi_occ, *other)


def xor_sum(block, bits):
    count = lax.axis_size("space") * lax.axis_size("occ")
    masks = [0]
    for bit in bits:
        masks = masks + [mask | bit for mask in masks]
    parts = [block]
    for mask in masks[1:]:
        parts.append(lax.ppermute(block, ("space", "occ"), [(i, i ^ mask) for i in range(count)]))
    while len(parts) > 1:
        parts = [parts[j] + parts[j + 1] for j in range(0, len(parts), 2)]
    return parts[0]


def total(block, groups=None):
    count = lax.axis_size("space")
    bit = 2
    steps = []
    while count > 1:
        wide = count % 4 == 0
        steps.append((bit, 2 * bit) if wide else (bit,))
        bit, count = (4 * bit, count // 4) if wide else (2 * bit, count // 2)
    steps.append((1,))
    for bits in steps[groups] if groups is not None else steps:
        block = xor_sum(block, bits)
    return block


def exchange(block):
    return lax.ppermute(block, "occ", SWAP)


def from_behind(block, distance):
    count = lax.axis_size("space")
    return lax.ppermute(block, "space", [((i - distance) % count, i) for i in range(count)])


def window_images(x_cell, y_cell, offsets, values, theta_y, rows_y, planes):
    y_raw = y_cell[:, None] + offsets[None, :, 2]
    y_wrap = jnp.floor_divide(y_raw, rows_y)
    y_at = y_raw - y_wrap * rows_y
    angles = theta_y * y_wrap.astype(jnp.float32)
    row = x_cell[:, None] + offsets[None, :, 1] + RAD
    slot = []
    for plane in planes:
        wanted = (row[:, None, :] == jnp.arange(WIN, dtype=jnp.int32)[None, :, None]) & (
            offsets[:, 0] == plane
        )[None, None, :]
        slot.append(wanted)
    slots = jnp.stack(slot, axis=1)
    weights = jnp.stack([values * jnp.cos(angles), values * jnp.sin(angles)], axis=1)
    left = jnp.where(slots[:, :, None], weights[:, None, :, None, :], 0.0)
    atoms = left.shape[0]
    left = left.reshape(atoms, len(planes) * 2 * WIN, -1)
    right = (y_at[:, :, None] == jnp.arange(rows_y, dtype=jnp.int32)[None, None, :]).astype(jnp.float32)
    image = jnp.einsum("apk,aky->apy", left, right, precision=PRECISE)
    return image.reshape(atoms, len(planes), 2, WIN, rows_y)


def shards(
    psi_occ,
    psi_resp,
    initial_guess,
    local_potential,
    potential_change,
    band_energy,
    q_index,
    atom_cells,
    offsets,
    projector,
    strength,
):
    slab_count = lax.axis_size("space")
    slab_index = lax.axis_index("space")
    side = lax.axis_index("occ")
    layers, rows_x, rows_y = local_potential.shape
    half = rows_x // 2
    atoms = atom_cells.shape[0]
    bands = psi_resp.shape[0]
    fields = 2 * bands
    weight = 1.0 / (layers * slab_count * rows_x * rows_y)
    thetas = q_index.astype(jnp.float32) * (2.0 * math.pi / QDIV)
    which = side.astype(jnp.int32).reshape(1)
    where = jnp.stack([side, slab_index]).astype(jnp.int32)

    occ = psi_occ.reshape(psi_occ.shape[0], 2, rows_x, rows_y)
    resp = psi_resp.reshape(bands, 2, rows_x, rows_y)
    guess = initial_guess.reshape(bands, 2, rows_x, rows_y)
    change = potential_change.reshape(2, rows_x, rows_y)

    cell_rows = jnp.pad(
        jnp.concatenate([atom_cells.astype(jnp.float32), strength[:, None]], axis=1),
        ((0, 0), (0, projector.shape[1] - 4)),
    )
    packed = jnp.concatenate([projector, cell_rows], axis=0)
    guess_mid, *rot = prep_call(slab_count, where, q_index, guess, packed)
    first_sums, *occ_send = first_corr(which, occ, resp, change, guess)
    occ_other = [exchange(block) for block in occ_send]
    first_sums = total(first_sums, slice(0, 1))
    first_sums, guess_mid = lax.optimization_barrier((first_sums, guess_mid))
    first_sums = xor_sum(xor_sum(first_sums, (8,)), (16,))
    first_sums = xor_sum(first_sums, (32,))
    first_sums, occ_other[0] = lax.optimization_barrier((first_sums, occ_other[0]))
    first_sums = xor_sum(first_sums, (64,))
    guess_low = from_behind(guess_mid, 1)
    guess_high = from_behind(guess_mid, -1)

    def unpack(block):
        rows = block[:, half + 2 * EDGE :].reshape(-1, rows_y)
        return rows[:atoms], rows[atoms : 2 * atoms]

    below, below_cells = unpack(guess_low)
    above, above_cells = unpack(guess_high)
    cells = [atom_cells]
    for rows in (below_cells, above_cells):
        cells.append(rows[:, :3].astype(jnp.int32))
    all_x = jnp.stack([c[:, 1] for c in cells])
    all_y = jnp.stack([c[:, 2] for c in cells])
    at_row = jnp.mod(all_x - RAD - side * half + EDGE, rows_x)
    inner = at_row % 8
    touching = at_row < half + EDGE
    put_starts = jnp.where(touching, at_row - inner, half + 2 * EDGE).astype(jnp.int32)
    get_starts = jnp.where(touching, at_row - inner, 0).astype(jnp.int32)
    own_row = jnp.mod(atom_cells[:, 1] - RAD - side * half + EDGE, rows_x)
    own_inner = own_row % 8
    own_starts = jnp.where(own_row < half + EDGE, own_row - own_inner, 0).astype(jnp.int32)
    strengths = jnp.stack([strength, below_cells[:, 3], above_cells[:, 3]])
    img = window_images(own_inner, atom_cells[:, 2], offsets, projector, thetas[2], rows_y, (-1, 0, 1))
    low_img = window_images(inner[1], all_y[1], offsets, below, thetas[2], rows_y, (0, 1))
    high_img = window_images(inner[2], all_y[2], offsets, above, thetas[2], rows_y, (-1, 0))
    images = (img, low_img, high_img)

    def local_part(mid, low, high):
        zsum, proj, up, down = gather(own_starts, rot, strength, mid, low, high, img, half)
        low_coef = from_behind(up, 1)
        high_coef = from_behind(down, -1)
        lap = stencil(which, band_energy, rot, put_starts, proj, mid, zsum, local_potential, img)
        return put_starts, low_coef, high_coef, lap

    def far_part(mid):
        low = from_behind(mid, 1)
        high = from_behind(mid, -1)
        plane, part_low, part_high, down, up = plane_call(
            which, band_energy, get_starts, rot, strengths, mid, local_potential, low_img, high_img
        )
        got = (from_behind(up, 2), from_behind(down, -2))
        zsum, coef = gather_all(get_starts, rot, strengths, mid, low, high, *images, (part_low, part_high), got)
        return coef, plane, zsum

    starts, low_coef, high_coef, lap = local_part(guess_mid, guess_low, guess_high)
    first_sums, lap = lax.optimization_barrier((first_sums, lap))
    first_sums = total(first_sums, slice(-1, None))
    residual, edges, part = residual_call(
        weight, which, starts, low_coef, high_coef, first_sums, lap, low_img, high_img, occ, occ_other, resp, change
    )
    tot = total(part)
    norm0 = tot[2, :bands]
    residual = fill_call(rot, exchange(edges), residual)
    starts, low_coef, high_coef, lap = local_part(residual, from_behind(residual, 1), from_behind(residual, -1))
    image, edges, part = image_call(
        SHIFT_WEIGHT * weight, which, starts, low_coef, high_coef, tot, lap, low_img, high_img, residual, occ, occ_other
    )
    image = fill_call(rot, exchange(edges), image)
    image_other = exchange(image)
    image2, part = local_call(put_starts, far_part(image), images, image, part)
    part, image_other, residual_send = lax.optimization_barrier((part, image_other, residual))
    residual_other = exchange(residual_send)
    tot = total(part, slice(0, 2))
    tot, residual_other = lax.optimization_barrier((tot, residual_other))
    tot = total(tot, slice(2, None))
    sums = tot[0:2]
    cross = tot[2, :bands]
    square = tot[2, bands : 2 * bands]
    occ_square = jnp.sum((sums * sums).reshape(-1, bands, 2), axis=(0, 2))
    triple = tot[3, :bands] + SHIFT_WEIGHT * weight * occ_square
    step0 = norm0 / cross
    norm1 = norm0 - 2.0 * step0 * cross + step0 * step0 * square
    growth = norm1 / norm0
    lead = 1.0 + growth
    curvature = lead * lead * cross - 2.0 * lead * step0 * square + step0 * step0 * triple
    step1 = norm1 / curvature
    mix0 = -step0 - step1 * lead
    mix1 = step1 * step0
    per_lane = jnp.tile(jnp.repeat(mix1, 2), sums.shape[1] // fields)
    last_sums = SHIFT_WEIGHT * weight * sums * per_lane[None, :]
    mine = last_call(which, last_sums, jnp.stack([mix0, mix1]), residual, image, image2, occ, occ_other)
    mine, residual_other, image_other = lax.optimization_barrier((mine, residual_other, image_other))
    theirs = exchange(mine)

    def join(own_half, other_half):
        lower = jnp.where(side == 0, own_half, other_half)
        upper = jnp.where(side == 0, other_half, own_half)
        return jnp.concatenate([lower, upper], axis=1).reshape(bands, 2, 1, rows_x, rows_y)

    inside = lambda v: v[:, EDGE : EDGE + half]
    wide = lambda v: v[:, None, None, None, None]
    response = (
        initial_guess
        + wide(step0 + step1 * lead) * join(inside(residual), inside(residual_other))
        - wide(step0 * step1) * join(inside(image), inside(image_other))
    )
    return response, join(mine, theirs)


def solution(mesh):
    return jax.shard_map(
        shards,
        mesh=mesh,
        in_specs=(
            P("occ", None, "space", None, None),
            P("resp", None, "space", None, None),
            P("resp", None, "space", None, None),
            P("space", None, None),
            P(None, "space", None, None),
            P("resp"),
            P(),
            P("space", None),
            P(),
            P("space", None),
            P("space"),
        ),
        out_specs=(P("resp", None, "space", None, None), P("resp", None, "space", None, None)),
        check_vma=False,
    )
```
